32 devices in a mesh: trow: 16 (over z, x, core), tcol: 2 (over y).
Axes of the slice: x: 2, y: 2, z: 4, core: 2. Of those that a mesh axis runs over, the one named last changes fastest.
Arguments:
- green_lesser: bfloat16 [2, 128, 128, 512], P(None, 'trow', 'tcol'), may hold values from -6 to 6
- green_greater: bfloat16 [2, 128, 128, 512], P(None, 'trow', 'tcol'), may hold values from -6 to 6
- lattice_map: int32 [512], replicated, may hold values from 0 to 511, each once
- time_offset: int32 [1], replicated, may hold values from 0 to 63
Outputs:
- collision_lesser: bfloat16 [2, 128, 128, 512], P(None, 'trow', 'tcol')
- collision_greater: bfloat16 [2, 128, 128, 512], P(None, 'trow', 'tcol')
The draws below stay inside these ranges and needn't reach their ends.
Inputs may be any that keep to these rules, and one draw needn't show every extreme that they name: `lattice_map`: every lattice momentum index 0 to 511 appears exactly once.
All inputs are finite; a program needn't handle non-finite values.
Results may differ from the reference program's by a relative error of at most 0.011.
Values may be sent and summed in bfloat16 or wider, within the bound.
No kernel may reach another device: no remote copies, remote signals or barrier semaphores. Data moves between devices by JAX's collectives and lax.ppermute only.
A program may use at most 64 MiB of HBM per device.

```python
import math
import jax
import jax.numpy as jnp
from jax import lax

K = 512
PERIOD = 64
NT = 128


def block_levels(own_key, dims, shards, least, top_value):
    def one(axis_at, blocks):
        heights = jax.random.uniform(jax.random.fold_in(jax.random.fold_in(own_key, 6), axis_at), (blocks,), jnp.float32, least / len(shards), top_value / len(shards))
        return jnp.repeat(jnp.exp(heights), dims[axis_at] // blocks).reshape((-1,) + (1,) * (len(dims) - axis_at - 1))

    loudness = one(*shards[0])
    for cut in shards[1:]:
        loudness = loudness * one(*cut)
    return loudness


def bell_draw(own_key, extent, scale, reach, pieces=(), kind=jnp.bfloat16):
    array = jax.random.normal(own_key, extent, jnp.float32) * scale
    if len(pieces) > 0:
        array = block_levels(own_key, extent, pieces, -0.22, 0.18) * array
    return jnp.clip(array, min=-reach, max=reach).astype(kind)


def setup_inputs(seed: int = 0) -> dict:
    key_list = jax.random.split(jax.random.key(seed), 5)
    return {
        "green_lesser": bell_draw(key_list[0], (2, NT, NT, K), 1.0, 6.0, ((1, 16), (2, 2))),
        "green_greater": bell_draw(key_list[1], (2, NT, NT, K), 1.0, 6.0, ((1, 16), (2, 2))),
        "lattice_map": jax.random.permutation(key_list[2], K).astype(jnp.int32),
        "time_offset": jax.random.randint(key_list[3], (1,), 0, PERIOD).astype(jnp.int32),
    }


step_size = 0.01
drive_depth = 0.5

def widened(values):
    return lax.optimization_barrier(values).astype(jnp.float32)

def transform(real_part, imaginary_part, cosines, sines, sign, norm_factor):
    old_shape = real_part.shape
    flat_real = real_part.reshape(-1, old_shape[-1])
    flat_imaginary = imaginary_part.reshape(-1, old_shape[-1])
    cosine_real = jnp.dot(flat_real, cosines, preferred_element_type=jnp.float32)
    cosine_imaginary = jnp.dot(flat_imaginary, cosines, preferred_element_type=jnp.float32)
    sine_real = jnp.dot(flat_real, sines, preferred_element_type=jnp.float32)
    sine_imaginary = jnp.dot(flat_imaginary, sines, preferred_element_type=jnp.float32)
    out_real = ((cosine_real - sign * sine_imaginary) * norm_factor).reshape(old_shape).astype(jnp.bfloat16)
    out_imaginary = ((sign * sine_real + cosine_imaginary) * norm_factor).reshape(old_shape).astype(jnp.bfloat16)
    return (out_real, out_imaginary)

def second_born(first_real, first_imaginary, other_real, other_imaginary, coupling):
    square_real = first_real * first_real - first_imaginary * first_imaginary
    square_imaginary = 2.0 * first_real * first_imaginary
    out_real = coupling * (square_real * other_real - square_imaginary * other_imaginary)
    out_imaginary = coupling * (square_real * other_imaginary + square_imaginary * other_real)
    return (out_real.astype(jnp.bfloat16), out_imaginary.astype(jnp.bfloat16))

def contract(left, right):
    return jnp.einsum('kts,ksu->ktu', left, right, precision=lax.Precision.HIGHEST)

def volterra(retarded, sigma, greens, advanced):
    real_sum = contract(retarded[0], greens[0]) - contract(retarded[1], greens[1]) + contract(sigma[0], advanced[0]) - contract(sigma[1], advanced[1])
    imaginary_sum = contract(retarded[0], greens[1]) + contract(retarded[1], greens[0]) + contract(sigma[0], advanced[1]) + contract(sigma[1], advanced[0])
    return (real_sum, imaginary_sum)

def finish(parts):
    return jnp.stack([jnp.transpose(step_size * component, (1, 2, 0)) for component in parts]).astype(jnp.bfloat16)

def momentum_first(values):
    return jnp.transpose(widened(values), (2, 0, 1))

def reference(green_lesser, green_greater, lattice_map, time_offset):
    site_index = jnp.arange(K, dtype=jnp.int32)
    phases = (lattice_map[:, None] * site_index[None, :] % K).astype(jnp.float32) * (2.0 * math.pi / K)
    cosines = jnp.cos(phases).astype(jnp.bfloat16)
    sines = jnp.sin(phases).astype(jnp.bfloat16)
    norm_factor = 1.0 / math.sqrt(K)
    site_lesser = transform(green_lesser[0], green_lesser[1], cosines, sines, 1.0, norm_factor)
    site_greater = transform(green_greater[0], green_greater[1], cosines, sines, 1.0, norm_factor)
    partner = (K - site_index) % K

    def mirror_of(field):
        return jnp.swapaxes(widened(field)[:, :, partner], 0, 1)
    time_steps = jnp.arange(NT, dtype=jnp.int32)
    coupling_line = 1.0 + drive_depth * jnp.cos(((time_offset[0] + time_steps) % PERIOD).astype(jnp.float32) * (2.0 * math.pi / PERIOD))
    coupling = (coupling_line[:, None] * coupling_line[None, :])[:, :, None]
    self_lesser = second_born(widened(site_lesser[0]), widened(site_lesser[1]), mirror_of(site_greater[0]), mirror_of(site_greater[1]), coupling)
    self_greater = second_born(widened(site_greater[0]), widened(site_greater[1]), mirror_of(site_lesser[0]), mirror_of(site_lesser[1]), coupling)
    sigma_lesser = [momentum_first(component) for component in transform(self_lesser[0], self_lesser[1], cosines.T, sines.T, -1.0, norm_factor)]
    sigma_greater = [momentum_first(component) for component in transform(self_greater[0], self_greater[1], cosines.T, sines.T, -1.0, norm_factor)]
    green_less = [momentum_first(green_lesser[0]), momentum_first(green_lesser[1])]
    green_more = [momentum_first(green_greater[0]), momentum_first(green_greater[1])]
    lower_mask = time_steps[None, :] <= time_steps[:, None]
    upper_mask = time_steps[:, None] <= time_steps[None, :]
    retarded = [widened(jnp.where(lower_mask, sigma_greater[index] - sigma_lesser[index], 0.0).astype(jnp.bfloat16)) for index in range(2)]
    advanced = [widened(jnp.where(upper_mask, green_less[index] - green_more[index], 0.0).astype(jnp.bfloat16)) for index in range(2)]
    lesser_out = volterra(retarded, sigma_lesser, green_less, advanced)
    greater_out = volterra(retarded, sigma_greater, green_more, advanced)
    return (finish(lesser_out), finish(greater_out))
```

```python
import functools
import math

import jax
import jax.numpy as jnp
from jax import lax
from jax.experimental import pallas as pl
from jax.experimental.pallas import tpu as pltpu
from jax.sharding import Mesh, PartitionSpec as P

F32 = jnp.float32
BF16 = jnp.bfloat16
LANES = 128

PERIOD = 64


step_size = 0.01
drive_depth = 0.5


def regroup(blocks):
    return lax.all_to_all(
        lax.all_to_all(blocks, "trow", split_axis=1, concat_axis=1, tiled=True),
        "tcol",
        split_axis=2,
        concat_axis=2,
        tiled=True,
    )


def pack_blocks(spectral, row_parts, col_parts):
    stacked, extent, tile_cells = spectral.shape
    return spectral.reshape(
        stacked, row_parts, col_parts, extent // (row_parts * col_parts), tile_cells
    )


def spread_times(blocks, tile_rows, tile_cols):
    stacked, row_parts, col_parts, local_count, tile_cells = blocks.shape
    shaped = blocks.reshape(stacked, row_parts, col_parts, local_count, tile_rows, tile_cols)
    return shaped.transpose(0, 3, 1, 4, 2, 5).reshape(
        stacked, local_count, row_parts * tile_rows, col_parts * tile_cols
    )


def gather_tiles(full, row_parts, col_parts):
    stacked, local_count, window, window_cols = full.shape
    tile_rows = window // row_parts
    tile_cols = window_cols // col_parts
    shaped = full.reshape(stacked, local_count, row_parts, tile_rows, col_parts, tile_cols)
    return shaped.transpose(0, 2, 4, 1, 3, 5).reshape(
        stacked, row_parts, col_parts, local_count, tile_rows * tile_cols
    )


def mirrored(full, keep_pair):
    stacked, local_count, window, window_cols = full.shape
    paired = full.reshape(stacked, local_count // 2, 2, window, window_cols)
    swapped = jnp.where(keep_pair[None, :, None, None, None], paired, paired[:, :, ::-1])
    return jnp.swapaxes(swapped.reshape(stacked, local_count, window, window_cols), 2, 3)


def second_born(first_real, first_imaginary, other_real, other_imaginary, coupling):
    square_real = first_real * first_real - first_imaginary * first_imaginary
    square_imaginary = 2.0 * first_real * first_imaginary
    out_real = coupling * (square_real * other_real - square_imaginary * other_imaginary)
    out_imaginary = coupling * (square_real * other_imaginary + square_imaginary * other_real)
    return (out_real, out_imaginary)


def collide(
    retarded_real,
    retarded_imaginary,
    self_real,
    self_imaginary,
    green_real,
    green_imaginary,
    advanced_real,
    advanced_imaginary,
):
    minus_left = jnp.concatenate(
        [retarded_real, -retarded_imaginary, self_real, -self_imaginary], axis=2
    )
    plus_left = jnp.concatenate(
        [retarded_real, retarded_imaginary, self_real, self_imaginary], axis=2
    )
    real_right = jnp.concatenate(
        [green_real, green_imaginary, advanced_real, advanced_imaginary], axis=1
    )
    imaginary_right = jnp.concatenate(
        [green_imaginary, green_real, advanced_imaginary, advanced_real], axis=1
    )
    out_real = jnp.einsum(
        "kts,ksu->ktu", minus_left, real_right, preferred_element_type=jnp.float32
    )
    out_imaginary = jnp.einsum(
        "kts,ksu->ktu", plus_left, imaginary_right, preferred_element_type=jnp.float32
    )
    return (out_real, out_imaginary)


def general_body(green_lesser, green_greater, lattice_map, time_offset):
    tile_rows = green_lesser.shape[1]
    tile_cols = green_lesser.shape[2]
    momenta = green_lesser.shape[3]
    row_parts = lax.axis_size("trow")
    col_parts = lax.axis_size("tcol")
    window = tile_rows * row_parts
    tile_cells = tile_rows * tile_cols
    local_count = momenta // (row_parts * col_parts)
    norm_factor = 1.0 / math.sqrt(momenta)
    greens = (
        jnp.concatenate([green_lesser, green_greater], axis=0)
        .reshape(4, tile_cells, momenta)
        .transpose(0, 2, 1)
    )
    positions = jnp.arange(momenta, dtype=jnp.int32)
    halves = positions // 2
    site_order = jnp.where(
        positions == 1, momenta // 2, jnp.where(positions % 2 == 0, halves, momenta - halves)
    )
    phases = (lattice_map[:, None] * site_order[None, :] % momenta).astype(jnp.float32) * (
        2.0 * math.pi / momenta
    )
    cosines = jnp.cos(phases).astype(jnp.bfloat16)
    sines = jnp.sin(phases).astype(jnp.bfloat16)
    ahead_blocks = lax.all_to_all(
        lax.all_to_all(
            pack_blocks(greens, row_parts, col_parts),
            "trow",
            split_axis=1,
            concat_axis=1,
            tiled=True,
        ),
        "tcol",
        split_axis=2,
        concat_axis=2,
        tiled=True,
    )
    green_moment = spread_times(ahead_blocks, tile_rows, tile_cols)
    forward_table = jnp.concatenate([cosines, sines], axis=1)
    products = jnp.einsum("cjm,jr->crm", greens, forward_table, preferred_element_type=jnp.float32)
    site_space = jnp.stack(
        [
            (products[0, :momenta] - products[1, momenta:]) * norm_factor,
            (products[0, momenta:] + products[1, :momenta]) * norm_factor,
            (products[2, :momenta] - products[3, momenta:]) * norm_factor,
            (products[2, momenta:] + products[3, :momenta]) * norm_factor,
        ]
    ).astype(jnp.bfloat16)
    site_full = spread_times(
        regroup(pack_blocks(site_space, row_parts, col_parts)), tile_rows, tile_cols
    )
    site_block = lax.axis_index("trow") * col_parts + lax.axis_index("tcol")
    keep_pair = site_block * (local_count // 2) + jnp.arange(local_count // 2, dtype=jnp.int32) == 0
    mirror = mirrored(site_full, keep_pair).astype(jnp.float32)
    direct = site_full.astype(jnp.float32)
    time_steps = jnp.arange(window, dtype=jnp.int32)
    coupling_line = 1.0 + drive_depth * jnp.cos(
        ((time_offset[0] + time_steps) % PERIOD).astype(jnp.float32) * (2.0 * math.pi / PERIOD)
    )
    coupling = coupling_line[:, None] * coupling_line[None, :]
    self_lesser = second_born(direct[0], direct[1], mirror[2], mirror[3], coupling)
    self_greater = second_born(direct[2], direct[3], mirror[0], mirror[1], coupling)
    self_sites = jnp.stack(
        [self_lesser[0], self_lesser[1], self_greater[0], self_greater[1]]
    ).astype(jnp.bfloat16)
    self_tiles = regroup(gather_tiles(self_sites, row_parts, col_parts)).reshape(
        4, momenta, tile_cells
    )
    inverse_table = jnp.concatenate([cosines, sines], axis=0)
    spectral_terms = jnp.einsum(
        "cum,ju->cjm", self_tiles, inverse_table, preferred_element_type=jnp.float32
    )
    self_spectral = jnp.stack(
        [
            (spectral_terms[0, :momenta] + spectral_terms[1, momenta:]) * norm_factor,
            (spectral_terms[1, :momenta] - spectral_terms[0, momenta:]) * norm_factor,
            (spectral_terms[2, :momenta] + spectral_terms[3, momenta:]) * norm_factor,
            (spectral_terms[3, :momenta] - spectral_terms[2, momenta:]) * norm_factor,
        ]
    ).astype(jnp.bfloat16)
    self_moment = spread_times(
        regroup(pack_blocks(self_spectral, row_parts, col_parts)), tile_rows, tile_cols
    )
    lower_mask = time_steps[None, :] <= time_steps[:, None]
    upper_mask = time_steps[:, None] <= time_steps[None, :]
    retarded = jnp.where(
        lower_mask, self_moment[2:4].astype(jnp.float32) - self_moment[0:2].astype(jnp.float32), 0.0
    ).astype(jnp.bfloat16)
    advanced = jnp.where(
        upper_mask,
        green_moment[0:2].astype(jnp.float32) - green_moment[2:4].astype(jnp.float32),
        0.0,
    ).astype(jnp.bfloat16)
    lesser_out = collide(
        retarded[0],
        retarded[1],
        self_moment[0],
        self_moment[1],
        green_moment[0],
        green_moment[1],
        advanced[0],
        advanced[1],
    )
    greater_out = collide(
        retarded[0],
        retarded[1],
        self_moment[2],
        self_moment[3],
        green_moment[2],
        green_moment[3],
        advanced[0],
        advanced[1],
    )
    collisions = (
        jnp.stack([lesser_out[0], lesser_out[1], greater_out[0], greater_out[1]]) * step_size
    ).astype(jnp.bfloat16)
    out_tiles = regroup(gather_tiles(collisions, row_parts, col_parts)).reshape(
        4, momenta, tile_cells
    )
    out_tiles = out_tiles.transpose(0, 2, 1).reshape(4, tile_rows, tile_cols, momenta)
    return (out_tiles[0:2], out_tiles[2:4])


def vmem_params():
    return pltpu.CompilerParams(vmem_limit_bytes=48 * 1024 * 1024)


def whole(count):
    return [pl.BlockSpec(memory_space=pltpu.VMEM)] * count


def spread_kernel(tile, out, lines):
    _, rows, _, momenta = tile.shape
    for t in range(rows):
        slab = jnp.concatenate([tile[0, t], tile[1, t]], axis=0).astype(F32)
        lines[pl.ds(t, momenta, stride=rows), :] = slab.T
    out[...] = lines[...].astype(BF16)


def spread(tile):
    _, rows, cols, momenta = tile.shape
    shape = (momenta * rows, 2 * cols)
    return pl.pallas_call(
        spread_kernel,
        out_shape=jax.ShapeDtypeStruct(shape, BF16),
        in_specs=whole(1),
        out_specs=whole(1)[0],
        scratch_shapes=[pltpu.VMEM(shape, F32)],
        compiler_params=vmem_params(),
        name="spread",
    )(tile)


def collect_kernel(rows_ref, lesser, greater, lines):
    lines[...] = rows_ref[...].astype(F32)
    _, rows, cols, momenta = lesser.shape
    for k in range(2 * rows):
        slab = lines[pl.ds(k, momenta, stride=2 * rows), :].T.astype(BF16)
        out = lesser if k < rows else greater
        out[0, k % rows] = slab[:cols]
        out[1, k % rows] = slab[cols:]


def collect(rows_array, tile_shape):
    shape = jax.ShapeDtypeStruct(tile_shape, BF16)
    return pl.pallas_call(
        collect_kernel,
        out_shape=(shape, shape),
        in_specs=whole(1),
        out_specs=tuple(whole(2)),
        scratch_shapes=[pltpu.VMEM(rows_array.shape, F32)],
        compiler_params=vmem_params(),
        name="collect",
    )(rows_array)


def site_kernel(norm_factor, tile, table, out):
    both = jnp.concatenate([tile[0], tile[1]], axis=1)
    momenta = tile.shape[2]
    for part in range(2):
        product = jnp.dot(
            both, table[:, part * momenta : (part + 1) * momenta], preferred_element_type=F32
        )
        out[part] = (product * norm_factor).astype(BF16)


def to_sites(tile, table, norm_factor):
    return pl.pallas_call(
        functools.partial(site_kernel, norm_factor),
        out_shape=jax.ShapeDtypeStruct(tile.shape, BF16),
        in_specs=whole(2),
        out_specs=whole(1)[0],
        compiler_params=vmem_params(),
        name="to_sites",
    )(tile, table)


def sigma_kernel(norm_factor, rows, own, crossed, table, inverse, coupling, out, mirror, lines):
    blocks, _, block_rows, momenta = crossed.shape
    cols = blocks * block_rows // rows
    real = jnp.concatenate([crossed[i, 0] for i in range(blocks)], axis=0)
    imaginary = jnp.concatenate([crossed[i, 1] for i in range(blocks)], axis=0)
    both = jnp.concatenate([real, -imaginary], axis=1)
    for part in range(2):
        product = jnp.dot(
            both, table[:, part * momenta : (part + 1) * momenta], preferred_element_type=F32
        )
        product = (product * norm_factor).astype(BF16).astype(F32)
        for at in range(momenta // LANES):
            mirror[part, at] = product[:, at * LANES : (at + 1) * LANES]
    for pair in range(rows // 2):
        rights = []
        for t in (2 * pair, 2 * pair + 1):
            other_real, other_imaginary = (
                jnp.concatenate(
                    [
                        mirror[part, at, pl.ds(t, cols, stride=rows), :]
                        for at in range(momenta // LANES)
                    ],
                    axis=1,
                )
                for part in range(2)
            )
            cells = pl.ds(t * cols, cols)
            self_real, self_imaginary = second_born(
                own[0, cells, :].astype(F32),
                own[1, cells, :].astype(F32),
                other_real,
                -other_imaginary,
                coupling[cells, :],
            )
            self_real = self_real.astype(BF16)
            self_imaginary = self_imaginary.astype(BF16)
            rights.append(jnp.concatenate([self_real, self_imaginary], axis=1))
            rights.append(jnp.concatenate([self_imaginary, -self_real], axis=1))
        product = lax.dot_general(
            inverse[...],
            jnp.concatenate(rights, axis=0),
            (((1,), (1,)), ((), ())),
            preferred_element_type=F32,
        ) * norm_factor
        lines[pl.ds(2 * pair, momenta, stride=rows), :] = product[:, : 2 * cols]
        lines[pl.ds(2 * pair + 1, momenta, stride=rows), :] = product[:, 2 * cols :]
    out[...] = lines[...].astype(BF16)


def to_sigma(own, crossed, table, inverse, coupling, rows, norm_factor):
    _, cells, momenta = own.shape
    shape = (momenta * rows, 2 * cells // rows)
    return pl.pallas_call(
        functools.partial(sigma_kernel, norm_factor, rows),
        out_shape=jax.ShapeDtypeStruct(shape, BF16),
        in_specs=whole(5),
        out_specs=whole(1)[0],
        scratch_shapes=[
            pltpu.VMEM((2, momenta // LANES, cells, LANES), F32),
            pltpu.VMEM(shape, F32),
        ],
        compiler_params=vmem_params(),
        name="to_sigma",
    )(own, crossed, table, inverse, coupling)


def volterra_kernel(rows, half_ref, own_l, own_g, far_l, far_g, sig_l, sig_g, out):
    half = half_ref[0]
    sources = own_l.shape[0]
    blocks = sources // 2
    lanes = own_l.shape[2]
    cols = lanes // 2
    near = half * cols
    away = (1 - half) * cols
    first_times = half * cols + lax.broadcasted_iota(jnp.int32, (cols, lanes), 0)
    left_lane = lax.broadcasted_iota(jnp.int32, (cols, lanes), 1)
    left_times = jnp.where(left_lane < cols, near + left_lane, away + left_lane - cols)
    keep_left = left_times <= first_times
    row_at = lax.broadcasted_iota(jnp.int32, (lanes, 2 * lanes), 0)
    inner_times = jnp.where(row_at < cols, near + row_at, away + row_at - cols)
    lane_at = lax.broadcasted_iota(jnp.int32, (lanes, 2 * lanes), 1)
    last_times = lane_at // lanes * cols + lane_at % cols
    keep_right = inner_times <= last_times
    low_lanes = left_lane < cols
    pairs = []

    def tall(ref, at, flipped):
        lines = []
        for block in range(blocks):
            parts = []
            for side in range(2):
                source = 2 * block + (1 - side if flipped else side)
                parts.append(ref[source].astype(F32)[at * rows : (at + 1) * rows])
            lines.append(jnp.concatenate(parts, axis=1))
        return jnp.concatenate(lines, axis=0)

    def wide(ref, at):
        near_lines = []
        far_lines = []
        for block in range(blocks):
            near_lines.append(ref[2 * block + half].astype(F32)[at * rows : (at + 1) * rows])
            far_lines.append(ref[2 * block + 1 - half].astype(F32)[at * rows : (at + 1) * rows])
        near_part = jnp.concatenate(near_lines, axis=0)
        far_part = jnp.concatenate(far_lines, axis=0)
        return (
            jnp.where(low_lanes, near_part, pltpu.roll(far_part, cols, 1)),
            jnp.where(low_lanes, pltpu.roll(near_part, cols, 1), far_part),
        )

    for at in range(2):
        green_l = jnp.concatenate([tall(own_l, at, False), tall(far_l, at, True)], axis=0)
        green_g = jnp.concatenate([tall(own_g, at, False), tall(far_g, at, True)], axis=0)
        advanced = jnp.where(keep_right, green_l - green_g, 0.0).astype(BF16)
        real_l, imaginary_l = wide(sig_l, at)
        real_g, imaginary_g = wide(sig_g, at)
        retarded = jnp.concatenate(
            [
                jnp.where(keep_left, real_g - real_l, 0.0),
                jnp.where(keep_left, imaginary_g - imaginary_l, 0.0),
            ],
            axis=0,
        ).astype(BF16)
        results = []
        for real, imaginary, green in (
            (real_l, imaginary_l, green_l),
            (real_g, imaginary_g, green_g),
        ):
            sigma = jnp.concatenate([real, imaginary], axis=0).astype(BF16)
            left = jnp.concatenate([retarded, sigma], axis=1)
            right = jnp.concatenate([green.astype(BF16), advanced], axis=0)
            product = jnp.dot(left, right, preferred_element_type=F32)
            sides = []
            for side in range(2):
                straight = product[:cols, side * lanes : (side + 1) * lanes]
                turned = pltpu.roll(product[cols:, side * lanes : (side + 1) * lanes], cols, 1)
                sides.append((straight + jnp.where(low_lanes, -turned, turned)) * step_size)
            results.append(sides)
        pairs.append(results)
    for block in range(blocks):
        span = slice(block * rows, (block + 1) * rows)
        for side in range(2):
            lines = [pairs[at][g][side][span] for at in range(2) for g in range(2)]
            out[2 * block + side] = jnp.concatenate(lines, axis=0).astype(BF16)


def volterra(half, own, far, sigma, rows):
    sources, lines, lanes = own[0].shape
    steps = lines // (2 * rows)
    spec = pl.BlockSpec((sources, 2 * rows, lanes), lambda p: (0, p, 0))
    return pl.pallas_call(
        functools.partial(volterra_kernel, rows),
        grid=(steps,),
        out_shape=jax.ShapeDtypeStruct((sources, 2 * lines, lanes), BF16),
        in_specs=[pl.BlockSpec(memory_space=pltpu.SMEM)] + [spec] * 6,
        out_specs=pl.BlockSpec((sources, 4 * rows, lanes), lambda p: (0, p, 0)),
        compiler_params=vmem_params(),
        name="volterra",
    )(half, *own, *far, *sigma)


def halved_body(green_lesser, green_greater, lattice_map, time_offset):
    _, rows, cols, momenta = green_lesser.shape
    half = lax.axis_index("half")
    line = lax.axis_index("line")
    side = lax.axis_index("tcol")
    lines = lax.axis_size("line")
    sides = lax.axis_size("tcol")
    group = lines * sides
    window = rows * lines * lax.axis_size("half")
    norm_factor = 1.0 / math.sqrt(momenta)
    greens = (green_lesser, green_greater)
    corners = [(a, b) for a in range(2) for b in range(2)]
    opposite = [(2 * a + b, 2 * (1 - a) + 1 - b) for a, b in corners]

    def momentum_blocks(rows_array):
        shaped = rows_array.reshape(group, rows_array.shape[0] // group, rows_array.shape[1])
        return lax.all_to_all(shaped, ("line", "tcol"), 0, 0, tiled=True)

    far_tiles = [lax.ppermute(green, ("half", "tcol"), opposite) for green in greens]
    own_moment = [momentum_blocks(spread(green)) for green in greens]
    positions = jnp.arange(momenta, dtype=jnp.int32)
    phases = (lattice_map[:, None] * positions[None, :] % momenta).astype(F32) * (
        2.0 * math.pi / momenta
    )
    cosines = jnp.cos(phases).astype(BF16)
    sines = jnp.sin(phases).astype(BF16)
    inverse = jnp.concatenate([cosines, sines], axis=1)
    table = jnp.concatenate([inverse, jnp.concatenate([-sines, cosines], axis=1)], axis=0)
    sites = [to_sites(green.reshape(2, rows * cols, momenta), table, norm_factor) for green in greens]
    time_steps = jnp.arange(window, dtype=jnp.int32)
    coupling_line = 1.0 + drive_depth * jnp.cos(
        ((time_offset[0] + time_steps) % PERIOD).astype(F32) * (2.0 * math.pi / PERIOD)
    )
    first = lax.dynamic_slice_in_dim(coupling_line, (half * lines + line) * rows, rows)
    second = lax.dynamic_slice_in_dim(coupling_line, side * cols, cols)
    coupling = (first[:, None] * second[None, :]).reshape(rows * cols, 1)
    crossed = []
    far_moment = []
    for green, far in zip(greens, far_tiles):
        chosen = jnp.where(side == half, green, far)
        sent = chosen.reshape(2, rows, lines, cols // lines, momenta).transpose(2, 0, 1, 3, 4)
        crossed.append(
            lax.all_to_all(sent, "line", 0, 0, tiled=True).reshape(
                lines, 2, rows * cols // lines, momenta
            )
        )
        far_moment.append(momentum_blocks(spread(far)))
    sigma = [
        momentum_blocks(
            to_sigma(sites[g], crossed[1 - g], table, inverse, coupling, rows, norm_factor)
        )
        for g in range(2)
    ]
    collisions = volterra(half[None], own_moment, far_moment, sigma, rows)
    returned = lax.all_to_all(collisions, ("line", "tcol"), 0, 0, tiled=True)
    return collect(returned.reshape(-1, 2 * cols), green_lesser.shape)


def solution(mesh):
    row_parts = mesh.shape["trow"]
    col_parts = mesh.shape["tcol"]

    def call(green_lesser, green_greater, lattice_map, time_offset):
        window, window_cols, momenta = green_lesser.shape[1:]
        rows = window // row_parts
        cols = window_cols // col_parts
        halved = (
            col_parts == 2
            and row_parts % 2 == 0
            and window == window_cols
            and 2 * cols == LANES
            and cols == rows * (row_parts // 2)
            and rows % 8 == 0
            and momenta % (row_parts * LANES // 8) == 0
        )
        if halved:
            devices = mesh.devices.reshape(2, row_parts // 2, col_parts)
            used = Mesh(devices, ("half", "line", "tcol"))
            spec = P(None, ("half", "line"), "tcol", None)
            inner = halved_body
        else:
            used = mesh
            spec = P(None, "trow", "tcol", None)
            inner = general_body
        return jax.shard_map(
            inner, mesh=used, in_specs=(spec, spec, P(), P()), out_specs=(spec, spec), check_vma=False
        )(green_lesser, green_greater, lattice_map, time_offset)

    return call
```

```python
import functools
import math

import jax
import jax.numpy as jnp
from jax import lax
from jax.experimental import pallas as pl
from jax.experimental.pallas import tpu as pltpu
from jax.sharding import Mesh, PartitionSpec as P

F32 = jnp.float32
BF16 = jnp.bfloat16
LANES = 128

PERIOD = 64


step_size = 0.01
drive_depth = 0.5


def regroup(blocks):
    return lax.all_to_all(
        lax.all_to_all(blocks, "trow", split_axis=1, concat_axis=1, tiled=True),
        "tcol",
        split_axis=2,
        concat_axis=2,
        tiled=True,
    )


def pack_blocks(spectral, row_parts, col_parts):
    stacked, extent, tile_cells = spectral.shape
    return spectral.reshape(
        stacked, row_parts, col_parts, extent // (row_parts * col_parts), tile_cells
    )


def spread_times(blocks, tile_rows, tile_cols):
    stacked, row_parts, col_parts, local_count, tile_cells = blocks.shape
    shaped = blocks.reshape(stacked, row_parts, col_parts, local_count, tile_rows, tile_cols)
    return shaped.transpose(0, 3, 1, 4, 2, 5).reshape(
        stacked, local_count, row_parts * tile_rows, col_parts * tile_cols
    )


def gather_tiles(full, row_parts, col_parts):
    stacked, local_count, window, window_cols = full.shape
    tile_rows = window // row_parts
    tile_cols = window_cols // col_parts
    shaped = full.reshape(stacked, local_count, row_parts, tile_rows, col_parts, tile_cols)
    return shaped.transpose(0, 2, 4, 1, 3, 5).reshape(
        stacked, row_parts, col_parts, local_count, tile_rows * tile_cols
    )


def mirrored(full, keep_pair):
    stacked, local_count, window, window_cols = full.shape
    paired = full.reshape(stacked, local_count // 2, 2, window, window_cols)
    swapped = jnp.where(keep_pair[None, :, None, None, None], paired, paired[:, :, ::-1])
    return jnp.swapaxes(swapped.reshape(stacked, local_count, window, window_cols), 2, 3)


def second_born(first_real, first_imaginary, other_real, other_imaginary, coupling):
    square_real = first_real * first_real - first_imaginary * first_imaginary
    square_imaginary = 2.0 * first_real * first_imaginary
    out_real = coupling * (square_real * other_real - square_imaginary * other_imaginary)
    out_imaginary = coupling * (square_real * other_imaginary + square_imaginary * other_real)
    return (out_real, out_imaginary)


def collide(
    retarded_real,
    retarded_imaginary,
    self_real,
    self_imaginary,
    green_real,
    green_imaginary,
    advanced_real,
    advanced_imaginary,
):
    minus_left = jnp.concatenate(
        [retarded_real, -retarded_imaginary, self_real, -self_imaginary], axis=2
    )
    plus_left = jnp.concatenate(
        [retarded_real, retarded_imaginary, self_real, self_imaginary], axis=2
    )
    real_right = jnp.concatenate(
        [green_real, green_imaginary, advanced_real, advanced_imaginary], axis=1
    )
    imaginary_right = jnp.concatenate(
        [green_imaginary, green_real, advanced_imaginary, advanced_real], axis=1
    )
    out_real = jnp.einsum(
        "kts,ksu->ktu", minus_left, real_right, preferred_element_type=jnp.float32
    )
    out_imaginary = jnp.einsum(
        "kts,ksu->ktu", plus_left, imaginary_right, preferred_element_type=jnp.float32
    )
    return (out_real, out_imaginary)


def general_body(green_lesser, green_greater, lattice_map, time_offset):
    tile_rows = green_lesser.shape[1]
    tile_cols = green_lesser.shape[2]
    momenta = green_lesser.shape[3]
    row_parts = lax.axis_size("trow")
    col_parts = lax.axis_size("tcol")
    window = tile_rows * row_parts
    tile_cells = tile_rows * tile_cols
    local_count = momenta // (row_parts * col_parts)
    norm_factor = 1.0 / math.sqrt(momenta)
    greens = (
        jnp.concatenate([green_lesser, green_greater], axis=0)
        .reshape(4, tile_cells, momenta)
        .transpose(0, 2, 1)
    )
    positions = jnp.arange(momenta, dtype=jnp.int32)
    halves = positions // 2
    site_order = jnp.where(
        positions == 1, momenta // 2, jnp.where(positions % 2 == 0, halves, momenta - halves)
    )
    phases = (lattice_map[:, None] * site_order[None, :] % momenta).astype(jnp.float32) * (
        2.0 * math.pi / momenta
    )
    cosines = jnp.cos(phases).astype(jnp.bfloat16)
    sines = jnp.sin(phases).astype(jnp.bfloat16)
    ahead_blocks = lax.all_to_all(
        lax.all_to_all(
            pack_blocks(greens, row_parts, col_parts),
            "trow",
            split_axis=1,
            concat_axis=1,
            tiled=True,
        ),
        "tcol",
        split_axis=2,
        concat_axis=2,
        tiled=True,
    )
    green_moment = spread_times(ahead_blocks, tile_rows, tile_cols)
    forward_table = jnp.concatenate([cosines, sines], axis=1)
    products = jnp.einsum("cjm,jr->crm", greens, forward_table, preferred_element_type=jnp.float32)
    site_space = jnp.stack(
        [
            (products[0, :momenta] - products[1, momenta:]) * norm_factor,
            (products[0, momenta:] + products[1, :momenta]) * norm_factor,
            (products[2, :momenta] - products[3, momenta:]) * norm_factor,
            (products[2, momenta:] + products[3, :momenta]) * norm_factor,
        ]
    ).astype(jnp.bfloat16)
    site_full = spread_times(
        regroup(pack_blocks(site_space, row_parts, col_parts)), tile_rows, tile_cols
    )
    site_block = lax.axis_index("trow") * col_parts + lax.axis_index("tcol")
    keep_pair = site_block * (local_count // 2) + jnp.arange(local_count // 2, dtype=jnp.int32) == 0
    mirror = mirrored(site_full, keep_pair).astype(jnp.float32)
    direct = site_full.astype(jnp.float32)
    time_steps = jnp.arange(window, dtype=jnp.int32)
    coupling_line = 1.0 + drive_depth * jnp.cos(
        ((time_offset[0] + time_steps) % PERIOD).astype(jnp.float32) * (2.0 * math.pi / PERIOD)
    )
    coupling = coupling_line[:, None] * coupling_line[None, :]
    self_lesser = second_born(direct[0], direct[1], mirror[2], mirror[3], coupling)
    self_greater = second_born(direct[2], direct[3], mirror[0], mirror[1], coupling)
    self_sites = jnp.stack(
        [self_lesser[0], self_lesser[1], self_greater[0], self_greater[1]]
    ).astype(jnp.bfloat16)
    self_tiles = regroup(gather_tiles(self_sites, row_parts, col_parts)).reshape(
        4, momenta, tile_cells
    )
    inverse_table = jnp.concatenate([cosines, sines], axis=0)
    spectral_terms = jnp.einsum(
        "cum,ju->cjm", self_tiles, inverse_table, preferred_element_type=jnp.float32
    )
    self_spectral = jnp.stack(
        [
            (spectral_terms[0, :momenta] + spectral_terms[1, momenta:]) * norm_factor,
            (spectral_terms[1, :momenta] - spectral_terms[0, momenta:]) * norm_factor,
            (spectral_terms[2, :momenta] + spectral_terms[3, momenta:]) * norm_factor,
            (spectral_terms[3, :momenta] - spectral_terms[2, momenta:]) * norm_factor,
        ]
    ).astype(jnp.bfloat16)
    self_moment = spread_times(
        regroup(pack_blocks(self_spectral, row_parts, col_parts)), tile_rows, tile_cols
    )
    lower_mask = time_steps[None, :] <= time_steps[:, None]
    upper_mask = time_steps[:, None] <= time_steps[None, :]
    retarded = jnp.where(
        lower_mask, self_moment[2:4].astype(jnp.float32) - self_moment[0:2].astype(jnp.float32), 0.0
    ).astype(jnp.bfloat16)
    advanced = jnp.where(
        upper_mask,
        green_moment[0:2].astype(jnp.float32) - green_moment[2:4].astype(jnp.float32),
        0.0,
    ).astype(jnp.bfloat16)
    lesser_out = collide(
        retarded[0],
        retarded[1],
        self_moment[0],
        self_moment[1],
        green_moment[0],
        green_moment[1],
        advanced[0],
        advanced[1],
    )
    greater_out = collide(
        retarded[0],
        retarded[1],
        self_moment[2],
        self_moment[3],
        green_moment[2],
        green_moment[3],
        advanced[0],
        advanced[1],
    )
    collisions = (
        jnp.stack([lesser_out[0], lesser_out[1], greater_out[0], greater_out[1]]) * step_size
    ).astype(jnp.bfloat16)
    out_tiles = regroup(gather_tiles(collisions, row_parts, col_parts)).reshape(
        4, momenta, tile_cells
    )
    out_tiles = out_tiles.transpose(0, 2, 1).reshape(4, tile_rows, tile_cols, momenta)
    return (out_tiles[0:2], out_tiles[2:4])


def vmem_params():
    return pltpu.CompilerParams(vmem_limit_bytes=48 * 1024 * 1024)


def whole(count):
    return [pl.BlockSpec(memory_space=pltpu.VMEM)] * count


def spread_kernel(first, lesser, greater, out, lines):
    _, rows, _, _ = lesser.shape
    count = lines.shape[0] // (2 * rows)
    for g, tile in enumerate((lesser, greater)):
        for t in range(rows):
            span = slice(first, first + count)
            slab = jnp.concatenate([tile[0, t, :, span], tile[1, t, :, span]], axis=0)
            lines[pl.ds(g * rows + t, count, stride=2 * rows), :] = slab.astype(F32).T
    out[...] = lines[...].astype(BF16)


def spread(tiles, first, count):
    _, rows, cols, _ = tiles[0].shape
    shape = (count * 2 * rows, 2 * cols)
    return pl.pallas_call(
        functools.partial(spread_kernel, first),
        out_shape=jax.ShapeDtypeStruct(shape, BF16),
        in_specs=whole(2),
        out_specs=whole(1)[0],
        scratch_shapes=[pltpu.VMEM(shape, F32)],
        compiler_params=vmem_params(),
        name="spread",
    )(*tiles)


def collect_kernel(*refs):
    *parts, lesser, greater, lines = refs
    _, rows, cols, momenta = lesser.shape
    count = momenta // len(parts)
    for at, part in enumerate(parts):
        lines[...] = part[...].astype(F32)
        span = slice(at * count, (at + 1) * count)
        for k in range(2 * rows):
            slab = lines[pl.ds(k, count, stride=2 * rows), :].T.astype(BF16)
            out = lesser if k < rows else greater
            out[0, k % rows, :, span] = slab[:cols]
            out[1, k % rows, :, span] = slab[cols:]


def collect(parts, tile_shape):
    shape = jax.ShapeDtypeStruct(tile_shape, BF16)
    return pl.pallas_call(
        collect_kernel,
        out_shape=(shape, shape),
        in_specs=whole(len(parts)),
        out_specs=tuple(whole(2)),
        scratch_shapes=[pltpu.VMEM(parts[0].shape, F32)],
        compiler_params=vmem_params(),
        name="collect",
    )(*parts)


def site_kernel(norm_factor, lesser, greater, table, out):
    _, rows, cols, _ = lesser.shape
    wide = 4 * cols
    for pair in range(rows // 2):
        slabs = [
            jnp.concatenate([tile[0, t], tile[1, t]], axis=1)
            for t in (2 * pair, 2 * pair + 1)
            for tile in (lesser, greater)
        ]
        product = lax.dot_general(
            table[...],
            jnp.concatenate(slabs, axis=0),
            (((1,), (1,)), ((), ())),
            preferred_element_type=F32,
        )
        out[:, pair * wide : (pair + 1) * wide] = (product * norm_factor).astype(BF16)


def to_sites(tiles, table, norm_factor):
    _, rows, cols, momenta = tiles[0].shape
    return pl.pallas_call(
        functools.partial(site_kernel, norm_factor),
        out_shape=jax.ShapeDtypeStruct((2 * momenta, rows * 2 * cols), BF16),
        in_specs=whole(3),
        out_specs=whole(1)[0],
        compiler_params=vmem_params(),
        name="to_sites",
    )(*tiles, table)


def cross_kernel(rows, half_ref, own, far, out):
    half = half_ref[0]
    blocks = far.shape[0]
    cols = blocks * rows
    for at in range(far.shape[1] // (2 * rows)):
        span = slice(at * 2 * rows, (at + 1) * 2 * rows)
        for source, offset, target in ((own, half * blocks, half), (far, 0, 1 - half)):
            loaded = [source[offset + block, span].astype(F32) for block in range(blocks)]
            stacked = jnp.concatenate(
                [lines[rows:] for lines in loaded] + [lines[:rows] for lines in loaded], axis=0
            )
            turned = stacked.T
            for block in range(blocks):
                out[target * blocks + block, span] = jnp.concatenate(
                    [
                        turned[block * rows : (block + 1) * rows],
                        turned[cols + block * rows : cols + (block + 1) * rows],
                    ],
                    axis=0,
                ).astype(BF16)


def to_crossed(half, own, far, rows):
    return pl.pallas_call(
        functools.partial(cross_kernel, rows),
        out_shape=jax.ShapeDtypeStruct(own.shape, BF16),
        in_specs=[pl.BlockSpec(memory_space=pltpu.SMEM)] + whole(2),
        out_specs=whole(1)[0],
        compiler_params=vmem_params(),
        name="to_crossed",
    )(half, own, far)


def self_kernel(norm_factor, parts, *refs):
    crossed = refs[:parts]
    own, table, coupling, out, lines = refs[parts:]
    rows = coupling.shape[0]
    momenta = own.shape[0] // 2
    count = momenta // parts
    for part in range(parts):
        lines[part] = crossed[part][...].astype(F32)
    for pair in range(rows // 2):
        rights = []
        for t in (2 * pair, 2 * pair + 1):
            real = [lines[part, pl.ds(t, count, stride=2 * rows), :] for part in range(parts)]
            imaginary = [
                -lines[part, pl.ds(rows + t, count, stride=2 * rows), :] for part in range(parts)
            ]
            rights.append(jnp.concatenate(real + imaginary, axis=0).astype(BF16))
        other = jnp.dot(
            table[...], jnp.concatenate(rights, axis=1), preferred_element_type=F32
        )
        other = (other * norm_factor).astype(BF16).astype(F32)
        for at in range(2):
            t = 2 * pair + at
            span = slice(t * LANES, (t + 1) * LANES)
            self_real, self_imaginary = second_born(
                own[:momenta, span].astype(F32),
                own[momenta:, span].astype(F32),
                other[:momenta, at * LANES : (at + 1) * LANES],
                -other[momenta:, at * LANES : (at + 1) * LANES],
                coupling[t : t + 1, :],
            )
            out[:momenta, span] = self_real.astype(BF16)
            out[momenta:, span] = self_imaginary.astype(BF16)


def to_self(crossed, own, table, coupling, norm_factor):
    parts = len(crossed)
    return pl.pallas_call(
        functools.partial(self_kernel, norm_factor, parts),
        out_shape=jax.ShapeDtypeStruct(own.shape, BF16),
        in_specs=whole(parts + 3),
        out_specs=whole(1)[0],
        scratch_shapes=[pltpu.VMEM((parts,) + crossed[0].shape, F32)],
        compiler_params=vmem_params(),
        name="to_self",
    )(*crossed, own, table, coupling)


def sigma_kernel(norm_factor, rows, sites, table, out, lines):
    count = table.shape[0] // 2
    for pair in range(rows // 2):
        product = jnp.dot(
            table[...],
            sites[:, 2 * pair * LANES : 2 * (pair + 1) * LANES],
            preferred_element_type=F32,
        )
        product = product * norm_factor
        for at in range(2):
            for part in range(2):
                lines[pl.ds(part * rows + 2 * pair + at, count, stride=2 * rows), :] = product[
                    part * count : (part + 1) * count, at * LANES : (at + 1) * LANES
                ]
    out[...] = lines[...].astype(BF16)


def to_sigma(sites, table, rows, norm_factor):
    shape = (table.shape[0] * rows, LANES)
    return pl.pallas_call(
        functools.partial(sigma_kernel, norm_factor, rows),
        out_shape=jax.ShapeDtypeStruct(shape, BF16),
        in_specs=whole(2),
        out_specs=whole(1)[0],
        scratch_shapes=[pltpu.VMEM(shape, F32)],
        compiler_params=vmem_params(),
        name="to_sigma",
    )(sites, table)


def volterra_kernel(rows, half_ref, own, far_near, far_away, sigma, out):
    half = half_ref[0]
    blocks = far_near.shape[0]
    lanes = own.shape[2]
    cols = lanes // 2
    near = half * cols
    away = (1 - half) * cols
    near_at = half * blocks
    away_at = (1 - half) * blocks
    first_times = near + lax.broadcasted_iota(jnp.int32, (cols, lanes), 0)
    left_lane = lax.broadcasted_iota(jnp.int32, (cols, lanes), 1)
    low_lanes = left_lane < cols
    left_times = jnp.where(low_lanes, near + left_lane, away + left_lane - cols)
    keep_left = left_times <= first_times
    row_at = lax.broadcasted_iota(jnp.int32, (lanes, 2 * lanes), 0)
    inner_times = jnp.where(row_at < cols, near + row_at, away + row_at - cols)
    lane_at = lax.broadcasted_iota(jnp.int32, (lanes, 2 * lanes), 1)
    last_times = jnp.where(lane_at < lanes, near, away) + lane_at % cols
    keep_right = inner_times <= last_times
    for at in range(own.shape[1] // (2 * rows)):
        span = slice(at * 2 * rows, (at + 1) * 2 * rows)

        def stacked(ref, offset):
            loaded = [ref[offset + block, span].astype(F32) for block in range(blocks)]
            return [
                jnp.concatenate([lines[part * rows : (part + 1) * rows] for lines in loaded], axis=0)
                for part in range(2)
            ]

        own_near = stacked(own, near_at)
        own_away = stacked(own, away_at)
        cross_near = stacked(far_near, 0)
        cross_away = stacked(far_away, 0)
        greens = [
            jnp.concatenate(
                [
                    jnp.concatenate([own_near[g], own_away[g]], axis=1),
                    jnp.concatenate([cross_near[g], cross_away[g]], axis=1),
                ],
                axis=0,
            )
            for g in range(2)
        ]
        advanced = jnp.where(keep_right, greens[0] - greens[1], 0.0).astype(BF16)
        sigma_near = stacked(sigma, near_at)
        sigma_away = stacked(sigma, away_at)
        retarded = []
        lefts = [[], []]
        for part in range(2):
            lesser = jnp.where(
                low_lanes, sigma_near[part], pltpu.roll(sigma_away[part], cols, 1)
            )
            greater = jnp.where(
                low_lanes, pltpu.roll(sigma_near[part], cols, 1), sigma_away[part]
            )
            retarded.append(jnp.where(keep_left, greater - lesser, 0.0))
            lefts[0].append(lesser)
            lefts[1].append(greater)
        retarded = jnp.concatenate(retarded, axis=0).astype(BF16)
        results = []
        for g in range(2):
            left = jnp.concatenate(
                [retarded, jnp.concatenate(lefts[g], axis=0).astype(BF16)], axis=1
            )
            right = jnp.concatenate([greens[g].astype(BF16), advanced], axis=0)
            product = jnp.dot(left, right, preferred_element_type=F32)
            sides = []
            for side in range(2):
                straight = product[:cols, side * lanes : (side + 1) * lanes]
                turned = pltpu.roll(product[cols:, side * lanes : (side + 1) * lanes], cols, 1)
                sides.append((straight + jnp.where(low_lanes, -turned, turned)) * step_size)
            results.append(sides)
        for block in range(blocks):
            piece = slice(block * rows, (block + 1) * rows)
            for side, offset in enumerate((near_at, away_at)):
                out[offset + block, span] = jnp.concatenate(
                    [results[0][side][piece], results[1][side][piece]], axis=0
                ).astype(BF16)


def volterra(half, own, far_near, far_away, sigma, rows):
    sources, lines, lanes = own.shape
    blocks = far_near.shape[0]
    step = 4 * rows
    spec = pl.BlockSpec((sources, step, lanes), lambda p: (0, p, 0))
    far_spec = pl.BlockSpec((blocks, step, lanes), lambda p: (0, p, 0))
    return pl.pallas_call(
        functools.partial(volterra_kernel, rows),
        grid=(lines // step,),
        out_shape=jax.ShapeDtypeStruct(own.shape, BF16),
        in_specs=[pl.BlockSpec(memory_space=pltpu.SMEM), spec, far_spec, far_spec, spec],
        out_specs=spec,
        compiler_params=vmem_params(),
        name="volterra",
    )(half, own, far_near, far_away, sigma)


PARTS = 2


def halved_body(green_lesser, green_greater, lattice_map, time_offset):
    _, rows, cols, momenta = green_lesser.shape
    half = lax.axis_index("half")
    line = lax.axis_index("line")
    side = lax.axis_index("tcol")
    lines = lax.axis_size("line")
    group = lines * lax.axis_size("tcol")
    window = rows * lines * lax.axis_size("half")
    norm_factor = 1.0 / math.sqrt(momenta)
    tiles = (green_lesser, green_greater)
    count = momenta // PARTS
    half_at = half[None]

    def exchange(blocks):
        return lax.all_to_all(blocks, ("tcol", "line"), 0, 0, tiled=True)

    def blocked(rows_array):
        return rows_array.reshape(group, rows_array.shape[0] // group, rows_array.shape[1])

    def swap(blocks, at):
        sent = lax.dynamic_slice_in_dim(blocks, at * lines, lines)
        return lax.ppermute(sent, "half", [(0, 1), (1, 0)])

    own = [exchange(blocked(spread(tiles, part * count, count))) for part in range(PARTS)]
    far_near = [swap(blocks, 1 - half) for blocks in own]
    far_away = [swap(blocks, half) for blocks in own]

    positions = jnp.arange(momenta, dtype=jnp.int32)
    phases = (lattice_map[:, None] * positions[None, :] % momenta).astype(F32) * (
        2.0 * math.pi / momenta
    )
    cosines = jnp.cos(phases).astype(BF16)
    sines = jnp.sin(phases).astype(BF16)
    inverse = jnp.concatenate([cosines, sines], axis=1)
    turned = jnp.concatenate([-sines, cosines], axis=1)
    table = jnp.concatenate([inverse, turned], axis=0).T
    sites = to_sites(tiles, table, norm_factor)
    time_steps = jnp.arange(window, dtype=jnp.int32)
    coupling_line = 1.0 + drive_depth * jnp.cos(
        ((time_offset[0] + time_steps) % PERIOD).astype(F32) * (2.0 * math.pi / PERIOD)
    )
    first = lax.dynamic_slice_in_dim(coupling_line, (half * lines + line) * rows, rows)
    second = lax.dynamic_slice_in_dim(coupling_line, side * cols, cols)
    coupling = first[:, None] * jnp.concatenate([second, second])[None, :]

    crossed = [
        exchange(to_crossed(half_at, own[part], far_near[part], rows)).reshape(-1, 2 * cols)
        for part in range(PARTS)
    ]
    self_sites = to_self(crossed, sites, table, coupling, norm_factor)
    returned = []
    for part in range(PARTS):
        span = slice(part * count, (part + 1) * count)
        inverse_part = jnp.concatenate([inverse[span], turned[span]], axis=0)
        sigma = exchange(blocked(to_sigma(self_sites, inverse_part, rows, norm_factor)))
        collisions = volterra(half_at, own[part], far_near[part], far_away[part], sigma, rows)
        returned.append(exchange(collisions).reshape(-1, 2 * cols))
    return collect(returned, green_lesser.shape)


def solution(mesh):
    row_parts = mesh.shape["trow"]
    col_parts = mesh.shape["tcol"]

    def call(green_lesser, green_greater, lattice_map, time_offset):
        window, window_cols, momenta = green_lesser.shape[1:]
        rows = window // row_parts
        cols = window_cols // col_parts
        halved = (
            col_parts == 2
            and row_parts % 2 == 0
            and window == window_cols
            and 2 * cols == LANES
            and cols == rows * (row_parts // 2)
            and rows % 8 == 0
            and momenta % (PARTS * LANES) == 0
            and momenta % (PARTS * row_parts * 2) == 0
        )
        if halved:
            devices = mesh.devices.reshape(2, row_parts // 2, col_parts)
            used = Mesh(devices, ("half", "line", "tcol"))
            spec = P(None, ("half", "line"), "tcol", None)
            inner = halved_body
        else:
            used = mesh
            spec = P(None, "trow", "tcol", None)
            inner = general_body
        return jax.shard_map(
            inner, mesh=used, in_specs=(spec, spec, P(), P()), out_specs=(spec, spec), check_vma=False
        )(green_lesser, green_greater, lattice_map, time_offset)

    return call
```

```python
import functools
import math

import jax
import jax.numpy as jnp
from jax import lax
from jax.experimental import pallas as pl
from jax.experimental.pallas import tpu as pltpu
from jax.sharding import Mesh, PartitionSpec as P

F32 = jnp.float32
BF16 = jnp.bfloat16
LANES = 128

PERIOD = 64


step_size = 0.01
drive_depth = 0.5


def regroup(blocks):
    return lax.all_to_all(
        lax.all_to_all(blocks, "trow", split_axis=1, concat_axis=1, tiled=True),
        "tcol",
        split_axis=2,
        concat_axis=2,
        tiled=True,
    )


def pack_blocks(spectral, row_parts, col_parts):
    stacked, extent, tile_cells = spectral.shape
    return spectral.reshape(
        stacked, row_parts, col_parts, extent // (row_parts * col_parts), tile_cells
    )


def spread_times(blocks, tile_rows, tile_cols):
    stacked, row_parts, col_parts, local_count, tile_cells = blocks.shape
    shaped = blocks.reshape(stacked, row_parts, col_parts, local_count, tile_rows, tile_cols)
    return shaped.transpose(0, 3, 1, 4, 2, 5).reshape(
        stacked, local_count, row_parts * tile_rows, col_parts * tile_cols
    )


def gather_tiles(full, row_parts, col_parts):
    stacked, local_count, window, window_cols = full.shape
    tile_rows = window // row_parts
    tile_cols = window_cols // col_parts
    shaped = full.reshape(stacked, local_count, row_parts, tile_rows, col_parts, tile_cols)
    return shaped.transpose(0, 2, 4, 1, 3, 5).reshape(
        stacked, row_parts, col_parts, local_count, tile_rows * tile_cols
    )


def mirrored(full, keep_pair):
    stacked, local_count, window, window_cols = full.shape
    paired = full.reshape(stacked, local_count // 2, 2, window, window_cols)
    swapped = jnp.where(keep_pair[None, :, None, None, None], paired, paired[:, :, ::-1])
    return jnp.swapaxes(swapped.reshape(stacked, local_count, window, window_cols), 2, 3)


def second_born(first_real, first_imaginary, other_real, other_imaginary, coupling):
    square_real = first_real * first_real - first_imaginary * first_imaginary
    square_imaginary = 2.0 * first_real * first_imaginary
    out_real = coupling * (square_real * other_real - square_imaginary * other_imaginary)
    out_imaginary = coupling * (square_real * other_imaginary + square_imaginary * other_real)
    return (out_real, out_imaginary)


def collide(
    retarded_real,
    retarded_imaginary,
    self_real,
    self_imaginary,
    green_real,
    green_imaginary,
    advanced_real,
    advanced_imaginary,
):
    minus_left = jnp.concatenate(
        [retarded_real, -retarded_imaginary, self_real, -self_imaginary], axis=2
    )
    plus_left = jnp.concatenate(
        [retarded_real, retarded_imaginary, self_real, self_imaginary], axis=2
    )
    real_right = jnp.concatenate(
        [green_real, green_imaginary, advanced_real, advanced_imaginary], axis=1
    )
    imaginary_right = jnp.concatenate(
        [green_imaginary, green_real, advanced_imaginary, advanced_real], axis=1
    )
    out_real = jnp.einsum(
        "kts,ksu->ktu", minus_left, real_right, preferred_element_type=jnp.float32
    )
    out_imaginary = jnp.einsum(
        "kts,ksu->ktu", plus_left, imaginary_right, preferred_element_type=jnp.float32
    )
    return (out_real, out_imaginary)


def general_body(green_lesser, green_greater, lattice_map, time_offset):
    tile_rows = green_lesser.shape[1]
    tile_cols = green_lesser.shape[2]
    momenta = green_lesser.shape[3]
    row_parts = lax.axis_size("trow")
    col_parts = lax.axis_size("tcol")
    window = tile_rows * row_parts
    tile_cells = tile_rows * tile_cols
    local_count = momenta // (row_parts * col_parts)
    norm_factor = 1.0 / math.sqrt(momenta)
    greens = (
        jnp.concatenate([green_lesser, green_greater], axis=0)
        .reshape(4, tile_cells, momenta)
        .transpose(0, 2, 1)
    )
    positions = jnp.arange(momenta, dtype=jnp.int32)
    halves = positions // 2
    site_order = jnp.where(
        positions == 1, momenta // 2, jnp.where(positions % 2 == 0, halves, momenta - halves)
    )
    phases = (lattice_map[:, None] * site_order[None, :] % momenta).astype(jnp.float32) * (
        2.0 * math.pi / momenta
    )
    cosines = jnp.cos(phases).astype(jnp.bfloat16)
    sines = jnp.sin(phases).astype(jnp.bfloat16)
    ahead_blocks = lax.all_to_all(
        lax.all_to_all(
            pack_blocks(greens, row_parts, col_parts),
            "trow",
            split_axis=1,
            concat_axis=1,
            tiled=True,
        ),
        "tcol",
        split_axis=2,
        concat_axis=2,
        tiled=True,
    )
    green_moment = spread_times(ahead_blocks, tile_rows, tile_cols)
    forward_table = jnp.concatenate([cosines, sines], axis=1)
    products = jnp.einsum("cjm,jr->crm", greens, forward_table, preferred_element_type=jnp.float32)
    site_space = jnp.stack(
        [
            (products[0, :momenta] - products[1, momenta:]) * norm_factor,
            (products[0, momenta:] + products[1, :momenta]) * norm_factor,
            (products[2, :momenta] - products[3, momenta:]) * norm_factor,
            (products[2, momenta:] + products[3, :momenta]) * norm_factor,
        ]
    ).astype(jnp.bfloat16)
    site_full = spread_times(
        regroup(pack_blocks(site_space, row_parts, col_parts)), tile_rows, tile_cols
    )
    site_block = lax.axis_index("trow") * col_parts + lax.axis_index("tcol")
    keep_pair = site_block * (local_count // 2) + jnp.arange(local_count // 2, dtype=jnp.int32) == 0
    mirror = mirrored(site_full, keep_pair).astype(jnp.float32)
    direct = site_full.astype(jnp.float32)
    time_steps = jnp.arange(window, dtype=jnp.int32)
    coupling_line = 1.0 + drive_depth * jnp.cos(
        ((time_offset[0] + time_steps) % PERIOD).astype(jnp.float32) * (2.0 * math.pi / PERIOD)
    )
    coupling = coupling_line[:, None] * coupling_line[None, :]
    self_lesser = second_born(direct[0], direct[1], mirror[2], mirror[3], coupling)
    self_greater = second_born(direct[2], direct[3], mirror[0], mirror[1], coupling)
    self_sites = jnp.stack(
        [self_lesser[0], self_lesser[1], self_greater[0], self_greater[1]]
    ).astype(jnp.bfloat16)
    self_tiles = regroup(gather_tiles(self_sites, row_parts, col_parts)).reshape(
        4, momenta, tile_cells
    )
    inverse_table = jnp.concatenate([cosines, sines], axis=0)
    spectral_terms = jnp.einsum(
        "cum,ju->cjm", self_tiles, inverse_table, preferred_element_type=jnp.float32
    )
    self_spectral = jnp.stack(
        [
            (spectral_terms[0, :momenta] + spectral_terms[1, momenta:]) * norm_factor,
            (spectral_terms[1, :momenta] - spectral_terms[0, momenta:]) * norm_factor,
            (spectral_terms[2, :momenta] + spectral_terms[3, momenta:]) * norm_factor,
            (spectral_terms[3, :momenta] - spectral_terms[2, momenta:]) * norm_factor,
        ]
    ).astype(jnp.bfloat16)
    self_moment = spread_times(
        regroup(pack_blocks(self_spectral, row_parts, col_parts)), tile_rows, tile_cols
    )
    lower_mask = time_steps[None, :] <= time_steps[:, None]
    upper_mask = time_steps[:, None] <= time_steps[None, :]
    retarded = jnp.where(
        lower_mask, self_moment[2:4].astype(jnp.float32) - self_moment[0:2].astype(jnp.float32), 0.0
    ).astype(jnp.bfloat16)
    advanced = jnp.where(
        upper_mask,
        green_moment[0:2].astype(jnp.float32) - green_moment[2:4].astype(jnp.float32),
        0.0,
    ).astype(jnp.bfloat16)
    lesser_out = collide(
        retarded[0],
        retarded[1],
        self_moment[0],
        self_moment[1],
        green_moment[0],
        green_moment[1],
        advanced[0],
        advanced[1],
    )
    greater_out = collide(
        retarded[0],
        retarded[1],
        self_moment[2],
        self_moment[3],
        green_moment[2],
        green_moment[3],
        advanced[0],
        advanced[1],
    )
    collisions = (
        jnp.stack([lesser_out[0], lesser_out[1], greater_out[0], greater_out[1]]) * step_size
    ).astype(jnp.bfloat16)
    out_tiles = regroup(gather_tiles(collisions, row_parts, col_parts)).reshape(
        4, momenta, tile_cells
    )
    out_tiles = out_tiles.transpose(0, 2, 1).reshape(4, tile_rows, tile_cols, momenta)
    return (out_tiles[0:2], out_tiles[2:4])


def vmem_params():
    return pltpu.CompilerParams(vmem_limit_bytes=48 * 1024 * 1024)


def unread(arrays):
    return [pl.BlockSpec(memory_space=pl.ANY)] * len(arrays)


def whole(count):
    return [pl.BlockSpec(memory_space=pltpu.VMEM)] * count


def spread_kernel(first, lesser, greater, *rest):
    out, lines = rest[-2:]
    _, rows, _, _ = lesser.shape
    count = lines.shape[0] // (2 * rows)
    for g, tile in enumerate((lesser, greater)):
        for t in range(rows):
            span = slice(first, first + count)
            slab = jnp.concatenate([tile[0, t, :, span], tile[1, t, :, span]], axis=0)
            lines[pl.ds(g * rows + t, count, stride=2 * rows), :] = slab.astype(F32).T
    out[...] = lines[...].astype(BF16)


def spread(tiles, first, count, after):
    _, rows, cols, _ = tiles[0].shape
    shape = (count * 2 * rows, 2 * cols)
    return pl.pallas_call(
        functools.partial(spread_kernel, first),
        out_shape=jax.ShapeDtypeStruct(shape, BF16),
        in_specs=whole(2) + unread(after),
        out_specs=whole(1)[0],
        scratch_shapes=[pltpu.VMEM(shape, F32)],
        compiler_params=vmem_params(),
        name="spread",
    )(*tiles, *after)


def collect_kernel(*refs):
    *parts, lesser, greater, lines = refs
    _, rows, cols, momenta = lesser.shape
    count = momenta // len(parts)
    for at, part in enumerate(parts):
        lines[...] = part[...].astype(F32)
        span = slice(at * count, (at + 1) * count)
        for k in range(2 * rows):
            slab = lines[pl.ds(k, count, stride=2 * rows), :].T.astype(BF16)
            out = lesser if k < rows else greater
            out[0, k % rows, :, span] = slab[:cols]
            out[1, k % rows, :, span] = slab[cols:]


def collect(parts, tile_shape):
    shape = jax.ShapeDtypeStruct(tile_shape, BF16)
    return pl.pallas_call(
        collect_kernel,
        out_shape=(shape, shape),
        in_specs=whole(len(parts)),
        out_specs=tuple(whole(2)),
        scratch_shapes=[pltpu.VMEM(parts[0].shape, F32)],
        compiler_params=vmem_params(),
        name="collect",
    )(*parts)


def table_kernel(column_ref, table, *inverse):
    momenta = column_ref.shape[0]
    count = momenta // len(inverse)
    positions = lax.broadcasted_iota(jnp.int32, (momenta, momenta), 1)
    phases = (column_ref[...] * positions % momenta).astype(F32) * (2.0 * math.pi / momenta)
    cosines = jnp.cos(phases).astype(BF16)
    sines = jnp.sin(phases).astype(BF16)
    for part, ref in enumerate(inverse):
        span = slice(part * count, (part + 1) * count)
        ref[:count, :momenta] = cosines[span]
        ref[:count, momenta:] = sines[span]
        ref[count:, :momenta] = -sines[span]
        ref[count:, momenta:] = cosines[span]
    cosines = cosines.astype(F32).T.astype(BF16)
    sines = sines.astype(F32).T.astype(BF16)
    table[:momenta, :momenta] = cosines
    table[:momenta, momenta:] = -sines
    table[momenta:, :momenta] = sines
    table[momenta:, momenta:] = cosines


def make_tables(lattice_map, parts):
    momenta = lattice_map.shape[0]
    count = momenta // parts
    shapes = [(2 * momenta, 2 * momenta)] + [(2 * count, 2 * momenta)] * parts
    return pl.pallas_call(
        table_kernel,
        out_shape=tuple(jax.ShapeDtypeStruct(shape, BF16) for shape in shapes),
        in_specs=whole(1),
        out_specs=tuple(whole(1 + parts)),
        compiler_params=vmem_params(),
        name="make_tables",
    )(lattice_map[:, None])


def site_kernel(norm_factor, lesser, greater, table, out):
    _, rows, cols, _ = lesser.shape
    wide = 4 * cols
    for pair in range(rows // 2):
        slabs = [
            jnp.concatenate([tile[0, t], tile[1, t]], axis=1)
            for t in (2 * pair, 2 * pair + 1)
            for tile in (lesser, greater)
        ]
        product = lax.dot_general(
            table[...],
            jnp.concatenate(slabs, axis=0),
            (((1,), (1,)), ((), ())),
            preferred_element_type=F32,
        )
        out[:, pair * wide : (pair + 1) * wide] = (product * norm_factor).astype(BF16)


def to_sites(tiles, table, norm_factor):
    _, rows, cols, momenta = tiles[0].shape
    return pl.pallas_call(
        functools.partial(site_kernel, norm_factor),
        out_shape=jax.ShapeDtypeStruct((2 * momenta, rows * 2 * cols), BF16),
        in_specs=whole(3),
        out_specs=whole(1)[0],
        compiler_params=vmem_params(),
        name="to_sites",
    )(*tiles, table)


def cross_kernel(rows, half_ref, own, far, *rest):
    out = rest[-1]
    half = half_ref[0]
    blocks = far.shape[0]
    cols = blocks * rows
    for at in range(far.shape[1] // (2 * rows)):
        span = slice(at * 2 * rows, (at + 1) * 2 * rows)
        for source, offset, target in ((own, half * blocks, half), (far, 0, 1 - half)):
            loaded = [source[offset + block, span].astype(F32) for block in range(blocks)]
            stacked = jnp.concatenate(
                [lines[rows:] for lines in loaded] + [lines[:rows] for lines in loaded], axis=0
            )
            turned = stacked.T
            for block in range(blocks):
                out[target * blocks + block, span] = jnp.concatenate(
                    [
                        turned[block * rows : (block + 1) * rows],
                        turned[cols + block * rows : cols + (block + 1) * rows],
                    ],
                    axis=0,
                ).astype(BF16)


def to_crossed(half, own, far, rows, after):
    return pl.pallas_call(
        functools.partial(cross_kernel, rows),
        out_shape=jax.ShapeDtypeStruct(own.shape, BF16),
        in_specs=[pl.BlockSpec(memory_space=pltpu.SMEM)] + whole(2) + unread(after),
        out_specs=whole(1)[0],
        compiler_params=vmem_params(),
        name="to_crossed",
    )(half, own, far, *after)


def self_kernel(norm_factor, parts, *refs):
    crossed = refs[:parts]
    own, table, coupling = refs[parts : parts + 3]
    out, lines = refs[-2:]
    rows = coupling.shape[0]
    momenta = own.shape[0] // 2
    count = momenta // parts
    for part in range(parts):
        lines[part] = crossed[part][...].astype(F32)
    for pair in range(rows // 2):
        rights = []
        for t in (2 * pair, 2 * pair + 1):
            real = [lines[part, pl.ds(t, count, stride=2 * rows), :] for part in range(parts)]
            imaginary = [
                -lines[part, pl.ds(rows + t, count, stride=2 * rows), :] for part in range(parts)
            ]
            rights.append(jnp.concatenate(real + imaginary, axis=0).astype(BF16))
        other = jnp.dot(
            table[...], jnp.concatenate(rights, axis=1), preferred_element_type=F32
        )
        other = (other * norm_factor).astype(BF16).astype(F32)
        for at in range(2):
            t = 2 * pair + at
            span = slice(t * LANES, (t + 1) * LANES)
            self_real, self_imaginary = second_born(
                own[:momenta, span].astype(F32),
                own[momenta:, span].astype(F32),
                other[:momenta, at * LANES : (at + 1) * LANES],
                -other[momenta:, at * LANES : (at + 1) * LANES],
                coupling[t : t + 1, :],
            )
            out[:momenta, span] = self_real.astype(BF16)
            out[momenta:, span] = self_imaginary.astype(BF16)


def to_self(crossed, own, table, coupling, norm_factor, after):
    parts = len(crossed)
    return pl.pallas_call(
        functools.partial(self_kernel, norm_factor, parts),
        out_shape=jax.ShapeDtypeStruct(own.shape, BF16),
        in_specs=whole(parts + 3) + unread(after),
        out_specs=whole(1)[0],
        scratch_shapes=[pltpu.VMEM((parts,) + crossed[0].shape, F32)],
        compiler_params=vmem_params(),
        name="to_self",
    )(*crossed, own, table, coupling, *after)


def sigma_kernel(norm_factor, rows, sites, table, out, lines):
    count = table.shape[0] // 2
    for pair in range(rows // 2):
        product = jnp.dot(
            table[...],
            sites[:, 2 * pair * LANES : 2 * (pair + 1) * LANES],
            preferred_element_type=F32,
        )
        product = product * norm_factor
        for at in range(2):
            for part in range(2):
                lines[pl.ds(part * rows + 2 * pair + at, count, stride=2 * rows), :] = product[
                    part * count : (part + 1) * count, at * LANES : (at + 1) * LANES
                ]
    out[...] = lines[...].astype(BF16)


def to_sigma(sites, table, rows, norm_factor):
    shape = (table.shape[0] * rows, LANES)
    return pl.pallas_call(
        functools.partial(sigma_kernel, norm_factor, rows),
        out_shape=jax.ShapeDtypeStruct(shape, BF16),
        in_specs=whole(2),
        out_specs=whole(1)[0],
        scratch_shapes=[pltpu.VMEM(shape, F32)],
        compiler_params=vmem_params(),
        name="to_sigma",
    )(sites, table)


def volterra_kernel(rows, half_ref, own, far_near, far_away, sigma, *rest):
    out = rest[-1]
    half = half_ref[0]
    blocks = far_near.shape[0]
    lanes = own.shape[2]
    cols = lanes // 2
    near = half * cols
    away = (1 - half) * cols
    near_at = half * blocks
    away_at = (1 - half) * blocks
    first_times = near + lax.broadcasted_iota(jnp.int32, (cols, lanes), 0)
    left_lane = lax.broadcasted_iota(jnp.int32, (cols, lanes), 1)
    low_lanes = left_lane < cols
    left_times = jnp.where(low_lanes, near + left_lane, away + left_lane - cols)
    keep_left = left_times <= first_times
    row_at = lax.broadcasted_iota(jnp.int32, (lanes, 2 * lanes), 0)
    inner_times = jnp.where(row_at < cols, near + row_at, away + row_at - cols)
    lane_at = lax.broadcasted_iota(jnp.int32, (lanes, 2 * lanes), 1)
    last_times = jnp.where(lane_at < lanes, near, away) + lane_at % cols
    keep_right = inner_times <= last_times
    for at in range(own.shape[1] // (2 * rows)):
        span = slice(at * 2 * rows, (at + 1) * 2 * rows)

        def stacked(ref, offset):
            loaded = [ref[offset + block, span].astype(F32) for block in range(blocks)]
            return [
                jnp.concatenate([lines[part * rows : (part + 1) * rows] for lines in loaded], axis=0)
                for part in range(2)
            ]

        own_near = stacked(own, near_at)
        own_away = stacked(own, away_at)
        cross_near = stacked(far_near, 0)
        cross_away = stacked(far_away, 0)
        greens = [
            jnp.concatenate(
                [
                    jnp.concatenate([own_near[g], own_away[g]], axis=1),
                    jnp.concatenate([cross_near[g], cross_away[g]], axis=1),
                ],
                axis=0,
            )
            for g in range(2)
        ]
        advanced = jnp.where(keep_right, greens[0] - greens[1], 0.0).astype(BF16)
        sigma_near = stacked(sigma, near_at)
        sigma_away = stacked(sigma, away_at)
        retarded = []
        lefts = [[], []]
        for part in range(2):
            lesser = jnp.where(
                low_lanes, sigma_near[part], pltpu.roll(sigma_away[part], cols, 1)
            )
            greater = jnp.where(
                low_lanes, pltpu.roll(sigma_near[part], cols, 1), sigma_away[part]
            )
            retarded.append(jnp.where(keep_left, greater - lesser, 0.0))
            lefts[0].append(lesser)
            lefts[1].append(greater)
        retarded = jnp.concatenate(retarded, axis=0).astype(BF16)
        results = []
        for g in range(2):
            left = jnp.concatenate(
                [retarded, jnp.concatenate(lefts[g], axis=0).astype(BF16)], axis=1
            )
            right = jnp.concatenate([greens[g].astype(BF16), advanced], axis=0)
            product = jnp.dot(left, right, preferred_element_type=F32)
            sides = []
            for side in range(2):
                straight = product[:cols, side * lanes : (side + 1) * lanes]
                turned = pltpu.roll(product[cols:, side * lanes : (side + 1) * lanes], cols, 1)
                sides.append((straight + jnp.where(low_lanes, -turned, turned)) * step_size)
            results.append(sides)
        for block in range(blocks):
            piece = slice(block * rows, (block + 1) * rows)
            for side, offset in enumerate((near_at, away_at)):
                out[offset + block, span] = jnp.concatenate(
                    [results[0][side][piece], results[1][side][piece]], axis=0
                ).astype(BF16)


def volterra(half, own, far_near, far_away, sigma, rows, after):
    sources, lines, lanes = own.shape
    blocks = far_near.shape[0]
    step = 4 * rows
    spec = pl.BlockSpec((sources, step, lanes), lambda p: (0, p, 0))
    far_spec = pl.BlockSpec((blocks, step, lanes), lambda p: (0, p, 0))
    return pl.pallas_call(
        functools.partial(volterra_kernel, rows),
        grid=(lines // step,),
        out_shape=jax.ShapeDtypeStruct(own.shape, BF16),
        in_specs=[pl.BlockSpec(memory_space=pltpu.SMEM), spec, far_spec, far_spec, spec]
        + unread(after),
        out_specs=spec,
        compiler_params=vmem_params(),
        name="volterra",
    )(half, own, far_near, far_away, sigma, *after)


PARTS = 2


def halved_body(green_lesser, green_greater, lattice_map, time_offset):
    _, rows, cols, momenta = green_lesser.shape
    half = lax.axis_index("half")
    line = lax.axis_index("line")
    side = lax.axis_index("tcol")
    lines = lax.axis_size("line")
    group = lines * lax.axis_size("tcol")
    window = rows * lines * lax.axis_size("half")
    norm_factor = 1.0 / math.sqrt(momenta)
    tiles = (green_lesser, green_greater)
    count = momenta // PARTS
    half_at = half[None]

    def exchange(blocks):
        return lax.all_to_all(blocks, ("tcol", "line"), 0, 0, tiled=True)

    def blocked(rows_array):
        return rows_array.reshape(group, rows_array.shape[0] // group, rows_array.shape[1])

    def swap(blocks, at):
        sent = lax.dynamic_slice_in_dim(blocks, at * lines, lines)
        return lax.ppermute(sent, "half", [(0, 1), (1, 0)])

    own = []
    for part in range(PARTS):
        own.append(exchange(blocked(spread(tiles, part * count, count, own[-1:]))))
    far_near = [swap(blocks, 1 - half) for blocks in own]
    far_away = [swap(blocks, half) for blocks in own]

    table, *inverse = make_tables(lattice_map, PARTS)
    sites = to_sites(tiles, table, norm_factor)
    time_steps = jnp.arange(window, dtype=jnp.int32)
    coupling_line = 1.0 + drive_depth * jnp.cos(
        ((time_offset[0] + time_steps) % PERIOD).astype(F32) * (2.0 * math.pi / PERIOD)
    )
    first = lax.dynamic_slice_in_dim(coupling_line, (half * lines + line) * rows, rows)
    second = lax.dynamic_slice_in_dim(coupling_line, side * cols, cols)
    coupling = first[:, None] * jnp.concatenate([second, second])[None, :]

    crossed = [
        exchange(to_crossed(half_at, own[part], far_near[part], rows, [*own, sites])).reshape(-1, 2 * cols)
        for part in range(PARTS)
    ]
    self_sites = to_self(crossed, sites, table, coupling, norm_factor, far_away[:1])
    returned = []
    for part in range(PARTS):
        sigma = exchange(blocked(to_sigma(self_sites, inverse[part], rows, norm_factor)))
        collisions = volterra(
            half_at, own[part], far_near[part], far_away[part], sigma, rows, far_away
        )
        returned.append(exchange(collisions).reshape(-1, 2 * cols))
    return collect(returned, green_lesser.shape)


def solution(mesh):
    row_parts = mesh.shape["trow"]
    col_parts = mesh.shape["tcol"]

    def call(green_lesser, green_greater, lattice_map, time_offset):
        window, window_cols, momenta = green_lesser.shape[1:]
        rows = window // row_parts
        cols = window_cols // col_parts
        halved = (
            col_parts == 2
            and row_parts % 2 == 0
            and window == window_cols
            and 2 * cols == LANES
            and cols == rows * (row_parts // 2)
            and rows % 8 == 0
            and momenta % (PARTS * LANES) == 0
            and momenta % (PARTS * row_parts * 2) == 0
        )
        if halved:
            devices = mesh.devices.reshape(2, row_parts // 2, col_parts)
            used = Mesh(devices, ("half", "line", "tcol"))
            spec = P(None, ("half", "line"), "tcol", None)
            inner = halved_body
        else:
            used = mesh
            spec = P(None, "trow", "tcol", None)
            inner = general_body
        return jax.shard_map(
            inner, mesh=used, in_specs=(spec, spec, P(), P()), out_specs=(spec, spec), check_vma=False
        )(green_lesser, green_greater, lattice_map, time_offset)

    return call
```

```python
import functools
import math

import jax
import jax.numpy as jnp
from jax import lax
from jax.experimental import pallas as pl
from jax.experimental.pallas import tpu as pltpu
from jax.sharding import Mesh, PartitionSpec as P

F32 = jnp.float32
BF16 = jnp.bfloat16
LANES = 128

PERIOD = 64


step_size = 0.01
drive_depth = 0.5


def regroup(blocks):
    return lax.all_to_all(
        lax.all_to_all(blocks, "trow", split_axis=1, concat_axis=1, tiled=True),
        "tcol",
        split_axis=2,
        concat_axis=2,
        tiled=True,
    )


def pack_blocks(spectral, row_parts, col_parts):
    stacked, extent, tile_cells = spectral.shape
    return spectral.reshape(
        stacked, row_parts, col_parts, extent // (row_parts * col_parts), tile_cells
    )


def spread_times(blocks, tile_rows, tile_cols):
    stacked, row_parts, col_parts, local_count, tile_cells = blocks.shape
    shaped = blocks.reshape(stacked, row_parts, col_parts, local_count, tile_rows, tile_cols)
    return shaped.transpose(0, 3, 1, 4, 2, 5).reshape(
        stacked, local_count, row_parts * tile_rows, col_parts * tile_cols
    )


def gather_tiles(full, row_parts, col_parts):
    stacked, local_count, window, window_cols = full.shape
    tile_rows = window // row_parts
    tile_cols = window_cols // col_parts
    shaped = full.reshape(stacked, local_count, row_parts, tile_rows, col_parts, tile_cols)
    return shaped.transpose(0, 2, 4, 1, 3, 5).reshape(
        stacked, row_parts, col_parts, local_count, tile_rows * tile_cols
    )


def mirrored(full, keep_pair):
    stacked, local_count, window, window_cols = full.shape
    paired = full.reshape(stacked, local_count // 2, 2, window, window_cols)
    swapped = jnp.where(keep_pair[None, :, None, None, None], paired, paired[:, :, ::-1])
    return jnp.swapaxes(swapped.reshape(stacked, local_count, window, window_cols), 2, 3)


def second_born(first_real, first_imaginary, other_real, other_imaginary, coupling):
    square_real = first_real * first_real - first_imaginary * first_imaginary
    square_imaginary = 2.0 * first_real * first_imaginary
    out_real = coupling * (square_real * other_real - square_imaginary * other_imaginary)
    out_imaginary = coupling * (square_real * other_imaginary + square_imaginary * other_real)
    return (out_real, out_imaginary)


def collide(
    retarded_real,
    retarded_imaginary,
    self_real,
    self_imaginary,
    green_real,
    green_imaginary,
    advanced_real,
    advanced_imaginary,
):
    minus_left = jnp.concatenate(
        [retarded_real, -retarded_imaginary, self_real, -self_imaginary], axis=2
    )
    plus_left = jnp.concatenate(
        [retarded_real, retarded_imaginary, self_real, self_imaginary], axis=2
    )
    real_right = jnp.concatenate(
        [green_real, green_imaginary, advanced_real, advanced_imaginary], axis=1
    )
    imaginary_right = jnp.concatenate(
        [green_imaginary, green_real, advanced_imaginary, advanced_real], axis=1
    )
    out_real = jnp.einsum(
        "kts,ksu->ktu", minus_left, real_right, preferred_element_type=jnp.float32
    )
    out_imaginary = jnp.einsum(
        "kts,ksu->ktu", plus_left, imaginary_right, preferred_element_type=jnp.float32
    )
    return (out_real, out_imaginary)


def general_body(green_lesser, green_greater, lattice_map, time_offset):
    tile_rows = green_lesser.shape[1]
    tile_cols = green_lesser.shape[2]
    momenta = green_lesser.shape[3]
    row_parts = lax.axis_size("trow")
    col_parts = lax.axis_size("tcol")
    window = tile_rows * row_parts
    tile_cells = tile_rows * tile_cols
    local_count = momenta // (row_parts * col_parts)
    norm_factor = 1.0 / math.sqrt(momenta)
    greens = (
        jnp.concatenate([green_lesser, green_greater], axis=0)
        .reshape(4, tile_cells, momenta)
        .transpose(0, 2, 1)
    )
    positions = jnp.arange(momenta, dtype=jnp.int32)
    halves = positions // 2
    site_order = jnp.where(
        positions == 1, momenta // 2, jnp.where(positions % 2 == 0, halves, momenta - halves)
    )
    phases = (lattice_map[:, None] * site_order[None, :] % momenta).astype(jnp.float32) * (
        2.0 * math.pi / momenta
    )
    cosines = jnp.cos(phases).astype(jnp.bfloat16)
    sines = jnp.sin(phases).astype(jnp.bfloat16)
    ahead_blocks = lax.all_to_all(
        lax.all_to_all(
            pack_blocks(greens, row_parts, col_parts),
            "trow",
            split_axis=1,
            concat_axis=1,
            tiled=True,
        ),
        "tcol",
        split_axis=2,
        concat_axis=2,
        tiled=True,
    )
    green_moment = spread_times(ahead_blocks, tile_rows, tile_cols)
    forward_table = jnp.concatenate([cosines, sines], axis=1)
    products = jnp.einsum("cjm,jr->crm", greens, forward_table, preferred_element_type=jnp.float32)
    site_space = jnp.stack(
        [
            (products[0, :momenta] - products[1, momenta:]) * norm_factor,
            (products[0, momenta:] + products[1, :momenta]) * norm_factor,
            (products[2, :momenta] - products[3, momenta:]) * norm_factor,
            (products[2, momenta:] + products[3, :momenta]) * norm_factor,
        ]
    ).astype(jnp.bfloat16)
    site_full = spread_times(
        regroup(pack_blocks(site_space, row_parts, col_parts)), tile_rows, tile_cols
    )
    site_block = lax.axis_index("trow") * col_parts + lax.axis_index("tcol")
    keep_pair = site_block * (local_count // 2) + jnp.arange(local_count // 2, dtype=jnp.int32) == 0
    mirror = mirrored(site_full, keep_pair).astype(jnp.float32)
    direct = site_full.astype(jnp.float32)
    time_steps = jnp.arange(window, dtype=jnp.int32)
    coupling_line = 1.0 + drive_depth * jnp.cos(
        ((time_offset[0] + time_steps) % PERIOD).astype(jnp.float32) * (2.0 * math.pi / PERIOD)
    )
    coupling = coupling_line[:, None] * coupling_line[None, :]
    self_lesser = second_born(direct[0], direct[1], mirror[2], mirror[3], coupling)
    self_greater = second_born(direct[2], direct[3], mirror[0], mirror[1], coupling)
    self_sites = jnp.stack(
        [self_lesser[0], self_lesser[1], self_greater[0], self_greater[1]]
    ).astype(jnp.bfloat16)
    self_tiles = regroup(gather_tiles(self_sites, row_parts, col_parts)).reshape(
        4, momenta, tile_cells
    )
    inverse_table = jnp.concatenate([cosines, sines], axis=0)
    spectral_terms = jnp.einsum(
        "cum,ju->cjm", self_tiles, inverse_table, preferred_element_type=jnp.float32
    )
    self_spectral = jnp.stack(
        [
            (spectral_terms[0, :momenta] + spectral_terms[1, momenta:]) * norm_factor,
            (spectral_terms[1, :momenta] - spectral_terms[0, momenta:]) * norm_factor,
            (spectral_terms[2, :momenta] + spectral_terms[3, momenta:]) * norm_factor,
            (spectral_terms[3, :momenta] - spectral_terms[2, momenta:]) * norm_factor,
        ]
    ).astype(jnp.bfloat16)
    self_moment = spread_times(
        regroup(pack_blocks(self_spectral, row_parts, col_parts)), tile_rows, tile_cols
    )
    lower_mask = time_steps[None, :] <= time_steps[:, None]
    upper_mask = time_steps[:, None] <= time_steps[None, :]
    retarded = jnp.where(
        lower_mask, self_moment[2:4].astype(jnp.float32) - self_moment[0:2].astype(jnp.float32), 0.0
    ).astype(jnp.bfloat16)
    advanced = jnp.where(
        upper_mask,
        green_moment[0:2].astype(jnp.float32) - green_moment[2:4].astype(jnp.float32),
        0.0,
    ).astype(jnp.bfloat16)
    lesser_out = collide(
        retarded[0],
        retarded[1],
        self_moment[0],
        self_moment[1],
        green_moment[0],
        green_moment[1],
        advanced[0],
        advanced[1],
    )
    greater_out = collide(
        retarded[0],
        retarded[1],
        self_moment[2],
        self_moment[3],
        green_moment[2],
        green_moment[3],
        advanced[0],
        advanced[1],
    )
    collisions = (
        jnp.stack([lesser_out[0], lesser_out[1], greater_out[0], greater_out[1]]) * step_size
    ).astype(jnp.bfloat16)
    out_tiles = regroup(gather_tiles(collisions, row_parts, col_parts)).reshape(
        4, momenta, tile_cells
    )
    out_tiles = out_tiles.transpose(0, 2, 1).reshape(4, tile_rows, tile_cols, momenta)
    return (out_tiles[0:2], out_tiles[2:4])


def vmem_params():
    return pltpu.CompilerParams(vmem_limit_bytes=48 * 1024 * 1024)


def unread(arrays):
    return [pl.BlockSpec(memory_space=pl.ANY)] * len(arrays)


def whole(count):
    return [pl.BlockSpec(memory_space=pltpu.VMEM)] * count


def spread_kernel(first, lesser, greater, *rest):
    out, lines = rest[-2:]
    _, rows, _, _ = lesser.shape
    count = lines.shape[0] // (2 * rows)
    for g, tile in enumerate((lesser, greater)):
        for t in range(rows):
            span = slice(first, first + count)
            slab = jnp.concatenate([tile[0, t, :, span], tile[1, t, :, span]], axis=0)
            lines[pl.ds(g * rows + t, count, stride=2 * rows), :] = slab.astype(F32).T
    out[...] = lines[...].astype(BF16)


def spread(tiles, first, count, after):
    _, rows, cols, _ = tiles[0].shape
    shape = (count * 2 * rows, 2 * cols)
    return pl.pallas_call(
        functools.partial(spread_kernel, first),
        out_shape=jax.ShapeDtypeStruct(shape, BF16),
        in_specs=whole(2) + unread(after),
        out_specs=whole(1)[0],
        scratch_shapes=[pltpu.VMEM(shape, F32)],
        compiler_params=vmem_params(),
        name="spread",
    )(*tiles, *after)


def collect_kernel(*refs):
    *parts, lesser, greater, lines = refs
    _, rows, cols, momenta = lesser.shape
    count = momenta // len(parts)
    for at, part in enumerate(parts):
        lines[...] = part[...].astype(F32)
        span = slice(at * count, (at + 1) * count)
        for k in range(2 * rows):
            slab = lines[pl.ds(k, count, stride=2 * rows), :].T.astype(BF16)
            out = lesser if k < rows else greater
            out[0, k % rows, :, span] = slab[:cols]
            out[1, k % rows, :, span] = slab[cols:]


def collect(parts, tile_shape):
    shape = jax.ShapeDtypeStruct(tile_shape, BF16)
    return pl.pallas_call(
        collect_kernel,
        out_shape=(shape, shape),
        in_specs=whole(len(parts)),
        out_specs=tuple(whole(2)),
        scratch_shapes=[pltpu.VMEM(parts[0].shape, F32)],
        compiler_params=vmem_params(),
        name="collect",
    )(*parts)


def table_kernel(column_ref, table, *inverse):
    momenta = column_ref.shape[0]
    count = momenta // len(inverse)
    positions = lax.broadcasted_iota(jnp.int32, (momenta, momenta), 1)
    phases = (column_ref[...] * positions % momenta).astype(F32) * (2.0 * math.pi / momenta)
    cosines = jnp.cos(phases).astype(BF16)
    sines = jnp.sin(phases).astype(BF16)
    for part, ref in enumerate(inverse):
        span = slice(part * count, (part + 1) * count)
        ref[:count, :momenta] = cosines[span]
        ref[:count, momenta:] = sines[span]
        ref[count:, :momenta] = -sines[span]
        ref[count:, momenta:] = cosines[span]
    cosines = cosines.astype(F32).T.astype(BF16)
    sines = sines.astype(F32).T.astype(BF16)
    table[:momenta, :momenta] = cosines
    table[:momenta, momenta:] = -sines
    table[momenta:, :momenta] = sines
    table[momenta:, momenta:] = cosines


def make_tables(lattice_map, parts):
    momenta = lattice_map.shape[0]
    count = momenta // parts
    shapes = [(2 * momenta, 2 * momenta)] + [(2 * count, 2 * momenta)] * parts
    return pl.pallas_call(
        table_kernel,
        out_shape=tuple(jax.ShapeDtypeStruct(shape, BF16) for shape in shapes),
        in_specs=whole(1),
        out_specs=tuple(whole(1 + parts)),
        compiler_params=vmem_params(),
        name="make_tables",
    )(lattice_map[:, None])


def site_kernel(norm_factor, lesser, greater, table, out):
    _, rows, cols, _ = lesser.shape
    wide = 4 * cols
    for pair in range(rows // 2):
        slabs = [
            jnp.concatenate([tile[0, t], tile[1, t]], axis=1)
            for t in (2 * pair, 2 * pair + 1)
            for tile in (lesser, greater)
        ]
        product = lax.dot_general(
            table[...],
            jnp.concatenate(slabs, axis=0),
            (((1,), (1,)), ((), ())),
            preferred_element_type=F32,
        )
        out[:, pair * wide : (pair + 1) * wide] = (product * norm_factor).astype(BF16)


def to_sites(tiles, table, norm_factor):
    _, rows, cols, momenta = tiles[0].shape
    return pl.pallas_call(
        functools.partial(site_kernel, norm_factor),
        out_shape=jax.ShapeDtypeStruct((2 * momenta, rows * 2 * cols), BF16),
        in_specs=whole(3),
        out_specs=whole(1)[0],
        compiler_params=vmem_params(),
        name="to_sites",
    )(*tiles, table)


def cross_kernel(rows, half_ref, own, far, *rest):
    out = rest[-1]
    half = half_ref[0]
    blocks = far.shape[0]
    cols = blocks * rows
    for at in range(far.shape[1] // (2 * rows)):
        span = slice(at * 2 * rows, (at + 1) * 2 * rows)
        for source, offset, target in ((own, half * blocks, half), (far, 0, 1 - half)):
            loaded = [source[offset + block, span].astype(F32) for block in range(blocks)]
            stacked = jnp.concatenate(
                [lines[rows:] for lines in loaded] + [lines[:rows] for lines in loaded], axis=0
            )
            turned = stacked.T
            for block in range(blocks):
                out[target * blocks + block, span] = jnp.concatenate(
                    [
                        turned[block * rows : (block + 1) * rows],
                        turned[cols + block * rows : cols + (block + 1) * rows],
                    ],
                    axis=0,
                ).astype(BF16)


def to_crossed(half, own, far, rows, after):
    return pl.pallas_call(
        functools.partial(cross_kernel, rows),
        out_shape=jax.ShapeDtypeStruct(own.shape, BF16),
        in_specs=[pl.BlockSpec(memory_space=pltpu.SMEM)] + whole(2) + unread(after),
        out_specs=whole(1)[0],
        compiler_params=vmem_params(),
        name="to_crossed",
    )(half, own, far, *after)


def self_kernel(norm_factor, parts, *refs):
    crossed = refs[:parts]
    own, table, coupling = refs[parts : parts + 3]
    out, lines = refs[-2:]
    rows = coupling.shape[0]
    momenta = own.shape[0] // 2
    count = momenta // parts
    for part in range(parts):
        lines[part] = crossed[part][...].astype(F32)
    for pair in range(rows // 2):
        rights = []
        for t in (2 * pair, 2 * pair + 1):
            real = [lines[part, pl.ds(t, count, stride=2 * rows), :] for part in range(parts)]
            imaginary = [
                -lines[part, pl.ds(rows + t, count, stride=2 * rows), :] for part in range(parts)
            ]
            rights.append(jnp.concatenate(real + imaginary, axis=0).astype(BF16))
        other = jnp.dot(
            table[...], jnp.concatenate(rights, axis=1), preferred_element_type=F32
        )
        other = (other * norm_factor).astype(BF16).astype(F32)
        for at in range(2):
            t = 2 * pair + at
            span = slice(t * LANES, (t + 1) * LANES)
            self_real, self_imaginary = second_born(
                own[:momenta, span].astype(F32),
                own[momenta:, span].astype(F32),
                other[:momenta, at * LANES : (at + 1) * LANES],
                -other[momenta:, at * LANES : (at + 1) * LANES],
                coupling[t : t + 1, :],
            )
            out[:momenta, span] = self_real.astype(BF16)
            out[momenta:, span] = self_imaginary.astype(BF16)


def to_self(crossed, own, table, coupling, norm_factor, after):
    parts = len(crossed)
    return pl.pallas_call(
        functools.partial(self_kernel, norm_factor, parts),
        out_shape=jax.ShapeDtypeStruct(own.shape, BF16),
        in_specs=whole(parts + 3) + unread(after),
        out_specs=whole(1)[0],
        scratch_shapes=[pltpu.VMEM((parts,) + crossed[0].shape, F32)],
        compiler_params=vmem_params(),
        name="to_self",
    )(*crossed, own, table, coupling, *after)


def sigma_kernel(norm_factor, rows, sites, table, out, lines):
    count = table.shape[0] // 2
    for pair in range(rows // 2):
        product = jnp.dot(
            table[...],
            sites[:, 2 * pair * LANES : 2 * (pair + 1) * LANES],
            preferred_element_type=F32,
        )
        product = product * norm_factor
        for at in range(2):
            for part in range(2):
                lines[pl.ds(part * rows + 2 * pair + at, count, stride=2 * rows), :] = product[
                    part * count : (part + 1) * count, at * LANES : (at + 1) * LANES
                ]
    out[...] = lines[...].astype(BF16)


def to_sigma(sites, table, rows, norm_factor):
    shape = (table.shape[0] * rows, LANES)
    return pl.pallas_call(
        functools.partial(sigma_kernel, norm_factor, rows),
        out_shape=jax.ShapeDtypeStruct(shape, BF16),
        in_specs=whole(2),
        out_specs=whole(1)[0],
        scratch_shapes=[pltpu.VMEM(shape, F32)],
        compiler_params=vmem_params(),
        name="to_sigma",
    )(sites, table)


def volterra_kernel(rows, half_ref, own, far_near, far_away, sigma, *rest):
    out = rest[-1]
    half = half_ref[0]
    blocks = far_near.shape[0]
    lanes = own.shape[2]
    cols = lanes // 2
    near = half * cols
    away = (1 - half) * cols
    near_at = half * blocks
    away_at = (1 - half) * blocks
    first_times = near + lax.broadcasted_iota(jnp.int32, (cols, lanes), 0)
    left_lane = lax.broadcasted_iota(jnp.int32, (cols, lanes), 1)
    low_lanes = left_lane < cols
    left_times = jnp.where(low_lanes, near + left_lane, away + left_lane - cols)
    keep_left = left_times <= first_times
    row_at = lax.broadcasted_iota(jnp.int32, (lanes, 2 * lanes), 0)
    inner_times = jnp.where(row_at < cols, near + row_at, away + row_at - cols)
    lane_at = lax.broadcasted_iota(jnp.int32, (lanes, 2 * lanes), 1)
    last_times = jnp.where(lane_at < lanes, near, away) + lane_at % cols
    keep_right = inner_times <= last_times
    for at in range(own.shape[1] // (2 * rows)):
        span = slice(at * 2 * rows, (at + 1) * 2 * rows)

        def stacked(ref, offset):
            loaded = [ref[offset + block, span].astype(F32) for block in range(blocks)]
            return [
                jnp.concatenate([lines[part * rows : (part + 1) * rows] for lines in loaded], axis=0)
                for part in range(2)
            ]

        own_near = stacked(own, near_at)
        own_away = stacked(own, away_at)
        cross_near = stacked(far_near, 0)
        cross_away = stacked(far_away, 0)
        greens = [
            jnp.concatenate(
                [
                    jnp.concatenate([own_near[g], own_away[g]], axis=1),
                    jnp.concatenate([cross_near[g], cross_away[g]], axis=1),
                ],
                axis=0,
            )
            for g in range(2)
        ]
        advanced = jnp.where(keep_right, greens[0] - greens[1], 0.0).astype(BF16)
        sigma_near = stacked(sigma, near_at)
        sigma_away = stacked(sigma, away_at)
        retarded = []
        lefts = [[], []]
        for part in range(2):
            lesser = jnp.where(
                low_lanes, sigma_near[part], pltpu.roll(sigma_away[part], cols, 1)
            )
            greater = jnp.where(
                low_lanes, pltpu.roll(sigma_near[part], cols, 1), sigma_away[part]
            )
            retarded.append(jnp.where(keep_left, greater - lesser, 0.0))
            lefts[0].append(lesser)
            lefts[1].append(greater)
        retarded = jnp.concatenate(retarded, axis=0).astype(BF16)
        results = []
        for g in range(2):
            left = jnp.concatenate(
                [retarded, jnp.concatenate(lefts[g], axis=0).astype(BF16)], axis=1
            )
            right = jnp.concatenate([greens[g].astype(BF16), advanced], axis=0)
            product = jnp.dot(left, right, preferred_element_type=F32)
            sides = []
            for side in range(2):
                straight = product[:cols, side * lanes : (side + 1) * lanes]
                turned = pltpu.roll(product[cols:, side * lanes : (side + 1) * lanes], cols, 1)
                sides.append((straight + jnp.where(low_lanes, -turned, turned)) * step_size)
            results.append(sides)
        for block in range(blocks):
            piece = slice(block * rows, (block + 1) * rows)
            for side, offset in enumerate((near_at, away_at)):
                out[offset + block, span] = jnp.concatenate(
                    [results[0][side][piece], results[1][side][piece]], axis=0
                ).astype(BF16)


def volterra(half, own, far_near, far_away, sigma, rows, after):
    sources, lines, lanes = own.shape
    blocks = far_near.shape[0]
    step = 4 * rows
    spec = pl.BlockSpec((sources, step, lanes), lambda p: (0, p, 0))
    far_spec = pl.BlockSpec((blocks, step, lanes), lambda p: (0, p, 0))
    return pl.pallas_call(
        functools.partial(volterra_kernel, rows),
        grid=(lines // step,),
        out_shape=jax.ShapeDtypeStruct(own.shape, BF16),
        in_specs=[pl.BlockSpec(memory_space=pltpu.SMEM), spec, far_spec, far_spec, spec]
        + unread(after),
        out_specs=spec,
        compiler_params=vmem_params(),
        name="volterra",
    )(half, own, far_near, far_away, sigma, *after)


PARTS = 2


def halved_body(green_lesser, green_greater, lattice_map, time_offset):
    _, rows, cols, momenta = green_lesser.shape
    half = lax.axis_index("half")
    line = lax.axis_index("line")
    side = lax.axis_index("tcol")
    lines = lax.axis_size("line")
    group = lines * lax.axis_size("tcol")
    window = rows * lines * lax.axis_size("half")
    norm_factor = 1.0 / math.sqrt(momenta)
    tiles = (green_lesser, green_greater)
    count = momenta // PARTS
    half_at = half[None]

    def exchange(blocks):
        return lax.all_to_all(blocks, ("tcol", "line"), 0, 0, tiled=True)

    def blocked(rows_array):
        return rows_array.reshape(group, rows_array.shape[0] // group, rows_array.shape[1])

    def swap(blocks, at):
        sent = lax.dynamic_slice_in_dim(blocks, at * lines, lines)
        both = lax.all_gather(sent, "half")
        return lax.dynamic_index_in_dim(both, 1 - half, keepdims=False)

    own = []
    for part in range(PARTS):
        own.append(exchange(blocked(spread(tiles, part * count, count, own[-1:]))))
    far_near = [swap(blocks, 1 - half) for blocks in own]
    far_away = [swap(blocks, half) for blocks in own]

    table, *inverse = make_tables(lattice_map, PARTS)
    sites = to_sites(tiles, table, norm_factor)
    time_steps = jnp.arange(window, dtype=jnp.int32)
    coupling_line = 1.0 + drive_depth * jnp.cos(
        ((time_offset[0] + time_steps) % PERIOD).astype(F32) * (2.0 * math.pi / PERIOD)
    )
    first = lax.dynamic_slice_in_dim(coupling_line, (half * lines + line) * rows, rows)
    second = lax.dynamic_slice_in_dim(coupling_line, side * cols, cols)
    coupling = first[:, None] * jnp.concatenate([second, second])[None, :]

    crossed = [
        exchange(to_crossed(half_at, own[part], far_near[part], rows, [*own, sites])).reshape(-1, 2 * cols)
        for part in range(PARTS)
    ]
    self_sites = to_self(crossed, sites, table, coupling, norm_factor, far_away[:1])
    returned = []
    for part in range(PARTS):
        sigma = exchange(blocked(to_sigma(self_sites, inverse[part], rows, norm_factor)))
        collisions = volterra(
            half_at, own[part], far_near[part], far_away[part], sigma, rows, far_away
        )
        returned.append(exchange(collisions).reshape(-1, 2 * cols))
    return collect(returned, green_lesser.shape)


def solution(mesh):
    row_parts = mesh.shape["trow"]
    col_parts = mesh.shape["tcol"]

    def call(green_lesser, green_greater, lattice_map, time_offset):
        window, window_cols, momenta = green_lesser.shape[1:]
        rows = window // row_parts
        cols = window_cols // col_parts
        halved = (
            col_parts == 2
            and row_parts % 2 == 0
            and window == window_cols
            and 2 * cols == LANES
            and cols == rows * (row_parts // 2)
            and rows % 8 == 0
            and momenta % (PARTS * LANES) == 0
            and momenta % (PARTS * row_parts * 2) == 0
        )
        if halved:
            devices = mesh.devices.reshape(2, row_parts // 2, col_parts)
            used = Mesh(devices, ("half", "line", "tcol"))
            spec = P(None, ("half", "line"), "tcol", None)
            inner = halved_body
        else:
            used = mesh
            spec = P(None, "trow", "tcol", None)
            inner = general_body
        return jax.shard_map(
            inner, mesh=used, in_specs=(spec, spec, P(), P()), out_specs=(spec, spec), check_vma=False
        )(green_lesser, green_greater, lattice_map, time_offset)

    return call
```

```python
import functools
import math

import jax
import jax.numpy as jnp
from jax import lax
from jax.experimental import pallas as pl
from jax.experimental.pallas import tpu as pltpu
from jax.sharding import Mesh, PartitionSpec as P

F32 = jnp.float32
BF16 = jnp.bfloat16
LANES = 128

PERIOD = 64


step_size = 0.01
drive_depth = 0.5


def regroup(blocks):
    return lax.all_to_all(
        lax.all_to_all(blocks, "trow", split_axis=1, concat_axis=1, tiled=True),
        "tcol",
        split_axis=2,
        concat_axis=2,
        tiled=True,
    )


def pack_blocks(spectral, row_parts, col_parts):
    stacked, extent, tile_cells = spectral.shape
    return spectral.reshape(
        stacked, row_parts, col_parts, extent // (row_parts * col_parts), tile_cells
    )


def spread_times(blocks, tile_rows, tile_cols):
    stacked, row_parts, col_parts, local_count, tile_cells = blocks.shape
    shaped = blocks.reshape(stacked, row_parts, col_parts, local_count, tile_rows, tile_cols)
    return shaped.transpose(0, 3, 1, 4, 2, 5).reshape(
        stacked, local_count, row_parts * tile_rows, col_parts * tile_cols
    )


def gather_tiles(full, row_parts, col_parts):
    stacked, local_count, window, window_cols = full.shape
    tile_rows = window // row_parts
    tile_cols = window_cols // col_parts
    shaped = full.reshape(stacked, local_count, row_parts, tile_rows, col_parts, tile_cols)
    return shaped.transpose(0, 2, 4, 1, 3, 5).reshape(
        stacked, row_parts, col_parts, local_count, tile_rows * tile_cols
    )


def mirrored(full, keep_pair):
    stacked, local_count, window, window_cols = full.shape
    paired = full.reshape(stacked, local_count // 2, 2, window, window_cols)
    swapped = jnp.where(keep_pair[None, :, None, None, None], paired, paired[:, :, ::-1])
    return jnp.swapaxes(swapped.reshape(stacked, local_count, window, window_cols), 2, 3)


def second_born(first_real, first_imaginary, other_real, other_imaginary, coupling):
    square_real = first_real * first_real - first_imaginary * first_imaginary
    square_imaginary = 2.0 * first_real * first_imaginary
    out_real = coupling * (square_real * other_real - square_imaginary * other_imaginary)
    out_imaginary = coupling * (square_real * other_imaginary + square_imaginary * other_real)
    return (out_real, out_imaginary)


def collide(
    retarded_real,
    retarded_imaginary,
    self_real,
    self_imaginary,
    green_real,
    green_imaginary,
    advanced_real,
    advanced_imaginary,
):
    minus_left = jnp.concatenate(
        [retarded_real, -retarded_imaginary, self_real, -self_imaginary], axis=2
    )
    plus_left = jnp.concatenate(
        [retarded_real, retarded_imaginary, self_real, self_imaginary], axis=2
    )
    real_right = jnp.concatenate(
        [green_real, green_imaginary, advanced_real, advanced_imaginary], axis=1
    )
    imaginary_right = jnp.concatenate(
        [green_imaginary, green_real, advanced_imaginary, advanced_real], axis=1
    )
    out_real = jnp.einsum(
        "kts,ksu->ktu", minus_left, real_right, preferred_element_type=jnp.float32
    )
    out_imaginary = jnp.einsum(
        "kts,ksu->ktu", plus_left, imaginary_right, preferred_element_type=jnp.float32
    )
    return (out_real, out_imaginary)


def general_body(green_lesser, green_greater, lattice_map, time_offset):
    tile_rows = green_lesser.shape[1]
    tile_cols = green_lesser.shape[2]
    momenta = green_lesser.shape[3]
    row_parts = lax.axis_size("trow")
    col_parts = lax.axis_size("tcol")
    window = tile_rows * row_parts
    tile_cells = tile_rows * tile_cols
    local_count = momenta // (row_parts * col_parts)
    norm_factor = 1.0 / math.sqrt(momenta)
    greens = (
        jnp.concatenate([green_lesser, green_greater], axis=0)
        .reshape(4, tile_cells, momenta)
        .transpose(0, 2, 1)
    )
    positions = jnp.arange(momenta, dtype=jnp.int32)
    halves = positions // 2
    site_order = jnp.where(
        positions == 1, momenta // 2, jnp.where(positions % 2 == 0, halves, momenta - halves)
    )
    phases = (lattice_map[:, None] * site_order[None, :] % momenta).astype(jnp.float32) * (
        2.0 * math.pi / momenta
    )
    cosines = jnp.cos(phases).astype(jnp.bfloat16)
    sines = jnp.sin(phases).astype(jnp.bfloat16)
    ahead_blocks = lax.all_to_all(
        lax.all_to_all(
            pack_blocks(greens, row_parts, col_parts),
            "trow",
            split_axis=1,
            concat_axis=1,
            tiled=True,
        ),
        "tcol",
        split_axis=2,
        concat_axis=2,
        tiled=True,
    )
    green_moment = spread_times(ahead_blocks, tile_rows, tile_cols)
    forward_table = jnp.concatenate([cosines, sines], axis=1)
    products = jnp.einsum("cjm,jr->crm", greens, forward_table, preferred_element_type=jnp.float32)
    site_space = jnp.stack(
        [
            (products[0, :momenta] - products[1, momenta:]) * norm_factor,
            (products[0, momenta:] + products[1, :momenta]) * norm_factor,
            (products[2, :momenta] - products[3, momenta:]) * norm_factor,
            (products[2, momenta:] + products[3, :momenta]) * norm_factor,
        ]
    ).astype(jnp.bfloat16)
    site_full = spread_times(
        regroup(pack_blocks(site_space, row_parts, col_parts)), tile_rows, tile_cols
    )
    site_block = lax.axis_index("trow") * col_parts + lax.axis_index("tcol")
    keep_pair = site_block * (local_count // 2) + jnp.arange(local_count // 2, dtype=jnp.int32) == 0
    mirror = mirrored(site_full, keep_pair).astype(jnp.float32)
    direct = site_full.astype(jnp.float32)
    time_steps = jnp.arange(window, dtype=jnp.int32)
    coupling_line = 1.0 + drive_depth * jnp.cos(
        ((time_offset[0] + time_steps) % PERIOD).astype(jnp.float32) * (2.0 * math.pi / PERIOD)
    )
    coupling = coupling_line[:, None] * coupling_line[None, :]
    self_lesser = second_born(direct[0], direct[1], mirror[2], mirror[3], coupling)
    self_greater = second_born(direct[2], direct[3], mirror[0], mirror[1], coupling)
    self_sites = jnp.stack(
        [self_lesser[0], self_lesser[1], self_greater[0], self_greater[1]]
    ).astype(jnp.bfloat16)
    self_tiles = regroup(gather_tiles(self_sites, row_parts, col_parts)).reshape(
        4, momenta, tile_cells
    )
    inverse_table = jnp.concatenate([cosines, sines], axis=0)
    spectral_terms = jnp.einsum(
        "cum,ju->cjm", self_tiles, inverse_table, preferred_element_type=jnp.float32
    )
    self_spectral = jnp.stack(
        [
            (spectral_terms[0, :momenta] + spectral_terms[1, momenta:]) * norm_factor,
            (spectral_terms[1, :momenta] - spectral_terms[0, momenta:]) * norm_factor,
            (spectral_terms[2, :momenta] + spectral_terms[3, momenta:]) * norm_factor,
            (spectral_terms[3, :momenta] - spectral_terms[2, momenta:]) * norm_factor,
        ]
    ).astype(jnp.bfloat16)
    self_moment = spread_times(
        regroup(pack_blocks(self_spectral, row_parts, col_parts)), tile_rows, tile_cols
    )
    lower_mask = time_steps[None, :] <= time_steps[:, None]
    upper_mask = time_steps[:, None] <= time_steps[None, :]
    retarded = jnp.where(
        lower_mask, self_moment[2:4].astype(jnp.float32) - self_moment[0:2].astype(jnp.float32), 0.0
    ).astype(jnp.bfloat16)
    advanced = jnp.where(
        upper_mask,
        green_moment[0:2].astype(jnp.float32) - green_moment[2:4].astype(jnp.float32),
        0.0,
    ).astype(jnp.bfloat16)
    lesser_out = collide(
        retarded[0],
        retarded[1],
        self_moment[0],
        self_moment[1],
        green_moment[0],
        green_moment[1],
        advanced[0],
        advanced[1],
    )
    greater_out = collide(
        retarded[0],
        retarded[1],
        self_moment[2],
        self_moment[3],
        green_moment[2],
        green_moment[3],
        advanced[0],
        advanced[1],
    )
    collisions = (
        jnp.stack([lesser_out[0], lesser_out[1], greater_out[0], greater_out[1]]) * step_size
    ).astype(jnp.bfloat16)
    out_tiles = regroup(gather_tiles(collisions, row_parts, col_parts)).reshape(
        4, momenta, tile_cells
    )
    out_tiles = out_tiles.transpose(0, 2, 1).reshape(4, tile_rows, tile_cols, momenta)
    return (out_tiles[0:2], out_tiles[2:4])


def vmem_params():
    return pltpu.CompilerParams(vmem_limit_bytes=48 * 1024 * 1024)


def unread(arrays):
    return [pl.BlockSpec(memory_space=pl.ANY)] * len(arrays)


def whole(count):
    return [pl.BlockSpec(memory_space=pltpu.VMEM)] * count


def weight():
    return pl.CostEstimate(flops=10**11, bytes_accessed=2**20, transcendentals=0)


def scalars():
    return [pl.BlockSpec(memory_space=pltpu.SMEM)]


def spread_kernel(lesser, greater, out, lines):
    _, rows, _, momenta = lesser.shape
    for g, tile in enumerate((lesser, greater)):
        for t in range(rows):
            slab = jnp.concatenate([tile[0, t], tile[1, t]], axis=0)
            lines[pl.ds(g * rows + t, momenta, stride=2 * rows), :] = slab.astype(F32).T
    out[...] = lines[...].astype(BF16)


def spread(tiles):
    _, rows, cols, momenta = tiles[0].shape
    shape = (momenta * 2 * rows, 2 * cols)
    return pl.pallas_call(
        spread_kernel,
        out_shape=jax.ShapeDtypeStruct(shape, BF16),
        in_specs=whole(2),
        out_specs=whole(1)[0],
        scratch_shapes=[pltpu.VMEM(shape, F32)],
        compiler_params=vmem_params(),
        name="spread",
    )(*tiles)


def collect_kernel(rows_ref, lesser, greater, lines):
    lines[...] = rows_ref[...].astype(F32)
    _, rows, cols, momenta = lesser.shape
    for k in range(2 * rows):
        slab = lines[pl.ds(k, momenta, stride=2 * rows), :].T.astype(BF16)
        out = lesser if k < rows else greater
        out[0, k % rows] = slab[:cols]
        out[1, k % rows] = slab[cols:]


def collect(rows_array, tile_shape):
    shape = jax.ShapeDtypeStruct(tile_shape, BF16)
    return pl.pallas_call(
        collect_kernel,
        out_shape=(shape, shape),
        in_specs=whole(1),
        out_specs=tuple(whole(2)),
        scratch_shapes=[pltpu.VMEM(rows_array.shape, F32)],
        compiler_params=vmem_params(),
        name="collect",
    )(rows_array)


def table_kernel(column_ref, table, inverse):
    momenta = column_ref.shape[0]
    positions = lax.broadcasted_iota(jnp.int32, (momenta, momenta), 1)
    phases = (column_ref[...] * positions % momenta).astype(F32) * (2.0 * math.pi / momenta)
    cosines = jnp.cos(phases).astype(BF16)
    sines = jnp.sin(phases).astype(BF16)
    inverse[:momenta, :momenta] = cosines
    inverse[:momenta, momenta:] = sines
    inverse[momenta:, :momenta] = -sines
    inverse[momenta:, momenta:] = cosines
    cosines = cosines.astype(F32).T.astype(BF16)
    sines = sines.astype(F32).T.astype(BF16)
    table[:momenta, :momenta] = cosines
    table[:momenta, momenta:] = -sines
    table[momenta:, :momenta] = sines
    table[momenta:, momenta:] = cosines


def make_tables(lattice_map):
    momenta = lattice_map.shape[0]
    shape = jax.ShapeDtypeStruct((2 * momenta, 2 * momenta), BF16)
    return pl.pallas_call(
        table_kernel,
        out_shape=(shape, shape),
        in_specs=whole(1),
        out_specs=tuple(whole(2)),
        compiler_params=vmem_params(),
        name="make_tables",
    )(lattice_map[:, None])


def site_kernel(norm_factor, first_ref, lesser, greater, got, table, out):
    first = first_ref[0]
    _, _, count, cols, _ = got.shape
    wide = 4 * cols
    for which in range(2):
        for pair in range(count // 2):
            slabs = []
            for t in (2 * pair, 2 * pair + 1):
                for g, tile in enumerate((lesser, greater)):
                    if which == 0:
                        parts = [tile[c, first + t] for c in range(2)]
                    else:
                        parts = [got[g, c, t] for c in range(2)]
                    slabs.append(jnp.concatenate(parts, axis=1))
            product = lax.dot_general(
                table[...],
                jnp.concatenate(slabs, axis=0),
                (((1,), (1,)), ((), ())),
                preferred_element_type=F32,
            )
            out[which, :, pair * wide : (pair + 1) * wide] = (product * norm_factor).astype(BF16)


def to_sites(first, tiles, got, table, norm_factor):
    _, _, count, cols, momenta = got.shape
    return pl.pallas_call(
        functools.partial(site_kernel, norm_factor),
        out_shape=jax.ShapeDtypeStruct((2, 2 * momenta, count * 2 * cols), BF16),
        in_specs=scalars() + whole(4),
        out_specs=whole(1)[0],
        compiler_params=vmem_params(),
        name="to_sites",
    )(first, *tiles, got, table)


def cross_kernel(rows, blocks, first_ref, source, *rest):
    out = rest[-1]
    first = first_ref[0]
    cols = blocks * rows
    count = rows // 2
    for pair in range(source.shape[1] // (4 * rows)):
        turned = []
        for at in (2 * pair, 2 * pair + 1):
            span = slice(at * 2 * rows, (at + 1) * 2 * rows)
            loaded = [source[first + block, span].astype(F32) for block in range(blocks)]
            stacked = jnp.concatenate(
                [lines[rows:] for lines in loaded] + [lines[:rows] for lines in loaded], axis=0
            )
            turned.append(stacked.T)
        span = slice(pair * 2 * rows, (pair + 1) * 2 * rows)
        for side in range(2):
            for block in range(blocks):
                start = block * rows + side * count
                out[side * blocks + block, span] = jnp.concatenate(
                    [
                        lines[c * cols + start : c * cols + start + count]
                        for lines in turned
                        for c in range(2)
                    ],
                    axis=0,
                ).astype(BF16)


def to_crossed(first, source, rows, blocks, after, cost):
    shape = (2 * blocks, source.shape[1] // 2, source.shape[2])
    return pl.pallas_call(
        functools.partial(cross_kernel, rows, blocks),
        out_shape=jax.ShapeDtypeStruct(shape, BF16),
        in_specs=scalars() + whole(1) + unread(after),
        out_specs=whole(1)[0],
        compiler_params=vmem_params(),
        cost_estimate=cost,
        name="to_crossed",
    )(first, source, *after)


def gate_kernel(*refs):
    del refs


def gate(array, after):
    return pl.pallas_call(
        gate_kernel,
        out_shape=jax.ShapeDtypeStruct(array.shape, array.dtype),
        in_specs=unread([array, *after]),
        out_specs=unread([array])[0],
        input_output_aliases={0: 0},
        name="gate",
    )(array, *after)


def sigma_kernel(norm_factor, which_ref, crossed, sites, table, inverse, coupling, *rest):
    out, read, written = rest[-3:]
    which = which_ref[0]
    count = coupling.shape[0]
    momenta = table.shape[0] // 2
    read[...] = crossed[...].astype(F32)
    for pair in range(count // 2):
        rights = []
        for t in (2 * pair, 2 * pair + 1):
            real = read[pl.ds(t, momenta, stride=2 * count), :]
            imaginary = -read[pl.ds(count + t, momenta, stride=2 * count), :]
            rights.append(jnp.concatenate([real, imaginary], axis=0).astype(BF16))
        other = jnp.dot(
            table[...], jnp.concatenate(rights, axis=1), preferred_element_type=F32
        )
        other = (other * norm_factor).astype(BF16).astype(F32)
        span = slice(2 * pair * LANES, 2 * (pair + 1) * LANES)
        self_real, self_imaginary = second_born(
            sites[which, :momenta, span].astype(F32),
            sites[which, momenta:, span].astype(F32),
            other[:momenta],
            -other[momenta:],
            jnp.concatenate([coupling[t : t + 1] for t in (2 * pair, 2 * pair + 1)], axis=1),
        )
        product = jnp.dot(
            inverse[...],
            jnp.concatenate([self_real, self_imaginary], axis=0).astype(BF16),
            preferred_element_type=F32,
        )
        product = product * norm_factor
        for at in range(2):
            for part in range(2):
                written[pl.ds(part * count + 2 * pair + at, momenta, stride=2 * count), :] = product[
                    part * momenta : (part + 1) * momenta, at * LANES : (at + 1) * LANES
                ]
    out[...] = written[...].astype(BF16)


def to_sigma(which, crossed, sites, table, inverse, coupling, norm_factor, after):
    return pl.pallas_call(
        functools.partial(sigma_kernel, norm_factor),
        out_shape=jax.ShapeDtypeStruct(crossed.shape, BF16),
        in_specs=scalars() + whole(5) + unread(after),
        out_specs=whole(1)[0],
        scratch_shapes=[pltpu.VMEM(crossed.shape, F32)] * 2,
        compiler_params=vmem_params(),
        name="to_sigma",
    )(which, crossed, sites, table, inverse, coupling, *after)


def rights_kernel(rows, half_ref, own, far_near, far_away, out):
    half = half_ref[0]
    blocks = far_near.shape[0]
    lanes = own.shape[2]
    cols = lanes // 2
    near = half * cols
    away = (1 - half) * cols
    row_at = lax.broadcasted_iota(jnp.int32, (lanes, 2 * lanes), 0)
    inner_times = jnp.where(row_at < cols, near + row_at, away + row_at - cols)
    lane_at = lax.broadcasted_iota(jnp.int32, (lanes, 2 * lanes), 1)
    last_times = jnp.where(lane_at < lanes, near, away) + lane_at % cols
    keep = inner_times <= last_times
    for at in range(out.shape[0]):
        span = slice(at * 2 * rows, (at + 1) * 2 * rows)

        def stacked(ref, offset):
            loaded = [ref[offset + block, span].astype(F32) for block in range(blocks)]
            return [
                jnp.concatenate([lines[part * rows : (part + 1) * rows] for lines in loaded], axis=0)
                for part in range(2)
            ]

        own_near = stacked(own, half * blocks)
        own_away = stacked(own, (1 - half) * blocks)
        cross_near = stacked(far_near, 0)
        cross_away = stacked(far_away, 0)
        greens = [
            jnp.concatenate(
                [
                    jnp.concatenate([own_near[g], own_away[g]], axis=1),
                    jnp.concatenate([cross_near[g], cross_away[g]], axis=1),
                ],
                axis=0,
            )
            for g in range(2)
        ]
        out[at, :lanes] = greens[0].astype(BF16)
        out[at, lanes : 2 * lanes] = greens[1].astype(BF16)
        out[at, 2 * lanes :] = jnp.where(keep, greens[0] - greens[1], 0.0).astype(BF16)


def make_rights(half, own, far_near, far_away, rows):
    sources, lines, lanes = own.shape
    blocks = far_near.shape[0]
    step = 4 * rows
    spec = pl.BlockSpec((sources, step, lanes), lambda p: (0, p, 0))
    far_spec = pl.BlockSpec((blocks, step, lanes), lambda p: (0, p, 0))
    return pl.pallas_call(
        functools.partial(rights_kernel, rows),
        grid=(lines // step,),
        out_shape=jax.ShapeDtypeStruct((lines // (2 * rows), 3 * lanes, 2 * lanes), BF16),
        in_specs=scalars() + [spec, far_spec, far_spec],
        out_specs=pl.BlockSpec((2, 3 * lanes, 2 * lanes), lambda p: (p, 0, 0)),
        compiler_params=vmem_params(),
        cost_estimate=weight(),
        name="make_rights",
    )(half, own, far_near, far_away)


def volterra_kernel(rows, half_ref, diagonal, cross, rights, out):
    half = half_ref[0]
    blocks = diagonal.shape[0] // 2
    lanes = diagonal.shape[2]
    cols = lanes // 2
    count = rows // 2
    near = half * cols
    away = (1 - half) * cols
    first_times = near + lax.broadcasted_iota(jnp.int32, (cols, lanes), 0)
    left_lane = lax.broadcasted_iota(jnp.int32, (cols, lanes), 1)
    low_lanes = left_lane < cols
    left_times = jnp.where(low_lanes, near + left_lane, away + left_lane - cols)
    keep_left = left_times <= first_times
    pairs = []
    for at in range(2):
        piece = slice(at * rows, (at + 1) * rows)

        def stacked(ref):
            low = [ref[block].astype(F32)[piece] for block in range(blocks)]
            high = [ref[blocks + block].astype(F32)[piece] for block in range(blocks)]
            return [
                jnp.concatenate(
                    [
                        lines[block][part * count : (part + 1) * count]
                        for block in range(blocks)
                        for lines in (low, high)
                    ],
                    axis=0,
                )
                for part in range(2)
            ]

        sigma_near = stacked(diagonal)
        sigma_away = stacked(cross)
        retarded = []
        lefts = [[], []]
        for part in range(2):
            lesser = jnp.where(
                low_lanes, sigma_near[part], pltpu.roll(sigma_away[part], cols, 1)
            )
            greater = jnp.where(
                low_lanes, pltpu.roll(sigma_near[part], cols, 1), sigma_away[part]
            )
            retarded.append(jnp.where(keep_left, greater - lesser, 0.0))
            lefts[0].append(lesser)
            lefts[1].append(greater)
        retarded = jnp.concatenate(retarded, axis=0).astype(BF16)
        results = []
        for g in range(2):
            left = jnp.concatenate(
                [retarded, jnp.concatenate(lefts[g], axis=0).astype(BF16)], axis=1
            )
            right = jnp.concatenate(
                [rights[at, g * lanes : (g + 1) * lanes], rights[at, 2 * lanes :]], axis=0
            )
            product = jnp.dot(left, right, preferred_element_type=F32)
            sides = []
            for side in range(2):
                straight = product[:cols, side * lanes : (side + 1) * lanes]
                turned = pltpu.roll(product[cols:, side * lanes : (side + 1) * lanes], cols, 1)
                sides.append((straight + jnp.where(low_lanes, -turned, turned)) * step_size)
            results.append(sides)
        for block in range(blocks):
            lines = slice(block * rows, (block + 1) * rows)
            for side, offset in enumerate((half * blocks, (1 - half) * blocks)):
                out[offset + block, at * 2 * rows : (at + 1) * 2 * rows] = jnp.concatenate(
                    [results[0][side][lines], results[1][side][lines]], axis=0
                ).astype(BF16)


def volterra(half, diagonal, cross, rights, rows):
    sources, lines, lanes = diagonal.shape
    spec = pl.BlockSpec((sources, 2 * rows, lanes), lambda p: (0, p, 0))
    return pl.pallas_call(
        functools.partial(volterra_kernel, rows),
        grid=(lines // (2 * rows),),
        out_shape=jax.ShapeDtypeStruct((sources, 2 * lines, lanes), BF16),
        in_specs=scalars()
        + [spec, spec, pl.BlockSpec((2, 3 * lanes, 2 * lanes), lambda p: (p, 0, 0))],
        out_specs=pl.BlockSpec((sources, 4 * rows, lanes), lambda p: (0, p, 0)),
        compiler_params=vmem_params(),
        name="volterra",
    )(half, diagonal, cross, rights)


def halved_body(green_lesser, green_greater, lattice_map, time_offset):
    _, rows, cols, momenta = green_lesser.shape
    half = lax.axis_index("half")
    line = lax.axis_index("line")
    side = lax.axis_index("tcol")
    lines = lax.axis_size("line")
    group = lines * lax.axis_size("tcol")
    window = rows * lines * lax.axis_size("half")
    norm_factor = 1.0 / math.sqrt(momenta)
    tiles = (green_lesser, green_greater)
    count = rows // 2
    half_at = half[None]
    trade = [(0, 1), (1, 0)]

    def exchange(blocks):
        return lax.all_to_all(blocks, ("tcol", "line"), 0, 0, tiled=True)

    def blocked(rows_array):
        return rows_array.reshape(group, rows_array.shape[0] // group, rows_array.shape[1])

    def swap(blocks, at):
        return lax.ppermute(lax.dynamic_slice_in_dim(blocks, at * lines, lines), "half", trade)

    given = jnp.stack(
        [lax.dynamic_slice_in_dim(tile, (1 - side) * count, count, 1) for tile in tiles]
    )
    got = lax.ppermute(given, "tcol", trade)
    own = exchange(blocked(spread(tiles)))
    far_near = swap(own, 1 - half)
    far_away = swap(own, half)

    table, inverse = make_tables(lattice_map)
    kept = side * count
    sites = to_sites(kept[None], tiles, got, table, norm_factor)
    time_steps = jnp.arange(window, dtype=jnp.int32)
    coupling_line = 1.0 + drive_depth * jnp.cos(
        ((time_offset[0] + time_steps) % PERIOD).astype(F32) * (2.0 * math.pi / PERIOD)
    )
    first = lax.dynamic_slice_in_dim(coupling_line, (half * lines + line) * rows + kept, count)

    def phase_sigma(crossed, at, after):
        second = lax.dynamic_slice_in_dim(coupling_line, at * cols, cols)
        coupling = first[:, None] * jnp.concatenate([second, second])[None, :]
        which = (side != at).astype(jnp.int32)[None]
        return to_sigma(
            which,
            crossed.reshape(-1, 2 * cols),
            sites,
            table,
            inverse,
            coupling,
            norm_factor,
            after,
        )

    crossed = exchange(
        to_crossed((half * lines)[None], own, rows, lines, [sites], None)
    )
    sigma_rows = phase_sigma(crossed, half, [])
    diagonal = exchange(blocked(sigma_rows))
    sent = to_crossed(
        jnp.zeros((1,), jnp.int32), far_near, rows, lines, [sigma_rows], weight()
    )
    crossed = exchange(gate(sent, [diagonal]))
    cross = exchange(blocked(phase_sigma(crossed, 1 - half, [])))
    rights = make_rights(half_at, own, far_near, far_away, rows)
    collisions = volterra(half_at, diagonal, cross, rights, rows)
    returned = exchange(collisions)
    return collect(returned.reshape(-1, 2 * cols), green_lesser.shape)


def solution(mesh):
    row_parts = mesh.shape["trow"]
    col_parts = mesh.shape["tcol"]

    def call(green_lesser, green_greater, lattice_map, time_offset):
        window, window_cols, momenta = green_lesser.shape[1:]
        rows = window // row_parts
        cols = window_cols // col_parts
        halved = (
            col_parts == 2
            and row_parts % 2 == 0
            and window == window_cols
            and 2 * cols == LANES
            and cols == rows * (row_parts // 2)
            and rows % 8 == 0
            and momenta % (2 * row_parts) == 0 and momenta % LANES == 0
        )
        if halved:
            devices = mesh.devices.reshape(2, row_parts // 2, col_parts)
            used = Mesh(devices, ("half", "line", "tcol"))
            spec = P(None, ("half", "line"), "tcol", None)
            inner = halved_body
        else:
            used = mesh
            spec = P(None, "trow", "tcol", None)
            inner = general_body
        return jax.shard_map(
            inner, mesh=used, in_specs=(spec, spec, P(), P()), out_specs=(spec, spec), check_vma=False
        )(green_lesser, green_greater, lattice_map, time_offset)

    return call
```

```python
import functools
import math

import jax
import jax.numpy as jnp
from jax import lax
from jax.experimental import pallas as pl
from jax.experimental.pallas import tpu as pltpu
from jax.sharding import Mesh, PartitionSpec as P

F32 = jnp.float32
BF16 = jnp.bfloat16
LANES = 128

PERIOD = 64


step_size = 0.01
drive_depth = 0.5


def regroup(blocks):
    return lax.all_to_all(
        lax.all_to_all(blocks, "trow", split_axis=1, concat_axis=1, tiled=True),
        "tcol",
        split_axis=2,
        concat_axis=2,
        tiled=True,
    )


def pack_blocks(spectral, row_parts, col_parts):
    stacked, extent, tile_cells = spectral.shape
    return spectral.reshape(
        stacked, row_parts, col_parts, extent // (row_parts * col_parts), tile_cells
    )


def spread_times(blocks, tile_rows, tile_cols):
    stacked, row_parts, col_parts, local_count, tile_cells = blocks.shape
    shaped = blocks.reshape(stacked, row_parts, col_parts, local_count, tile_rows, tile_cols)
    return shaped.transpose(0, 3, 1, 4, 2, 5).reshape(
        stacked, local_count, row_parts * tile_rows, col_parts * tile_cols
    )


def gather_tiles(full, row_parts, col_parts):
    stacked, local_count, window, window_cols = full.shape
    tile_rows = window // row_parts
    tile_cols = window_cols // col_parts
    shaped = full.reshape(stacked, local_count, row_parts, tile_rows, col_parts, tile_cols)
    return shaped.transpose(0, 2, 4, 1, 3, 5).reshape(
        stacked, row_parts, col_parts, local_count, tile_rows * tile_cols
    )


def mirrored(full, keep_pair):
    stacked, local_count, window, window_cols = full.shape
    paired = full.reshape(stacked, local_count // 2, 2, window, window_cols)
    swapped = jnp.where(keep_pair[None, :, None, None, None], paired, paired[:, :, ::-1])
    return jnp.swapaxes(swapped.reshape(stacked, local_count, window, window_cols), 2, 3)


def second_born(first_real, first_imaginary, other_real, other_imaginary, coupling):
    square_real = first_real * first_real - first_imaginary * first_imaginary
    square_imaginary = 2.0 * first_real * first_imaginary
    out_real = coupling * (square_real * other_real - square_imaginary * other_imaginary)
    out_imaginary = coupling * (square_real * other_imaginary + square_imaginary * other_real)
    return (out_real, out_imaginary)


def collide(
    retarded_real,
    retarded_imaginary,
    self_real,
    self_imaginary,
    green_real,
    green_imaginary,
    advanced_real,
    advanced_imaginary,
):
    minus_left = jnp.concatenate(
        [retarded_real, -retarded_imaginary, self_real, -self_imaginary], axis=2
    )
    plus_left = jnp.concatenate(
        [retarded_real, retarded_imaginary, self_real, self_imaginary], axis=2
    )
    real_right = jnp.concatenate(
        [green_real, green_imaginary, advanced_real, advanced_imaginary], axis=1
    )
    imaginary_right = jnp.concatenate(
        [green_imaginary, green_real, advanced_imaginary, advanced_real], axis=1
    )
    out_real = jnp.einsum(
        "kts,ksu->ktu", minus_left, real_right, preferred_element_type=jnp.float32
    )
    out_imaginary = jnp.einsum(
        "kts,ksu->ktu", plus_left, imaginary_right, preferred_element_type=jnp.float32
    )
    return (out_real, out_imaginary)


def general_body(green_lesser, green_greater, lattice_map, time_offset):
    tile_rows = green_lesser.shape[1]
    tile_cols = green_lesser.shape[2]
    momenta = green_lesser.shape[3]
    row_parts = lax.axis_size("trow")
    col_parts = lax.axis_size("tcol")
    window = tile_rows * row_parts
    tile_cells = tile_rows * tile_cols
    local_count = momenta // (row_parts * col_parts)
    norm_factor = 1.0 / math.sqrt(momenta)
    greens = (
        jnp.concatenate([green_lesser, green_greater], axis=0)
        .reshape(4, tile_cells, momenta)
        .transpose(0, 2, 1)
    )
    positions = jnp.arange(momenta, dtype=jnp.int32)
    halves = positions // 2
    site_order = jnp.where(
        positions == 1, momenta // 2, jnp.where(positions % 2 == 0, halves, momenta - halves)
    )
    phases = (lattice_map[:, None] * site_order[None, :] % momenta).astype(jnp.float32) * (
        2.0 * math.pi / momenta
    )
    cosines = jnp.cos(phases).astype(jnp.bfloat16)
    sines = jnp.sin(phases).astype(jnp.bfloat16)
    ahead_blocks = lax.all_to_all(
        lax.all_to_all(
            pack_blocks(greens, row_parts, col_parts),
            "trow",
            split_axis=1,
            concat_axis=1,
            tiled=True,
        ),
        "tcol",
        split_axis=2,
        concat_axis=2,
        tiled=True,
    )
    green_moment = spread_times(ahead_blocks, tile_rows, tile_cols)
    forward_table = jnp.concatenate([cosines, sines], axis=1)
    products = jnp.einsum("cjm,jr->crm", greens, forward_table, preferred_element_type=jnp.float32)
    site_space = jnp.stack(
        [
            (products[0, :momenta] - products[1, momenta:]) * norm_factor,
            (products[0, momenta:] + products[1, :momenta]) * norm_factor,
            (products[2, :momenta] - products[3, momenta:]) * norm_factor,
            (products[2, momenta:] + products[3, :momenta]) * norm_factor,
        ]
    ).astype(jnp.bfloat16)
    site_full = spread_times(
        regroup(pack_blocks(site_space, row_parts, col_parts)), tile_rows, tile_cols
    )
    site_block = lax.axis_index("trow") * col_parts + lax.axis_index("tcol")
    keep_pair = site_block * (local_count // 2) + jnp.arange(local_count // 2, dtype=jnp.int32) == 0
    mirror = mirrored(site_full, keep_pair).astype(jnp.float32)
    direct = site_full.astype(jnp.float32)
    time_steps = jnp.arange(window, dtype=jnp.int32)
    coupling_line = 1.0 + drive_depth * jnp.cos(
        ((time_offset[0] + time_steps) % PERIOD).astype(jnp.float32) * (2.0 * math.pi / PERIOD)
    )
    coupling = coupling_line[:, None] * coupling_line[None, :]
    self_lesser = second_born(direct[0], direct[1], mirror[2], mirror[3], coupling)
    self_greater = second_born(direct[2], direct[3], mirror[0], mirror[1], coupling)
    self_sites = jnp.stack(
        [self_lesser[0], self_lesser[1], self_greater[0], self_greater[1]]
    ).astype(jnp.bfloat16)
    self_tiles = regroup(gather_tiles(self_sites, row_parts, col_parts)).reshape(
        4, momenta, tile_cells
    )
    inverse_table = jnp.concatenate([cosines, sines], axis=0)
    spectral_terms = jnp.einsum(
        "cum,ju->cjm", self_tiles, inverse_table, preferred_element_type=jnp.float32
    )
    self_spectral = jnp.stack(
        [
            (spectral_terms[0, :momenta] + spectral_terms[1, momenta:]) * norm_factor,
            (spectral_terms[1, :momenta] - spectral_terms[0, momenta:]) * norm_factor,
            (spectral_terms[2, :momenta] + spectral_terms[3, momenta:]) * norm_factor,
            (spectral_terms[3, :momenta] - spectral_terms[2, momenta:]) * norm_factor,
        ]
    ).astype(jnp.bfloat16)
    self_moment = spread_times(
        regroup(pack_blocks(self_spectral, row_parts, col_parts)), tile_rows, tile_cols
    )
    lower_mask = time_steps[None, :] <= time_steps[:, None]
    upper_mask = time_steps[:, None] <= time_steps[None, :]
    retarded = jnp.where(
        lower_mask, self_moment[2:4].astype(jnp.float32) - self_moment[0:2].astype(jnp.float32), 0.0
    ).astype(jnp.bfloat16)
    advanced = jnp.where(
        upper_mask,
        green_moment[0:2].astype(jnp.float32) - green_moment[2:4].astype(jnp.float32),
        0.0,
    ).astype(jnp.bfloat16)
    lesser_out = collide(
        retarded[0],
        retarded[1],
        self_moment[0],
        self_moment[1],
        green_moment[0],
        green_moment[1],
        advanced[0],
        advanced[1],
    )
    greater_out = collide(
        retarded[0],
        retarded[1],
        self_moment[2],
        self_moment[3],
        green_moment[2],
        green_moment[3],
        advanced[0],
        advanced[1],
    )
    collisions = (
        jnp.stack([lesser_out[0], lesser_out[1], greater_out[0], greater_out[1]]) * step_size
    ).astype(jnp.bfloat16)
    out_tiles = regroup(gather_tiles(collisions, row_parts, col_parts)).reshape(
        4, momenta, tile_cells
    )
    out_tiles = out_tiles.transpose(0, 2, 1).reshape(4, tile_rows, tile_cols, momenta)
    return (out_tiles[0:2], out_tiles[2:4])


def vmem_params():
    return pltpu.CompilerParams(vmem_limit_bytes=48 * 1024 * 1024)


def unread(arrays):
    return [pl.BlockSpec(memory_space=pl.ANY)] * len(arrays)


def whole(count):
    return [pl.BlockSpec(memory_space=pltpu.VMEM)] * count


def weight():
    return pl.CostEstimate(flops=10**11, bytes_accessed=2**20, transcendentals=0)


def scalars():
    return [pl.BlockSpec(memory_space=pltpu.SMEM)]


def spread_kernel(*refs):
    *tiles, out, lines = refs
    _, rows, _, momenta = tiles[0].shape
    blocks, height, _ = out.shape
    height = height // len(tiles)
    wide = momenta // 2
    for g, tile in enumerate(tiles):
        for first in range(0, momenta, wide):
            for t in range(rows):
                span = slice(first, first + wide)
                slab = jnp.concatenate([tile[0, t, :, span], tile[1, t, :, span]], axis=0)
                lines[pl.ds(first * rows + t, wide, stride=rows), :] = slab.astype(F32).T
        for block in range(blocks):
            out[block, g * height : (g + 1) * height] = lines[
                block * height : (block + 1) * height
            ].astype(BF16)


def spread(tiles, blocks, cost):
    _, rows, cols, momenta = tiles[0].shape
    lines = momenta * rows
    return pl.pallas_call(
        spread_kernel,
        out_shape=jax.ShapeDtypeStruct((blocks, len(tiles) * lines // blocks, 2 * cols), BF16),
        in_specs=whole(len(tiles)),
        out_specs=whole(1)[0],
        scratch_shapes=[pltpu.VMEM((lines, 2 * cols), F32)],
        compiler_params=vmem_params(),
        cost_estimate=cost,
        name="spread",
    )(*tiles)


def collect_kernel(rows_ref, lesser, greater, lines):
    lines[...] = rows_ref[...].astype(F32)
    _, rows, cols, momenta = lesser.shape
    for k in range(2 * rows):
        slab = lines[pl.ds(k, momenta, stride=2 * rows), :].T.astype(BF16)
        out = lesser if k < rows else greater
        out[0, k % rows] = slab[:cols]
        out[1, k % rows] = slab[cols:]


def collect(rows_array, tile_shape):
    shape = jax.ShapeDtypeStruct(tile_shape, BF16)
    return pl.pallas_call(
        collect_kernel,
        out_shape=(shape, shape),
        in_specs=whole(1),
        out_specs=tuple(whole(2)),
        scratch_shapes=[pltpu.VMEM(rows_array.shape, F32)],
        compiler_params=vmem_params(),
        name="collect",
    )(rows_array)


def table_kernel(column_ref, table, inverse):
    momenta = column_ref.shape[0]
    positions = lax.broadcasted_iota(jnp.int32, (momenta, momenta), 1)
    phases = (column_ref[...] * positions % momenta).astype(F32) * (2.0 * math.pi / momenta)
    cosines = jnp.cos(phases).astype(BF16)
    sines = jnp.sin(phases).astype(BF16)
    inverse[:momenta, :momenta] = cosines
    inverse[:momenta, momenta:] = sines
    inverse[momenta:, :momenta] = -sines
    inverse[momenta:, momenta:] = cosines
    cosines = cosines.astype(F32).T.astype(BF16)
    sines = sines.astype(F32).T.astype(BF16)
    table[:momenta, :momenta] = cosines
    table[:momenta, momenta:] = -sines
    table[momenta:, :momenta] = sines
    table[momenta:, momenta:] = cosines


def make_tables(lattice_map):
    momenta = lattice_map.shape[0]
    shape = jax.ShapeDtypeStruct((2 * momenta, 2 * momenta), BF16)
    return pl.pallas_call(
        table_kernel,
        out_shape=(shape, shape),
        in_specs=whole(1),
        out_specs=tuple(whole(2)),
        compiler_params=vmem_params(),
        name="make_tables",
    )(lattice_map[:, None])


def site_kernel(norm_factor, lesser, greater, table, out):
    _, rows, cols, _ = lesser.shape
    wide = 4 * cols
    for pair in range(rows // 2):
        slabs = [
            jnp.concatenate([tile[0, t], tile[1, t]], axis=1)
            for t in (2 * pair, 2 * pair + 1)
            for tile in (lesser, greater)
        ]
        product = lax.dot_general(
            table[...],
            jnp.concatenate(slabs, axis=0),
            (((1,), (1,)), ((), ())),
            preferred_element_type=F32,
        )
        out[:, pair * wide : (pair + 1) * wide] = (product * norm_factor).astype(BF16)


def to_sites(tiles, table, norm_factor):
    _, rows, cols, momenta = tiles[0].shape
    return pl.pallas_call(
        functools.partial(site_kernel, norm_factor),
        out_shape=jax.ShapeDtypeStruct((2 * momenta, rows * 2 * cols), BF16),
        in_specs=whole(3),
        out_specs=whole(1)[0],
        compiler_params=vmem_params(),
        name="to_sites",
    )(*tiles, table)


def cross_kernel(rows, half_ref, own, far_l, near_g, *rest):
    out = rest[-1]
    half = half_ref[0]
    blocks = near_g.shape[0]
    cols = blocks * rows
    height = near_g.shape[1]
    here = half * blocks
    for pair in range(height // (2 * rows)):
        low = slice(pair * 2 * rows, (pair + 1) * 2 * rows)
        high = slice(height + pair * 2 * rows, height + (pair + 1) * 2 * rows)
        for lesser, greater, target in (
            ([own[here + b, low] for b in range(blocks)], [own[here + b, high] for b in range(blocks)], half),
            ([far_l[here + b, low] for b in range(blocks)], [near_g[b, low] for b in range(blocks)], 1 - half),
        ):
            loaded = [lines.astype(F32) for lines in greater + lesser]
            for at in range(2):
                turned = jnp.concatenate(
                    [lines[at * rows : (at + 1) * rows] for lines in loaded], axis=0
                ).T
                start = (2 * pair + at) * 2 * rows
                for block in range(blocks):
                    out[target * blocks + block, start : start + 2 * rows] = jnp.concatenate(
                        [
                            turned[block * rows : (block + 1) * rows],
                            turned[cols + block * rows : cols + (block + 1) * rows],
                        ],
                        axis=0,
                    ).astype(BF16)


def to_crossed(half, own, far_l, near_g, rows, after):
    return pl.pallas_call(
        functools.partial(cross_kernel, rows),
        out_shape=jax.ShapeDtypeStruct(own.shape, BF16),
        in_specs=scalars() + whole(3) + unread(after),
        out_specs=whole(1)[0],
        compiler_params=vmem_params(),
        name="to_crossed",
    )(half, own, far_l, near_g, *after)


def gate_kernel(*refs):
    del refs


def gate(array, after):
    return pl.pallas_call(
        gate_kernel,
        out_shape=jax.ShapeDtypeStruct(array.shape, array.dtype),
        in_specs=unread([array, *after]),
        out_specs=unread([array])[0],
        input_output_aliases={0: 0},
        name="gate",
    )(array, *after)


def sigma_kernel(norm_factor, crossed, sites, table, inverse, coupling, out, read, written):
    count = coupling.shape[0]
    momenta = table.shape[0] // 2
    read[...] = crossed[...].astype(F32)
    for pair in range(count // 2):
        rights = []
        for t in (2 * pair, 2 * pair + 1):
            real = read[pl.ds(t, momenta, stride=2 * count), :]
            imaginary = -read[pl.ds(count + t, momenta, stride=2 * count), :]
            rights.append(jnp.concatenate([real, imaginary], axis=0).astype(BF16))
        other = jnp.dot(
            table[...], jnp.concatenate(rights, axis=1), preferred_element_type=F32
        )
        other = (other * norm_factor).astype(BF16).astype(F32)
        span = slice(2 * pair * LANES, 2 * (pair + 1) * LANES)
        self_real, self_imaginary = second_born(
            sites[:momenta, span].astype(F32),
            sites[momenta:, span].astype(F32),
            other[:momenta],
            -other[momenta:],
            jnp.concatenate([coupling[t : t + 1] for t in (2 * pair, 2 * pair + 1)], axis=1),
        )
        product = jnp.dot(
            inverse[...],
            jnp.concatenate([self_real, self_imaginary], axis=0).astype(BF16),
            preferred_element_type=F32,
        )
        product = product * norm_factor
        for at in range(2):
            for part in range(2):
                written[pl.ds(part * count + 2 * pair + at, momenta, stride=2 * count), :] = product[
                    part * momenta : (part + 1) * momenta, at * LANES : (at + 1) * LANES
                ]
    out[...] = written[...].astype(BF16)


def to_sigma(crossed, sites, table, inverse, coupling, norm_factor):
    return pl.pallas_call(
        functools.partial(sigma_kernel, norm_factor),
        out_shape=jax.ShapeDtypeStruct(crossed.shape, BF16),
        in_specs=whole(5),
        out_specs=whole(1)[0],
        scratch_shapes=[pltpu.VMEM(crossed.shape, F32)] * 2,
        compiler_params=vmem_params(),
        name="to_sigma",
    )(crossed, sites, table, inverse, coupling)


def rights_kernel(rows, half_ref, own_l, own_g, far_l, near_g, away_g, out):
    half = half_ref[0]
    blocks = near_g.shape[0]
    lanes = own_l.shape[2]
    cols = lanes // 2
    near = half * cols
    away = (1 - half) * cols
    row_at = lax.broadcasted_iota(jnp.int32, (lanes, 2 * lanes), 0)
    inner_times = jnp.where(row_at < cols, near + row_at, away + row_at - cols)
    lane_at = lax.broadcasted_iota(jnp.int32, (lanes, 2 * lanes), 1)
    last_times = jnp.where(lane_at < lanes, near, away) + lane_at % cols
    keep = inner_times <= last_times
    here = half * blocks
    there = (1 - half) * blocks
    for pair in range(out.shape[0] // 2):
        span = slice(pair * 2 * rows, (pair + 1) * 2 * rows)

        def stacked(ref, offset):
            loaded = [ref[offset + block, span].astype(F32) for block in range(blocks)]
            return [
                jnp.concatenate([lines[at * rows : (at + 1) * rows] for lines in loaded], axis=0)
                for at in range(2)
            ]

        parts = [
            [[stacked(own_l, here), stacked(own_l, there)], [stacked(far_l, here), stacked(far_l, there)]],
            [[stacked(own_g, here), stacked(own_g, there)], [stacked(near_g, 0), stacked(away_g, 0)]],
        ]
        for at in range(2):
            greens = [
                jnp.concatenate(
                    [jnp.concatenate([side[at] for side in line], axis=1) for line in part], axis=0
                )
                for part in parts
            ]
            out[2 * pair + at, :lanes] = greens[0].astype(BF16)
            out[2 * pair + at, lanes : 2 * lanes] = greens[1].astype(BF16)
            out[2 * pair + at, 2 * lanes :] = jnp.where(keep, greens[0] - greens[1], 0.0).astype(BF16)


STEPS = 4


def make_rights(half, own, far_l, near_g, away_g, rows):
    sources, lines, lanes = far_l.shape
    blocks = near_g.shape[0]
    step = lines // STEPS
    momenta = step // rows
    lesser = pl.BlockSpec((sources, step, lanes), lambda p: (0, p, 0))
    greater = pl.BlockSpec((sources, step, lanes), lambda p: (0, STEPS + p, 0))
    half_spec = pl.BlockSpec((blocks, step, lanes), lambda p: (0, p, 0))
    return pl.pallas_call(
        functools.partial(rights_kernel, rows),
        grid=(STEPS,),
        out_shape=jax.ShapeDtypeStruct((lines // rows, 3 * lanes, 2 * lanes), BF16),
        in_specs=scalars() + [lesser, greater, lesser, half_spec, half_spec],
        out_specs=pl.BlockSpec((momenta, 3 * lanes, 2 * lanes), lambda p: (p, 0, 0)),
        compiler_params=vmem_params(),
        cost_estimate=weight(),
        name="make_rights",
    )(half, own, own, far_l, near_g, away_g)


def volterra_kernel(rows, half_ref, sigma, rights, out):
    half = half_ref[0]
    blocks = sigma.shape[0] // 2
    lanes = sigma.shape[2]
    cols = lanes // 2
    near = half * cols
    away = (1 - half) * cols
    here = half * blocks
    there = (1 - half) * blocks
    first_times = near + lax.broadcasted_iota(jnp.int32, (cols, lanes), 0)
    left_lane = lax.broadcasted_iota(jnp.int32, (cols, lanes), 1)
    low_lanes = left_lane < cols
    left_times = jnp.where(low_lanes, near + left_lane, away + left_lane - cols)
    keep_left = left_times <= first_times
    for at in range(rights.shape[0]):
        span = slice(at * 2 * rows, (at + 1) * 2 * rows)

        def stacked(offset):
            loaded = [sigma[offset + block, span].astype(F32) for block in range(blocks)]
            return [
                jnp.concatenate([lines[part * rows : (part + 1) * rows] for lines in loaded], axis=0)
                for part in range(2)
            ]

        sigma_near = stacked(here)
        sigma_away = stacked(there)
        retarded = []
        lefts = [[], []]
        for part in range(2):
            lesser = jnp.where(
                low_lanes, sigma_near[part], pltpu.roll(sigma_away[part], cols, 1)
            )
            greater = jnp.where(
                low_lanes, pltpu.roll(sigma_near[part], cols, 1), sigma_away[part]
            )
            retarded.append(jnp.where(keep_left, greater - lesser, 0.0))
            lefts[0].append(lesser)
            lefts[1].append(greater)
        retarded = jnp.concatenate(retarded, axis=0).astype(BF16)
        results = []
        for g in range(2):
            left = jnp.concatenate(
                [retarded, jnp.concatenate(lefts[g], axis=0).astype(BF16)], axis=1
            )
            right = jnp.concatenate(
                [rights[at, g * lanes : (g + 1) * lanes], rights[at, 2 * lanes :]], axis=0
            )
            product = jnp.dot(left, right, preferred_element_type=F32)
            sides = []
            for side in range(2):
                straight = product[:cols, side * lanes : (side + 1) * lanes]
                turned = pltpu.roll(product[cols:, side * lanes : (side + 1) * lanes], cols, 1)
                sides.append((straight + jnp.where(low_lanes, -turned, turned)) * step_size)
            results.append(sides)
        for block in range(blocks):
            lines = slice(block * rows, (block + 1) * rows)
            for side, offset in enumerate((here, there)):
                out[offset + block, span] = jnp.concatenate(
                    [results[0][side][lines], results[1][side][lines]], axis=0
                ).astype(BF16)


def volterra(half, sigma, rights, rows):
    sources, lines, lanes = sigma.shape
    step = lines // STEPS
    momenta = step // (2 * rows)
    spec = pl.BlockSpec((sources, step, lanes), lambda p: (0, p, 0))
    return pl.pallas_call(
        functools.partial(volterra_kernel, rows),
        grid=(STEPS,),
        out_shape=jax.ShapeDtypeStruct(sigma.shape, BF16),
        in_specs=scalars()
        + [spec, pl.BlockSpec((momenta, 3 * lanes, 2 * lanes), lambda p: (p, 0, 0))],
        out_specs=spec,
        compiler_params=vmem_params(),
        name="volterra",
    )(half, sigma, rights)


def halved_body(green_lesser, green_greater, lattice_map, time_offset):
    _, rows, cols, momenta = green_lesser.shape
    half = lax.axis_index("half")
    line = lax.axis_index("line")
    side = lax.axis_index("tcol")
    lines = lax.axis_size("line")
    group = lines * lax.axis_size("tcol")
    window = rows * lines * lax.axis_size("half")
    norm_factor = 1.0 / math.sqrt(momenta)
    tiles = (green_lesser, green_greater)
    half_at = half[None]
    height = momenta * rows // group

    def exchange(blocks):
        return lax.all_to_all(blocks, ("tcol", "line"), 0, 0, tiled=True)

    def swap(array):
        return lax.ppermute(array, "half", [(0, 1), (1, 0)])

    def greater_blocks(at):
        zero = jnp.zeros((), jnp.int32)
        return lax.dynamic_slice(
            own, (at * lines, zero + height, zero), (lines, height, 2 * cols)
        )

    far_tile = swap(green_lesser)
    own = exchange(spread(tiles, group, None))
    far_l = exchange(gate(spread([far_tile], group, weight()), [own]))
    near_g = swap(greater_blocks(1 - half))
    away_g = swap(greater_blocks(half))

    table, inverse = make_tables(lattice_map)
    sites = to_sites(tiles, table, norm_factor)
    time_steps = jnp.arange(window, dtype=jnp.int32)
    coupling_line = 1.0 + drive_depth * jnp.cos(
        ((time_offset[0] + time_steps) % PERIOD).astype(F32) * (2.0 * math.pi / PERIOD)
    )
    first = lax.dynamic_slice_in_dim(coupling_line, (half * lines + line) * rows, rows)
    second = lax.dynamic_slice_in_dim(coupling_line, side * cols, cols)
    coupling = first[:, None] * jnp.concatenate([second, second])[None, :]

    crossed = exchange(to_crossed(half_at, own, far_l, near_g, rows, [sites]))
    sigma_rows = to_sigma(
        crossed.reshape(-1, 2 * cols), sites, table, inverse, coupling, norm_factor
    )
    sigma = exchange(sigma_rows.reshape(crossed.shape))
    rights = make_rights(half_at, own, far_l, near_g, away_g, rows)
    collisions = volterra(half_at, sigma, rights, rows)
    returned = exchange(collisions)
    return collect(returned.reshape(-1, 2 * cols), green_lesser.shape)


def solution(mesh):
    row_parts = mesh.shape["trow"]
    col_parts = mesh.shape["tcol"]

    def call(green_lesser, green_greater, lattice_map, time_offset):
        window, window_cols, momenta = green_lesser.shape[1:]
        rows = window // row_parts
        cols = window_cols // col_parts
        halved = (
            col_parts == 2
            and row_parts % 2 == 0
            and window == window_cols
            and 2 * cols == LANES
            and cols == rows * (row_parts // 2)
            and rows % 8 == 0
            and momenta % (2 * row_parts * STEPS) == 0
            and momenta % LANES == 0
        )
        if halved:
            devices = mesh.devices.reshape(2, row_parts // 2, col_parts)
            used = Mesh(devices, ("half", "line", "tcol"))
            spec = P(None, ("half", "line"), "tcol", None)
            inner = halved_body
        else:
            used = mesh
            spec = P(None, "trow", "tcol", None)
            inner = general_body
        return jax.shard_map(
            inner, mesh=used, in_specs=(spec, spec, P(), P()), out_specs=(spec, spec), check_vma=False
        )(green_lesser, green_greater, lattice_map, time_offset)

    return call
```

```python
import functools
import math

import jax
import jax.numpy as jnp
from jax import lax
from jax.experimental import pallas as pl
from jax.experimental.pallas import tpu as pltpu
from jax.sharding import Mesh, PartitionSpec as P

F32 = jnp.float32
BF16 = jnp.bfloat16
LANES = 128

PERIOD = 64


step_size = 0.01
drive_depth = 0.5


def regroup(blocks):
    return lax.all_to_all(
        lax.all_to_all(blocks, "trow", split_axis=1, concat_axis=1, tiled=True),
        "tcol",
        split_axis=2,
        concat_axis=2,
        tiled=True,
    )


def pack_blocks(spectral, row_parts, col_parts):
    stacked, extent, tile_cells = spectral.shape
    return spectral.reshape(
        stacked, row_parts, col_parts, extent // (row_parts * col_parts), tile_cells
    )


def spread_times(blocks, tile_rows, tile_cols):
    stacked, row_parts, col_parts, local_count, tile_cells = blocks.shape
    shaped = blocks.reshape(stacked, row_parts, col_parts, local_count, tile_rows, tile_cols)
    return shaped.transpose(0, 3, 1, 4, 2, 5).reshape(
        stacked, local_count, row_parts * tile_rows, col_parts * tile_cols
    )


def gather_tiles(full, row_parts, col_parts):
    stacked, local_count, window, window_cols = full.shape
    tile_rows = window // row_parts
    tile_cols = window_cols // col_parts
    shaped = full.reshape(stacked, local_count, row_parts, tile_rows, col_parts, tile_cols)
    return shaped.transpose(0, 2, 4, 1, 3, 5).reshape(
        stacked, row_parts, col_parts, local_count, tile_rows * tile_cols
    )


def mirrored(full, keep_pair):
    stacked, local_count, window, window_cols = full.shape
    paired = full.reshape(stacked, local_count // 2, 2, window, window_cols)
    swapped = jnp.where(keep_pair[None, :, None, None, None], paired, paired[:, :, ::-1])
    return jnp.swapaxes(swapped.reshape(stacked, local_count, window, window_cols), 2, 3)


def second_born(first_real, first_imaginary, other_real, other_imaginary, coupling):
    square_real = first_real * first_real - first_imaginary * first_imaginary
    square_imaginary = 2.0 * first_real * first_imaginary
    out_real = coupling * (square_real * other_real - square_imaginary * other_imaginary)
    out_imaginary = coupling * (square_real * other_imaginary + square_imaginary * other_real)
    return (out_real, out_imaginary)


def collide(
    retarded_real,
    retarded_imaginary,
    self_real,
    self_imaginary,
    green_real,
    green_imaginary,
    advanced_real,
    advanced_imaginary,
):
    minus_left = jnp.concatenate(
        [retarded_real, -retarded_imaginary, self_real, -self_imaginary], axis=2
    )
    plus_left = jnp.concatenate(
        [retarded_real, retarded_imaginary, self_real, self_imaginary], axis=2
    )
    real_right = jnp.concatenate(
        [green_real, green_imaginary, advanced_real, advanced_imaginary], axis=1
    )
    imaginary_right = jnp.concatenate(
        [green_imaginary, green_real, advanced_imaginary, advanced_real], axis=1
    )
    out_real = jnp.einsum(
        "kts,ksu->ktu", minus_left, real_right, preferred_element_type=jnp.float32
    )
    out_imaginary = jnp.einsum(
        "kts,ksu->ktu", plus_left, imaginary_right, preferred_element_type=jnp.float32
    )
    return (out_real, out_imaginary)


def general_body(green_lesser, green_greater, lattice_map, time_offset):
    tile_rows = green_lesser.shape[1]
    tile_cols = green_lesser.shape[2]
    momenta = green_lesser.shape[3]
    row_parts = lax.axis_size("trow")
    col_parts = lax.axis_size("tcol")
    window = tile_rows * row_parts
    tile_cells = tile_rows * tile_cols
    local_count = momenta // (row_parts * col_parts)
    norm_factor = 1.0 / math.sqrt(momenta)
    greens = (
        jnp.concatenate([green_lesser, green_greater], axis=0)
        .reshape(4, tile_cells, momenta)
        .transpose(0, 2, 1)
    )
    positions = jnp.arange(momenta, dtype=jnp.int32)
    halves = positions // 2
    site_order = jnp.where(
        positions == 1, momenta // 2, jnp.where(positions % 2 == 0, halves, momenta - halves)
    )
    phases = (lattice_map[:, None] * site_order[None, :] % momenta).astype(jnp.float32) * (
        2.0 * math.pi / momenta
    )
    cosines = jnp.cos(phases).astype(jnp.bfloat16)
    sines = jnp.sin(phases).astype(jnp.bfloat16)
    ahead_blocks = lax.all_to_all(
        lax.all_to_all(
            pack_blocks(greens, row_parts, col_parts),
            "trow",
            split_axis=1,
            concat_axis=1,
            tiled=True,
        ),
        "tcol",
        split_axis=2,
        concat_axis=2,
        tiled=True,
    )
    green_moment = spread_times(ahead_blocks, tile_rows, tile_cols)
    forward_table = jnp.concatenate([cosines, sines], axis=1)
    products = jnp.einsum("cjm,jr->crm", greens, forward_table, preferred_element_type=jnp.float32)
    site_space = jnp.stack(
        [
            (products[0, :momenta] - products[1, momenta:]) * norm_factor,
            (products[0, momenta:] + products[1, :momenta]) * norm_factor,
            (products[2, :momenta] - products[3, momenta:]) * norm_factor,
            (products[2, momenta:] + products[3, :momenta]) * norm_factor,
        ]
    ).astype(jnp.bfloat16)
    site_full = spread_times(
        regroup(pack_blocks(site_space, row_parts, col_parts)), tile_rows, tile_cols
    )
    site_block = lax.axis_index("trow") * col_parts + lax.axis_index("tcol")
    keep_pair = site_block * (local_count // 2) + jnp.arange(local_count // 2, dtype=jnp.int32) == 0
    mirror = mirrored(site_full, keep_pair).astype(jnp.float32)
    direct = site_full.astype(jnp.float32)
    time_steps = jnp.arange(window, dtype=jnp.int32)
    coupling_line = 1.0 + drive_depth * jnp.cos(
        ((time_offset[0] + time_steps) % PERIOD).astype(jnp.float32) * (2.0 * math.pi / PERIOD)
    )
    coupling = coupling_line[:, None] * coupling_line[None, :]
    self_lesser = second_born(direct[0], direct[1], mirror[2], mirror[3], coupling)
    self_greater = second_born(direct[2], direct[3], mirror[0], mirror[1], coupling)
    self_sites = jnp.stack(
        [self_lesser[0], self_lesser[1], self_greater[0], self_greater[1]]
    ).astype(jnp.bfloat16)
    self_tiles = regroup(gather_tiles(self_sites, row_parts, col_parts)).reshape(
        4, momenta, tile_cells
    )
    inverse_table = jnp.concatenate([cosines, sines], axis=0)
    spectral_terms = jnp.einsum(
        "cum,ju->cjm", self_tiles, inverse_table, preferred_element_type=jnp.float32
    )
    self_spectral = jnp.stack(
        [
            (spectral_terms[0, :momenta] + spectral_terms[1, momenta:]) * norm_factor,
            (spectral_terms[1, :momenta] - spectral_terms[0, momenta:]) * norm_factor,
            (spectral_terms[2, :momenta] + spectral_terms[3, momenta:]) * norm_factor,
            (spectral_terms[3, :momenta] - spectral_terms[2, momenta:]) * norm_factor,
        ]
    ).astype(jnp.bfloat16)
    self_moment = spread_times(
        regroup(pack_blocks(self_spectral, row_parts, col_parts)), tile_rows, tile_cols
    )
    lower_mask = time_steps[None, :] <= time_steps[:, None]
    upper_mask = time_steps[:, None] <= time_steps[None, :]
    retarded = jnp.where(
        lower_mask, self_moment[2:4].astype(jnp.float32) - self_moment[0:2].astype(jnp.float32), 0.0
    ).astype(jnp.bfloat16)
    advanced = jnp.where(
        upper_mask,
        green_moment[0:2].astype(jnp.float32) - green_moment[2:4].astype(jnp.float32),
        0.0,
    ).astype(jnp.bfloat16)
    lesser_out = collide(
        retarded[0],
        retarded[1],
        self_moment[0],
        self_moment[1],
        green_moment[0],
        green_moment[1],
        advanced[0],
        advanced[1],
    )
    greater_out = collide(
        retarded[0],
        retarded[1],
        self_moment[2],
        self_moment[3],
        green_moment[2],
        green_moment[3],
        advanced[0],
        advanced[1],
    )
    collisions = (
        jnp.stack([lesser_out[0], lesser_out[1], greater_out[0], greater_out[1]]) * step_size
    ).astype(jnp.bfloat16)
    out_tiles = regroup(gather_tiles(collisions, row_parts, col_parts)).reshape(
        4, momenta, tile_cells
    )
    out_tiles = out_tiles.transpose(0, 2, 1).reshape(4, tile_rows, tile_cols, momenta)
    return (out_tiles[0:2], out_tiles[2:4])


def vmem_params():
    return pltpu.CompilerParams(vmem_limit_bytes=48 * 1024 * 1024)


def unread(arrays):
    return [pl.BlockSpec(memory_space=pl.ANY)] * len(arrays)


def whole(count):
    return [pl.BlockSpec(memory_space=pltpu.VMEM)] * count


def weight():
    return pl.CostEstimate(flops=10**11, bytes_accessed=2**20, transcendentals=0)


def scalars():
    return [pl.BlockSpec(memory_space=pltpu.SMEM)]


def spread_kernel(first, lesser, greater, *rest):
    out, lines = rest[-2:]
    _, rows, _, _ = lesser.shape
    count = lines.shape[0] // (2 * rows)
    for g, tile in enumerate((lesser, greater)):
        for t in range(rows):
            span = slice(first, first + count)
            slab = jnp.concatenate([tile[0, t, :, span], tile[1, t, :, span]], axis=0)
            lines[pl.ds(g * rows + t, count, stride=2 * rows), :] = slab.astype(F32).T
    out[...] = lines[...].astype(BF16)


def spread(tiles, first, count, after):
    _, rows, cols, _ = tiles[0].shape
    shape = (count * 2 * rows, 2 * cols)
    return pl.pallas_call(
        functools.partial(spread_kernel, first),
        out_shape=jax.ShapeDtypeStruct(shape, BF16),
        in_specs=whole(2) + unread(after),
        out_specs=whole(1)[0],
        scratch_shapes=[pltpu.VMEM(shape, F32)],
        compiler_params=vmem_params(),
        name="spread",
    )(*tiles, *after)


def collect_kernel(parts, blocks_ref, lesser, greater, lines):
    _, rows, cols, momenta = lesser.shape
    blocks, height, _ = blocks_ref.shape
    height = height // parts
    for part in range(parts):
        for block in range(blocks):
            lines[block * height : (block + 1) * height] = blocks_ref[
                block, part * height : (part + 1) * height
            ].astype(F32)
        count = momenta // parts
        span = slice(part * count, (part + 1) * count)
        for k in range(2 * rows):
            slab = lines[pl.ds(k, count, stride=2 * rows), :].T.astype(BF16)
            out = lesser if k < rows else greater
            out[0, k % rows, :, span] = slab[:cols]
            out[1, k % rows, :, span] = slab[cols:]


def collect(blocks, tile_shape):
    shape = jax.ShapeDtypeStruct(tile_shape, BF16)
    lines = blocks.shape[0] * blocks.shape[1] // PARTS
    return pl.pallas_call(
        functools.partial(collect_kernel, PARTS),
        out_shape=(shape, shape),
        in_specs=whole(1),
        out_specs=tuple(whole(2)),
        scratch_shapes=[pltpu.VMEM((lines, blocks.shape[2]), F32)],
        compiler_params=vmem_params(),
        name="collect",
    )(blocks)


def table_kernel(column_ref, table, inverse):
    momenta = column_ref.shape[0]
    positions = lax.broadcasted_iota(jnp.int32, (momenta, momenta), 1)
    phases = (column_ref[...] * positions % momenta).astype(F32) * (2.0 * math.pi / momenta)
    cosines = jnp.cos(phases).astype(BF16)
    sines = jnp.sin(phases).astype(BF16)
    inverse[:momenta, :momenta] = cosines
    inverse[:momenta, momenta:] = sines
    inverse[momenta:, :momenta] = -sines
    inverse[momenta:, momenta:] = cosines
    cosines = cosines.astype(F32).T.astype(BF16)
    sines = sines.astype(F32).T.astype(BF16)
    table[:momenta, :momenta] = cosines
    table[:momenta, momenta:] = -sines
    table[momenta:, :momenta] = sines
    table[momenta:, momenta:] = cosines


def make_tables(lattice_map):
    momenta = lattice_map.shape[0]
    shape = jax.ShapeDtypeStruct((2 * momenta, 2 * momenta), BF16)
    return pl.pallas_call(
        table_kernel,
        out_shape=(shape, shape),
        in_specs=whole(1),
        out_specs=tuple(whole(2)),
        compiler_params=vmem_params(),
        name="make_tables",
    )(lattice_map[:, None])


def site_kernel(norm_factor, lesser, greater, table, out):
    _, rows, cols, _ = lesser.shape
    wide = 4 * cols
    for pair in range(rows // 2):
        slabs = [
            jnp.concatenate([tile[0, t], tile[1, t]], axis=1)
            for t in (2 * pair, 2 * pair + 1)
            for tile in (lesser, greater)
        ]
        product = lax.dot_general(
            table[...],
            jnp.concatenate(slabs, axis=0),
            (((1,), (1,)), ((), ())),
            preferred_element_type=F32,
        )
        out[:, pair * wide : (pair + 1) * wide] = (product * norm_factor).astype(BF16)


def to_sites(tiles, table, norm_factor):
    _, rows, cols, momenta = tiles[0].shape
    return pl.pallas_call(
        functools.partial(site_kernel, norm_factor),
        out_shape=jax.ShapeDtypeStruct((2 * momenta, rows * 2 * cols), BF16),
        in_specs=whole(3),
        out_specs=whole(1)[0],
        compiler_params=vmem_params(),
        name="to_sites",
    )(*tiles, table)


def cross_kernel(rows, half_ref, own, far, *rest):
    out = rest[-1]
    half = half_ref[0]
    blocks = far.shape[0]
    cols = blocks * rows
    for at in range(far.shape[1] // (2 * rows)):
        span = slice(at * 2 * rows, (at + 1) * 2 * rows)
        for source, offset, target in ((own, half * blocks, half), (far, 0, 1 - half)):
            loaded = [source[offset + block, span].astype(F32) for block in range(blocks)]
            stacked = jnp.concatenate(
                [lines[rows:] for lines in loaded] + [lines[:rows] for lines in loaded], axis=0
            )
            turned = stacked.T
            for block in range(blocks):
                out[target * blocks + block, span] = jnp.concatenate(
                    [
                        turned[block * rows : (block + 1) * rows],
                        turned[cols + block * rows : cols + (block + 1) * rows],
                    ],
                    axis=0,
                ).astype(BF16)


def to_crossed(half, own, far, rows, after, cost):
    return pl.pallas_call(
        functools.partial(cross_kernel, rows),
        out_shape=jax.ShapeDtypeStruct(own.shape, BF16),
        in_specs=[pl.BlockSpec(memory_space=pltpu.SMEM)] + whole(2) + unread(after),
        out_specs=whole(1)[0],
        compiler_params=vmem_params(),
        cost_estimate=cost,
        name="to_crossed",
    )(half, own, far, *after)


def gate_kernel(*refs):
    del refs


def gate(array, after):
    return pl.pallas_call(
        gate_kernel,
        out_shape=jax.ShapeDtypeStruct(array.shape, array.dtype),
        in_specs=unread([array, *after]),
        out_specs=unread([array])[0],
        input_output_aliases={0: 0},
        name="gate",
    )(array, *after)


def sigma_kernel(norm_factor, parts, *refs):
    crossed = refs[:parts]
    sites, table, inverse, coupling, out, read, written = refs[parts:]
    count = coupling.shape[0]
    momenta = table.shape[0] // 2
    for part in range(parts):
        lines = crossed[part].shape[0]
        read[part * lines : (part + 1) * lines] = crossed[part][...].astype(F32)
    for pair in range(count // 2):
        rights = []
        for t in (2 * pair, 2 * pair + 1):
            real = read[pl.ds(t, momenta, stride=2 * count), :]
            imaginary = -read[pl.ds(count + t, momenta, stride=2 * count), :]
            rights.append(jnp.concatenate([real, imaginary], axis=0).astype(BF16))
        other = jnp.dot(
            table[...], jnp.concatenate(rights, axis=1), preferred_element_type=F32
        )
        other = (other * norm_factor).astype(BF16).astype(F32)
        span = slice(2 * pair * LANES, 2 * (pair + 1) * LANES)
        self_real, self_imaginary = second_born(
            sites[:momenta, span].astype(F32),
            sites[momenta:, span].astype(F32),
            other[:momenta],
            -other[momenta:],
            jnp.concatenate([coupling[t : t + 1] for t in (2 * pair, 2 * pair + 1)], axis=1),
        )
        product = jnp.dot(
            inverse[...],
            jnp.concatenate([self_real, self_imaginary], axis=0).astype(BF16),
            preferred_element_type=F32,
        )
        product = product * norm_factor
        for at in range(2):
            for part in range(2):
                written[pl.ds(part * count + 2 * pair + at, momenta, stride=2 * count), :] = product[
                    part * momenta : (part + 1) * momenta, at * LANES : (at + 1) * LANES
                ]
    blocks, height, _ = out.shape
    height = height // parts
    for part in range(parts):
        for block in range(blocks):
            start = (part * blocks + block) * height
            out[block, part * height : (part + 1) * height] = written[
                start : start + height
            ].astype(BF16)


def to_sigma(crossed, sites, table, inverse, coupling, norm_factor, blocks):
    parts = len(crossed)
    lines, lanes = crossed[0].shape
    return pl.pallas_call(
        functools.partial(sigma_kernel, norm_factor, parts),
        out_shape=jax.ShapeDtypeStruct((blocks, parts * lines // blocks, lanes), BF16),
        in_specs=whole(parts + 4),
        out_specs=whole(1)[0],
        scratch_shapes=[pltpu.VMEM((parts * lines, lanes), F32)] * 2,
        compiler_params=vmem_params(),
        name="to_sigma",
    )(*crossed, sites, table, inverse, coupling)


def rights_kernel(rows, half_ref, own, near_ref, away_ref, *rest):
    out = rest[-1]
    half = half_ref[0]
    blocks = near_ref.shape[0]
    lanes = own.shape[2]
    cols = lanes // 2
    near = half * cols
    away = (1 - half) * cols
    row_at = lax.broadcasted_iota(jnp.int32, (lanes, 2 * lanes), 0)
    inner_times = jnp.where(row_at < cols, near + row_at, away + row_at - cols)
    lane_at = lax.broadcasted_iota(jnp.int32, (lanes, 2 * lanes), 1)
    last_times = jnp.where(lane_at < lanes, near, away) + lane_at % cols
    keep = inner_times <= last_times
    for at in range(out.shape[0]):
        span = slice(at * 2 * rows, (at + 1) * 2 * rows)

        def stacked(read):
            loaded = [read(block).astype(F32) for block in range(blocks)]
            return [
                jnp.concatenate([lines[g * rows : (g + 1) * rows] for lines in loaded], axis=0)
                for g in range(2)
            ]

        own_near = stacked(lambda block: own[half * blocks + block, span])
        own_away = stacked(lambda block: own[(1 - half) * blocks + block, span])
        far_near = stacked(lambda block: near_ref[block, span])
        far_away = stacked(lambda block: away_ref[0, block, span])
        greens = [
            jnp.concatenate(
                [
                    jnp.concatenate([own_near[g], own_away[g]], axis=1),
                    jnp.concatenate([far_near[g], far_away[g]], axis=1),
                ],
                axis=0,
            )
            for g in range(2)
        ]
        out[at, :lanes] = greens[0].astype(BF16)
        out[at, lanes : 2 * lanes] = greens[1].astype(BF16)
        out[at, 2 * lanes :] = jnp.where(keep, greens[0] - greens[1], 0.0).astype(BF16)


STEPS = 4
PARTS = 2


def make_rights(half, own, far_near, far_away, rows, part, before):
    sources, lines, lanes = own.shape
    blocks = far_near.shape[0]
    steps = STEPS // PARTS
    step = lines // steps
    momenta = step // (2 * rows)
    return pl.pallas_call(
        functools.partial(rights_kernel, rows),
        grid=(steps,),
        out_shape=jax.ShapeDtypeStruct((STEPS * momenta, 3 * lanes, 2 * lanes), BF16),
        in_specs=scalars()
        + [
            pl.BlockSpec((sources, step, lanes), lambda p: (0, p, 0)),
            pl.BlockSpec((blocks, step, lanes), lambda p: (0, p, 0)),
            pl.BlockSpec((1, blocks, step, lanes), lambda p: (part, 0, p, 0)),
        ]
        + unread(before),
        out_specs=pl.BlockSpec(
            (momenta, 3 * lanes, 2 * lanes), lambda p: (part * steps + p, 0, 0)
        ),
        input_output_aliases={4: 0} if before else {},
        compiler_params=vmem_params(),
        cost_estimate=weight(),
        name="make_rights",
    )(half, own, far_near, far_away, *before)


def volterra_kernel(rows, half_ref, sigma, rights, out):
    half = half_ref[0]
    blocks = sigma.shape[0] // 2
    lanes = sigma.shape[2]
    cols = lanes // 2
    near = half * cols
    away = (1 - half) * cols
    here = half * blocks
    there = (1 - half) * blocks
    first_times = near + lax.broadcasted_iota(jnp.int32, (cols, lanes), 0)
    left_lane = lax.broadcasted_iota(jnp.int32, (cols, lanes), 1)
    low_lanes = left_lane < cols
    left_times = jnp.where(low_lanes, near + left_lane, away + left_lane - cols)
    keep_left = left_times <= first_times
    for at in range(rights.shape[0]):
        span = slice(at * 2 * rows, (at + 1) * 2 * rows)

        def stacked(offset):
            loaded = [sigma[offset + block, span].astype(F32) for block in range(blocks)]
            return [
                jnp.concatenate([lines[part * rows : (part + 1) * rows] for lines in loaded], axis=0)
                for part in range(2)
            ]

        sigma_near = stacked(here)
        sigma_away = stacked(there)
        retarded = []
        lefts = [[], []]
        for part in range(2):
            lesser = jnp.where(
                low_lanes, sigma_near[part], pltpu.roll(sigma_away[part], cols, 1)
            )
            greater = jnp.where(
                low_lanes, pltpu.roll(sigma_near[part], cols, 1), sigma_away[part]
            )
            retarded.append(jnp.where(keep_left, greater - lesser, 0.0))
            lefts[0].append(lesser)
            lefts[1].append(greater)
        retarded = jnp.concatenate(retarded, axis=0).astype(BF16)
        results = []
        for g in range(2):
            left = jnp.concatenate(
                [retarded, jnp.concatenate(lefts[g], axis=0).astype(BF16)], axis=1
            )
            right = jnp.concatenate(
                [rights[at, g * lanes : (g + 1) * lanes], rights[at, 2 * lanes :]], axis=0
            )
            product = jnp.dot(left, right, preferred_element_type=F32)
            sides = []
            for side in range(2):
                straight = product[:cols, side * lanes : (side + 1) * lanes]
                turned = pltpu.roll(product[cols:, side * lanes : (side + 1) * lanes], cols, 1)
                sides.append((straight + jnp.where(low_lanes, -turned, turned)) * step_size)
            results.append(sides)
        for block in range(blocks):
            lines = slice(block * rows, (block + 1) * rows)
            for side, offset in enumerate((here, there)):
                out[offset + block, span] = jnp.concatenate(
                    [results[0][side][lines], results[1][side][lines]], axis=0
                ).astype(BF16)


def volterra(half, sigma, rights, rows):
    sources, lines, lanes = sigma.shape
    step = lines // STEPS
    momenta = step // (2 * rows)
    spec = pl.BlockSpec((sources, step, lanes), lambda p: (0, p, 0))
    return pl.pallas_call(
        functools.partial(volterra_kernel, rows),
        grid=(STEPS,),
        out_shape=jax.ShapeDtypeStruct(sigma.shape, BF16),
        in_specs=scalars()
        + [spec, pl.BlockSpec((momenta, 3 * lanes, 2 * lanes), lambda p: (p, 0, 0))],
        out_specs=spec,
        compiler_params=vmem_params(),
        name="volterra",
    )(half, sigma, rights)


def halved_body(green_lesser, green_greater, lattice_map, time_offset):
    _, rows, cols, momenta = green_lesser.shape
    half = lax.axis_index("half")
    line = lax.axis_index("line")
    side = lax.axis_index("tcol")
    lines = lax.axis_size("line")
    group = lines * lax.axis_size("tcol")
    window = rows * lines * lax.axis_size("half")
    norm_factor = 1.0 / math.sqrt(momenta)
    tiles = (green_lesser, green_greater)
    half_at = half[None]
    count = momenta // PARTS

    def exchange(blocks):
        return lax.all_to_all(blocks, ("tcol", "line"), 0, 0, tiled=True)

    def blocked(rows_array):
        return rows_array.reshape(group, rows_array.shape[0] // group, rows_array.shape[1])

    def swap(array):
        return lax.ppermute(array, "half", [(0, 1), (1, 0)])

    own = []
    far_near = []
    for part in range(PARTS):
        own.append(exchange(blocked(spread(tiles, part * count, count, own[-1:]))))
        far_near.append(swap(lax.dynamic_slice_in_dim(own[-1], (1 - half) * lines, lines)))

    table, inverse = make_tables(lattice_map)
    sites = to_sites(tiles, table, norm_factor)
    time_steps = jnp.arange(window, dtype=jnp.int32)
    coupling_line = 1.0 + drive_depth * jnp.cos(
        ((time_offset[0] + time_steps) % PERIOD).astype(F32) * (2.0 * math.pi / PERIOD)
    )
    first = lax.dynamic_slice_in_dim(coupling_line, (half * lines + line) * rows, rows)
    second = lax.dynamic_slice_in_dim(coupling_line, side * cols, cols)
    coupling = first[:, None] * jnp.concatenate([second, second])[None, :]

    sent = []
    for part in range(PARTS):
        sent.append(
            to_crossed(
                half_at,
                own[part],
                far_near[part],
                rows,
                [sites, own[-1]] + sent[-1:],
                weight() if part > 0 else None,
            )
        )
    crossed = [exchange(blocks) for blocks in sent]
    kept = jnp.stack(
        [lax.dynamic_slice_in_dim(blocks, half * lines, lines) for blocks in own]
    )
    far_away = swap(gate(kept, crossed))
    sigma = exchange(
        to_sigma(
            [blocks.reshape(-1, 2 * cols) for blocks in crossed],
            sites,
            table,
            inverse,
            coupling,
            norm_factor,
            group,
        )
    )
    rights = []
    for part in range(PARTS):
        rights = [
            make_rights(half_at, own[part], far_near[part], far_away, rows, part, rights)
        ]
    returned = exchange(volterra(half_at, sigma, rights[0], rows))
    return collect(returned, green_lesser.shape)


def solution(mesh):
    row_parts = mesh.shape["trow"]
    col_parts = mesh.shape["tcol"]

    def call(green_lesser, green_greater, lattice_map, time_offset):
        window, window_cols, momenta = green_lesser.shape[1:]
        rows = window // row_parts
        cols = window_cols // col_parts
        halved = (
            col_parts == 2
            and row_parts % 2 == 0
            and window == window_cols
            and 2 * cols == LANES
            and cols == rows * (row_parts // 2)
            and rows % 8 == 0
            and momenta % (2 * row_parts * STEPS) == 0
            and momenta % (PARTS * LANES) == 0
        )
        if halved:
            devices = mesh.devices.reshape(2, row_parts // 2, col_parts)
            used = Mesh(devices, ("half", "line", "tcol"))
            spec = P(None, ("half", "line"), "tcol", None)
            inner = halved_body
        else:
            used = mesh
            spec = P(None, "trow", "tcol", None)
            inner = general_body
        return jax.shard_map(
            inner, mesh=used, in_specs=(spec, spec, P(), P()), out_specs=(spec, spec), check_vma=False
        )(green_lesser, green_greater, lattice_map, time_offset)

    return call
```

```python
import functools
import math

import jax
import jax.numpy as jnp
from jax import lax
from jax.experimental import pallas as pl
from jax.experimental.pallas import tpu as pltpu
from jax.sharding import Mesh, PartitionSpec as P

F32 = jnp.float32
BF16 = jnp.bfloat16
LANES = 128

PERIOD = 64


step_size = 0.01
drive_depth = 0.5


def regroup(blocks):
    return lax.all_to_all(
        lax.all_to_all(blocks, "trow", split_axis=1, concat_axis=1, tiled=True),
        "tcol",
        split_axis=2,
        concat_axis=2,
        tiled=True,
    )


def pack_blocks(spectral, row_parts, col_parts):
    stacked, extent, tile_cells = spectral.shape
    return spectral.reshape(
        stacked, row_parts, col_parts, extent // (row_parts * col_parts), tile_cells
    )


def spread_times(blocks, tile_rows, tile_cols):
    stacked, row_parts, col_parts, local_count, tile_cells = blocks.shape
    shaped = blocks.reshape(stacked, row_parts, col_parts, local_count, tile_rows, tile_cols)
    return shaped.transpose(0, 3, 1, 4, 2, 5).reshape(
        stacked, local_count, row_parts * tile_rows, col_parts * tile_cols
    )


def gather_tiles(full, row_parts, col_parts):
    stacked, local_count, window, window_cols = full.shape
    tile_rows = window // row_parts
    tile_cols = window_cols // col_parts
    shaped = full.reshape(stacked, local_count, row_parts, tile_rows, col_parts, tile_cols)
    return shaped.transpose(0, 2, 4, 1, 3, 5).reshape(
        stacked, row_parts, col_parts, local_count, tile_rows * tile_cols
    )


def mirrored(full, keep_pair):
    stacked, local_count, window, window_cols = full.shape
    paired = full.reshape(stacked, local_count // 2, 2, window, window_cols)
    swapped = jnp.where(keep_pair[None, :, None, None, None], paired, paired[:, :, ::-1])
    return jnp.swapaxes(swapped.reshape(stacked, local_count, window, window_cols), 2, 3)


def second_born(first_real, first_imaginary, other_real, other_imaginary, coupling):
    square_real = first_real * first_real - first_imaginary * first_imaginary
    square_imaginary = 2.0 * first_real * first_imaginary
    out_real = coupling * (square_real * other_real - square_imaginary * other_imaginary)
    out_imaginary = coupling * (square_real * other_imaginary + square_imaginary * other_real)
    return (out_real, out_imaginary)


def collide(
    retarded_real,
    retarded_imaginary,
    self_real,
    self_imaginary,
    green_real,
    green_imaginary,
    advanced_real,
    advanced_imaginary,
):
    minus_left = jnp.concatenate(
        [retarded_real, -retarded_imaginary, self_real, -self_imaginary], axis=2
    )
    plus_left = jnp.concatenate(
        [retarded_real, retarded_imaginary, self_real, self_imaginary], axis=2
    )
    real_right = jnp.concatenate(
        [green_real, green_imaginary, advanced_real, advanced_imaginary], axis=1
    )
    imaginary_right = jnp.concatenate(
        [green_imaginary, green_real, advanced_imaginary, advanced_real], axis=1
    )
    out_real = jnp.einsum(
        "kts,ksu->ktu", minus_left, real_right, preferred_element_type=jnp.float32
    )
    out_imaginary = jnp.einsum(
        "kts,ksu->ktu", plus_left, imaginary_right, preferred_element_type=jnp.float32
    )
    return (out_real, out_imaginary)


def general_body(green_lesser, green_greater, lattice_map, time_offset):
    tile_rows = green_lesser.shape[1]
    tile_cols = green_lesser.shape[2]
    momenta = green_lesser.shape[3]
    row_parts = lax.axis_size("trow")
    col_parts = lax.axis_size("tcol")
    window = tile_rows * row_parts
    tile_cells = tile_rows * tile_cols
    local_count = momenta // (row_parts * col_parts)
    norm_factor = 1.0 / math.sqrt(momenta)
    greens = (
        jnp.concatenate([green_lesser, green_greater], axis=0)
        .reshape(4, tile_cells, momenta)
        .transpose(0, 2, 1)
    )
    positions = jnp.arange(momenta, dtype=jnp.int32)
    halves = positions // 2
    site_order = jnp.where(
        positions == 1, momenta // 2, jnp.where(positions % 2 == 0, halves, momenta - halves)
    )
    phases = (lattice_map[:, None] * site_order[None, :] % momenta).astype(jnp.float32) * (
        2.0 * math.pi / momenta
    )
    cosines = jnp.cos(phases).astype(jnp.bfloat16)
    sines = jnp.sin(phases).astype(jnp.bfloat16)
    ahead_blocks = lax.all_to_all(
        lax.all_to_all(
            pack_blocks(greens, row_parts, col_parts),
            "trow",
            split_axis=1,
            concat_axis=1,
            tiled=True,
        ),
        "tcol",
        split_axis=2,
        concat_axis=2,
        tiled=True,
    )
    green_moment = spread_times(ahead_blocks, tile_rows, tile_cols)
    forward_table = jnp.concatenate([cosines, sines], axis=1)
    products = jnp.einsum("cjm,jr->crm", greens, forward_table, preferred_element_type=jnp.float32)
    site_space = jnp.stack(
        [
            (products[0, :momenta] - products[1, momenta:]) * norm_factor,
            (products[0, momenta:] + products[1, :momenta]) * norm_factor,
            (products[2, :momenta] - products[3, momenta:]) * norm_factor,
            (products[2, momenta:] + products[3, :momenta]) * norm_factor,
        ]
    ).astype(jnp.bfloat16)
    site_full = spread_times(
        regroup(pack_blocks(site_space, row_parts, col_parts)), tile_rows, tile_cols
    )
    site_block = lax.axis_index("trow") * col_parts + lax.axis_index("tcol")
    keep_pair = site_block * (local_count // 2) + jnp.arange(local_count // 2, dtype=jnp.int32) == 0
    mirror = mirrored(site_full, keep_pair).astype(jnp.float32)
    direct = site_full.astype(jnp.float32)
    time_steps = jnp.arange(window, dtype=jnp.int32)
    coupling_line = 1.0 + drive_depth * jnp.cos(
        ((time_offset[0] + time_steps) % PERIOD).astype(jnp.float32) * (2.0 * math.pi / PERIOD)
    )
    coupling = coupling_line[:, None] * coupling_line[None, :]
    self_lesser = second_born(direct[0], direct[1], mirror[2], mirror[3], coupling)
    self_greater = second_born(direct[2], direct[3], mirror[0], mirror[1], coupling)
    self_sites = jnp.stack(
        [self_lesser[0], self_lesser[1], self_greater[0], self_greater[1]]
    ).astype(jnp.bfloat16)
    self_tiles = regroup(gather_tiles(self_sites, row_parts, col_parts)).reshape(
        4, momenta, tile_cells
    )
    inverse_table = jnp.concatenate([cosines, sines], axis=0)
    spectral_terms = jnp.einsum(
        "cum,ju->cjm", self_tiles, inverse_table, preferred_element_type=jnp.float32
    )
    self_spectral = jnp.stack(
        [
            (spectral_terms[0, :momenta] + spectral_terms[1, momenta:]) * norm_factor,
            (spectral_terms[1, :momenta] - spectral_terms[0, momenta:]) * norm_factor,
            (spectral_terms[2, :momenta] + spectral_terms[3, momenta:]) * norm_factor,
            (spectral_terms[3, :momenta] - spectral_terms[2, momenta:]) * norm_factor,
        ]
    ).astype(jnp.bfloat16)
    self_moment = spread_times(
        regroup(pack_blocks(self_spectral, row_parts, col_parts)), tile_rows, tile_cols
    )
    lower_mask = time_steps[None, :] <= time_steps[:, None]
    upper_mask = time_steps[:, None] <= time_steps[None, :]
    retarded = jnp.where(
        lower_mask, self_moment[2:4].astype(jnp.float32) - self_moment[0:2].astype(jnp.float32), 0.0
    ).astype(jnp.bfloat16)
    advanced = jnp.where(
        upper_mask,
        green_moment[0:2].astype(jnp.float32) - green_moment[2:4].astype(jnp.float32),
        0.0,
    ).astype(jnp.bfloat16)
    lesser_out = collide(
        retarded[0],
        retarded[1],
        self_moment[0],
        self_moment[1],
        green_moment[0],
        green_moment[1],
        advanced[0],
        advanced[1],
    )
    greater_out = collide(
        retarded[0],
        retarded[1],
        self_moment[2],
        self_moment[3],
        green_moment[2],
        green_moment[3],
        advanced[0],
        advanced[1],
    )
    collisions = (
        jnp.stack([lesser_out[0], lesser_out[1], greater_out[0], greater_out[1]]) * step_size
    ).astype(jnp.bfloat16)
    out_tiles = regroup(gather_tiles(collisions, row_parts, col_parts)).reshape(
        4, momenta, tile_cells
    )
    out_tiles = out_tiles.transpose(0, 2, 1).reshape(4, tile_rows, tile_cols, momenta)
    return (out_tiles[0:2], out_tiles[2:4])


def vmem_params():
    return pltpu.CompilerParams(vmem_limit_bytes=48 * 1024 * 1024)


def unread(arrays):
    return [pl.BlockSpec(memory_space=pl.ANY)] * len(arrays)


def whole(count):
    return [pl.BlockSpec(memory_space=pltpu.VMEM)] * count


def weight():
    return pl.CostEstimate(flops=10**11, bytes_accessed=2**20, transcendentals=0)


def scalars():
    return [pl.BlockSpec(memory_space=pltpu.SMEM)]


def spread_kernel(first, lesser, greater, *rest):
    out, lines = rest[-2:]
    _, rows, _, _ = lesser.shape
    count = lines.shape[0] // (2 * rows)
    for g, tile in enumerate((lesser, greater)):
        for t in range(rows):
            span = slice(first, first + count)
            slab = jnp.concatenate([tile[0, t, :, span], tile[1, t, :, span]], axis=0)
            lines[pl.ds(g * rows + t, count, stride=2 * rows), :] = slab.astype(F32).T
    out[...] = lines[...].astype(BF16)


def spread(tiles, first, count, after):
    _, rows, cols, _ = tiles[0].shape
    shape = (count * 2 * rows, 2 * cols)
    return pl.pallas_call(
        functools.partial(spread_kernel, first),
        out_shape=jax.ShapeDtypeStruct(shape, BF16),
        in_specs=whole(2) + unread(after),
        out_specs=whole(1)[0],
        scratch_shapes=[pltpu.VMEM(shape, F32)],
        compiler_params=vmem_params(),
        name="spread",
    )(*tiles, *after)


def collect_kernel(parts, blocks_ref, lesser, greater, lines):
    _, rows, cols, momenta = lesser.shape
    blocks, height, _ = blocks_ref.shape
    height = height // parts
    for part in range(parts):
        for block in range(blocks):
            lines[block * height : (block + 1) * height] = blocks_ref[
                block, part * height : (part + 1) * height
            ].astype(F32)
        count = momenta // parts
        span = slice(part * count, (part + 1) * count)
        for k in range(2 * rows):
            slab = lines[pl.ds(k, count, stride=2 * rows), :].T.astype(BF16)
            out = lesser if k < rows else greater
            out[0, k % rows, :, span] = slab[:cols]
            out[1, k % rows, :, span] = slab[cols:]


def collect(blocks, tile_shape):
    shape = jax.ShapeDtypeStruct(tile_shape, BF16)
    lines = blocks.shape[0] * blocks.shape[1] // PARTS
    return pl.pallas_call(
        functools.partial(collect_kernel, PARTS),
        out_shape=(shape, shape),
        in_specs=whole(1),
        out_specs=tuple(whole(2)),
        scratch_shapes=[pltpu.VMEM((lines, blocks.shape[2]), F32)],
        compiler_params=vmem_params(),
        name="collect",
    )(blocks)


def table_kernel(column_ref, table, inverse):
    momenta = column_ref.shape[0]
    positions = lax.broadcasted_iota(jnp.int32, (momenta, momenta), 1)
    phases = (column_ref[...] * positions % momenta).astype(F32) * (2.0 * math.pi / momenta)
    cosines = jnp.cos(phases).astype(BF16)
    sines = jnp.sin(phases).astype(BF16)
    inverse[:momenta, :momenta] = cosines
    inverse[:momenta, momenta:] = sines
    inverse[momenta:, :momenta] = -sines
    inverse[momenta:, momenta:] = cosines
    cosines = cosines.astype(F32).T.astype(BF16)
    sines = sines.astype(F32).T.astype(BF16)
    table[:momenta, :momenta] = cosines
    table[:momenta, momenta:] = -sines
    table[momenta:, :momenta] = sines
    table[momenta:, momenta:] = cosines


def make_tables(lattice_map):
    momenta = lattice_map.shape[0]
    shape = jax.ShapeDtypeStruct((2 * momenta, 2 * momenta), BF16)
    return pl.pallas_call(
        table_kernel,
        out_shape=(shape, shape),
        in_specs=whole(1),
        out_specs=tuple(whole(2)),
        compiler_params=vmem_params(),
        name="make_tables",
    )(lattice_map[:, None])


def site_kernel(norm_factor, lesser, greater, table, out):
    _, rows, cols, _ = lesser.shape
    wide = 4 * cols
    for pair in range(rows // 2):
        slabs = [
            jnp.concatenate([tile[0, t], tile[1, t]], axis=1)
            for t in (2 * pair, 2 * pair + 1)
            for tile in (lesser, greater)
        ]
        product = lax.dot_general(
            table[...],
            jnp.concatenate(slabs, axis=0),
            (((1,), (1,)), ((), ())),
            preferred_element_type=F32,
        )
        out[:, pair * wide : (pair + 1) * wide] = (product * norm_factor).astype(BF16)


def to_sites(tiles, table, norm_factor):
    _, rows, cols, momenta = tiles[0].shape
    return pl.pallas_call(
        functools.partial(site_kernel, norm_factor),
        out_shape=jax.ShapeDtypeStruct((2 * momenta, rows * 2 * cols), BF16),
        in_specs=whole(3),
        out_specs=whole(1)[0],
        compiler_params=vmem_params(),
        name="to_sites",
    )(*tiles, table)


def cross_kernel(rows, half_ref, own, far, *rest):
    out = rest[-1]
    half = half_ref[0]
    blocks = far.shape[0]
    cols = blocks * rows
    for at in range(far.shape[1] // (2 * rows)):
        span = slice(at * 2 * rows, (at + 1) * 2 * rows)
        for source, offset, target in ((own, half * blocks, half), (far, 0, 1 - half)):
            loaded = [source[offset + block, span].astype(F32) for block in range(blocks)]
            stacked = jnp.concatenate(
                [lines[rows:] for lines in loaded] + [lines[:rows] for lines in loaded], axis=0
            )
            turned = stacked.T
            for block in range(blocks):
                out[target * blocks + block, span] = jnp.concatenate(
                    [
                        turned[block * rows : (block + 1) * rows],
                        turned[cols + block * rows : cols + (block + 1) * rows],
                    ],
                    axis=0,
                ).astype(BF16)


def to_crossed(half, own, far, rows, after, cost):
    return pl.pallas_call(
        functools.partial(cross_kernel, rows),
        out_shape=jax.ShapeDtypeStruct(own.shape, BF16),
        in_specs=[pl.BlockSpec(memory_space=pltpu.SMEM)] + whole(2) + unread(after),
        out_specs=whole(1)[0],
        compiler_params=vmem_params(),
        cost_estimate=cost,
        name="to_crossed",
    )(half, own, far, *after)


def gate_kernel(*refs):
    del refs


def gate(array, after):
    return pl.pallas_call(
        gate_kernel,
        out_shape=jax.ShapeDtypeStruct(array.shape, array.dtype),
        in_specs=unread([array, *after]),
        out_specs=unread([array])[0],
        input_output_aliases={0: 0},
        name="gate",
    )(array, *after)


def sigma_kernel(norm_factor, parts, *refs):
    crossed = refs[:parts]
    sites, table, inverse, coupling, out, read, written = refs[parts:]
    count = coupling.shape[0]
    momenta = table.shape[0] // 2
    for part in range(parts):
        lines = crossed[part].shape[0]
        read[part * lines : (part + 1) * lines] = crossed[part][...].astype(F32)
    for pair in range(count // 2):
        rights = []
        for t in (2 * pair, 2 * pair + 1):
            real = read[pl.ds(t, momenta, stride=2 * count), :]
            imaginary = -read[pl.ds(count + t, momenta, stride=2 * count), :]
            rights.append(jnp.concatenate([real, imaginary], axis=0).astype(BF16))
        other = jnp.dot(
            table[...], jnp.concatenate(rights, axis=1), preferred_element_type=F32
        )
        other = (other * norm_factor).astype(BF16).astype(F32)
        span = slice(2 * pair * LANES, 2 * (pair + 1) * LANES)
        self_real, self_imaginary = second_born(
            sites[:momenta, span].astype(F32),
            sites[momenta:, span].astype(F32),
            other[:momenta],
            -other[momenta:],
            jnp.concatenate([coupling[t : t + 1] for t in (2 * pair, 2 * pair + 1)], axis=1),
        )
        product = jnp.dot(
            inverse[...],
            jnp.concatenate([self_real, self_imaginary], axis=0).astype(BF16),
            preferred_element_type=F32,
        )
        product = product * norm_factor
        for at in range(2):
            for part in range(2):
                written[pl.ds(part * count + 2 * pair + at, momenta, stride=2 * count), :] = product[
                    part * momenta : (part + 1) * momenta, at * LANES : (at + 1) * LANES
                ]
    blocks, height, _ = out.shape
    height = height // parts
    for part in range(parts):
        for block in range(blocks):
            start = (part * blocks + block) * height
            out[block, part * height : (part + 1) * height] = written[
                start : start + height
            ].astype(BF16)


def to_sigma(crossed, sites, table, inverse, coupling, norm_factor, blocks):
    parts = len(crossed)
    lines, lanes = crossed[0].shape
    return pl.pallas_call(
        functools.partial(sigma_kernel, norm_factor, parts),
        out_shape=jax.ShapeDtypeStruct((blocks, parts * lines // blocks, lanes), BF16),
        in_specs=whole(parts + 4),
        out_specs=whole(1)[0],
        scratch_shapes=[pltpu.VMEM((parts * lines, lanes), F32)] * 2,
        compiler_params=vmem_params(),
        name="to_sigma",
    )(*crossed, sites, table, inverse, coupling)


def rights_kernel(rows, half_ref, own, near_ref, away_ref, *rest):
    out = rest[-1]
    half = half_ref[0]
    blocks = near_ref.shape[0]
    lanes = own.shape[2]
    cols = lanes // 2
    near = half * cols
    away = (1 - half) * cols
    row_at = lax.broadcasted_iota(jnp.int32, (lanes, 2 * lanes), 0)
    inner_times = jnp.where(row_at < cols, near + row_at, away + row_at - cols)
    lane_at = lax.broadcasted_iota(jnp.int32, (lanes, 2 * lanes), 1)
    last_times = jnp.where(lane_at < lanes, near, away) + lane_at % cols
    keep = inner_times <= last_times
    for at in range(out.shape[0]):
        span = slice(at * 2 * rows, (at + 1) * 2 * rows)

        def stacked(read):
            loaded = [read(block).astype(F32) for block in range(blocks)]
            return [
                jnp.concatenate([lines[g * rows : (g + 1) * rows] for lines in loaded], axis=0)
                for g in range(2)
            ]

        own_near = stacked(lambda block: own[half * blocks + block, span])
        own_away = stacked(lambda block: own[(1 - half) * blocks + block, span])
        far_near = stacked(lambda block: near_ref[block, span])
        far_away = stacked(lambda block: away_ref[0, block, span])
        greens = [
            jnp.concatenate(
                [
                    jnp.concatenate([own_near[g], own_away[g]], axis=1),
                    jnp.concatenate([far_near[g], far_away[g]], axis=1),
                ],
                axis=0,
            )
            for g in range(2)
        ]
        out[at, :lanes] = greens[0].astype(BF16)
        out[at, lanes : 2 * lanes] = greens[1].astype(BF16)
        out[at, 2 * lanes :] = jnp.where(keep, greens[0] - greens[1], 0.0).astype(BF16)


STEPS = 4
PARTS = 2


def make_rights(half, own, far_near, far_away, rows, part, before):
    sources, lines, lanes = own.shape
    blocks = far_near.shape[0]
    steps = STEPS // PARTS
    step = lines // steps
    momenta = step // (2 * rows)
    return pl.pallas_call(
        functools.partial(rights_kernel, rows),
        grid=(steps,),
        out_shape=jax.ShapeDtypeStruct((STEPS * momenta, 3 * lanes, 2 * lanes), BF16),
        in_specs=scalars()
        + [
            pl.BlockSpec((sources, step, lanes), lambda p: (0, p, 0)),
            pl.BlockSpec((blocks, step, lanes), lambda p: (0, p, 0)),
            pl.BlockSpec((1, blocks, step, lanes), lambda p: (part, 0, p, 0)),
        ]
        + unread(before),
        out_specs=pl.BlockSpec(
            (momenta, 3 * lanes, 2 * lanes), lambda p: (part * steps + p, 0, 0)
        ),
        input_output_aliases={4: 0} if before else {},
        compiler_params=vmem_params(),
        cost_estimate=weight(),
        name="make_rights",
    )(half, own, far_near, far_away, *before)


def volterra_kernel(rows, half_ref, sigma, rights, out):
    half = half_ref[0]
    blocks = sigma.shape[0] // 2
    lanes = sigma.shape[2]
    cols = lanes // 2
    near = half * cols
    away = (1 - half) * cols
    here = half * blocks
    there = (1 - half) * blocks
    first_times = near + lax.broadcasted_iota(jnp.int32, (cols, lanes), 0)
    left_lane = lax.broadcasted_iota(jnp.int32, (cols, lanes), 1)
    low_lanes = left_lane < cols
    left_times = jnp.where(low_lanes, near + left_lane, away + left_lane - cols)
    keep_left = left_times <= first_times
    for at in range(rights.shape[0]):
        span = slice(at * 2 * rows, (at + 1) * 2 * rows)

        def stacked(offset):
            loaded = [sigma[offset + block, span].astype(F32) for block in range(blocks)]
            return [
                jnp.concatenate([lines[part * rows : (part + 1) * rows] for lines in loaded], axis=0)
                for part in range(2)
            ]

        sigma_near = stacked(here)
        sigma_away = stacked(there)
        retarded = []
        lefts = [[], []]
        for part in range(2):
            lesser = jnp.where(
                low_lanes, sigma_near[part], pltpu.roll(sigma_away[part], cols, 1)
            )
            greater = jnp.where(
                low_lanes, pltpu.roll(sigma_near[part], cols, 1), sigma_away[part]
            )
            retarded.append(jnp.where(keep_left, greater - lesser, 0.0))
            lefts[0].append(lesser)
            lefts[1].append(greater)
        retarded = jnp.concatenate(retarded, axis=0).astype(BF16)
        results = []
        for g in range(2):
            left = jnp.concatenate(
                [retarded, jnp.concatenate(lefts[g], axis=0).astype(BF16)], axis=1
            )
            right = jnp.concatenate(
                [rights[at, g * lanes : (g + 1) * lanes], rights[at, 2 * lanes :]], axis=0
            )
            product = jnp.dot(left, right, preferred_element_type=F32)
            sides = []
            for side in range(2):
                straight = product[:cols, side * lanes : (side + 1) * lanes]
                turned = pltpu.roll(product[cols:, side * lanes : (side + 1) * lanes], cols, 1)
                sides.append((straight + jnp.where(low_lanes, -turned, turned)) * step_size)
            results.append(sides)
        for block in range(blocks):
            lines = slice(block * rows, (block + 1) * rows)
            for side, offset in enumerate((here, there)):
                out[offset + block, span] = jnp.concatenate(
                    [results[0][side][lines], results[1][side][lines]], axis=0
                ).astype(BF16)


def volterra(half, sigma, rights, rows):
    sources, lines, lanes = sigma.shape
    step = lines // STEPS
    momenta = step // (2 * rows)
    spec = pl.BlockSpec((sources, step, lanes), lambda p: (0, p, 0))
    return pl.pallas_call(
        functools.partial(volterra_kernel, rows),
        grid=(STEPS,),
        out_shape=jax.ShapeDtypeStruct(sigma.shape, BF16),
        in_specs=scalars()
        + [spec, pl.BlockSpec((momenta, 3 * lanes, 2 * lanes), lambda p: (p, 0, 0))],
        out_specs=spec,
        compiler_params=vmem_params(),
        name="volterra",
    )(half, sigma, rights)


def halved_body(green_lesser, green_greater, lattice_map, time_offset):
    _, rows, cols, momenta = green_lesser.shape
    half = lax.axis_index("half")
    line = lax.axis_index("line")
    side = lax.axis_index("tcol")
    lines = lax.axis_size("line")
    group = lines * lax.axis_size("tcol")
    window = rows * lines * lax.axis_size("half")
    norm_factor = 1.0 / math.sqrt(momenta)
    tiles = (green_lesser, green_greater)
    half_at = half[None]
    count = momenta // PARTS

    def exchange(blocks):
        return lax.all_to_all(blocks, ("tcol", "line"), 0, 0, tiled=True)

    def blocked(rows_array):
        return rows_array.reshape(group, rows_array.shape[0] // group, rows_array.shape[1])

    def swap(array):
        return lax.ppermute(array, "half", [(0, 1), (1, 0)])

    table, inverse = make_tables(lattice_map)
    sites = to_sites(tiles, table, norm_factor)
    time_steps = jnp.arange(window, dtype=jnp.int32)
    coupling_line = 1.0 + drive_depth * jnp.cos(
        ((time_offset[0] + time_steps) % PERIOD).astype(F32) * (2.0 * math.pi / PERIOD)
    )
    first = lax.dynamic_slice_in_dim(coupling_line, (half * lines + line) * rows, rows)
    second = lax.dynamic_slice_in_dim(coupling_line, side * cols, cols)
    coupling = first[:, None] * jnp.concatenate([second, second])[None, :]

    spread_parts = [spread(tiles, part * count, count, []) for part in range(PARTS)]
    own = [exchange(blocked(spread_parts[0]))]
    for rows_array in spread_parts[1:]:
        own.append(exchange(gate(blocked(rows_array), [own[-1], sites, coupling])))
    far_near = [swap(lax.dynamic_slice_in_dim(blocks, (1 - half) * lines, lines)) for blocks in own]

    sent = []
    for part in range(PARTS):
        sent.append(
            to_crossed(
                half_at,
                own[part],
                far_near[part],
                rows,
                own[-1:] + sent[-1:],
                weight() if part > 0 else None,
            )
        )
    crossed = [exchange(blocks) for blocks in sent]
    kept = jnp.stack(
        [lax.dynamic_slice_in_dim(blocks, half * lines, lines) for blocks in own]
    )
    far_away = swap(gate(kept, sent[-1:]))
    sigma = exchange(
        to_sigma(
            [blocks.reshape(-1, 2 * cols) for blocks in crossed],
            sites,
            table,
            inverse,
            coupling,
            norm_factor,
            group,
        )
    )
    rights = []
    for part in range(PARTS):
        rights = [
            make_rights(half_at, own[part], far_near[part], far_away, rows, part, rights)
        ]
    returned = exchange(volterra(half_at, sigma, rights[0], rows))
    return collect(returned, green_lesser.shape)


def solution(mesh):
    row_parts = mesh.shape["trow"]
    col_parts = mesh.shape["tcol"]

    def call(green_lesser, green_greater, lattice_map, time_offset):
        window, window_cols, momenta = green_lesser.shape[1:]
        rows = window // row_parts
        cols = window_cols // col_parts
        halved = (
            col_parts == 2
            and row_parts % 2 == 0
            and window == window_cols
            and 2 * cols == LANES
            and cols == rows * (row_parts // 2)
            and rows % 8 == 0
            and momenta % (2 * row_parts * STEPS) == 0
            and momenta % (PARTS * LANES) == 0
        )
        if halved:
            devices = mesh.devices.reshape(2, row_parts // 2, col_parts)
            used = Mesh(devices, ("half", "line", "tcol"))
            spec = P(None, ("half", "line"), "tcol", None)
            inner = halved_body
        else:
            used = mesh
            spec = P(None, "trow", "tcol", None)
            inner = general_body
        return jax.shard_map(
            inner, mesh=used, in_specs=(spec, spec, P(), P()), out_specs=(spec, spec), check_vma=False
        )(green_lesser, green_greater, lattice_map, time_offset)

    return call
```

```python
import functools
import math

import jax
import jax.numpy as jnp
from jax import lax
from jax.experimental import pallas as pl
from jax.experimental.pallas import tpu as pltpu
from jax.sharding import Mesh, PartitionSpec as P

F32 = jnp.float32
BF16 = jnp.bfloat16
LANES = 128

PERIOD = 64


step_size = 0.01
drive_depth = 0.5


def regroup(blocks):
    return lax.all_to_all(
        lax.all_to_all(blocks, "trow", split_axis=1, concat_axis=1, tiled=True),
        "tcol",
        split_axis=2,
        concat_axis=2,
        tiled=True,
    )


def pack_blocks(spectral, row_parts, col_parts):
    stacked, extent, tile_cells = spectral.shape
    return spectral.reshape(
        stacked, row_parts, col_parts, extent // (row_parts * col_parts), tile_cells
    )


def spread_times(blocks, tile_rows, tile_cols):
    stacked, row_parts, col_parts, local_count, tile_cells = blocks.shape
    shaped = blocks.reshape(stacked, row_parts, col_parts, local_count, tile_rows, tile_cols)
    return shaped.transpose(0, 3, 1, 4, 2, 5).reshape(
        stacked, local_count, row_parts * tile_rows, col_parts * tile_cols
    )


def gather_tiles(full, row_parts, col_parts):
    stacked, local_count, window, window_cols = full.shape
    tile_rows = window // row_parts
    tile_cols = window_cols // col_parts
    shaped = full.reshape(stacked, local_count, row_parts, tile_rows, col_parts, tile_cols)
    return shaped.transpose(0, 2, 4, 1, 3, 5).reshape(
        stacked, row_parts, col_parts, local_count, tile_rows * tile_cols
    )


def mirrored(full, keep_pair):
    stacked, local_count, window, window_cols = full.shape
    paired = full.reshape(stacked, local_count // 2, 2, window, window_cols)
    swapped = jnp.where(keep_pair[None, :, None, None, None], paired, paired[:, :, ::-1])
    return jnp.swapaxes(swapped.reshape(stacked, local_count, window, window_cols), 2, 3)


def second_born(first_real, first_imaginary, other_real, other_imaginary, coupling):
    square_real = first_real * first_real - first_imaginary * first_imaginary
    square_imaginary = 2.0 * first_real * first_imaginary
    out_real = coupling * (square_real * other_real - square_imaginary * other_imaginary)
    out_imaginary = coupling * (square_real * other_imaginary + square_imaginary * other_real)
    return (out_real, out_imaginary)


def collide(
    retarded_real,
    retarded_imaginary,
    self_real,
    self_imaginary,
    green_real,
    green_imaginary,
    advanced_real,
    advanced_imaginary,
):
    minus_left = jnp.concatenate(
        [retarded_real, -retarded_imaginary, self_real, -self_imaginary], axis=2
    )
    plus_left = jnp.concatenate(
        [retarded_real, retarded_imaginary, self_real, self_imaginary], axis=2
    )
    real_right = jnp.concatenate(
        [green_real, green_imaginary, advanced_real, advanced_imaginary], axis=1
    )
    imaginary_right = jnp.concatenate(
        [green_imaginary, green_real, advanced_imaginary, advanced_real], axis=1
    )
    out_real = jnp.einsum(
        "kts,ksu->ktu", minus_left, real_right, preferred_element_type=jnp.float32
    )
    out_imaginary = jnp.einsum(
        "kts,ksu->ktu", plus_left, imaginary_right, preferred_element_type=jnp.float32
    )
    return (out_real, out_imaginary)


def general_body(green_lesser, green_greater, lattice_map, time_offset):
    tile_rows = green_lesser.shape[1]
    tile_cols = green_lesser.shape[2]
    momenta = green_lesser.shape[3]
    row_parts = lax.axis_size("trow")
    col_parts = lax.axis_size("tcol")
    window = tile_rows * row_parts
    tile_cells = tile_rows * tile_cols
    local_count = momenta // (row_parts * col_parts)
    norm_factor = 1.0 / math.sqrt(momenta)
    greens = (
        jnp.concatenate([green_lesser, green_greater], axis=0)
        .reshape(4, tile_cells, momenta)
        .transpose(0, 2, 1)
    )
    positions = jnp.arange(momenta, dtype=jnp.int32)
    halves = positions // 2
    site_order = jnp.where(
        positions == 1, momenta // 2, jnp.where(positions % 2 == 0, halves, momenta - halves)
    )
    phases = (lattice_map[:, None] * site_order[None, :] % momenta).astype(jnp.float32) * (
        2.0 * math.pi / momenta
    )
    cosines = jnp.cos(phases).astype(jnp.bfloat16)
    sines = jnp.sin(phases).astype(jnp.bfloat16)
    ahead_blocks = lax.all_to_all(
        lax.all_to_all(
            pack_blocks(greens, row_parts, col_parts),
            "trow",
            split_axis=1,
            concat_axis=1,
            tiled=True,
        ),
        "tcol",
        split_axis=2,
        concat_axis=2,
        tiled=True,
    )
    green_moment = spread_times(ahead_blocks, tile_rows, tile_cols)
    forward_table = jnp.concatenate([cosines, sines], axis=1)
    products = jnp.einsum("cjm,jr->crm", greens, forward_table, preferred_element_type=jnp.float32)
    site_space = jnp.stack(
        [
            (products[0, :momenta] - products[1, momenta:]) * norm_factor,
            (products[0, momenta:] + products[1, :momenta]) * norm_factor,
            (products[2, :momenta] - products[3, momenta:]) * norm_factor,
            (products[2, momenta:] + products[3, :momenta]) * norm_factor,
        ]
    ).astype(jnp.bfloat16)
    site_full = spread_times(
        regroup(pack_blocks(site_space, row_parts, col_parts)), tile_rows, tile_cols
    )
    site_block = lax.axis_index("trow") * col_parts + lax.axis_index("tcol")
    keep_pair = site_block * (local_count // 2) + jnp.arange(local_count // 2, dtype=jnp.int32) == 0
    mirror = mirrored(site_full, keep_pair).astype(jnp.float32)
    direct = site_full.astype(jnp.float32)
    time_steps = jnp.arange(window, dtype=jnp.int32)
    coupling_line = 1.0 + drive_depth * jnp.cos(
        ((time_offset[0] + time_steps) % PERIOD).astype(jnp.float32) * (2.0 * math.pi / PERIOD)
    )
    coupling = coupling_line[:, None] * coupling_line[None, :]
    self_lesser = second_born(direct[0], direct[1], mirror[2], mirror[3], coupling)
    self_greater = second_born(direct[2], direct[3], mirror[0], mirror[1], coupling)
    self_sites = jnp.stack(
        [self_lesser[0], self_lesser[1], self_greater[0], self_greater[1]]
    ).astype(jnp.bfloat16)
    self_tiles = regroup(gather_tiles(self_sites, row_parts, col_parts)).reshape(
        4, momenta, tile_cells
    )
    inverse_table = jnp.concatenate([cosines, sines], axis=0)
    spectral_terms = jnp.einsum(
        "cum,ju->cjm", self_tiles, inverse_table, preferred_element_type=jnp.float32
    )
    self_spectral = jnp.stack(
        [
            (spectral_terms[0, :momenta] + spectral_terms[1, momenta:]) * norm_factor,
            (spectral_terms[1, :momenta] - spectral_terms[0, momenta:]) * norm_factor,
            (spectral_terms[2, :momenta] + spectral_terms[3, momenta:]) * norm_factor,
            (spectral_terms[3, :momenta] - spectral_terms[2, momenta:]) * norm_factor,
        ]
    ).astype(jnp.bfloat16)
    self_moment = spread_times(
        regroup(pack_blocks(self_spectral, row_parts, col_parts)), tile_rows, tile_cols
    )
    lower_mask = time_steps[None, :] <= time_steps[:, None]
    upper_mask = time_steps[:, None] <= time_steps[None, :]
    retarded = jnp.where(
        lower_mask, self_moment[2:4].astype(jnp.float32) - self_moment[0:2].astype(jnp.float32), 0.0
    ).astype(jnp.bfloat16)
    advanced = jnp.where(
        upper_mask,
        green_moment[0:2].astype(jnp.float32) - green_moment[2:4].astype(jnp.float32),
        0.0,
    ).astype(jnp.bfloat16)
    lesser_out = collide(
        retarded[0],
        retarded[1],
        self_moment[0],
        self_moment[1],
        green_moment[0],
        green_moment[1],
        advanced[0],
        advanced[1],
    )
    greater_out = collide(
        retarded[0],
        retarded[1],
        self_moment[2],
        self_moment[3],
        green_moment[2],
        green_moment[3],
        advanced[0],
        advanced[1],
    )
    collisions = (
        jnp.stack([lesser_out[0], lesser_out[1], greater_out[0], greater_out[1]]) * step_size
    ).astype(jnp.bfloat16)
    out_tiles = regroup(gather_tiles(collisions, row_parts, col_parts)).reshape(
        4, momenta, tile_cells
    )
    out_tiles = out_tiles.transpose(0, 2, 1).reshape(4, tile_rows, tile_cols, momenta)
    return (out_tiles[0:2], out_tiles[2:4])


def vmem_params():
    return pltpu.CompilerParams(vmem_limit_bytes=48 * 1024 * 1024)


def unread(arrays):
    return [pl.BlockSpec(memory_space=pl.ANY)] * len(arrays)


def whole(count):
    return [pl.BlockSpec(memory_space=pltpu.VMEM)] * count


def weight():
    return pl.CostEstimate(flops=10**11, bytes_accessed=2**20, transcendentals=0)


def scalars():
    return [pl.BlockSpec(memory_space=pltpu.SMEM)]


def spread_kernel(first, lesser, greater, *rest):
    out, lines = rest[-2:]
    _, rows, _, _ = lesser.shape
    count = lines.shape[0] // (2 * rows)
    for g, tile in enumerate((lesser, greater)):
        for t in range(rows):
            span = slice(first, first + count)
            slab = jnp.concatenate([tile[0, t, :, span], tile[1, t, :, span]], axis=0)
            lines[pl.ds(g * rows + t, count, stride=2 * rows), :] = slab.astype(F32).T
    out[...] = lines[...].astype(BF16)


def spread(tiles, first, count, after):
    _, rows, cols, _ = tiles[0].shape
    shape = (count * 2 * rows, 2 * cols)
    return pl.pallas_call(
        functools.partial(spread_kernel, first),
        out_shape=jax.ShapeDtypeStruct(shape, BF16),
        in_specs=whole(2) + unread(after),
        out_specs=whole(1)[0],
        scratch_shapes=[pltpu.VMEM(shape, F32)],
        compiler_params=vmem_params(),
        name="spread",
    )(*tiles, *after)


def collect_kernel(parts, blocks_ref, lesser, greater, lines):
    _, rows, cols, momenta = lesser.shape
    blocks, height, _ = blocks_ref.shape
    height = height // parts
    for part in range(parts):
        for block in range(blocks):
            lines[block * height : (block + 1) * height] = blocks_ref[
                block, part * height : (part + 1) * height
            ].astype(F32)
        count = momenta // parts
        span = slice(part * count, (part + 1) * count)
        for k in range(2 * rows):
            slab = lines[pl.ds(k, count, stride=2 * rows), :].T.astype(BF16)
            out = lesser if k < rows else greater
            out[0, k % rows, :, span] = slab[:cols]
            out[1, k % rows, :, span] = slab[cols:]


def collect(blocks, tile_shape):
    shape = jax.ShapeDtypeStruct(tile_shape, BF16)
    lines = blocks.shape[0] * blocks.shape[1] // PARTS
    return pl.pallas_call(
        functools.partial(collect_kernel, PARTS),
        out_shape=(shape, shape),
        in_specs=whole(1),
        out_specs=tuple(whole(2)),
        scratch_shapes=[pltpu.VMEM((lines, blocks.shape[2]), F32)],
        compiler_params=vmem_params(),
        name="collect",
    )(blocks)


def table_kernel(column_ref, table, inverse):
    momenta = column_ref.shape[0]
    positions = lax.broadcasted_iota(jnp.int32, (momenta, momenta), 1)
    phases = (column_ref[...] * positions % momenta).astype(F32) * (2.0 * math.pi / momenta)
    cosines = jnp.cos(phases).astype(BF16)
    sines = jnp.sin(phases).astype(BF16)
    inverse[:momenta, :momenta] = cosines
    inverse[:momenta, momenta:] = sines
    inverse[momenta:, :momenta] = -sines
    inverse[momenta:, momenta:] = cosines
    cosines = cosines.astype(F32).T.astype(BF16)
    sines = sines.astype(F32).T.astype(BF16)
    table[:momenta, :momenta] = cosines
    table[:momenta, momenta:] = -sines
    table[momenta:, :momenta] = sines
    table[momenta:, momenta:] = cosines


def make_tables(lattice_map):
    momenta = lattice_map.shape[0]
    shape = jax.ShapeDtypeStruct((2 * momenta, 2 * momenta), BF16)
    return pl.pallas_call(
        table_kernel,
        out_shape=(shape, shape),
        in_specs=whole(1),
        out_specs=tuple(whole(2)),
        compiler_params=vmem_params(),
        name="make_tables",
    )(lattice_map[:, None])


def site_kernel(norm_factor, lesser, greater, table, out):
    _, rows, cols, _ = lesser.shape
    wide = 4 * cols
    for pair in range(rows // 2):
        slabs = [
            jnp.concatenate([tile[0, t], tile[1, t]], axis=1)
            for t in (2 * pair, 2 * pair + 1)
            for tile in (lesser, greater)
        ]
        product = lax.dot_general(
            table[...],
            jnp.concatenate(slabs, axis=0),
            (((1,), (1,)), ((), ())),
            preferred_element_type=F32,
        )
        out[:, pair * wide : (pair + 1) * wide] = (product * norm_factor).astype(BF16)


def to_sites(tiles, table, norm_factor):
    _, rows, cols, momenta = tiles[0].shape
    return pl.pallas_call(
        functools.partial(site_kernel, norm_factor),
        out_shape=jax.ShapeDtypeStruct((2 * momenta, rows * 2 * cols), BF16),
        in_specs=whole(3),
        out_specs=whole(1)[0],
        compiler_params=vmem_params(),
        name="to_sites",
    )(*tiles, table)


def cross_kernel(rows, half_ref, own, far, *rest):
    out = rest[-1]
    half = half_ref[0]
    blocks = far.shape[0]
    cols = blocks * rows
    for at in range(far.shape[1] // (2 * rows)):
        span = slice(at * 2 * rows, (at + 1) * 2 * rows)
        for source, offset, target in ((own, half * blocks, half), (far, 0, 1 - half)):
            loaded = [source[offset + block, span].astype(F32) for block in range(blocks)]
            stacked = jnp.concatenate(
                [lines[rows:] for lines in loaded] + [lines[:rows] for lines in loaded], axis=0
            )
            turned = stacked.T
            for block in range(blocks):
                out[target * blocks + block, span] = jnp.concatenate(
                    [
                        turned[block * rows : (block + 1) * rows],
                        turned[cols + block * rows : cols + (block + 1) * rows],
                    ],
                    axis=0,
                ).astype(BF16)


def to_crossed(half, own, far, rows, after, cost):
    return pl.pallas_call(
        functools.partial(cross_kernel, rows),
        out_shape=jax.ShapeDtypeStruct(own.shape, BF16),
        in_specs=[pl.BlockSpec(memory_space=pltpu.SMEM)] + whole(2) + unread(after),
        out_specs=whole(1)[0],
        compiler_params=vmem_params(),
        cost_estimate=cost,
        name="to_crossed",
    )(half, own, far, *after)


def gate_kernel(*refs):
    del refs


def gate(array, after):
    return pl.pallas_call(
        gate_kernel,
        out_shape=jax.ShapeDtypeStruct(array.shape, array.dtype),
        in_specs=unread([array, *after]),
        out_specs=unread([array])[0],
        input_output_aliases={0: 0},
        name="gate",
    )(array, *after)


def mirrored_term(table, part, parts, read, pair, count):
    momenta = table.shape[1] // 2
    wide = momenta // parts
    rights = []
    for t in (2 * pair, 2 * pair + 1):
        real = read[pl.ds(t, wide, stride=2 * count), :]
        imaginary = -read[pl.ds(count + t, wide, stride=2 * count), :]
        rights.append(jnp.concatenate([real, imaginary], axis=0).astype(BF16))
    columns = jnp.concatenate(
        [
            table[:, part * wide : (part + 1) * wide],
            table[:, momenta + part * wide : momenta + (part + 1) * wide],
        ],
        axis=1,
    )
    return jnp.dot(columns, jnp.concatenate(rights, axis=1), preferred_element_type=F32)


def mirror_kernel(part, parts, count, crossed, table, out, read):
    read[...] = crossed[...].astype(F32)
    wide = 2 * crossed.shape[1]
    for pair in range(count // 2):
        out[:, pair * wide : (pair + 1) * wide] = mirrored_term(
            table, part, parts, read, pair, count
        )


def to_mirror(crossed, table, part, parts, count):
    lines, lanes = crossed.shape
    return pl.pallas_call(
        functools.partial(mirror_kernel, part, parts, count),
        out_shape=jax.ShapeDtypeStruct((table.shape[0], count * lanes), F32),
        in_specs=whole(2),
        out_specs=whole(1)[0],
        scratch_shapes=[pltpu.VMEM((lines, lanes), F32)],
        compiler_params=vmem_params(),
        name="to_mirror",
    )(crossed, table)


def sigma_kernel(norm_factor, parts, *refs):
    mirrors = refs[: parts - 1]
    crossed, sites, table, inverse, coupling, out, read, written = refs[parts - 1 :]
    count = coupling.shape[0]
    momenta = table.shape[0] // 2
    read[...] = crossed[...].astype(F32)
    for pair in range(count // 2):
        span = slice(2 * pair * LANES, 2 * (pair + 1) * LANES)
        other = mirrored_term(table, parts - 1, parts, read, pair, count)
        for mirror in mirrors:
            other = other + mirror[:, span]
        other = (other * norm_factor).astype(BF16).astype(F32)
        self_real, self_imaginary = second_born(
            sites[:momenta, span].astype(F32),
            sites[momenta:, span].astype(F32),
            other[:momenta],
            -other[momenta:],
            jnp.concatenate([coupling[t : t + 1] for t in (2 * pair, 2 * pair + 1)], axis=1),
        )
        product = jnp.dot(
            inverse[...],
            jnp.concatenate([self_real, self_imaginary], axis=0).astype(BF16),
            preferred_element_type=F32,
        )
        product = product * norm_factor
        for at in range(2):
            for part in range(2):
                written[pl.ds(part * count + 2 * pair + at, momenta, stride=2 * count), :] = product[
                    part * momenta : (part + 1) * momenta, at * LANES : (at + 1) * LANES
                ]
    blocks, height, _ = out.shape
    height = height // parts
    for part in range(parts):
        for block in range(blocks):
            start = (part * blocks + block) * height
            out[block, part * height : (part + 1) * height] = written[
                start : start + height
            ].astype(BF16)


def to_sigma(mirrors, crossed, sites, table, inverse, coupling, norm_factor, blocks):
    parts = len(mirrors) + 1
    lines, lanes = crossed.shape
    return pl.pallas_call(
        functools.partial(sigma_kernel, norm_factor, parts),
        out_shape=jax.ShapeDtypeStruct((blocks, parts * lines // blocks, lanes), BF16),
        in_specs=whole(parts + 4),
        out_specs=whole(1)[0],
        scratch_shapes=[pltpu.VMEM((lines, lanes), F32), pltpu.VMEM((parts * lines, lanes), F32)],
        compiler_params=vmem_params(),
        name="to_sigma",
    )(*mirrors, crossed, sites, table, inverse, coupling)


def rights_kernel(rows, half_ref, own, near_ref, away_ref, *rest):
    out = rest[-1]
    half = half_ref[0]
    blocks = near_ref.shape[0]
    lanes = own.shape[2]
    cols = lanes // 2
    near = half * cols
    away = (1 - half) * cols
    row_at = lax.broadcasted_iota(jnp.int32, (lanes, 2 * lanes), 0)
    inner_times = jnp.where(row_at < cols, near + row_at, away + row_at - cols)
    lane_at = lax.broadcasted_iota(jnp.int32, (lanes, 2 * lanes), 1)
    last_times = jnp.where(lane_at < lanes, near, away) + lane_at % cols
    keep = inner_times <= last_times
    for at in range(out.shape[0]):
        span = slice(at * 2 * rows, (at + 1) * 2 * rows)

        def stacked(read):
            loaded = [read(block).astype(F32) for block in range(blocks)]
            return [
                jnp.concatenate([lines[g * rows : (g + 1) * rows] for lines in loaded], axis=0)
                for g in range(2)
            ]

        own_near = stacked(lambda block: own[half * blocks + block, span])
        own_away = stacked(lambda block: own[(1 - half) * blocks + block, span])
        far_near = stacked(lambda block: near_ref[block, span])
        far_away = stacked(lambda block: away_ref[0, block, span])
        greens = [
            jnp.concatenate(
                [
                    jnp.concatenate([own_near[g], own_away[g]], axis=1),
                    jnp.concatenate([far_near[g], far_away[g]], axis=1),
                ],
                axis=0,
            )
            for g in range(2)
        ]
        out[at, :lanes] = greens[0].astype(BF16)
        out[at, lanes : 2 * lanes] = greens[1].astype(BF16)
        out[at, 2 * lanes :] = jnp.where(keep, greens[0] - greens[1], 0.0).astype(BF16)


STEPS = 4
PARTS = 2


def make_rights(half, own, far_near, far_away, rows, part, before):
    sources, lines, lanes = own.shape
    blocks = far_near.shape[0]
    steps = STEPS // PARTS
    step = lines // steps
    momenta = step // (2 * rows)
    return pl.pallas_call(
        functools.partial(rights_kernel, rows),
        grid=(steps,),
        out_shape=jax.ShapeDtypeStruct((STEPS * momenta, 3 * lanes, 2 * lanes), BF16),
        in_specs=scalars()
        + [
            pl.BlockSpec((sources, step, lanes), lambda p: (0, p, 0)),
            pl.BlockSpec((blocks, step, lanes), lambda p: (0, p, 0)),
            pl.BlockSpec((1, blocks, step, lanes), lambda p: (part, 0, p, 0)),
        ]
        + unread(before),
        out_specs=pl.BlockSpec(
            (momenta, 3 * lanes, 2 * lanes), lambda p: (part * steps + p, 0, 0)
        ),
        input_output_aliases={4: 0} if part > 0 else {},
        compiler_params=vmem_params(),
        cost_estimate=weight(),
        name="make_rights",
    )(half, own, far_near, far_away, *before)


def volterra_kernel(rows, half_ref, sigma, rights, out):
    half = half_ref[0]
    blocks = sigma.shape[0] // 2
    lanes = sigma.shape[2]
    cols = lanes // 2
    near = half * cols
    away = (1 - half) * cols
    here = half * blocks
    there = (1 - half) * blocks
    first_times = near + lax.broadcasted_iota(jnp.int32, (cols, lanes), 0)
    left_lane = lax.broadcasted_iota(jnp.int32, (cols, lanes), 1)
    low_lanes = left_lane < cols
    left_times = jnp.where(low_lanes, near + left_lane, away + left_lane - cols)
    keep_left = left_times <= first_times
    for at in range(rights.shape[0]):
        span = slice(at * 2 * rows, (at + 1) * 2 * rows)

        def stacked(offset):
            loaded = [sigma[offset + block, span].astype(F32) for block in range(blocks)]
            return [
                jnp.concatenate([lines[part * rows : (part + 1) * rows] for lines in loaded], axis=0)
                for part in range(2)
            ]

        sigma_near = stacked(here)
        sigma_away = stacked(there)
        retarded = []
        lefts = [[], []]
        for part in range(2):
            lesser = jnp.where(
                low_lanes, sigma_near[part], pltpu.roll(sigma_away[part], cols, 1)
            )
            greater = jnp.where(
                low_lanes, pltpu.roll(sigma_near[part], cols, 1), sigma_away[part]
            )
            retarded.append(jnp.where(keep_left, greater - lesser, 0.0))
            lefts[0].append(lesser)
            lefts[1].append(greater)
        retarded = jnp.concatenate(retarded, axis=0).astype(BF16)
        results = []
        for g in range(2):
            left = jnp.concatenate(
                [retarded, jnp.concatenate(lefts[g], axis=0).astype(BF16)], axis=1
            )
            right = jnp.concatenate(
                [rights[at, g * lanes : (g + 1) * lanes], rights[at, 2 * lanes :]], axis=0
            )
            product = jnp.dot(left, right, preferred_element_type=F32)
            sides = []
            for side in range(2):
                straight = product[:cols, side * lanes : (side + 1) * lanes]
                turned = pltpu.roll(product[cols:, side * lanes : (side + 1) * lanes], cols, 1)
                sides.append((straight + jnp.where(low_lanes, -turned, turned)) * step_size)
            results.append(sides)
        for block in range(blocks):
            lines = slice(block * rows, (block + 1) * rows)
            for side, offset in enumerate((here, there)):
                out[offset + block, span] = jnp.concatenate(
                    [results[0][side][lines], results[1][side][lines]], axis=0
                ).astype(BF16)


def volterra(half, sigma, rights, rows):
    sources, lines, lanes = sigma.shape
    step = lines // STEPS
    momenta = step // (2 * rows)
    spec = pl.BlockSpec((sources, step, lanes), lambda p: (0, p, 0))
    return pl.pallas_call(
        functools.partial(volterra_kernel, rows),
        grid=(STEPS,),
        out_shape=jax.ShapeDtypeStruct(sigma.shape, BF16),
        in_specs=scalars()
        + [spec, pl.BlockSpec((momenta, 3 * lanes, 2 * lanes), lambda p: (p, 0, 0))],
        out_specs=spec,
        compiler_params=vmem_params(),
        name="volterra",
    )(half, sigma, rights)


def halved_body(green_lesser, green_greater, lattice_map, time_offset):
    _, rows, cols, momenta = green_lesser.shape
    half = lax.axis_index("half")
    line = lax.axis_index("line")
    side = lax.axis_index("tcol")
    lines = lax.axis_size("line")
    group = lines * lax.axis_size("tcol")
    window = rows * lines * lax.axis_size("half")
    norm_factor = 1.0 / math.sqrt(momenta)
    tiles = (green_lesser, green_greater)
    half_at = half[None]
    count = momenta // PARTS

    def exchange(blocks):
        return lax.all_to_all(blocks, ("tcol", "line"), 0, 0, tiled=True)

    def blocked(rows_array):
        return rows_array.reshape(group, rows_array.shape[0] // group, rows_array.shape[1])

    def swap(array):
        return lax.ppermute(array, "half", [(0, 1), (1, 0)])

    table, inverse = make_tables(lattice_map)
    sites = to_sites(tiles, table, norm_factor)
    time_steps = jnp.arange(window, dtype=jnp.int32)
    coupling_line = 1.0 + drive_depth * jnp.cos(
        ((time_offset[0] + time_steps) % PERIOD).astype(F32) * (2.0 * math.pi / PERIOD)
    )
    first = lax.dynamic_slice_in_dim(coupling_line, (half * lines + line) * rows, rows)
    second = lax.dynamic_slice_in_dim(coupling_line, side * cols, cols)
    coupling = first[:, None] * jnp.concatenate([second, second])[None, :]

    spread_parts = [spread(tiles, part * count, count, []) for part in range(PARTS)]
    own = [exchange(blocked(spread_parts[0]))]
    for rows_array in spread_parts[1:]:
        own.append(exchange(gate(blocked(rows_array), [own[-1], sites, coupling])))
    far_near = [swap(lax.dynamic_slice_in_dim(blocks, (1 - half) * lines, lines)) for blocks in own]

    sent = []
    for part in range(PARTS):
        sent.append(
            to_crossed(
                half_at,
                own[part],
                far_near[part],
                rows,
                own[-1:] + sent[-1:],
                weight() if part > 0 else None,
            )
        )
    crossed = [exchange(blocks) for blocks in sent]
    kept = jnp.stack(
        [lax.dynamic_slice_in_dim(blocks, half * lines, lines) for blocks in own]
    )
    far_away = swap(gate(kept, sent[-1:] + crossed[:-1]))
    flat = [blocks.reshape(-1, 2 * cols) for blocks in crossed]
    mirrors = [to_mirror(flat[part], table, part, PARTS, rows) for part in range(PARTS - 1)]
    sigma_rows = to_sigma(
        mirrors, flat[-1], sites, table, inverse, coupling, norm_factor, group
    )
    sigma = exchange(sigma_rows)
    rights = []
    for part in range(PARTS):
        rights = [
            make_rights(
                half_at, own[part], far_near[part], far_away, rows, part, rights + [sigma_rows]
            )
        ]
    returned = exchange(volterra(half_at, sigma, rights[0], rows))
    return collect(returned, green_lesser.shape)


def solution(mesh):
    row_parts = mesh.shape["trow"]
    col_parts = mesh.shape["tcol"]

    def call(green_lesser, green_greater, lattice_map, time_offset):
        window, window_cols, momenta = green_lesser.shape[1:]
        rows = window // row_parts
        cols = window_cols // col_parts
        halved = (
            col_parts == 2
            and row_parts % 2 == 0
            and window == window_cols
            and 2 * cols == LANES
            and cols == rows * (row_parts // 2)
            and rows % 8 == 0
            and momenta % (2 * row_parts * STEPS) == 0
            and momenta % (PARTS * LANES) == 0
        )
        if halved:
            devices = mesh.devices.reshape(2, row_parts // 2, col_parts)
            used = Mesh(devices, ("half", "line", "tcol"))
            spec = P(None, ("half", "line"), "tcol", None)
            inner = halved_body
        else:
            used = mesh
            spec = P(None, "trow", "tcol", None)
            inner = general_body
        return jax.shard_map(
            inner, mesh=used, in_specs=(spec, spec, P(), P()), out_specs=(spec, spec), check_vma=False
        )(green_lesser, green_greater, lattice_map, time_offset)

    return call
```

```python
import functools
import math

import jax
import jax.numpy as jnp
from jax import lax
from jax.experimental import pallas as pl
from jax.experimental.pallas import tpu as pltpu
from jax.sharding import Mesh, PartitionSpec as P

F32 = jnp.float32
BF16 = jnp.bfloat16
LANES = 128

PERIOD = 64


step_size = 0.01
drive_depth = 0.5


def regroup(blocks):
    return lax.all_to_all(
        lax.all_to_all(blocks, "trow", split_axis=1, concat_axis=1, tiled=True),
        "tcol",
        split_axis=2,
        concat_axis=2,
        tiled=True,
    )


def pack_blocks(spectral, row_parts, col_parts):
    stacked, extent, tile_cells = spectral.shape
    return spectral.reshape(
        stacked, row_parts, col_parts, extent // (row_parts * col_parts), tile_cells
    )


def spread_times(blocks, tile_rows, tile_cols):
    stacked, row_parts, col_parts, local_count, tile_cells = blocks.shape
    shaped = blocks.reshape(stacked, row_parts, col_parts, local_count, tile_rows, tile_cols)
    return shaped.transpose(0, 3, 1, 4, 2, 5).reshape(
        stacked, local_count, row_parts * tile_rows, col_parts * tile_cols
    )


def gather_tiles(full, row_parts, col_parts):
    stacked, local_count, window, window_cols = full.shape
    tile_rows = window // row_parts
    tile_cols = window_cols // col_parts
    shaped = full.reshape(stacked, local_count, row_parts, tile_rows, col_parts, tile_cols)
    return shaped.transpose(0, 2, 4, 1, 3, 5).reshape(
        stacked, row_parts, col_parts, local_count, tile_rows * tile_cols
    )


def mirrored(full, keep_pair):
    stacked, local_count, window, window_cols = full.shape
    paired = full.reshape(stacked, local_count // 2, 2, window, window_cols)
    swapped = jnp.where(keep_pair[None, :, None, None, None], paired, paired[:, :, ::-1])
    return jnp.swapaxes(swapped.reshape(stacked, local_count, window, window_cols), 2, 3)


def second_born(first_real, first_imaginary, other_real, other_imaginary, coupling):
    square_real = first_real * first_real - first_imaginary * first_imaginary
    square_imaginary = 2.0 * first_real * first_imaginary
    out_real = coupling * (square_real * other_real - square_imaginary * other_imaginary)
    out_imaginary = coupling * (square_real * other_imaginary + square_imaginary * other_real)
    return (out_real, out_imaginary)


def collide(
    retarded_real,
    retarded_imaginary,
    self_real,
    self_imaginary,
    green_real,
    green_imaginary,
    advanced_real,
    advanced_imaginary,
):
    minus_left = jnp.concatenate(
        [retarded_real, -retarded_imaginary, self_real, -self_imaginary], axis=2
    )
    plus_left = jnp.concatenate(
        [retarded_real, retarded_imaginary, self_real, self_imaginary], axis=2
    )
    real_right = jnp.concatenate(
        [green_real, green_imaginary, advanced_real, advanced_imaginary], axis=1
    )
    imaginary_right = jnp.concatenate(
        [green_imaginary, green_real, advanced_imaginary, advanced_real], axis=1
    )
    out_real = jnp.einsum(
        "kts,ksu->ktu", minus_left, real_right, preferred_element_type=jnp.float32
    )
    out_imaginary = jnp.einsum(
        "kts,ksu->ktu", plus_left, imaginary_right, preferred_element_type=jnp.float32
    )
    return (out_real, out_imaginary)


def general_body(green_lesser, green_greater, lattice_map, time_offset):
    tile_rows = green_lesser.shape[1]
    tile_cols = green_lesser.shape[2]
    momenta = green_lesser.shape[3]
    row_parts = lax.axis_size("trow")
    col_parts = lax.axis_size("tcol")
    window = tile_rows * row_parts
    tile_cells = tile_rows * tile_cols
    local_count = momenta // (row_parts * col_parts)
    norm_factor = 1.0 / math.sqrt(momenta)
    greens = (
        jnp.concatenate([green_lesser, green_greater], axis=0)
        .reshape(4, tile_cells, momenta)
        .transpose(0, 2, 1)
    )
    positions = jnp.arange(momenta, dtype=jnp.int32)
    halves = positions // 2
    site_order = jnp.where(
        positions == 1, momenta // 2, jnp.where(positions % 2 == 0, halves, momenta - halves)
    )
    phases = (lattice_map[:, None] * site_order[None, :] % momenta).astype(jnp.float32) * (
        2.0 * math.pi / momenta
    )
    cosines = jnp.cos(phases).astype(jnp.bfloat16)
    sines = jnp.sin(phases).astype(jnp.bfloat16)
    ahead_blocks = lax.all_to_all(
        lax.all_to_all(
            pack_blocks(greens, row_parts, col_parts),
            "trow",
            split_axis=1,
            concat_axis=1,
            tiled=True,
        ),
        "tcol",
        split_axis=2,
        concat_axis=2,
        tiled=True,
    )
    green_moment = spread_times(ahead_blocks, tile_rows, tile_cols)
    forward_table = jnp.concatenate([cosines, sines], axis=1)
    products = jnp.einsum("cjm,jr->crm", greens, forward_table, preferred_element_type=jnp.float32)
    site_space = jnp.stack(
        [
            (products[0, :momenta] - products[1, momenta:]) * norm_factor,
            (products[0, momenta:] + products[1, :momenta]) * norm_factor,
            (products[2, :momenta] - products[3, momenta:]) * norm_factor,
            (products[2, momenta:] + products[3, :momenta]) * norm_factor,
        ]
    ).astype(jnp.bfloat16)
    site_full = spread_times(
        regroup(pack_blocks(site_space, row_parts, col_parts)), tile_rows, tile_cols
    )
    site_block = lax.axis_index("trow") * col_parts + lax.axis_index("tcol")
    keep_pair = site_block * (local_count // 2) + jnp.arange(local_count // 2, dtype=jnp.int32) == 0
    mirror = mirrored(site_full, keep_pair).astype(jnp.float32)
    direct = site_full.astype(jnp.float32)
    time_steps = jnp.arange(window, dtype=jnp.int32)
    coupling_line = 1.0 + drive_depth * jnp.cos(
        ((time_offset[0] + time_steps) % PERIOD).astype(jnp.float32) * (2.0 * math.pi / PERIOD)
    )
    coupling = coupling_line[:, None] * coupling_line[None, :]
    self_lesser = second_born(direct[0], direct[1], mirror[2], mirror[3], coupling)
    self_greater = second_born(direct[2], direct[3], mirror[0], mirror[1], coupling)
    self_sites = jnp.stack(
        [self_lesser[0], self_lesser[1], self_greater[0], self_greater[1]]
    ).astype(jnp.bfloat16)
    self_tiles = regroup(gather_tiles(self_sites, row_parts, col_parts)).reshape(
        4, momenta, tile_cells
    )
    inverse_table = jnp.concatenate([cosines, sines], axis=0)
    spectral_terms = jnp.einsum(
        "cum,ju->cjm", self_tiles, inverse_table, preferred_element_type=jnp.float32
    )
    self_spectral = jnp.stack(
        [
            (spectral_terms[0, :momenta] + spectral_terms[1, momenta:]) * norm_factor,
            (spectral_terms[1, :momenta] - spectral_terms[0, momenta:]) * norm_factor,
            (spectral_terms[2, :momenta] + spectral_terms[3, momenta:]) * norm_factor,
            (spectral_terms[3, :momenta] - spectral_terms[2, momenta:]) * norm_factor,
        ]
    ).astype(jnp.bfloat16)
    self_moment = spread_times(
        regroup(pack_blocks(self_spectral, row_parts, col_parts)), tile_rows, tile_cols
    )
    lower_mask = time_steps[None, :] <= time_steps[:, None]
    upper_mask = time_steps[:, None] <= time_steps[None, :]
    retarded = jnp.where(
        lower_mask, self_moment[2:4].astype(jnp.float32) - self_moment[0:2].astype(jnp.float32), 0.0
    ).astype(jnp.bfloat16)
    advanced = jnp.where(
        upper_mask,
        green_moment[0:2].astype(jnp.float32) - green_moment[2:4].astype(jnp.float32),
        0.0,
    ).astype(jnp.bfloat16)
    lesser_out = collide(
        retarded[0],
        retarded[1],
        self_moment[0],
        self_moment[1],
        green_moment[0],
        green_moment[1],
        advanced[0],
        advanced[1],
    )
    greater_out = collide(
        retarded[0],
        retarded[1],
        self_moment[2],
        self_moment[3],
        green_moment[2],
        green_moment[3],
        advanced[0],
        advanced[1],
    )
    collisions = (
        jnp.stack([lesser_out[0], lesser_out[1], greater_out[0], greater_out[1]]) * step_size
    ).astype(jnp.bfloat16)
    out_tiles = regroup(gather_tiles(collisions, row_parts, col_parts)).reshape(
        4, momenta, tile_cells
    )
    out_tiles = out_tiles.transpose(0, 2, 1).reshape(4, tile_rows, tile_cols, momenta)
    return (out_tiles[0:2], out_tiles[2:4])


def vmem_params(mebibytes):
    return pltpu.CompilerParams(vmem_limit_bytes=mebibytes * 1024 * 1024)


def unread(arrays):
    return [pl.BlockSpec(memory_space=pl.ANY)] * len(arrays)


def token(array):
    return lax.slice(array, (0,) * array.ndim, (1,) * (array.ndim - 2) + (16, LANES))


def whole(count):
    return [pl.BlockSpec(memory_space=pltpu.VMEM)] * count


def weight():
    return pl.CostEstimate(flops=10**11, bytes_accessed=2**20, transcendentals=0)


def scalars():
    return [pl.BlockSpec(memory_space=pltpu.SMEM)]


def spread_kernel(first, lesser, greater, *rest):
    out, lines = rest[-2:]
    _, rows, _, _ = lesser.shape
    count = lines.shape[0] // (2 * rows)
    for g, tile in enumerate((lesser, greater)):
        for t in range(rows):
            span = slice(first, first + count)
            slab = jnp.concatenate([tile[0, t, :, span], tile[1, t, :, span]], axis=0)
            lines[pl.ds(g * rows + t, count, stride=2 * rows), :] = slab.astype(F32).T
    out[...] = lines[...].astype(BF16)


def spread(tiles, first, count, after):
    _, rows, cols, _ = tiles[0].shape
    shape = (count * 2 * rows, 2 * cols)
    return pl.pallas_call(
        functools.partial(spread_kernel, first),
        out_shape=pltpu.HBM(shape, BF16),
        in_specs=whole(2) + unread(after),
        out_specs=whole(1)[0],
        scratch_shapes=[pltpu.VMEM(shape, F32)],
        compiler_params=vmem_params(14),
        name="spread",
    )(*tiles, *after)


def collect_kernel(parts, blocks_ref, lesser, greater, lines):
    _, rows, cols, momenta = lesser.shape
    blocks, height, _ = blocks_ref.shape
    height = height // parts
    for part in range(parts):
        for block in range(blocks):
            lines[block * height : (block + 1) * height] = blocks_ref[
                block, part * height : (part + 1) * height
            ].astype(F32)
        count = momenta // parts
        span = slice(part * count, (part + 1) * count)
        for k in range(2 * rows):
            slab = lines[pl.ds(k, count, stride=2 * rows), :].T.astype(BF16)
            out = lesser if k < rows else greater
            out[0, k % rows, :, span] = slab[:cols]
            out[1, k % rows, :, span] = slab[cols:]


def collect(blocks, tile_shape):
    shape = jax.ShapeDtypeStruct(tile_shape, BF16)
    lines = blocks.shape[0] * blocks.shape[1] // PARTS
    return pl.pallas_call(
        functools.partial(collect_kernel, PARTS),
        out_shape=(shape, shape),
        in_specs=whole(1),
        out_specs=tuple(whole(2)),
        scratch_shapes=[pltpu.VMEM((lines, blocks.shape[2]), F32)],
        compiler_params=vmem_params(20),
        name="collect",
    )(blocks)


def table_kernel(column_ref, table, inverse):
    momenta = column_ref.shape[0]
    positions = lax.broadcasted_iota(jnp.int32, (momenta, momenta), 1)
    phases = (column_ref[...] * positions % momenta).astype(F32) * (2.0 * math.pi / momenta)
    cosines = jnp.cos(phases).astype(BF16)
    sines = jnp.sin(phases).astype(BF16)
    inverse[:momenta, :momenta] = cosines
    inverse[:momenta, momenta:] = sines
    inverse[momenta:, :momenta] = -sines
    inverse[momenta:, momenta:] = cosines
    cosines = cosines.astype(F32).T.astype(BF16)
    sines = sines.astype(F32).T.astype(BF16)
    table[:momenta, :momenta] = cosines
    table[:momenta, momenta:] = -sines
    table[momenta:, :momenta] = sines
    table[momenta:, momenta:] = cosines


def make_tables(lattice_map):
    momenta = lattice_map.shape[0]
    shape = jax.ShapeDtypeStruct((2 * momenta, 2 * momenta), BF16)
    return pl.pallas_call(
        table_kernel,
        out_shape=(shape, shape),
        in_specs=whole(1),
        out_specs=tuple(whole(2)),
        compiler_params=vmem_params(20),
        name="make_tables",
    )(lattice_map[:, None])


def site_kernel(norm_factor, lesser, greater, table, out):
    _, rows, cols, _ = lesser.shape
    wide = 4 * cols
    for pair in range(rows // 2):
        slabs = [
            jnp.concatenate([tile[0, t], tile[1, t]], axis=1)
            for t in (2 * pair, 2 * pair + 1)
            for tile in (lesser, greater)
        ]
        product = lax.dot_general(
            table[...],
            jnp.concatenate(slabs, axis=0),
            (((1,), (1,)), ((), ())),
            preferred_element_type=F32,
        )
        out[:, pair * wide : (pair + 1) * wide] = (product * norm_factor).astype(BF16)


def to_sites(tiles, table, norm_factor):
    _, rows, cols, momenta = tiles[0].shape
    return pl.pallas_call(
        functools.partial(site_kernel, norm_factor),
        out_shape=jax.ShapeDtypeStruct((2 * momenta, rows * 2 * cols), BF16),
        in_specs=whole(3),
        out_specs=whole(1)[0],
        compiler_params=vmem_params(20),
        name="to_sites",
    )(*tiles, table)


def cross_kernel(rows, half_ref, own, far, *rest):
    out = rest[-1]
    half = half_ref[0]
    blocks = far.shape[0]
    cols = blocks * rows
    for at in range(far.shape[1] // (2 * rows)):
        span = slice(at * 2 * rows, (at + 1) * 2 * rows)
        for source, offset, target in ((own, half * blocks, half), (far, 0, 1 - half)):
            loaded = [source[offset + block, span].astype(F32) for block in range(blocks)]
            stacked = jnp.concatenate(
                [lines[rows:] for lines in loaded] + [lines[:rows] for lines in loaded], axis=0
            )
            turned = stacked.T
            for block in range(blocks):
                out[target * blocks + block, span] = jnp.concatenate(
                    [
                        turned[block * rows : (block + 1) * rows],
                        turned[cols + block * rows : cols + (block + 1) * rows],
                    ],
                    axis=0,
                ).astype(BF16)


def to_crossed(half, own, far, rows, after, cost):
    return pl.pallas_call(
        functools.partial(cross_kernel, rows),
        out_shape=pltpu.HBM(own.shape, BF16),
        in_specs=[pl.BlockSpec(memory_space=pltpu.SMEM)] + whole(2) + unread(after),
        out_specs=whole(1)[0],
        compiler_params=vmem_params(10),
        cost_estimate=cost,
        name="to_crossed",
    )(half, own, far, *after)


def gate_kernel(*refs):
    del refs


def gate(array, after):
    return pl.pallas_call(
        gate_kernel,
        out_shape=jax.ShapeDtypeStruct(array.shape, array.dtype),
        in_specs=unread([array, *after]),
        out_specs=unread([array])[0],
        input_output_aliases={0: 0},
        name="gate",
    )(array, *after)


def mirrored_term(table, part, parts, read, pair, count):
    momenta = table.shape[1] // 2
    wide = momenta // parts
    rights = []
    for t in (2 * pair, 2 * pair + 1):
        real = read[pl.ds(t, wide, stride=2 * count), :]
        imaginary = -read[pl.ds(count + t, wide, stride=2 * count), :]
        rights.append(jnp.concatenate([real, imaginary], axis=0).astype(BF16))
    columns = jnp.concatenate(
        [
            table[:, part * wide : (part + 1) * wide],
            table[:, momenta + part * wide : momenta + (part + 1) * wide],
        ],
        axis=1,
    )
    return jnp.dot(columns, jnp.concatenate(rights, axis=1), preferred_element_type=F32)


def mirror_kernel(part, parts, count, crossed, table, out, read):
    read[...] = crossed[...].astype(F32)
    wide = 2 * crossed.shape[1]
    for pair in range(count // 2):
        out[:, pair * wide : (pair + 1) * wide] = mirrored_term(
            table, part, parts, read, pair, count
        )


def to_mirror(crossed, table, part, parts, count):
    lines, lanes = crossed.shape
    return pl.pallas_call(
        functools.partial(mirror_kernel, part, parts, count),
        out_shape=jax.ShapeDtypeStruct((table.shape[0], count * lanes), F32),
        in_specs=whole(2),
        out_specs=whole(1)[0],
        scratch_shapes=[pltpu.VMEM((lines, lanes), F32)],
        compiler_params=vmem_params(18),
        name="to_mirror",
    )(crossed, table)


def sigma_kernel(norm_factor, parts, *refs):
    mirrors = refs[: parts - 1]
    crossed, sites, table, inverse, coupling, out, read, written = refs[parts - 1 :]
    count = coupling.shape[0]
    momenta = table.shape[0] // 2
    read[...] = crossed[...].astype(F32)
    for pair in range(count // 2):
        span = slice(2 * pair * LANES, 2 * (pair + 1) * LANES)
        other = mirrored_term(table, parts - 1, parts, read, pair, count)
        for mirror in mirrors:
            other = other + mirror[:, span]
        other = (other * norm_factor).astype(BF16).astype(F32)
        self_real, self_imaginary = second_born(
            sites[:momenta, span].astype(F32),
            sites[momenta:, span].astype(F32),
            other[:momenta],
            -other[momenta:],
            jnp.concatenate([coupling[t : t + 1] for t in (2 * pair, 2 * pair + 1)], axis=1),
        )
        product = jnp.dot(
            inverse[...],
            jnp.concatenate([self_real, self_imaginary], axis=0).astype(BF16),
            preferred_element_type=F32,
        )
        product = product * norm_factor
        for at in range(2):
            for part in range(2):
                written[pl.ds(part * count + 2 * pair + at, momenta, stride=2 * count), :] = product[
                    part * momenta : (part + 1) * momenta, at * LANES : (at + 1) * LANES
                ]
    blocks, height, _ = out.shape
    height = height // parts
    for part in range(parts):
        for block in range(blocks):
            start = (part * blocks + block) * height
            out[block, part * height : (part + 1) * height] = written[
                start : start + height
            ].astype(BF16)


def to_sigma(mirrors, crossed, sites, table, inverse, coupling, norm_factor, blocks):
    parts = len(mirrors) + 1
    lines, lanes = crossed.shape
    return pl.pallas_call(
        functools.partial(sigma_kernel, norm_factor, parts),
        out_shape=jax.ShapeDtypeStruct((blocks, parts * lines // blocks, lanes), BF16),
        in_specs=whole(parts + 4),
        out_specs=whole(1)[0],
        scratch_shapes=[pltpu.VMEM((lines, lanes), F32), pltpu.VMEM((parts * lines, lanes), F32)],
        compiler_params=vmem_params(34),
        name="to_sigma",
    )(*mirrors, crossed, sites, table, inverse, coupling)


def rights_kernel(rows, half_ref, own, near_ref, away_ref, *rest):
    out = rest[-1]
    half = half_ref[0]
    blocks = near_ref.shape[0]
    lanes = own.shape[2]
    cols = lanes // 2
    near = half * cols
    away = (1 - half) * cols
    row_at = lax.broadcasted_iota(jnp.int32, (lanes, 2 * lanes), 0)
    inner_times = jnp.where(row_at < cols, near + row_at, away + row_at - cols)
    lane_at = lax.broadcasted_iota(jnp.int32, (lanes, 2 * lanes), 1)
    last_times = jnp.where(lane_at < lanes, near, away) + lane_at % cols
    keep = inner_times <= last_times
    for at in range(out.shape[0]):
        span = slice(at * 2 * rows, (at + 1) * 2 * rows)

        def stacked(read):
            loaded = [read(block).astype(F32) for block in range(blocks)]
            return [
                jnp.concatenate([lines[g * rows : (g + 1) * rows] for lines in loaded], axis=0)
                for g in range(2)
            ]

        own_near = stacked(lambda block: own[half * blocks + block, span])
        own_away = stacked(lambda block: own[(1 - half) * blocks + block, span])
        far_near = stacked(lambda block: near_ref[block, span])
        far_away = stacked(lambda block: away_ref[0, block, span])
        greens = [
            jnp.concatenate(
                [
                    jnp.concatenate([own_near[g], own_away[g]], axis=1),
                    jnp.concatenate([far_near[g], far_away[g]], axis=1),
                ],
                axis=0,
            )
            for g in range(2)
        ]
        out[at, :lanes] = greens[0].astype(BF16)
        out[at, lanes : 2 * lanes] = greens[1].astype(BF16)
        out[at, 2 * lanes :] = jnp.where(keep, greens[0] - greens[1], 0.0).astype(BF16)


STEPS = 4
PARTS = 2


def make_rights(half, own, far_near, far_away, rows, part, before):
    sources, lines, lanes = own.shape
    blocks = far_near.shape[0]
    steps = STEPS // PARTS
    step = lines // steps
    momenta = step // (2 * rows)
    return pl.pallas_call(
        functools.partial(rights_kernel, rows),
        grid=(steps,),
        out_shape=jax.ShapeDtypeStruct((STEPS * momenta, 3 * lanes, 2 * lanes), BF16),
        in_specs=scalars()
        + [
            pl.BlockSpec((sources, step, lanes), lambda p: (0, p, 0)),
            pl.BlockSpec((blocks, step, lanes), lambda p: (0, p, 0)),
            pl.BlockSpec((1, blocks, step, lanes), lambda p: (part, 0, p, 0)),
        ]
        + unread(before),
        out_specs=pl.BlockSpec(
            (momenta, 3 * lanes, 2 * lanes), lambda p: (part * steps + p, 0, 0)
        ),
        input_output_aliases={4: 0} if part > 0 else {},
        compiler_params=vmem_params(14),
        cost_estimate=weight(),
        name="make_rights",
    )(half, own, far_near, far_away, *before)


def volterra_kernel(rows, half_ref, sigma, rights, out):
    half = half_ref[0]
    blocks = sigma.shape[0] // 2
    lanes = sigma.shape[2]
    cols = lanes // 2
    near = half * cols
    away = (1 - half) * cols
    here = half * blocks
    there = (1 - half) * blocks
    first_times = near + lax.broadcasted_iota(jnp.int32, (cols, lanes), 0)
    left_lane = lax.broadcasted_iota(jnp.int32, (cols, lanes), 1)
    low_lanes = left_lane < cols
    left_times = jnp.where(low_lanes, near + left_lane, away + left_lane - cols)
    keep_left = left_times <= first_times
    for at in range(rights.shape[0]):
        span = slice(at * 2 * rows, (at + 1) * 2 * rows)

        def stacked(offset):
            loaded = [sigma[offset + block, span].astype(F32) for block in range(blocks)]
            return [
                jnp.concatenate([lines[part * rows : (part + 1) * rows] for lines in loaded], axis=0)
                for part in range(2)
            ]

        sigma_near = stacked(here)
        sigma_away = stacked(there)
        retarded = []
        lefts = [[], []]
        for part in range(2):
            lesser = jnp.where(
                low_lanes, sigma_near[part], pltpu.roll(sigma_away[part], cols, 1)
            )
            greater = jnp.where(
                low_lanes, pltpu.roll(sigma_near[part], cols, 1), sigma_away[part]
            )
            retarded.append(jnp.where(keep_left, greater - lesser, 0.0))
            lefts[0].append(lesser)
            lefts[1].append(greater)
        retarded = jnp.concatenate(retarded, axis=0).astype(BF16)
        results = []
        for g in range(2):
            left = jnp.concatenate(
                [retarded, jnp.concatenate(lefts[g], axis=0).astype(BF16)], axis=1
            )
            right = jnp.concatenate(
                [rights[at, g * lanes : (g + 1) * lanes], rights[at, 2 * lanes :]], axis=0
            )
            product = jnp.dot(left, right, preferred_element_type=F32)
            sides = []
            for side in range(2):
                straight = product[:cols, side * lanes : (side + 1) * lanes]
                turned = pltpu.roll(product[cols:, side * lanes : (side + 1) * lanes], cols, 1)
                sides.append((straight + jnp.where(low_lanes, -turned, turned)) * step_size)
            results.append(sides)
        for block in range(blocks):
            lines = slice(block * rows, (block + 1) * rows)
            for side, offset in enumerate((here, there)):
                out[offset + block, span] = jnp.concatenate(
                    [results[0][side][lines], results[1][side][lines]], axis=0
                ).astype(BF16)


def volterra(half, sigma, rights, rows):
    sources, lines, lanes = sigma.shape
    step = lines // STEPS
    momenta = step // (2 * rows)
    spec = pl.BlockSpec((sources, step, lanes), lambda p: (0, p, 0))
    return pl.pallas_call(
        functools.partial(volterra_kernel, rows),
        grid=(STEPS,),
        out_shape=jax.ShapeDtypeStruct(sigma.shape, BF16),
        in_specs=scalars()
        + [spec, pl.BlockSpec((momenta, 3 * lanes, 2 * lanes), lambda p: (p, 0, 0))],
        out_specs=spec,
        compiler_params=vmem_params(14),
        name="volterra",
    )(half, sigma, rights)


def halved_body(green_lesser, green_greater, lattice_map, time_offset):
    _, rows, cols, momenta = green_lesser.shape
    half = lax.axis_index("half")
    line = lax.axis_index("line")
    side = lax.axis_index("tcol")
    lines = lax.axis_size("line")
    group = lines * lax.axis_size("tcol")
    window = rows * lines * lax.axis_size("half")
    norm_factor = 1.0 / math.sqrt(momenta)
    tiles = (green_lesser, green_greater)
    half_at = half[None]
    count = momenta // PARTS

    def exchange(blocks):
        return lax.all_to_all(blocks, ("tcol", "line"), 0, 0, tiled=True)

    def blocked(rows_array):
        return rows_array.reshape(group, rows_array.shape[0] // group, rows_array.shape[1])

    def swap(array):
        return lax.ppermute(array, "half", [(0, 1), (1, 0)])

    table, inverse = make_tables(lattice_map)
    sites = to_sites(tiles, table, norm_factor)
    time_steps = jnp.arange(window, dtype=jnp.int32)
    coupling_line = 1.0 + drive_depth * jnp.cos(
        ((time_offset[0] + time_steps) % PERIOD).astype(F32) * (2.0 * math.pi / PERIOD)
    )
    first = lax.dynamic_slice_in_dim(coupling_line, (half * lines + line) * rows, rows)
    second = lax.dynamic_slice_in_dim(coupling_line, side * cols, cols)
    coupling = first[:, None] * jnp.concatenate([second, second])[None, :]

    spread_parts = [spread(tiles, part * count, count, []) for part in range(PARTS)]
    own = [exchange(blocked(spread_parts[0]))]
    for rows_array in spread_parts[1:]:
        own.append(exchange(gate(blocked(rows_array), [token(own[-1]), token(sites), coupling])))
    far_near = [swap(lax.dynamic_slice_in_dim(blocks, (1 - half) * lines, lines)) for blocks in own]

    sent = []
    for part in range(PARTS):
        sent.append(
            to_crossed(
                half_at,
                own[part],
                far_near[part],
                rows,
                [token(blocks) for blocks in own[-1:] + sent[-1:]],
                weight() if part > 0 else None,
            )
        )
    crossed = [exchange(blocks) for blocks in sent]
    kept = jnp.stack(
        [lax.dynamic_slice_in_dim(blocks, half * lines, lines) for blocks in own]
    )
    far_away = swap(gate(kept, [token(blocks) for blocks in sent[-1:] + crossed[:-1]]))
    flat = [blocks.reshape(-1, 2 * cols) for blocks in crossed]
    mirrors = [to_mirror(flat[part], table, part, PARTS, rows) for part in range(PARTS - 1)]
    sigma_rows = to_sigma(
        mirrors, flat[-1], sites, table, inverse, coupling, norm_factor, group
    )
    sigma = exchange(sigma_rows)
    rights = []
    for part in range(PARTS):
        rights = [
            make_rights(
                half_at, own[part], far_near[part], far_away, rows, part, rights + [token(sigma_rows)]
            )
        ]
    returned = exchange(volterra(half_at, sigma, rights[0], rows))
    return collect(returned, green_lesser.shape)


def solution(mesh):
    row_parts = mesh.shape["trow"]
    col_parts = mesh.shape["tcol"]

    def call(green_lesser, green_greater, lattice_map, time_offset):
        window, window_cols, momenta = green_lesser.shape[1:]
        rows = window // row_parts
        cols = window_cols // col_parts
        halved = (
            col_parts == 2
            and row_parts % 2 == 0
            and window == window_cols
            and 2 * cols == LANES
            and cols == rows * (row_parts // 2)
            and rows % 8 == 0
            and momenta % (2 * row_parts * STEPS) == 0
            and momenta % (PARTS * LANES) == 0
        )
        if halved:
            devices = mesh.devices.reshape(2, row_parts // 2, col_parts)
            used = Mesh(devices, ("half", "line", "tcol"))
            spec = P(None, ("half", "line"), "tcol", None)
            inner = halved_body
        else:
            used = mesh
            spec = P(None, "trow", "tcol", None)
            inner = general_body
        return jax.shard_map(
            inner, mesh=used, in_specs=(spec, spec, P(), P()), out_specs=(spec, spec), check_vma=False
        )(green_lesser, green_greater, lattice_map, time_offset)

    return call
```

```python
import functools
import math

import jax
import jax.numpy as jnp
from jax import lax
from jax.experimental import pallas as pl
from jax.experimental.pallas import tpu as pltpu
from jax.sharding import Mesh, PartitionSpec as P

F32 = jnp.float32
BF16 = jnp.bfloat16
LANES = 128

PERIOD = 64


step_size = 0.01
drive_depth = 0.5


def regroup(blocks):
    return lax.all_to_all(
        lax.all_to_all(blocks, "trow", split_axis=1, concat_axis=1, tiled=True),
        "tcol",
        split_axis=2,
        concat_axis=2,
        tiled=True,
    )


def pack_blocks(spectral, row_parts, col_parts):
    stacked, extent, tile_cells = spectral.shape
    return spectral.reshape(
        stacked, row_parts, col_parts, extent // (row_parts * col_parts), tile_cells
    )


def spread_times(blocks, tile_rows, tile_cols):
    stacked, row_parts, col_parts, local_count, tile_cells = blocks.shape
    shaped = blocks.reshape(stacked, row_parts, col_parts, local_count, tile_rows, tile_cols)
    return shaped.transpose(0, 3, 1, 4, 2, 5).reshape(
        stacked, local_count, row_parts * tile_rows, col_parts * tile_cols
    )


def gather_tiles(full, row_parts, col_parts):
    stacked, local_count, window, window_cols = full.shape
    tile_rows = window // row_parts
    tile_cols = window_cols // col_parts
    shaped = full.reshape(stacked, local_count, row_parts, tile_rows, col_parts, tile_cols)
    return shaped.transpose(0, 2, 4, 1, 3, 5).reshape(
        stacked, row_parts, col_parts, local_count, tile_rows * tile_cols
    )


def mirrored(full, keep_pair):
    stacked, local_count, window, window_cols = full.shape
    paired = full.reshape(stacked, local_count // 2, 2, window, window_cols)
    swapped = jnp.where(keep_pair[None, :, None, None, None], paired, paired[:, :, ::-1])
    return jnp.swapaxes(swapped.reshape(stacked, local_count, window, window_cols), 2, 3)


def second_born(first_real, first_imaginary, other_real, other_imaginary, coupling):
    square_real = first_real * first_real - first_imaginary * first_imaginary
    square_imaginary = 2.0 * first_real * first_imaginary
    out_real = coupling * (square_real * other_real - square_imaginary * other_imaginary)
    out_imaginary = coupling * (square_real * other_imaginary + square_imaginary * other_real)
    return (out_real, out_imaginary)


def collide(
    retarded_real,
    retarded_imaginary,
    self_real,
    self_imaginary,
    green_real,
    green_imaginary,
    advanced_real,
    advanced_imaginary,
):
    minus_left = jnp.concatenate(
        [retarded_real, -retarded_imaginary, self_real, -self_imaginary], axis=2
    )
    plus_left = jnp.concatenate(
        [retarded_real, retarded_imaginary, self_real, self_imaginary], axis=2
    )
    real_right = jnp.concatenate(
        [green_real, green_imaginary, advanced_real, advanced_imaginary], axis=1
    )
    imaginary_right = jnp.concatenate(
        [green_imaginary, green_real, advanced_imaginary, advanced_real], axis=1
    )
    out_real = jnp.einsum(
        "kts,ksu->ktu", minus_left, real_right, preferred_element_type=jnp.float32
    )
    out_imaginary = jnp.einsum(
        "kts,ksu->ktu", plus_left, imaginary_right, preferred_element_type=jnp.float32
    )
    return (out_real, out_imaginary)


def general_body(green_lesser, green_greater, lattice_map, time_offset):
    tile_rows = green_lesser.shape[1]
    tile_cols = green_lesser.shape[2]
    momenta = green_lesser.shape[3]
    row_parts = lax.axis_size("trow")
    col_parts = lax.axis_size("tcol")
    window = tile_rows * row_parts
    tile_cells = tile_rows * tile_cols
    local_count = momenta // (row_parts * col_parts)
    norm_factor = 1.0 / math.sqrt(momenta)
    greens = (
        jnp.concatenate([green_lesser, green_greater], axis=0)
        .reshape(4, tile_cells, momenta)
        .transpose(0, 2, 1)
    )
    positions = jnp.arange(momenta, dtype=jnp.int32)
    halves = positions // 2
    site_order = jnp.where(
        positions == 1, momenta // 2, jnp.where(positions % 2 == 0, halves, momenta - halves)
    )
    phases = (lattice_map[:, None] * site_order[None, :] % momenta).astype(jnp.float32) * (
        2.0 * math.pi / momenta
    )
    cosines = jnp.cos(phases).astype(jnp.bfloat16)
    sines = jnp.sin(phases).astype(jnp.bfloat16)
    ahead_blocks = lax.all_to_all(
        lax.all_to_all(
            pack_blocks(greens, row_parts, col_parts),
            "trow",
            split_axis=1,
            concat_axis=1,
            tiled=True,
        ),
        "tcol",
        split_axis=2,
        concat_axis=2,
        tiled=True,
    )
    green_moment = spread_times(ahead_blocks, tile_rows, tile_cols)
    forward_table = jnp.concatenate([cosines, sines], axis=1)
    products = jnp.einsum("cjm,jr->crm", greens, forward_table, preferred_element_type=jnp.float32)
    site_space = jnp.stack(
        [
            (products[0, :momenta] - products[1, momenta:]) * norm_factor,
            (products[0, momenta:] + products[1, :momenta]) * norm_factor,
            (products[2, :momenta] - products[3, momenta:]) * norm_factor,
            (products[2, momenta:] + products[3, :momenta]) * norm_factor,
        ]
    ).astype(jnp.bfloat16)
    site_full = spread_times(
        regroup(pack_blocks(site_space, row_parts, col_parts)), tile_rows, tile_cols
    )
    site_block = lax.axis_index("trow") * col_parts + lax.axis_index("tcol")
    keep_pair = site_block * (local_count // 2) + jnp.arange(local_count // 2, dtype=jnp.int32) == 0
    mirror = mirrored(site_full, keep_pair).astype(jnp.float32)
    direct = site_full.astype(jnp.float32)
    time_steps = jnp.arange(window, dtype=jnp.int32)
    coupling_line = 1.0 + drive_depth * jnp.cos(
        ((time_offset[0] + time_steps) % PERIOD).astype(jnp.float32) * (2.0 * math.pi / PERIOD)
    )
    coupling = coupling_line[:, None] * coupling_line[None, :]
    self_lesser = second_born(direct[0], direct[1], mirror[2], mirror[3], coupling)
    self_greater = second_born(direct[2], direct[3], mirror[0], mirror[1], coupling)
    self_sites = jnp.stack(
        [self_lesser[0], self_lesser[1], self_greater[0], self_greater[1]]
    ).astype(jnp.bfloat16)
    self_tiles = regroup(gather_tiles(self_sites, row_parts, col_parts)).reshape(
        4, momenta, tile_cells
    )
    inverse_table = jnp.concatenate([cosines, sines], axis=0)
    spectral_terms = jnp.einsum(
        "cum,ju->cjm", self_tiles, inverse_table, preferred_element_type=jnp.float32
    )
    self_spectral = jnp.stack(
        [
            (spectral_terms[0, :momenta] + spectral_terms[1, momenta:]) * norm_factor,
            (spectral_terms[1, :momenta] - spectral_terms[0, momenta:]) * norm_factor,
            (spectral_terms[2, :momenta] + spectral_terms[3, momenta:]) * norm_factor,
            (spectral_terms[3, :momenta] - spectral_terms[2, momenta:]) * norm_factor,
        ]
    ).astype(jnp.bfloat16)
    self_moment = spread_times(
        regroup(pack_blocks(self_spectral, row_parts, col_parts)), tile_rows, tile_cols
    )
    lower_mask = time_steps[None, :] <= time_steps[:, None]
    upper_mask = time_steps[:, None] <= time_steps[None, :]
    retarded = jnp.where(
        lower_mask, self_moment[2:4].astype(jnp.float32) - self_moment[0:2].astype(jnp.float32), 0.0
    ).astype(jnp.bfloat16)
    advanced = jnp.where(
        upper_mask,
        green_moment[0:2].astype(jnp.float32) - green_moment[2:4].astype(jnp.float32),
        0.0,
    ).astype(jnp.bfloat16)
    lesser_out = collide(
        retarded[0],
        retarded[1],
        self_moment[0],
        self_moment[1],
        green_moment[0],
        green_moment[1],
        advanced[0],
        advanced[1],
    )
    greater_out = collide(
        retarded[0],
        retarded[1],
        self_moment[2],
        self_moment[3],
        green_moment[2],
        green_moment[3],
        advanced[0],
        advanced[1],
    )
    collisions = (
        jnp.stack([lesser_out[0], lesser_out[1], greater_out[0], greater_out[1]]) * step_size
    ).astype(jnp.bfloat16)
    out_tiles = regroup(gather_tiles(collisions, row_parts, col_parts)).reshape(
        4, momenta, tile_cells
    )
    out_tiles = out_tiles.transpose(0, 2, 1).reshape(4, tile_rows, tile_cols, momenta)
    return (out_tiles[0:2], out_tiles[2:4])


def vmem_params(mebibytes=48):
    return pltpu.CompilerParams(vmem_limit_bytes=mebibytes * 1024 * 1024)


def unread(arrays):
    return [pl.BlockSpec(memory_space=pl.ANY)] * len(arrays)


def whole(count):
    return [pl.BlockSpec(memory_space=pltpu.VMEM)] * count


def weight():
    return pl.CostEstimate(flops=10**11, bytes_accessed=2**20, transcendentals=0)


def scalars():
    return [pl.BlockSpec(memory_space=pltpu.SMEM)]


def spread_kernel(lesser, greater, out, lines):
    _, rows, _, count = lesser.shape
    for g, tile in enumerate((lesser, greater)):
        for t in range(rows):
            slab = jnp.concatenate([tile[0, t], tile[1, t]], axis=0)
            lines[pl.ds(g * rows + t, count, stride=2 * rows), :] = slab.astype(F32).T
    out[...] = lines[...].astype(BF16)


def spread(tiles, first, count):
    _, rows, cols, _ = tiles[0].shape
    height = 2 * rows * LANES
    tile_spec = pl.BlockSpec((2, rows, cols, LANES), lambda p: (0, 0, 0, first // LANES + p))
    return pl.pallas_call(
        spread_kernel,
        grid=(count // LANES,),
        out_shape=pltpu.HBM((count * 2 * rows, 2 * cols), BF16),
        in_specs=[tile_spec, tile_spec],
        out_specs=pl.BlockSpec((height, 2 * cols), lambda p: (p, 0)),
        scratch_shapes=[pltpu.VMEM((height, 2 * cols), F32)],
        compiler_params=vmem_params(58),
        name="spread",
    )(*tiles)


def collect_kernel(parts, blocks_ref, lesser, greater, lines):
    _, rows, cols, momenta = lesser.shape
    blocks, height, _ = blocks_ref.shape
    height = height // parts
    for part in range(parts):
        for block in range(blocks):
            lines[block * height : (block + 1) * height] = blocks_ref[
                block, part * height : (part + 1) * height
            ].astype(F32)
        count = momenta // parts
        span = slice(part * count, (part + 1) * count)
        for k in range(2 * rows):
            slab = lines[pl.ds(k, count, stride=2 * rows), :].T.astype(BF16)
            out = lesser if k < rows else greater
            out[0, k % rows, :, span] = slab[:cols]
            out[1, k % rows, :, span] = slab[cols:]


def collect(blocks, tile_shape):
    shape = jax.ShapeDtypeStruct(tile_shape, BF16)
    lines = blocks.shape[0] * blocks.shape[1] // PARTS
    return pl.pallas_call(
        functools.partial(collect_kernel, PARTS),
        out_shape=(shape, shape),
        in_specs=whole(1),
        out_specs=tuple(whole(2)),
        scratch_shapes=[pltpu.VMEM((lines, blocks.shape[2]), F32)],
        compiler_params=vmem_params(),
        name="collect",
    )(blocks)


def table_kernel(column_ref, table, inverse):
    momenta = column_ref.shape[0]
    positions = lax.broadcasted_iota(jnp.int32, (momenta, momenta), 1)
    phases = (column_ref[...] * positions % momenta).astype(F32) * (2.0 * math.pi / momenta)
    cosines = jnp.cos(phases).astype(BF16)
    sines = jnp.sin(phases).astype(BF16)
    inverse[:momenta, :momenta] = cosines
    inverse[:momenta, momenta:] = sines
    inverse[momenta:, :momenta] = -sines
    inverse[momenta:, momenta:] = cosines
    cosines = cosines.astype(F32).T.astype(BF16)
    sines = sines.astype(F32).T.astype(BF16)
    table[:momenta, :momenta] = cosines
    table[:momenta, momenta:] = -sines
    table[momenta:, :momenta] = sines
    table[momenta:, momenta:] = cosines


def make_tables(lattice_map):
    momenta = lattice_map.shape[0]
    shape = jax.ShapeDtypeStruct((2 * momenta, 2 * momenta), BF16)
    return pl.pallas_call(
        table_kernel,
        out_shape=(shape, shape),
        in_specs=whole(1),
        out_specs=tuple(whole(2)),
        compiler_params=vmem_params(),
        name="make_tables",
    )(lattice_map[:, None])


def site_kernel(norm_factor, lesser, greater, table, out):
    _, rows, cols, _ = lesser.shape
    wide = 4 * cols
    for pair in range(rows // 2):
        slabs = [
            jnp.concatenate([tile[0, t], tile[1, t]], axis=1)
            for t in (2 * pair, 2 * pair + 1)
            for tile in (lesser, greater)
        ]
        product = lax.dot_general(
            table[...],
            jnp.concatenate(slabs, axis=0),
            (((1,), (1,)), ((), ())),
            preferred_element_type=F32,
        )
        out[:, pair * wide : (pair + 1) * wide] = (product * norm_factor).astype(BF16)


def to_sites(tiles, table, norm_factor):
    _, rows, cols, momenta = tiles[0].shape
    return pl.pallas_call(
        functools.partial(site_kernel, norm_factor),
        out_shape=jax.ShapeDtypeStruct((2 * momenta, rows * 2 * cols), BF16),
        in_specs=whole(3),
        out_specs=whole(1)[0],
        compiler_params=vmem_params(),
        name="to_sites",
    )(*tiles, table)


def cross_kernel(rows, half_ref, own, far, *rest):
    out, mark = rest[-2:]
    mark[...] = jnp.zeros_like(mark)
    half = half_ref[0]
    blocks = far.shape[0]
    cols = blocks * rows
    for at in range(far.shape[1] // (2 * rows)):
        span = slice(at * 2 * rows, (at + 1) * 2 * rows)
        for source, offset, target in ((own, half * blocks, half), (far, 0, 1 - half)):
            loaded = [source[offset + block, span].astype(F32) for block in range(blocks)]
            stacked = jnp.concatenate(
                [lines[rows:] for lines in loaded] + [lines[:rows] for lines in loaded], axis=0
            )
            turned = stacked.T
            for block in range(blocks):
                out[target * blocks + block, span] = jnp.concatenate(
                    [
                        turned[block * rows : (block + 1) * rows],
                        turned[cols + block * rows : cols + (block + 1) * rows],
                    ],
                    axis=0,
                ).astype(BF16)


def to_crossed(half, own, far, rows, after, cost):
    sources, lines, lanes = own.shape
    blocks = far.shape[0]
    step = lines // STEPS
    spec = pl.BlockSpec((sources, step, lanes), lambda p: (0, p, 0))
    far_spec = pl.BlockSpec((blocks, step, lanes), lambda p: (0, p, 0))
    return pl.pallas_call(
        functools.partial(cross_kernel, rows),
        grid=(STEPS,),
        out_shape=(
            pltpu.HBM(own.shape, BF16),
            jax.ShapeDtypeStruct((8, LANES), F32),
        ),
        in_specs=scalars() + [spec, far_spec] + unread(after),
        out_specs=(spec, pl.BlockSpec((8, LANES), lambda p: (0, 0))),
        compiler_params=vmem_params(),
        cost_estimate=cost,
        name="to_crossed",
    )(half, own, far, *after)


def gate_kernel(*refs):
    del refs


def gate(array, after):
    return pl.pallas_call(
        gate_kernel,
        out_shape=jax.ShapeDtypeStruct(array.shape, array.dtype),
        in_specs=unread([array, *after]),
        out_specs=unread([array])[0],
        input_output_aliases={0: 0},
        name="gate",
    )(array, *after)


def mirrored_term(columns, read, first, count):
    wide = columns.shape[1] // 2
    rights = []
    for t in (first, first + 1):
        real = read[pl.ds(t, wide, stride=2 * count), :]
        imaginary = -read[pl.ds(count + t, wide, stride=2 * count), :]
        rights.append(jnp.concatenate([real, imaginary], axis=0).astype(BF16))
    return jnp.dot(columns, jnp.concatenate(rights, axis=1), preferred_element_type=F32)


def mirror_kernel(part, parts, count, crossed, table, out, read):
    read[...] = crossed[...].astype(F32)
    wide = 2 * crossed.shape[1]
    momenta = table.shape[1] // 2
    width = momenta // parts
    columns = jnp.concatenate(
        [
            table[:, part * width : (part + 1) * width],
            table[:, momenta + part * width : momenta + (part + 1) * width],
        ],
        axis=1,
    )
    for pair in range(count // 2):
        out[:, pair * wide : (pair + 1) * wide] = mirrored_term(columns, read, 2 * pair, count)


def to_mirror(crossed, table, part, parts, count):
    lines, lanes = crossed.shape
    return pl.pallas_call(
        functools.partial(mirror_kernel, part, parts, count),
        out_shape=jax.ShapeDtypeStruct((table.shape[0], count * lanes), F32),
        in_specs=whole(2),
        out_specs=whole(1)[0],
        scratch_shapes=[pltpu.VMEM((lines, lanes), F32)],
        compiler_params=vmem_params(),
        name="to_mirror",
    )(crossed, table)


def sigma_kernel(norm_factor, parts, *refs):
    mirrors = refs[: parts - 1]
    crossed, sites, cosines, sines, inverse, coupling, out, read, written = refs[parts - 1 :]
    count = coupling.shape[0]
    momenta = cosines.shape[0] // 2
    step = pl.program_id(0)

    @pl.when(step == 0)
    def _():
        read[...] = crossed[...].astype(F32)

    first = 2 * step
    columns = jnp.concatenate([cosines[...], sines[...]], axis=1)
    other = mirrored_term(columns, read, first, count)
    for mirror in mirrors:
        other = other + mirror[...]
    other = (other * norm_factor).astype(BF16).astype(F32)
    self_real, self_imaginary = second_born(
        sites[:momenta].astype(F32),
        sites[momenta:].astype(F32),
        other[:momenta],
        -other[momenta:],
        jnp.concatenate([coupling[pl.ds(first, 1), :], coupling[pl.ds(first + 1, 1), :]], axis=1),
    )
    product = jnp.dot(
        inverse[...],
        jnp.concatenate([self_real, self_imaginary], axis=0).astype(BF16),
        preferred_element_type=F32,
    )
    product = product * norm_factor
    for at in range(2):
        for part in range(2):
            written[pl.ds(part * count + first + at, momenta, stride=2 * count), :] = product[
                part * momenta : (part + 1) * momenta, at * LANES : (at + 1) * LANES
            ]

    @pl.when(step == count // 2 - 1)
    def _():
        blocks, height, _ = out.shape
        height = height // parts
        for part in range(parts):
            for block in range(blocks):
                start = (part * blocks + block) * height
                out[block, part * height : (part + 1) * height] = written[
                    start : start + height
                ].astype(BF16)


def to_sigma(mirrors, crossed, sites, table, inverse, coupling, norm_factor, blocks):
    parts = len(mirrors) + 1
    lines, lanes = crossed.shape
    size = table.shape[0]
    width = size // (2 * parts)
    shape = (blocks, parts * lines // blocks, lanes)
    by_step = pl.BlockSpec((size, 2 * lanes), lambda p: (0, p))
    fixed = lambda array: pl.BlockSpec(array.shape, lambda p: (0, 0))
    return pl.pallas_call(
        functools.partial(sigma_kernel, norm_factor, parts),
        grid=(coupling.shape[0] // 2,),
        out_shape=pltpu.HBM(shape, BF16),
        in_specs=[by_step] * (parts - 1)
        + [
            fixed(crossed),
            by_step,
            pl.BlockSpec((size, width), lambda p: (0, parts - 1)),
            pl.BlockSpec((size, width), lambda p: (0, 2 * parts - 1)),
            fixed(inverse),
            fixed(coupling),
        ],
        out_specs=pl.BlockSpec(shape, lambda p: (0, 0, 0)),
        scratch_shapes=[pltpu.VMEM((lines, lanes), F32), pltpu.VMEM((parts * lines, lanes), F32)],
        compiler_params=vmem_params(58),
        name="to_sigma",
    )(*mirrors, crossed, sites, table, table, inverse, coupling)


def rights_kernel(rows, half_ref, own, near_ref, away_ref, *rest):
    out = rest[-1]
    half = half_ref[0]
    blocks = near_ref.shape[0]
    lanes = own.shape[2]
    cols = lanes // 2
    near = half * cols
    away = (1 - half) * cols
    row_at = lax.broadcasted_iota(jnp.int32, (lanes, 2 * lanes), 0)
    inner_times = jnp.where(row_at < cols, near + row_at, away + row_at - cols)
    lane_at = lax.broadcasted_iota(jnp.int32, (lanes, 2 * lanes), 1)
    last_times = jnp.where(lane_at < lanes, near, away) + lane_at % cols
    keep = inner_times <= last_times
    for at in range(out.shape[0]):
        span = slice(at * 2 * rows, (at + 1) * 2 * rows)

        def stacked(read):
            loaded = [read(block).astype(F32) for block in range(blocks)]
            return [
                jnp.concatenate([lines[g * rows : (g + 1) * rows] for lines in loaded], axis=0)
                for g in range(2)
            ]

        own_near = stacked(lambda block: own[half * blocks + block, span])
        own_away = stacked(lambda block: own[(1 - half) * blocks + block, span])
        far_near = stacked(lambda block: near_ref[block, span])
        far_away = stacked(lambda block: away_ref[0, block, span])
        greens = [
            jnp.concatenate(
                [
                    jnp.concatenate([own_near[g], own_away[g]], axis=1),
                    jnp.concatenate([far_near[g], far_away[g]], axis=1),
                ],
                axis=0,
            )
            for g in range(2)
        ]
        out[at, :lanes] = greens[0].astype(BF16)
        out[at, lanes : 2 * lanes] = greens[1].astype(BF16)
        out[at, 2 * lanes :] = jnp.where(keep, greens[0] - greens[1], 0.0).astype(BF16)


STEPS = 4
PARTS = 2


def make_rights(half, own, far_near, far_away, rows, part, before):
    sources, lines, lanes = own.shape
    blocks = far_near.shape[0]
    steps = STEPS // PARTS
    step = lines // steps
    momenta = step // (2 * rows)
    return pl.pallas_call(
        functools.partial(rights_kernel, rows),
        grid=(steps,),
        out_shape=jax.ShapeDtypeStruct((STEPS * momenta, 3 * lanes, 2 * lanes), BF16),
        in_specs=scalars()
        + [
            pl.BlockSpec((sources, step, lanes), lambda p: (0, p, 0)),
            pl.BlockSpec((blocks, step, lanes), lambda p: (0, p, 0)),
            pl.BlockSpec((1, blocks, step, lanes), lambda p: (part, 0, p, 0)),
        ]
        + unread(before),
        out_specs=pl.BlockSpec(
            (momenta, 3 * lanes, 2 * lanes), lambda p: (part * steps + p, 0, 0)
        ),
        input_output_aliases={4: 0} if part > 0 else {},
        compiler_params=vmem_params(),
        cost_estimate=weight(),
        name="make_rights",
    )(half, own, far_near, far_away, *before)


def volterra_kernel(rows, half_ref, sigma, rights, out):
    half = half_ref[0]
    blocks = sigma.shape[0] // 2
    lanes = sigma.shape[2]
    cols = lanes // 2
    near = half * cols
    away = (1 - half) * cols
    here = half * blocks
    there = (1 - half) * blocks
    first_times = near + lax.broadcasted_iota(jnp.int32, (cols, lanes), 0)
    left_lane = lax.broadcasted_iota(jnp.int32, (cols, lanes), 1)
    low_lanes = left_lane < cols
    left_times = jnp.where(low_lanes, near + left_lane, away + left_lane - cols)
    keep_left = left_times <= first_times
    for at in range(rights.shape[0]):
        span = slice(at * 2 * rows, (at + 1) * 2 * rows)

        def stacked(offset):
            loaded = [sigma[offset + block, span].astype(F32) for block in range(blocks)]
            return [
                jnp.concatenate([lines[part * rows : (part + 1) * rows] for lines in loaded], axis=0)
                for part in range(2)
            ]

        sigma_near = stacked(here)
        sigma_away = stacked(there)
        retarded = []
        lefts = [[], []]
        for part in range(2):
            lesser = jnp.where(
                low_lanes, sigma_near[part], pltpu.roll(sigma_away[part], cols, 1)
            )
            greater = jnp.where(
                low_lanes, pltpu.roll(sigma_near[part], cols, 1), sigma_away[part]
            )
            retarded.append(jnp.where(keep_left, greater - lesser, 0.0))
            lefts[0].append(lesser)
            lefts[1].append(greater)
        retarded = jnp.concatenate(retarded, axis=0).astype(BF16)
        results = []
        for g in range(2):
            left = jnp.concatenate(
                [retarded, jnp.concatenate(lefts[g], axis=0).astype(BF16)], axis=1
            )
            right = jnp.concatenate(
                [rights[at, g * lanes : (g + 1) * lanes], rights[at, 2 * lanes :]], axis=0
            )
            product = jnp.dot(left, right, preferred_element_type=F32)
            sides = []
            for side in range(2):
                straight = product[:cols, side * lanes : (side + 1) * lanes]
                turned = pltpu.roll(product[cols:, side * lanes : (side + 1) * lanes], cols, 1)
                sides.append((straight + jnp.where(low_lanes, -turned, turned)) * step_size)
            results.append(sides)
        for block in range(blocks):
            lines = slice(block * rows, (block + 1) * rows)
            for side, offset in enumerate((here, there)):
                out[offset + block, span] = jnp.concatenate(
                    [results[0][side][lines], results[1][side][lines]], axis=0
                ).astype(BF16)


def volterra(half, sigma, rights, rows):
    sources, lines, lanes = sigma.shape
    step = lines // STEPS
    momenta = step // (2 * rows)
    spec = pl.BlockSpec((sources, step, lanes), lambda p: (0, p, 0))
    return pl.pallas_call(
        functools.partial(volterra_kernel, rows),
        grid=(STEPS,),
        out_shape=jax.ShapeDtypeStruct(sigma.shape, BF16),
        in_specs=scalars()
        + [spec, pl.BlockSpec((momenta, 3 * lanes, 2 * lanes), lambda p: (p, 0, 0))],
        out_specs=spec,
        compiler_params=vmem_params(),
        name="volterra",
    )(half, sigma, rights)


def halved_body(green_lesser, green_greater, lattice_map, time_offset):
    _, rows, cols, momenta = green_lesser.shape
    half = lax.axis_index("half")
    line = lax.axis_index("line")
    side = lax.axis_index("tcol")
    lines = lax.axis_size("line")
    group = lines * lax.axis_size("tcol")
    window = rows * lines * lax.axis_size("half")
    norm_factor = 1.0 / math.sqrt(momenta)
    tiles = (green_lesser, green_greater)
    half_at = half[None]
    count = momenta // PARTS

    def exchange(blocks):
        return lax.all_to_all(blocks, ("tcol", "line"), 0, 0, tiled=True)

    def blocked(rows_array):
        return rows_array.reshape(group, rows_array.shape[0] // group, rows_array.shape[1])

    def swap(array):
        return lax.ppermute(array, "half", [(0, 1), (1, 0)])

    table, inverse = make_tables(lattice_map)
    sites = to_sites(tiles, table, norm_factor)
    time_steps = jnp.arange(window, dtype=jnp.int32)
    coupling_line = 1.0 + drive_depth * jnp.cos(
        ((time_offset[0] + time_steps) % PERIOD).astype(F32) * (2.0 * math.pi / PERIOD)
    )
    first = lax.dynamic_slice_in_dim(coupling_line, (half * lines + line) * rows, rows)
    second = lax.dynamic_slice_in_dim(coupling_line, side * cols, cols)
    coupling = first[:, None] * jnp.concatenate([second, second])[None, :]

    spread_parts = [spread(tiles, part * count, count) for part in range(PARTS)]
    own = [exchange(blocked(spread_parts[0]))]
    for rows_array in spread_parts[1:]:
        own.append(exchange(gate(blocked(rows_array), [sites, coupling])))
    far_near = [swap(lax.dynamic_slice_in_dim(blocks, (1 - half) * lines, lines)) for blocks in own]

    sent = []
    marks = []
    for part in range(PARTS):
        blocks, mark = to_crossed(
            half_at,
            own[part],
            far_near[part],
            rows,
            own[-1:] + marks[-1:],
            weight() if part > 0 else None,
        )
        sent.append(blocks)
        marks.append(mark)
    crossed = [exchange(blocks) for blocks in sent]
    kept = jnp.stack(
        [lax.dynamic_slice_in_dim(blocks, half * lines, lines) for blocks in own]
    )
    far_away = swap(gate(kept, marks[-1:] + crossed[:-1]))
    flat = [blocks.reshape(-1, 2 * cols) for blocks in crossed]
    mirrors = [to_mirror(flat[part], table, part, PARTS, rows) for part in range(PARTS - 1)]
    sigma_rows = to_sigma(
        mirrors, flat[-1], sites, table, inverse, coupling, norm_factor, group
    )
    sigma = exchange(sigma_rows)
    rights = []
    for part in range(PARTS):
        rights = [
            make_rights(
                half_at, own[part], far_near[part], far_away, rows, part, rights + [sigma_rows]
            )
        ]
    returned = exchange(volterra(half_at, sigma, rights[0], rows))
    return collect(returned, green_lesser.shape)


def solution(mesh):
    row_parts = mesh.shape["trow"]
    col_parts = mesh.shape["tcol"]

    def call(green_lesser, green_greater, lattice_map, time_offset):
        window, window_cols, momenta = green_lesser.shape[1:]
        rows = window // row_parts
        cols = window_cols // col_parts
        halved = (
            col_parts == 2
            and row_parts % 2 == 0
            and window == window_cols
            and 2 * cols == LANES
            and cols == rows * (row_parts // 2)
            and rows % 8 == 0
            and momenta % (2 * row_parts * STEPS) == 0
            and momenta % (PARTS * LANES) == 0
        )
        if halved:
            devices = mesh.devices.reshape(2, row_parts // 2, col_parts)
            used = Mesh(devices, ("half", "line", "tcol"))
            spec = P(None, ("half", "line"), "tcol", None)
            inner = halved_body
        else:
            used = mesh
            spec = P(None, "trow", "tcol", None)
            inner = general_body
        return jax.shard_map(
            inner, mesh=used, in_specs=(spec, spec, P(), P()), out_specs=(spec, spec), check_vma=False
        )(green_lesser, green_greater, lattice_map, time_offset)

    return call
```

```python
import functools
import math

import jax
import jax.numpy as jnp
from jax import lax
from jax.experimental import pallas as pl
from jax.experimental.pallas import tpu as pltpu
from jax.sharding import Mesh, PartitionSpec as P

F32 = jnp.float32
BF16 = jnp.bfloat16
LANES = 128

PERIOD = 64


step_size = 0.01
drive_depth = 0.5


def regroup(blocks):
    return lax.all_to_all(
        lax.all_to_all(blocks, "trow", split_axis=1, concat_axis=1, tiled=True),
        "tcol",
        split_axis=2,
        concat_axis=2,
        tiled=True,
    )


def pack_blocks(spectral, row_parts, col_parts):
    stacked, extent, tile_cells = spectral.shape
    return spectral.reshape(
        stacked, row_parts, col_parts, extent // (row_parts * col_parts), tile_cells
    )


def spread_times(blocks, tile_rows, tile_cols):
    stacked, row_parts, col_parts, local_count, tile_cells = blocks.shape
    shaped = blocks.reshape(stacked, row_parts, col_parts, local_count, tile_rows, tile_cols)
    return shaped.transpose(0, 3, 1, 4, 2, 5).reshape(
        stacked, local_count, row_parts * tile_rows, col_parts * tile_cols
    )


def gather_tiles(full, row_parts, col_parts):
    stacked, local_count, window, window_cols = full.shape
    tile_rows = window // row_parts
    tile_cols = window_cols // col_parts
    shaped = full.reshape(stacked, local_count, row_parts, tile_rows, col_parts, tile_cols)
    return shaped.transpose(0, 2, 4, 1, 3, 5).reshape(
        stacked, row_parts, col_parts, local_count, tile_rows * tile_cols
    )


def mirrored(full, keep_pair):
    stacked, local_count, window, window_cols = full.shape
    paired = full.reshape(stacked, local_count // 2, 2, window, window_cols)
    swapped = jnp.where(keep_pair[None, :, None, None, None], paired, paired[:, :, ::-1])
    return jnp.swapaxes(swapped.reshape(stacked, local_count, window, window_cols), 2, 3)


def second_born(first_real, first_imaginary, other_real, other_imaginary, coupling):
    square_real = first_real * first_real - first_imaginary * first_imaginary
    square_imaginary = 2.0 * first_real * first_imaginary
    out_real = coupling * (square_real * other_real - square_imaginary * other_imaginary)
    out_imaginary = coupling * (square_real * other_imaginary + square_imaginary * other_real)
    return (out_real, out_imaginary)


def collide(
    retarded_real,
    retarded_imaginary,
    self_real,
    self_imaginary,
    green_real,
    green_imaginary,
    advanced_real,
    advanced_imaginary,
):
    minus_left = jnp.concatenate(
        [retarded_real, -retarded_imaginary, self_real, -self_imaginary], axis=2
    )
    plus_left = jnp.concatenate(
        [retarded_real, retarded_imaginary, self_real, self_imaginary], axis=2
    )
    real_right = jnp.concatenate(
        [green_real, green_imaginary, advanced_real, advanced_imaginary], axis=1
    )
    imaginary_right = jnp.concatenate(
        [green_imaginary, green_real, advanced_imaginary, advanced_real], axis=1
    )
    out_real = jnp.einsum(
        "kts,ksu->ktu", minus_left, real_right, preferred_element_type=jnp.float32
    )
    out_imaginary = jnp.einsum(
        "kts,ksu->ktu", plus_left, imaginary_right, preferred_element_type=jnp.float32
    )
    return (out_real, out_imaginary)


def general_body(green_lesser, green_greater, lattice_map, time_offset):
    tile_rows = green_lesser.shape[1]
    tile_cols = green_lesser.shape[2]
    momenta = green_lesser.shape[3]
    row_parts = lax.axis_size("trow")
    col_parts = lax.axis_size("tcol")
    window = tile_rows * row_parts
    tile_cells = tile_rows * tile_cols
    local_count = momenta // (row_parts * col_parts)
    norm_factor = 1.0 / math.sqrt(momenta)
    greens = (
        jnp.concatenate([green_lesser, green_greater], axis=0)
        .reshape(4, tile_cells, momenta)
        .transpose(0, 2, 1)
    )
    positions = jnp.arange(momenta, dtype=jnp.int32)
    halves = positions // 2
    site_order = jnp.where(
        positions == 1, momenta // 2, jnp.where(positions % 2 == 0, halves, momenta - halves)
    )
    phases = (lattice_map[:, None] * site_order[None, :] % momenta).astype(jnp.float32) * (
        2.0 * math.pi / momenta
    )
    cosines = jnp.cos(phases).astype(jnp.bfloat16)
    sines = jnp.sin(phases).astype(jnp.bfloat16)
    ahead_blocks = lax.all_to_all(
        lax.all_to_all(
            pack_blocks(greens, row_parts, col_parts),
            "trow",
            split_axis=1,
            concat_axis=1,
            tiled=True,
        ),
        "tcol",
        split_axis=2,
        concat_axis=2,
        tiled=True,
    )
    green_moment = spread_times(ahead_blocks, tile_rows, tile_cols)
    forward_table = jnp.concatenate([cosines, sines], axis=1)
    products = jnp.einsum("cjm,jr->crm", greens, forward_table, preferred_element_type=jnp.float32)
    site_space = jnp.stack(
        [
            (products[0, :momenta] - products[1, momenta:]) * norm_factor,
            (products[0, momenta:] + products[1, :momenta]) * norm_factor,
            (products[2, :momenta] - products[3, momenta:]) * norm_factor,
            (products[2, momenta:] + products[3, :momenta]) * norm_factor,
        ]
    ).astype(jnp.bfloat16)
    site_full = spread_times(
        regroup(pack_blocks(site_space, row_parts, col_parts)), tile_rows, tile_cols
    )
    site_block = lax.axis_index("trow") * col_parts + lax.axis_index("tcol")
    keep_pair = site_block * (local_count // 2) + jnp.arange(local_count // 2, dtype=jnp.int32) == 0
    mirror = mirrored(site_full, keep_pair).astype(jnp.float32)
    direct = site_full.astype(jnp.float32)
    time_steps = jnp.arange(window, dtype=jnp.int32)
    coupling_line = 1.0 + drive_depth * jnp.cos(
        ((time_offset[0] + time_steps) % PERIOD).astype(jnp.float32) * (2.0 * math.pi / PERIOD)
    )
    coupling = coupling_line[:, None] * coupling_line[None, :]
    self_lesser = second_born(direct[0], direct[1], mirror[2], mirror[3], coupling)
    self_greater = second_born(direct[2], direct[3], mirror[0], mirror[1], coupling)
    self_sites = jnp.stack(
        [self_lesser[0], self_lesser[1], self_greater[0], self_greater[1]]
    ).astype(jnp.bfloat16)
    self_tiles = regroup(gather_tiles(self_sites, row_parts, col_parts)).reshape(
        4, momenta, tile_cells
    )
    inverse_table = jnp.concatenate([cosines, sines], axis=0)
    spectral_terms = jnp.einsum(
        "cum,ju->cjm", self_tiles, inverse_table, preferred_element_type=jnp.float32
    )
    self_spectral = jnp.stack(
        [
            (spectral_terms[0, :momenta] + spectral_terms[1, momenta:]) * norm_factor,
            (spectral_terms[1, :momenta] - spectral_terms[0, momenta:]) * norm_factor,
            (spectral_terms[2, :momenta] + spectral_terms[3, momenta:]) * norm_factor,
            (spectral_terms[3, :momenta] - spectral_terms[2, momenta:]) * norm_factor,
        ]
    ).astype(jnp.bfloat16)
    self_moment = spread_times(
        regroup(pack_blocks(self_spectral, row_parts, col_parts)), tile_rows, tile_cols
    )
    lower_mask = time_steps[None, :] <= time_steps[:, None]
    upper_mask = time_steps[:, None] <= time_steps[None, :]
    retarded = jnp.where(
        lower_mask, self_moment[2:4].astype(jnp.float32) - self_moment[0:2].astype(jnp.float32), 0.0
    ).astype(jnp.bfloat16)
    advanced = jnp.where(
        upper_mask,
        green_moment[0:2].astype(jnp.float32) - green_moment[2:4].astype(jnp.float32),
        0.0,
    ).astype(jnp.bfloat16)
    lesser_out = collide(
        retarded[0],
        retarded[1],
        self_moment[0],
        self_moment[1],
        green_moment[0],
        green_moment[1],
        advanced[0],
        advanced[1],
    )
    greater_out = collide(
        retarded[0],
        retarded[1],
        self_moment[2],
        self_moment[3],
        green_moment[2],
        green_moment[3],
        advanced[0],
        advanced[1],
    )
    collisions = (
        jnp.stack([lesser_out[0], lesser_out[1], greater_out[0], greater_out[1]]) * step_size
    ).astype(jnp.bfloat16)
    out_tiles = regroup(gather_tiles(collisions, row_parts, col_parts)).reshape(
        4, momenta, tile_cells
    )
    out_tiles = out_tiles.transpose(0, 2, 1).reshape(4, tile_rows, tile_cols, momenta)
    return (out_tiles[0:2], out_tiles[2:4])


def vmem_params(mebibytes=48):
    return pltpu.CompilerParams(vmem_limit_bytes=mebibytes * 1024 * 1024)


def unread(arrays):
    return [pl.BlockSpec(memory_space=pl.ANY)] * len(arrays)


def whole(count):
    return [pl.BlockSpec(memory_space=pltpu.VMEM)] * count


def weight():
    return pl.CostEstimate(flops=10**11, bytes_accessed=2**20, transcendentals=0)


def scalars():
    return [pl.BlockSpec(memory_space=pltpu.SMEM)]


def spread_kernel(lesser, greater, out, lines):
    _, rows, _, count = lesser.shape
    for g, tile in enumerate((lesser, greater)):
        for t in range(rows):
            slab = jnp.concatenate([tile[0, t], tile[1, t]], axis=0)
            lines[pl.ds(g * rows + t, count, stride=2 * rows), :] = slab.astype(F32).T
    out[...] = lines[...].astype(BF16)


def spread(tiles, first, count):
    _, rows, cols, _ = tiles[0].shape
    height = 2 * rows * LANES
    tile_spec = pl.BlockSpec((2, rows, cols, LANES), lambda p: (0, 0, 0, first // LANES + p))
    return pl.pallas_call(
        spread_kernel,
        grid=(count // LANES,),
        out_shape=pltpu.HBM((count * 2 * rows, 2 * cols), BF16),
        in_specs=[tile_spec, tile_spec],
        out_specs=pl.BlockSpec((height, 2 * cols), lambda p: (p, 0)),
        scratch_shapes=[pltpu.VMEM((height, 2 * cols), F32)],
        compiler_params=vmem_params(58),
        name="spread",
    )(*tiles)


def collect_kernel(blocks_ref, lesser, greater, lines):
    _, rows, cols, count = lesser.shape
    blocks, height, _ = blocks_ref.shape
    for block in range(blocks):
        lines[block * height : (block + 1) * height] = blocks_ref[block].astype(F32)
    for k in range(2 * rows):
        slab = lines[pl.ds(k, count, stride=2 * rows), :].T.astype(BF16)
        out = lesser if k < rows else greater
        out[0, k % rows] = slab[:cols]
        out[1, k % rows] = slab[cols:]


def collect(blocks, tile_shape):
    shape = jax.ShapeDtypeStruct(tile_shape, BF16)
    sources, lines, lanes = blocks.shape
    height = lines // PARTS
    block_shape = tile_shape[:3] + (tile_shape[3] // PARTS,)
    tile_spec = pl.BlockSpec(block_shape, lambda p: (0, 0, 0, p))
    return pl.pallas_call(
        collect_kernel,
        grid=(PARTS,),
        out_shape=(shape, shape),
        in_specs=[pl.BlockSpec((sources, height, lanes), lambda p: (0, p, 0))],
        out_specs=(tile_spec, tile_spec),
        scratch_shapes=[pltpu.VMEM((sources * height, lanes), F32)],
        compiler_params=vmem_params(),
        name="collect",
    )(blocks)


def table_kernel(column_ref, table, inverse):
    momenta = column_ref.shape[0]
    positions = lax.broadcasted_iota(jnp.int32, (momenta, momenta), 1)
    phases = (column_ref[...] * positions % momenta).astype(F32) * (2.0 * math.pi / momenta)
    cosines = jnp.cos(phases).astype(BF16)
    sines = jnp.sin(phases).astype(BF16)
    inverse[:momenta, :momenta] = cosines
    inverse[:momenta, momenta:] = sines
    inverse[momenta:, :momenta] = -sines
    inverse[momenta:, momenta:] = cosines
    cosines = cosines.astype(F32).T.astype(BF16)
    sines = sines.astype(F32).T.astype(BF16)
    table[:momenta, :momenta] = cosines
    table[:momenta, momenta:] = -sines
    table[momenta:, :momenta] = sines
    table[momenta:, momenta:] = cosines


def make_tables(lattice_map):
    momenta = lattice_map.shape[0]
    shape = jax.ShapeDtypeStruct((2 * momenta, 2 * momenta), BF16)
    return pl.pallas_call(
        table_kernel,
        out_shape=(shape, shape),
        in_specs=whole(1),
        out_specs=tuple(whole(2)),
        compiler_params=vmem_params(),
        name="make_tables",
    )(lattice_map[:, None])


def site_kernel(norm_factor, lesser, greater, table, *rest):
    out = rest[-1]
    _, rows, cols, _ = lesser.shape
    wide = 4 * cols
    for pair in range(rows // 2):
        slabs = [
            jnp.concatenate([tile[0, t], tile[1, t]], axis=1)
            for t in (2 * pair, 2 * pair + 1)
            for tile in (lesser, greater)
        ]
        product = lax.dot_general(
            table[...],
            jnp.concatenate(slabs, axis=0),
            (((1,), (1,)), ((), ())),
            preferred_element_type=F32,
        )
        out[:, pair * wide : (pair + 1) * wide] = (product * norm_factor).astype(BF16)


def to_sites(tiles, table, norm_factor, after):
    _, rows, cols, momenta = tiles[0].shape
    return pl.pallas_call(
        functools.partial(site_kernel, norm_factor),
        out_shape=jax.ShapeDtypeStruct((2 * momenta, rows * 2 * cols), BF16),
        in_specs=whole(3) + unread(after),
        out_specs=whole(1)[0],
        compiler_params=vmem_params(24),
        name="to_sites",
    )(*tiles, table, *after)


def cross_kernel(rows, half_ref, own, far, *rest):
    out, mark = rest[-2:]
    mark[...] = jnp.zeros_like(mark)
    half = half_ref[0]
    blocks = far.shape[0]
    cols = blocks * rows
    for at in range(far.shape[1] // (2 * rows)):
        span = slice(at * 2 * rows, (at + 1) * 2 * rows)
        for source, offset, target in ((own, half * blocks, half), (far, 0, 1 - half)):
            loaded = [source[offset + block, span].astype(F32) for block in range(blocks)]
            stacked = jnp.concatenate(
                [lines[rows:] for lines in loaded] + [lines[:rows] for lines in loaded], axis=0
            )
            turned = stacked.T
            for block in range(blocks):
                out[target * blocks + block, span] = jnp.concatenate(
                    [
                        turned[block * rows : (block + 1) * rows],
                        turned[cols + block * rows : cols + (block + 1) * rows],
                    ],
                    axis=0,
                ).astype(BF16)


def to_crossed(half, own, far, rows, after, cost):
    sources, lines, lanes = own.shape
    blocks = far.shape[0]
    step = lines // STEPS
    spec = pl.BlockSpec((sources, step, lanes), lambda p: (0, p, 0))
    far_spec = pl.BlockSpec((blocks, step, lanes), lambda p: (0, p, 0))
    return pl.pallas_call(
        functools.partial(cross_kernel, rows),
        grid=(STEPS,),
        out_shape=(
            pltpu.HBM(own.shape, BF16),
            jax.ShapeDtypeStruct((8, LANES), F32),
        ),
        in_specs=scalars() + [spec, far_spec] + unread(after),
        out_specs=(spec, pl.BlockSpec((8, LANES), lambda p: (0, 0))),
        compiler_params=vmem_params(),
        cost_estimate=cost,
        name="to_crossed",
    )(half, own, far, *after)


def gate_kernel(*refs):
    del refs


def gate(array, after):
    return pl.pallas_call(
        gate_kernel,
        out_shape=jax.ShapeDtypeStruct(array.shape, array.dtype),
        in_specs=unread([array, *after]),
        out_specs=unread([array])[0],
        input_output_aliases={0: 0},
        name="gate",
    )(array, *after)


def mirrored_term(columns, read, first, count):
    wide = columns.shape[1] // 2
    rights = []
    for t in (first, first + 1):
        real = read[pl.ds(t, wide, stride=2 * count), :]
        imaginary = -read[pl.ds(count + t, wide, stride=2 * count), :]
        rights.append(jnp.concatenate([real, imaginary], axis=0).astype(BF16))
    return jnp.dot(columns, jnp.concatenate(rights, axis=1), preferred_element_type=F32)


def part_columns(table, part, parts):
    momenta = table.shape[1] // 2
    width = momenta // parts
    return jnp.concatenate(
        [
            table[:, part * width : (part + 1) * width],
            table[:, momenta + part * width : momenta + (part + 1) * width],
        ],
        axis=1,
    )


def mirror_kernel(part, parts, count, crossed, table, inverse, out, columns, handed, read):
    read[...] = crossed[...].astype(F32)
    wide = 2 * crossed.shape[1]
    own = part_columns(table, part, parts)
    for pair in range(count // 2):
        out[:, pair * wide : (pair + 1) * wide] = mirrored_term(own, read, 2 * pair, count)
    columns[...] = part_columns(table, parts - 1, parts)
    handed[...] = inverse[...]


def to_mirror(crossed, table, inverse, part, parts, count):
    lines, lanes = crossed.shape
    size = table.shape[0]
    return pl.pallas_call(
        functools.partial(mirror_kernel, part, parts, count),
        out_shape=(
            jax.ShapeDtypeStruct((size, count * lanes), F32),
            jax.ShapeDtypeStruct((size, size // parts), BF16),
            jax.ShapeDtypeStruct((size, size), BF16),
        ),
        in_specs=whole(3),
        out_specs=tuple(whole(3)),
        scratch_shapes=[pltpu.VMEM((lines, lanes), F32)],
        compiler_params=vmem_params(24),
        name="to_mirror",
    )(crossed, table, inverse)


def sigma_kernel(
    norm_factor, mirror, crossed, sites, columns, inverse, coupling, out, read, written
):
    count = coupling.shape[0]
    momenta = inverse.shape[0] // 2
    read[...] = crossed[...].astype(F32)
    for first in range(0, count, 2):
        span = slice(first * LANES, (first + 2) * LANES)
        other = mirrored_term(columns[...], read, first, count) + mirror[:, span]
        other = (other * norm_factor).astype(BF16).astype(F32)
        self_real, self_imaginary = second_born(
            sites[:momenta, span].astype(F32),
            sites[momenta:, span].astype(F32),
            other[:momenta],
            -other[momenta:],
            jnp.concatenate([coupling[t : t + 1] for t in (first, first + 1)], axis=1),
        )
        product = jnp.dot(
            inverse[...],
            jnp.concatenate([self_real, self_imaginary], axis=0).astype(BF16),
            preferred_element_type=F32,
        )
        product = product * norm_factor
        for at in range(2):
            for part in range(2):
                written[pl.ds(part * count + first + at, momenta, stride=2 * count), :] = product[
                    part * momenta : (part + 1) * momenta, at * LANES : (at + 1) * LANES
                ]
    blocks, height, _ = out.shape
    height = height // PARTS
    for part in range(PARTS):
        for block in range(blocks):
            start = (part * blocks + block) * height
            out[block, part * height : (part + 1) * height] = written[
                start : start + height
            ].astype(BF16)


def to_sigma(mirror, crossed, sites, columns, inverse, coupling, norm_factor, blocks):
    lines, lanes = crossed.shape
    return pl.pallas_call(
        functools.partial(sigma_kernel, norm_factor),
        out_shape=pltpu.HBM((blocks, PARTS * lines // blocks, lanes), BF16),
        in_specs=whole(6),
        out_specs=whole(1)[0],
        scratch_shapes=[pltpu.VMEM((lines, lanes), F32), pltpu.VMEM((PARTS * lines, lanes), F32)],
        compiler_params=vmem_params(34),
        name="to_sigma",
    )(mirror, crossed, sites, columns, inverse, coupling)


def rights_kernel(rows, half_ref, own, near_ref, away_ref, *rest):
    out = rest[-1]
    half = half_ref[0]
    blocks = near_ref.shape[0]
    lanes = own.shape[2]
    cols = lanes // 2
    near = half * cols
    away = (1 - half) * cols
    row_at = lax.broadcasted_iota(jnp.int32, (lanes, 2 * lanes), 0)
    inner_times = jnp.where(row_at < cols, near + row_at, away + row_at - cols)
    lane_at = lax.broadcasted_iota(jnp.int32, (lanes, 2 * lanes), 1)
    last_times = jnp.where(lane_at < lanes, near, away) + lane_at % cols
    keep = inner_times <= last_times
    for at in range(out.shape[0]):
        span = slice(at * 2 * rows, (at + 1) * 2 * rows)

        def stacked(read):
            loaded = [read(block).astype(F32) for block in range(blocks)]
            return [
                jnp.concatenate([lines[g * rows : (g + 1) * rows] for lines in loaded], axis=0)
                for g in range(2)
            ]

        own_near = stacked(lambda block: own[half * blocks + block, span])
        own_away = stacked(lambda block: own[(1 - half) * blocks + block, span])
        far_near = stacked(lambda block: near_ref[block, span])
        far_away = stacked(lambda block: away_ref[0, block, span])
        greens = [
            jnp.concatenate(
                [
                    jnp.concatenate([own_near[g], own_away[g]], axis=1),
                    jnp.concatenate([far_near[g], far_away[g]], axis=1),
                ],
                axis=0,
            )
            for g in range(2)
        ]
        out[at, :lanes] = greens[0].astype(BF16)
        out[at, lanes : 2 * lanes] = greens[1].astype(BF16)
        out[at, 2 * lanes :] = jnp.where(keep, greens[0] - greens[1], 0.0).astype(BF16)


STEPS = 4
PARTS = 2


def make_rights(half, own, far_near, far_away, rows, part, before):
    sources, lines, lanes = own.shape
    blocks = far_near.shape[0]
    steps = STEPS // PARTS
    step = lines // steps
    momenta = step // (2 * rows)
    return pl.pallas_call(
        functools.partial(rights_kernel, rows),
        grid=(steps,),
        out_shape=jax.ShapeDtypeStruct((STEPS * momenta, 3 * lanes, 2 * lanes), BF16),
        in_specs=scalars()
        + [
            pl.BlockSpec((sources, step, lanes), lambda p: (0, p, 0)),
            pl.BlockSpec((blocks, step, lanes), lambda p: (0, p, 0)),
            pl.BlockSpec((1, blocks, step, lanes), lambda p: (part, 0, p, 0)),
        ]
        + unread(before),
        out_specs=pl.BlockSpec(
            (momenta, 3 * lanes, 2 * lanes), lambda p: (part * steps + p, 0, 0)
        ),
        input_output_aliases={4: 0} if part > 0 else {},
        compiler_params=vmem_params(),
        cost_estimate=weight(),
        name="make_rights",
    )(half, own, far_near, far_away, *before)


def volterra_kernel(rows, half_ref, sigma, rights, out):
    half = half_ref[0]
    blocks = sigma.shape[0] // 2
    lanes = sigma.shape[2]
    cols = lanes // 2
    near = half * cols
    away = (1 - half) * cols
    here = half * blocks
    there = (1 - half) * blocks
    first_times = near + lax.broadcasted_iota(jnp.int32, (cols, lanes), 0)
    left_lane = lax.broadcasted_iota(jnp.int32, (cols, lanes), 1)
    low_lanes = left_lane < cols
    left_times = jnp.where(low_lanes, near + left_lane, away + left_lane - cols)
    keep_left = left_times <= first_times
    for at in range(rights.shape[0]):
        span = slice(at * 2 * rows, (at + 1) * 2 * rows)

        def stacked(offset):
            loaded = [sigma[offset + block, span].astype(F32) for block in range(blocks)]
            return [
                jnp.concatenate([lines[part * rows : (part + 1) * rows] for lines in loaded], axis=0)
                for part in range(2)
            ]

        sigma_near = stacked(here)
        sigma_away = stacked(there)
        retarded = []
        lefts = [[], []]
        for part in range(2):
            lesser = jnp.where(
                low_lanes, sigma_near[part], pltpu.roll(sigma_away[part], cols, 1)
            )
            greater = jnp.where(
                low_lanes, pltpu.roll(sigma_near[part], cols, 1), sigma_away[part]
            )
            retarded.append(jnp.where(keep_left, greater - lesser, 0.0))
            lefts[0].append(lesser)
            lefts[1].append(greater)
        retarded = jnp.concatenate(retarded, axis=0).astype(BF16)
        results = []
        for g in range(2):
            left = jnp.concatenate(
                [retarded, jnp.concatenate(lefts[g], axis=0).astype(BF16)], axis=1
            )
            right = jnp.concatenate(
                [rights[at, g * lanes : (g + 1) * lanes], rights[at, 2 * lanes :]], axis=0
            )
            product = jnp.dot(left, right, preferred_element_type=F32)
            sides = []
            for side in range(2):
                straight = product[:cols, side * lanes : (side + 1) * lanes]
                turned = pltpu.roll(product[cols:, side * lanes : (side + 1) * lanes], cols, 1)
                sides.append((straight + jnp.where(low_lanes, -turned, turned)) * step_size)
            results.append(sides)
        for block in range(blocks):
            lines = slice(block * rows, (block + 1) * rows)
            for side, offset in enumerate((here, there)):
                out[offset + block, span] = jnp.concatenate(
                    [results[0][side][lines], results[1][side][lines]], axis=0
                ).astype(BF16)


def volterra(half, sigma, rights, rows):
    sources, lines, lanes = sigma.shape
    step = lines // STEPS
    momenta = step // (2 * rows)
    spec = pl.BlockSpec((sources, step, lanes), lambda p: (0, p, 0))
    return pl.pallas_call(
        functools.partial(volterra_kernel, rows),
        grid=(STEPS,),
        out_shape=jax.ShapeDtypeStruct(sigma.shape, BF16),
        in_specs=scalars()
        + [spec, pl.BlockSpec((momenta, 3 * lanes, 2 * lanes), lambda p: (p, 0, 0))],
        out_specs=spec,
        compiler_params=vmem_params(),
        name="volterra",
    )(half, sigma, rights)


def halved_body(green_lesser, green_greater, lattice_map, time_offset):
    _, rows, cols, momenta = green_lesser.shape
    half = lax.axis_index("half")
    line = lax.axis_index("line")
    side = lax.axis_index("tcol")
    lines = lax.axis_size("line")
    group = lines * lax.axis_size("tcol")
    window = rows * lines * lax.axis_size("half")
    norm_factor = 1.0 / math.sqrt(momenta)
    tiles = (green_lesser, green_greater)
    half_at = half[None]
    count = momenta // PARTS

    def exchange(blocks):
        return lax.all_to_all(blocks, ("tcol", "line"), 0, 0, tiled=True)

    def blocked(rows_array):
        return rows_array.reshape(group, rows_array.shape[0] // group, rows_array.shape[1])

    def swap(array):
        return lax.ppermute(array, "half", [(0, 1), (1, 0)])

    table, inverse = make_tables(lattice_map)
    time_steps = jnp.arange(window, dtype=jnp.int32)
    coupling_line = 1.0 + drive_depth * jnp.cos(
        ((time_offset[0] + time_steps) % PERIOD).astype(F32) * (2.0 * math.pi / PERIOD)
    )
    first = lax.dynamic_slice_in_dim(coupling_line, (half * lines + line) * rows, rows)
    second = lax.dynamic_slice_in_dim(coupling_line, side * cols, cols)
    coupling = first[:, None] * jnp.concatenate([second, second])[None, :]

    spread_parts = [spread(tiles, part * count, count) for part in range(PARTS)]
    own = [exchange(blocked(spread_parts[0]))]
    for rows_array in spread_parts[1:]:
        own.append(exchange(gate(blocked(rows_array), [table, coupling])))
    far_near = [swap(lax.dynamic_slice_in_dim(blocks, (1 - half) * lines, lines)) for blocks in own]

    sent = []
    marks = []
    for part in range(PARTS):
        blocks, mark = to_crossed(
            half_at,
            own[part],
            far_near[part],
            rows,
            own[-1:] + marks[-1:],
            weight() if part > 0 else None,
        )
        sent.append(blocks)
        marks.append(mark)
    crossed = [exchange(blocks) for blocks in sent]
    kept = jnp.stack(
        [lax.dynamic_slice_in_dim(blocks, half * lines, lines) for blocks in own]
    )
    far_away = swap(gate(kept, marks[-1:] + crossed[:-1]))
    flat = [blocks.reshape(-1, 2 * cols) for blocks in crossed]
    sites = to_sites(tiles, table, norm_factor, marks[-1:])
    mirror, columns, handed = to_mirror(flat[0], table, inverse, 0, PARTS, rows)
    sigma_rows = to_sigma(mirror, flat[1], sites, columns, handed, coupling, norm_factor, group)
    sigma = exchange(sigma_rows)
    rights = []
    for part in range(PARTS):
        rights = [
            make_rights(
                half_at, own[part], far_near[part], far_away, rows, part, rights + [sigma_rows]
            )
        ]
    returned = exchange(volterra(half_at, sigma, rights[0], rows))
    return collect(returned, green_lesser.shape)


def solution(mesh):
    row_parts = mesh.shape["trow"]
    col_parts = mesh.shape["tcol"]

    def call(green_lesser, green_greater, lattice_map, time_offset):
        window, window_cols, momenta = green_lesser.shape[1:]
        rows = window // row_parts
        cols = window_cols // col_parts
        halved = (
            col_parts == 2
            and row_parts % 2 == 0
            and window == window_cols
            and 2 * cols == LANES
            and cols == rows * (row_parts // 2)
            and rows % 8 == 0
            and momenta % (2 * row_parts * STEPS) == 0
            and momenta % (PARTS * LANES) == 0
        )
        if halved:
            devices = mesh.devices.reshape(2, row_parts // 2, col_parts)
            used = Mesh(devices, ("half", "line", "tcol"))
            spec = P(None, ("half", "line"), "tcol", None)
            inner = halved_body
        else:
            used = mesh
            spec = P(None, "trow", "tcol", None)
            inner = general_body
        return jax.shard_map(
            inner, mesh=used, in_specs=(spec, spec, P(), P()), out_specs=(spec, spec), check_vma=False
        )(green_lesser, green_greater, lattice_map, time_offset)

    return call
```

```python
import functools
import math

import jax
import jax.numpy as jnp
from jax import lax
from jax.experimental import pallas as pl
from jax.experimental.pallas import tpu as pltpu
from jax.sharding import Mesh, PartitionSpec as P

F32 = jnp.float32
BF16 = jnp.bfloat16
LANES = 128

PERIOD = 64


step_size = 0.01
drive_depth = 0.5


def regroup(blocks):
    return lax.all_to_all(
        lax.all_to_all(blocks, "trow", split_axis=1, concat_axis=1, tiled=True),
        "tcol",
        split_axis=2,
        concat_axis=2,
        tiled=True,
    )


def pack_blocks(spectral, row_parts, col_parts):
    stacked, extent, tile_cells = spectral.shape
    return spectral.reshape(
        stacked, row_parts, col_parts, extent // (row_parts * col_parts), tile_cells
    )


def spread_times(blocks, tile_rows, tile_cols):
    stacked, row_parts, col_parts, local_count, tile_cells = blocks.shape
    shaped = blocks.reshape(stacked, row_parts, col_parts, local_count, tile_rows, tile_cols)
    return shaped.transpose(0, 3, 1, 4, 2, 5).reshape(
        stacked, local_count, row_parts * tile_rows, col_parts * tile_cols
    )


def gather_tiles(full, row_parts, col_parts):
    stacked, local_count, window, window_cols = full.shape
    tile_rows = window // row_parts
    tile_cols = window_cols // col_parts
    shaped = full.reshape(stacked, local_count, row_parts, tile_rows, col_parts, tile_cols)
    return shaped.transpose(0, 2, 4, 1, 3, 5).reshape(
        stacked, row_parts, col_parts, local_count, tile_rows * tile_cols
    )


def mirrored(full, keep_pair):
    stacked, local_count, window, window_cols = full.shape
    paired = full.reshape(stacked, local_count // 2, 2, window, window_cols)
    swapped = jnp.where(keep_pair[None, :, None, None, None], paired, paired[:, :, ::-1])
    return jnp.swapaxes(swapped.reshape(stacked, local_count, window, window_cols), 2, 3)


def second_born(first_real, first_imaginary, other_real, other_imaginary, coupling):
    square_real = first_real * first_real - first_imaginary * first_imaginary
    square_imaginary = 2.0 * first_real * first_imaginary
    out_real = coupling * (square_real * other_real - square_imaginary * other_imaginary)
    out_imaginary = coupling * (square_real * other_imaginary + square_imaginary * other_real)
    return (out_real, out_imaginary)


def collide(
    retarded_real,
    retarded_imaginary,
    self_real,
    self_imaginary,
    green_real,
    green_imaginary,
    advanced_real,
    advanced_imaginary,
):
    minus_left = jnp.concatenate(
        [retarded_real, -retarded_imaginary, self_real, -self_imaginary], axis=2
    )
    plus_left = jnp.concatenate(
        [retarded_real, retarded_imaginary, self_real, self_imaginary], axis=2
    )
    real_right = jnp.concatenate(
        [green_real, green_imaginary, advanced_real, advanced_imaginary], axis=1
    )
    imaginary_right = jnp.concatenate(
        [green_imaginary, green_real, advanced_imaginary, advanced_real], axis=1
    )
    out_real = jnp.einsum(
        "kts,ksu->ktu", minus_left, real_right, preferred_element_type=jnp.float32
    )
    out_imaginary = jnp.einsum(
        "kts,ksu->ktu", plus_left, imaginary_right, preferred_element_type=jnp.float32
    )
    return (out_real, out_imaginary)


def general_body(green_lesser, green_greater, lattice_map, time_offset):
    tile_rows = green_lesser.shape[1]
    tile_cols = green_lesser.shape[2]
    momenta = green_lesser.shape[3]
    row_parts = lax.axis_size("trow")
    col_parts = lax.axis_size("tcol")
    window = tile_rows * row_parts
    tile_cells = tile_rows * tile_cols
    local_count = momenta // (row_parts * col_parts)
    norm_factor = 1.0 / math.sqrt(momenta)
    greens = (
        jnp.concatenate([green_lesser, green_greater], axis=0)
        .reshape(4, tile_cells, momenta)
        .transpose(0, 2, 1)
    )
    positions = jnp.arange(momenta, dtype=jnp.int32)
    halves = positions // 2
    site_order = jnp.where(
        positions == 1, momenta // 2, jnp.where(positions % 2 == 0, halves, momenta - halves)
    )
    phases = (lattice_map[:, None] * site_order[None, :] % momenta).astype(jnp.float32) * (
        2.0 * math.pi / momenta
    )
    cosines = jnp.cos(phases).astype(jnp.bfloat16)
    sines = jnp.sin(phases).astype(jnp.bfloat16)
    ahead_blocks = lax.all_to_all(
        lax.all_to_all(
            pack_blocks(greens, row_parts, col_parts),
            "trow",
            split_axis=1,
            concat_axis=1,
            tiled=True,
        ),
        "tcol",
        split_axis=2,
        concat_axis=2,
        tiled=True,
    )
    green_moment = spread_times(ahead_blocks, tile_rows, tile_cols)
    forward_table = jnp.concatenate([cosines, sines], axis=1)
    products = jnp.einsum("cjm,jr->crm", greens, forward_table, preferred_element_type=jnp.float32)
    site_space = jnp.stack(
        [
            (products[0, :momenta] - products[1, momenta:]) * norm_factor,
            (products[0, momenta:] + products[1, :momenta]) * norm_factor,
            (products[2, :momenta] - products[3, momenta:]) * norm_factor,
            (products[2, momenta:] + products[3, :momenta]) * norm_factor,
        ]
    ).astype(jnp.bfloat16)
    site_full = spread_times(
        regroup(pack_blocks(site_space, row_parts, col_parts)), tile_rows, tile_cols
    )
    site_block = lax.axis_index("trow") * col_parts + lax.axis_index("tcol")
    keep_pair = site_block * (local_count // 2) + jnp.arange(local_count // 2, dtype=jnp.int32) == 0
    mirror = mirrored(site_full, keep_pair).astype(jnp.float32)
    direct = site_full.astype(jnp.float32)
    time_steps = jnp.arange(window, dtype=jnp.int32)
    coupling_line = 1.0 + drive_depth * jnp.cos(
        ((time_offset[0] + time_steps) % PERIOD).astype(jnp.float32) * (2.0 * math.pi / PERIOD)
    )
    coupling = coupling_line[:, None] * coupling_line[None, :]
    self_lesser = second_born(direct[0], direct[1], mirror[2], mirror[3], coupling)
    self_greater = second_born(direct[2], direct[3], mirror[0], mirror[1], coupling)
    self_sites = jnp.stack(
        [self_lesser[0], self_lesser[1], self_greater[0], self_greater[1]]
    ).astype(jnp.bfloat16)
    self_tiles = regroup(gather_tiles(self_sites, row_parts, col_parts)).reshape(
        4, momenta, tile_cells
    )
    inverse_table = jnp.concatenate([cosines, sines], axis=0)
    spectral_terms = jnp.einsum(
        "cum,ju->cjm", self_tiles, inverse_table, preferred_element_type=jnp.float32
    )
    self_spectral = jnp.stack(
        [
            (spectral_terms[0, :momenta] + spectral_terms[1, momenta:]) * norm_factor,
            (spectral_terms[1, :momenta] - spectral_terms[0, momenta:]) * norm_factor,
            (spectral_terms[2, :momenta] + spectral_terms[3, momenta:]) * norm_factor,
            (spectral_terms[3, :momenta] - spectral_terms[2, momenta:]) * norm_factor,
        ]
    ).astype(jnp.bfloat16)
    self_moment = spread_times(
        regroup(pack_blocks(self_spectral, row_parts, col_parts)), tile_rows, tile_cols
    )
    lower_mask = time_steps[None, :] <= time_steps[:, None]
    upper_mask = time_steps[:, None] <= time_steps[None, :]
    retarded = jnp.where(
        lower_mask, self_moment[2:4].astype(jnp.float32) - self_moment[0:2].astype(jnp.float32), 0.0
    ).astype(jnp.bfloat16)
    advanced = jnp.where(
        upper_mask,
        green_moment[0:2].astype(jnp.float32) - green_moment[2:4].astype(jnp.float32),
        0.0,
    ).astype(jnp.bfloat16)
    lesser_out = collide(
        retarded[0],
        retarded[1],
        self_moment[0],
        self_moment[1],
        green_moment[0],
        green_moment[1],
        advanced[0],
        advanced[1],
    )
    greater_out = collide(
        retarded[0],
        retarded[1],
        self_moment[2],
        self_moment[3],
        green_moment[2],
        green_moment[3],
        advanced[0],
        advanced[1],
    )
    collisions = (
        jnp.stack([lesser_out[0], lesser_out[1], greater_out[0], greater_out[1]]) * step_size
    ).astype(jnp.bfloat16)
    out_tiles = regroup(gather_tiles(collisions, row_parts, col_parts)).reshape(
        4, momenta, tile_cells
    )
    out_tiles = out_tiles.transpose(0, 2, 1).reshape(4, tile_rows, tile_cols, momenta)
    return (out_tiles[0:2], out_tiles[2:4])


def vmem_params(mebibytes=48):
    return pltpu.CompilerParams(vmem_limit_bytes=mebibytes * 1024 * 1024)


def unread(arrays):
    return [pl.BlockSpec(memory_space=pl.ANY)] * len(arrays)


def whole(count):
    return [pl.BlockSpec(memory_space=pltpu.VMEM)] * count


def weight():
    return pl.CostEstimate(flops=10**11, bytes_accessed=2**20, transcendentals=0)


def scalars():
    return [pl.BlockSpec(memory_space=pltpu.SMEM)]


def spread_kernel(lesser, greater, out, lines):
    _, rows, _, count = lesser.shape
    for g, tile in enumerate((lesser, greater)):
        for t in range(rows):
            slab = jnp.concatenate([tile[0, t], tile[1, t]], axis=0)
            lines[pl.ds(g * rows + t, count, stride=2 * rows), :] = slab.astype(F32).T
    out[...] = lines[...].astype(BF16)


def spread(tiles, first, count):
    _, rows, cols, _ = tiles[0].shape
    height = 2 * rows * LANES
    tile_spec = pl.BlockSpec((2, rows, cols, LANES), lambda p: (0, 0, 0, first // LANES + p))
    return pl.pallas_call(
        spread_kernel,
        grid=(count // LANES,),
        out_shape=pltpu.HBM((count * 2 * rows, 2 * cols), BF16),
        in_specs=[tile_spec, tile_spec],
        out_specs=pl.BlockSpec((height, 2 * cols), lambda p: (p, 0)),
        scratch_shapes=[pltpu.VMEM((height, 2 * cols), F32)],
        compiler_params=vmem_params(58),
        name="spread",
    )(*tiles)


def collect_kernel(blocks_ref, lesser, greater, lines):
    _, rows, cols, count = lesser.shape
    blocks, height, _ = blocks_ref.shape
    for block in range(blocks):
        lines[block * height : (block + 1) * height] = blocks_ref[block].astype(F32)
    for k in range(2 * rows):
        slab = lines[pl.ds(k, count, stride=2 * rows), :].T.astype(BF16)
        out = lesser if k < rows else greater
        out[0, k % rows] = slab[:cols]
        out[1, k % rows] = slab[cols:]


def collect(blocks, tile_shape):
    shape = jax.ShapeDtypeStruct(tile_shape, BF16)
    sources, lines, lanes = blocks.shape
    height = lines // PARTS
    block_shape = tile_shape[:3] + (tile_shape[3] // PARTS,)
    tile_spec = pl.BlockSpec(block_shape, lambda p: (0, 0, 0, p))
    return pl.pallas_call(
        collect_kernel,
        grid=(PARTS,),
        out_shape=(shape, shape),
        in_specs=[pl.BlockSpec((sources, height, lanes), lambda p: (0, p, 0))],
        out_specs=(tile_spec, tile_spec),
        scratch_shapes=[pltpu.VMEM((sources * height, lanes), F32)],
        compiler_params=vmem_params(),
        name="collect",
    )(blocks)


def table_kernel(column_ref, table, inverse):
    momenta = column_ref.shape[0]
    positions = lax.broadcasted_iota(jnp.int32, (momenta, momenta), 1)
    phases = (column_ref[...] * positions % momenta).astype(F32) * (2.0 * math.pi / momenta)
    cosines = jnp.cos(phases).astype(BF16)
    sines = jnp.sin(phases).astype(BF16)
    inverse[:momenta, :momenta] = cosines
    inverse[:momenta, momenta:] = sines
    inverse[momenta:, :momenta] = -sines
    inverse[momenta:, momenta:] = cosines
    cosines = cosines.astype(F32).T.astype(BF16)
    sines = sines.astype(F32).T.astype(BF16)
    table[:momenta, :momenta] = cosines
    table[:momenta, momenta:] = -sines
    table[momenta:, :momenta] = sines
    table[momenta:, momenta:] = cosines


def make_tables(lattice_map):
    momenta = lattice_map.shape[0]
    shape = jax.ShapeDtypeStruct((2 * momenta, 2 * momenta), BF16)
    return pl.pallas_call(
        table_kernel,
        out_shape=(shape, shape),
        in_specs=whole(1),
        out_specs=tuple(whole(2)),
        compiler_params=vmem_params(),
        name="make_tables",
    )(lattice_map[:, None])


def site_kernel(norm_factor, lesser, greater, table, *rest):
    out = rest[-1]
    _, rows, cols, _ = lesser.shape
    wide = 4 * cols
    for pair in range(rows // 2):
        slabs = [
            jnp.concatenate([tile[0, t], tile[1, t]], axis=1)
            for t in (2 * pair, 2 * pair + 1)
            for tile in (lesser, greater)
        ]
        product = lax.dot_general(
            table[...],
            jnp.concatenate(slabs, axis=0),
            (((1,), (1,)), ((), ())),
            preferred_element_type=F32,
        )
        out[:, pair * wide : (pair + 1) * wide] = (product * norm_factor).astype(BF16)


def to_sites(tiles, table, norm_factor, after):
    _, rows, cols, momenta = tiles[0].shape
    return pl.pallas_call(
        functools.partial(site_kernel, norm_factor),
        out_shape=jax.ShapeDtypeStruct((2 * momenta, rows * 2 * cols), BF16),
        in_specs=whole(3) + unread(after),
        out_specs=whole(1)[0],
        compiler_params=vmem_params(24),
        name="to_sites",
    )(*tiles, table, *after)


def cross_kernel(rows, half_ref, own, far, *rest):
    out, mark = rest[-2:]
    mark[...] = jnp.zeros_like(mark)
    half = half_ref[0]
    blocks = far.shape[0]
    cols = blocks * rows
    for at in range(far.shape[1] // (2 * rows)):
        span = slice(at * 2 * rows, (at + 1) * 2 * rows)
        for source, offset, target in ((own, half * blocks, half), (far, 0, 1 - half)):
            loaded = [source[offset + block, span].astype(F32) for block in range(blocks)]
            stacked = jnp.concatenate(
                [lines[rows:] for lines in loaded] + [lines[:rows] for lines in loaded], axis=0
            )
            turned = stacked.T
            for block in range(blocks):
                out[target * blocks + block, span] = jnp.concatenate(
                    [
                        turned[block * rows : (block + 1) * rows],
                        turned[cols + block * rows : cols + (block + 1) * rows],
                    ],
                    axis=0,
                ).astype(BF16)


def to_crossed(half, own, far, rows, after, cost):
    sources, lines, lanes = own.shape
    blocks = far.shape[0]
    step = lines // STEPS
    spec = pl.BlockSpec((sources, step, lanes), lambda p: (0, p, 0))
    far_spec = pl.BlockSpec((blocks, step, lanes), lambda p: (0, p, 0))
    return pl.pallas_call(
        functools.partial(cross_kernel, rows),
        grid=(STEPS,),
        out_shape=(
            pltpu.HBM(own.shape, BF16),
            jax.ShapeDtypeStruct((8, LANES), F32),
        ),
        in_specs=scalars() + [spec, far_spec] + unread(after),
        out_specs=(spec, pl.BlockSpec((8, LANES), lambda p: (0, 0))),
        compiler_params=vmem_params(),
        cost_estimate=cost,
        name="to_crossed",
    )(half, own, far, *after)


def gate_kernel(*refs):
    del refs


def gate(array, after):
    return pl.pallas_call(
        gate_kernel,
        out_shape=jax.ShapeDtypeStruct(array.shape, array.dtype),
        in_specs=unread([array, *after]),
        out_specs=unread([array])[0],
        input_output_aliases={0: 0},
        name="gate",
    )(array, *after)


def mirrored_term(columns, read, first, count):
    wide = columns.shape[1] // 2
    rights = []
    for t in (first, first + 1):
        real = read[pl.ds(t, wide, stride=2 * count), :]
        imaginary = -read[pl.ds(count + t, wide, stride=2 * count), :]
        rights.append(jnp.concatenate([real, imaginary], axis=0).astype(BF16))
    return jnp.dot(columns, jnp.concatenate(rights, axis=1), preferred_element_type=F32)


def part_columns(table, part, parts):
    momenta = table.shape[1] // 2
    width = momenta // parts
    return jnp.concatenate(
        [
            table[:, part * width : (part + 1) * width],
            table[:, momenta + part * width : momenta + (part + 1) * width],
        ],
        axis=1,
    )


def mirror_kernel(part, parts, count, crossed, table, out, read):
    read[...] = crossed[...].astype(F32)
    wide = 2 * crossed.shape[1]
    columns = part_columns(table, part, parts)
    for pair in range(count // 2):
        out[:, pair * wide : (pair + 1) * wide] = mirrored_term(columns, read, 2 * pair, count)


def to_mirror(crossed, table, part, parts, count):
    lines, lanes = crossed.shape
    return pl.pallas_call(
        functools.partial(mirror_kernel, part, parts, count),
        out_shape=pltpu.HBM((table.shape[0], count * lanes), F32),
        in_specs=whole(2),
        out_specs=whole(1)[0],
        scratch_shapes=[pltpu.VMEM((lines, lanes), F32)],
        compiler_params=vmem_params(),
        name="to_mirror",
    )(crossed, table)


def sigma_kernel(
    norm_factor,
    coupling,
    mirror_from,
    crossed_from,
    sites_from,
    table_from,
    inverse_from,
    out,
    mirror,
    crossed,
    sites,
    columns,
    inverse,
    staged,
    read,
    written,
    sems,
):
    count = coupling.shape[0]
    momenta = inverse.shape[0] // 2
    width = columns.shape[1] // 2

    def column_load(at):
        return pltpu.make_async_copy(
            table_from.at[:, pl.ds((at * PARTS + PARTS - 1) * width, width)],
            columns.at[:, pl.ds(at * width, width)],
            sems.at[1 + at],
        )

    crossed_load = pltpu.make_async_copy(crossed_from, crossed, sems.at[0])
    column_loads = [column_load(0), column_load(1)]
    mirror_load = pltpu.make_async_copy(mirror_from, mirror, sems.at[3])
    sites_load = pltpu.make_async_copy(sites_from, sites, sems.at[4])
    inverse_load = pltpu.make_async_copy(inverse_from, inverse, sems.at[5])
    crossed_load.start()
    for load in column_loads:
        load.start()
    crossed_load.wait()
    mirror_load.start()
    sites_load.start()
    inverse_load.start()
    read[...] = crossed[...].astype(F32)
    for load in column_loads:
        load.wait()
    for first in range(0, count, 2):
        span = slice(first * LANES, (first + 2) * LANES)
        other = mirrored_term(columns[...], read, first, count)
        if first == 0:
            mirror_load.wait()
            sites_load.wait()
        other = other + mirror[:, span]
        other = (other * norm_factor).astype(BF16).astype(F32)
        self_real, self_imaginary = second_born(
            sites[:momenta, span].astype(F32),
            sites[momenta:, span].astype(F32),
            other[:momenta],
            -other[momenta:],
            jnp.concatenate([coupling[t : t + 1] for t in (first, first + 1)], axis=1),
        )
        if first == 0:
            inverse_load.wait()
        product = jnp.dot(
            inverse[...],
            jnp.concatenate([self_real, self_imaginary], axis=0).astype(BF16),
            preferred_element_type=F32,
        )
        product = product * norm_factor
        for at in range(2):
            for part in range(2):
                written[pl.ds(part * count + first + at, momenta, stride=2 * count), :] = product[
                    part * momenta : (part + 1) * momenta, at * LANES : (at + 1) * LANES
                ]
    blocks, height, _ = out.shape
    height = height // PARTS
    stores = []
    for part in range(PARTS):
        lines = pl.ds(part * height, height)
        for block in range(blocks):
            start = (part * blocks + block) * height
            staged[part, block] = written[start : start + height].astype(BF16)
        store = pltpu.make_async_copy(staged.at[part], out.at[:, lines], sems.at[6 + part])
        store.start()
        stores.append(store)
    for store in stores:
        store.wait()


def to_sigma(mirror, crossed, sites, table, inverse, coupling, norm_factor, blocks):
    lines, lanes = crossed.shape
    size = table.shape[0]
    far = pl.BlockSpec(memory_space=pltpu.HBM)
    return pl.pallas_call(
        functools.partial(sigma_kernel, norm_factor),
        out_shape=pltpu.HBM((blocks, PARTS * lines // blocks, lanes), BF16),
        in_specs=whole(1) + [far] * 5,
        out_specs=far,
        scratch_shapes=[
            pltpu.VMEM(mirror.shape, F32),
            pltpu.VMEM(crossed.shape, BF16),
            pltpu.VMEM(sites.shape, BF16),
            pltpu.VMEM((size, size // PARTS), BF16),
            pltpu.VMEM(inverse.shape, BF16),
            pltpu.VMEM((PARTS, blocks, lines // blocks, lanes), BF16),
            pltpu.VMEM((lines, lanes), F32),
            pltpu.VMEM((PARTS * lines, lanes), F32),
            pltpu.SemaphoreType.DMA((6 + PARTS,)),
        ],
        compiler_params=vmem_params(),
        name="to_sigma",
    )(coupling, mirror, crossed, sites, table, inverse)


def rights_kernel(rows, half_ref, own, near_ref, away_ref, *rest):
    out = rest[-1]
    half = half_ref[0]
    blocks = near_ref.shape[0]
    lanes = own.shape[2]
    cols = lanes // 2
    near = half * cols
    away = (1 - half) * cols
    row_at = lax.broadcasted_iota(jnp.int32, (lanes, 2 * lanes), 0)
    inner_times = jnp.where(row_at < cols, near + row_at, away + row_at - cols)
    lane_at = lax.broadcasted_iota(jnp.int32, (lanes, 2 * lanes), 1)
    last_times = jnp.where(lane_at < lanes, near, away) + lane_at % cols
    keep = inner_times <= last_times
    for at in range(out.shape[0]):
        span = slice(at * 2 * rows, (at + 1) * 2 * rows)

        def stacked(read):
            loaded = [read(block).astype(F32) for block in range(blocks)]
            return [
                jnp.concatenate([lines[g * rows : (g + 1) * rows] for lines in loaded], axis=0)
                for g in range(2)
            ]

        own_near = stacked(lambda block: own[half * blocks + block, span])
        own_away = stacked(lambda block: own[(1 - half) * blocks + block, span])
        far_near = stacked(lambda block: near_ref[block, span])
        far_away = stacked(lambda block: away_ref[0, block, span])
        greens = [
            jnp.concatenate(
                [
                    jnp.concatenate([own_near[g], own_away[g]], axis=1),
                    jnp.concatenate([far_near[g], far_away[g]], axis=1),
                ],
                axis=0,
            )
            for g in range(2)
        ]
        out[at, :lanes] = greens[0].astype(BF16)
        out[at, lanes : 2 * lanes] = greens[1].astype(BF16)
        out[at, 2 * lanes :] = jnp.where(keep, greens[0] - greens[1], 0.0).astype(BF16)


STEPS = 4
PARTS = 2


def make_rights(half, own, far_near, far_away, rows, part, before):
    sources, lines, lanes = own.shape
    blocks = far_near.shape[0]
    steps = STEPS // PARTS
    step = lines // steps
    momenta = step // (2 * rows)
    return pl.pallas_call(
        functools.partial(rights_kernel, rows),
        grid=(steps,),
        out_shape=jax.ShapeDtypeStruct((STEPS * momenta, 3 * lanes, 2 * lanes), BF16),
        in_specs=scalars()
        + [
            pl.BlockSpec((sources, step, lanes), lambda p: (0, p, 0)),
            pl.BlockSpec((blocks, step, lanes), lambda p: (0, p, 0)),
            pl.BlockSpec((1, blocks, step, lanes), lambda p: (part, 0, p, 0)),
        ]
        + unread(before),
        out_specs=pl.BlockSpec(
            (momenta, 3 * lanes, 2 * lanes), lambda p: (part * steps + p, 0, 0)
        ),
        input_output_aliases={4: 0} if part > 0 else {},
        compiler_params=vmem_params(),
        cost_estimate=weight(),
        name="make_rights",
    )(half, own, far_near, far_away, *before)


def volterra_kernel(rows, half_ref, sigma, rights, out):
    half = half_ref[0]
    blocks = sigma.shape[0] // 2
    lanes = sigma.shape[2]
    cols = lanes // 2
    near = half * cols
    away = (1 - half) * cols
    here = half * blocks
    there = (1 - half) * blocks
    first_times = near + lax.broadcasted_iota(jnp.int32, (cols, lanes), 0)
    left_lane = lax.broadcasted_iota(jnp.int32, (cols, lanes), 1)
    low_lanes = left_lane < cols
    left_times = jnp.where(low_lanes, near + left_lane, away + left_lane - cols)
    keep_left = left_times <= first_times
    for at in range(rights.shape[0]):
        span = slice(at * 2 * rows, (at + 1) * 2 * rows)

        def stacked(offset):
            loaded = [sigma[offset + block, span].astype(F32) for block in range(blocks)]
            return [
                jnp.concatenate([lines[part * rows : (part + 1) * rows] for lines in loaded], axis=0)
                for part in range(2)
            ]

        sigma_near = stacked(here)
        sigma_away = stacked(there)
        retarded = []
        lefts = [[], []]
        for part in range(2):
            lesser = jnp.where(
                low_lanes, sigma_near[part], pltpu.roll(sigma_away[part], cols, 1)
            )
            greater = jnp.where(
                low_lanes, pltpu.roll(sigma_near[part], cols, 1), sigma_away[part]
            )
            retarded.append(jnp.where(keep_left, greater - lesser, 0.0))
            lefts[0].append(lesser)
            lefts[1].append(greater)
        retarded = jnp.concatenate(retarded, axis=0).astype(BF16)
        results = []
        for g in range(2):
            left = jnp.concatenate(
                [retarded, jnp.concatenate(lefts[g], axis=0).astype(BF16)], axis=1
            )
            right = jnp.concatenate(
                [rights[at, g * lanes : (g + 1) * lanes], rights[at, 2 * lanes :]], axis=0
            )
            product = jnp.dot(left, right, preferred_element_type=F32)
            sides = []
            for side in range(2):
                straight = product[:cols, side * lanes : (side + 1) * lanes]
                turned = pltpu.roll(product[cols:, side * lanes : (side + 1) * lanes], cols, 1)
                sides.append((straight + jnp.where(low_lanes, -turned, turned)) * step_size)
            results.append(sides)
        for block in range(blocks):
            lines = slice(block * rows, (block + 1) * rows)
            for side, offset in enumerate((here, there)):
                out[offset + block, span] = jnp.concatenate(
                    [results[0][side][lines], results[1][side][lines]], axis=0
                ).astype(BF16)


def volterra(half, sigma, rights, rows):
    sources, lines, lanes = sigma.shape
    step = lines // STEPS
    momenta = step // (2 * rows)
    spec = pl.BlockSpec((sources, step, lanes), lambda p: (0, p, 0))
    return pl.pallas_call(
        functools.partial(volterra_kernel, rows),
        grid=(STEPS,),
        out_shape=jax.ShapeDtypeStruct(sigma.shape, BF16),
        in_specs=scalars()
        + [spec, pl.BlockSpec((momenta, 3 * lanes, 2 * lanes), lambda p: (p, 0, 0))],
        out_specs=spec,
        compiler_params=vmem_params(),
        name="volterra",
    )(half, sigma, rights)


def halved_body(green_lesser, green_greater, lattice_map, time_offset):
    _, rows, cols, momenta = green_lesser.shape
    half = lax.axis_index("half")
    line = lax.axis_index("line")
    side = lax.axis_index("tcol")
    lines = lax.axis_size("line")
    group = lines * lax.axis_size("tcol")
    window = rows * lines * lax.axis_size("half")
    norm_factor = 1.0 / math.sqrt(momenta)
    tiles = (green_lesser, green_greater)
    half_at = half[None]
    count = momenta // PARTS

    def exchange(blocks):
        return lax.all_to_all(blocks, ("tcol", "line"), 0, 0, tiled=True)

    def blocked(rows_array):
        return rows_array.reshape(group, rows_array.shape[0] // group, rows_array.shape[1])

    def swap(array):
        return lax.ppermute(array, "half", [(0, 1), (1, 0)])

    table, inverse = make_tables(lattice_map)
    time_steps = jnp.arange(window, dtype=jnp.int32)
    coupling_line = 1.0 + drive_depth * jnp.cos(
        ((time_offset[0] + time_steps) % PERIOD).astype(F32) * (2.0 * math.pi / PERIOD)
    )
    first = lax.dynamic_slice_in_dim(coupling_line, (half * lines + line) * rows, rows)
    second = lax.dynamic_slice_in_dim(coupling_line, side * cols, cols)
    coupling = first[:, None] * jnp.concatenate([second, second])[None, :]

    spread_parts = [spread(tiles, part * count, count) for part in range(PARTS)]
    own = [exchange(blocked(spread_parts[0]))]
    for rows_array in spread_parts[1:]:
        own.append(exchange(gate(blocked(rows_array), [table, coupling])))
    far_near = [swap(lax.dynamic_slice_in_dim(blocks, (1 - half) * lines, lines)) for blocks in own]

    sent = []
    marks = []
    for part in range(PARTS):
        blocks, mark = to_crossed(
            half_at,
            own[part],
            far_near[part],
            rows,
            own[-1:] + marks[-1:],
            weight() if part > 0 else None,
        )
        sent.append(blocks)
        marks.append(mark)
    crossed = [exchange(blocks) for blocks in sent]
    kept = jnp.stack(
        [lax.dynamic_slice_in_dim(blocks, half * lines, lines) for blocks in own]
    )
    far_away = swap(gate(kept, marks[-1:] + crossed[:-1]))
    flat = [blocks.reshape(-1, 2 * cols) for blocks in crossed]
    sites = to_sites(tiles, table, norm_factor, marks[-1:])
    mirror = to_mirror(flat[0], table, 0, PARTS, rows)
    sigma_rows = to_sigma(mirror, flat[1], sites, table, inverse, coupling, norm_factor, group)
    sigma = exchange(sigma_rows)
    rights = []
    for part in range(PARTS):
        rights = [
            make_rights(
                half_at, own[part], far_near[part], far_away, rows, part, rights + [sigma_rows]
            )
        ]
    returned = exchange(volterra(half_at, sigma, rights[0], rows))
    return collect(returned, green_lesser.shape)


def solution(mesh):
    row_parts = mesh.shape["trow"]
    col_parts = mesh.shape["tcol"]

    def call(green_lesser, green_greater, lattice_map, time_offset):
        window, window_cols, momenta = green_lesser.shape[1:]
        rows = window // row_parts
        cols = window_cols // col_parts
        halved = (
            col_parts == 2
            and row_parts % 2 == 0
            and window == window_cols
            and 2 * cols == LANES
            and cols == rows * (row_parts // 2)
            and rows % 8 == 0
            and momenta % (2 * row_parts * STEPS) == 0
            and momenta % (PARTS * LANES) == 0
        )
        if halved:
            devices = mesh.devices.reshape(2, row_parts // 2, col_parts)
            used = Mesh(devices, ("half", "line", "tcol"))
            spec = P(None, ("half", "line"), "tcol", None)
            inner = halved_body
        else:
            used = mesh
            spec = P(None, "trow", "tcol", None)
            inner = general_body
        return jax.shard_map(
            inner, mesh=used, in_specs=(spec, spec, P(), P()), out_specs=(spec, spec), check_vma=False
        )(green_lesser, green_greater, lattice_map, time_offset)

    return call
```

```python
import functools
import math

import jax
import jax.numpy as jnp
from jax import lax
from jax.experimental import pallas as pl
from jax.experimental.pallas import tpu as pltpu
from jax.sharding import Mesh, PartitionSpec as P

F32 = jnp.float32
BF16 = jnp.bfloat16
LANES = 128

PERIOD = 64


step_size = 0.01
drive_depth = 0.5


def regroup(blocks):
    return lax.all_to_all(
        lax.all_to_all(blocks, "trow", split_axis=1, concat_axis=1, tiled=True),
        "tcol",
        split_axis=2,
        concat_axis=2,
        tiled=True,
    )


def pack_blocks(spectral, row_parts, col_parts):
    stacked, extent, tile_cells = spectral.shape
    return spectral.reshape(
        stacked, row_parts, col_parts, extent // (row_parts * col_parts), tile_cells
    )


def spread_times(blocks, tile_rows, tile_cols):
    stacked, row_parts, col_parts, local_count, tile_cells = blocks.shape
    shaped = blocks.reshape(stacked, row_parts, col_parts, local_count, tile_rows, tile_cols)
    return shaped.transpose(0, 3, 1, 4, 2, 5).reshape(
        stacked, local_count, row_parts * tile_rows, col_parts * tile_cols
    )


def gather_tiles(full, row_parts, col_parts):
    stacked, local_count, window, window_cols = full.shape
    tile_rows = window // row_parts
    tile_cols = window_cols // col_parts
    shaped = full.reshape(stacked, local_count, row_parts, tile_rows, col_parts, tile_cols)
    return shaped.transpose(0, 2, 4, 1, 3, 5).reshape(
        stacked, row_parts, col_parts, local_count, tile_rows * tile_cols
    )


def mirrored(full, keep_pair):
    stacked, local_count, window, window_cols = full.shape
    paired = full.reshape(stacked, local_count // 2, 2, window, window_cols)
    swapped = jnp.where(keep_pair[None, :, None, None, None], paired, paired[:, :, ::-1])
    return jnp.swapaxes(swapped.reshape(stacked, local_count, window, window_cols), 2, 3)


def second_born(first_real, first_imaginary, other_real, other_imaginary, coupling):
    square_real = first_real * first_real - first_imaginary * first_imaginary
    square_imaginary = 2.0 * first_real * first_imaginary
    out_real = coupling * (square_real * other_real - square_imaginary * other_imaginary)
    out_imaginary = coupling * (square_real * other_imaginary + square_imaginary * other_real)
    return (out_real, out_imaginary)


def collide(
    retarded_real,
    retarded_imaginary,
    self_real,
    self_imaginary,
    green_real,
    green_imaginary,
    advanced_real,
    advanced_imaginary,
):
    minus_left = jnp.concatenate(
        [retarded_real, -retarded_imaginary, self_real, -self_imaginary], axis=2
    )
    plus_left = jnp.concatenate(
        [retarded_real, retarded_imaginary, self_real, self_imaginary], axis=2
    )
    real_right = jnp.concatenate(
        [green_real, green_imaginary, advanced_real, advanced_imaginary], axis=1
    )
    imaginary_right = jnp.concatenate(
        [green_imaginary, green_real, advanced_imaginary, advanced_real], axis=1
    )
    out_real = jnp.einsum(
        "kts,ksu->ktu", minus_left, real_right, preferred_element_type=jnp.float32
    )
    out_imaginary = jnp.einsum(
        "kts,ksu->ktu", plus_left, imaginary_right, preferred_element_type=jnp.float32
    )
    return (out_real, out_imaginary)


def general_body(green_lesser, green_greater, lattice_map, time_offset):
    tile_rows = green_lesser.shape[1]
    tile_cols = green_lesser.shape[2]
    momenta = green_lesser.shape[3]
    row_parts = lax.axis_size("trow")
    col_parts = lax.axis_size("tcol")
    window = tile_rows * row_parts
    tile_cells = tile_rows * tile_cols
    local_count = momenta // (row_parts * col_parts)
    norm_factor = 1.0 / math.sqrt(momenta)
    greens = (
        jnp.concatenate([green_lesser, green_greater], axis=0)
        .reshape(4, tile_cells, momenta)
        .transpose(0, 2, 1)
    )
    positions = jnp.arange(momenta, dtype=jnp.int32)
    halves = positions // 2
    site_order = jnp.where(
        positions == 1, momenta // 2, jnp.where(positions % 2 == 0, halves, momenta - halves)
    )
    phases = (lattice_map[:, None] * site_order[None, :] % momenta).astype(jnp.float32) * (
        2.0 * math.pi / momenta
    )
    cosines = jnp.cos(phases).astype(jnp.bfloat16)
    sines = jnp.sin(phases).astype(jnp.bfloat16)
    ahead_blocks = lax.all_to_all(
        lax.all_to_all(
            pack_blocks(greens, row_parts, col_parts),
            "trow",
            split_axis=1,
            concat_axis=1,
            tiled=True,
        ),
        "tcol",
        split_axis=2,
        concat_axis=2,
        tiled=True,
    )
    green_moment = spread_times(ahead_blocks, tile_rows, tile_cols)
    forward_table = jnp.concatenate([cosines, sines], axis=1)
    products = jnp.einsum("cjm,jr->crm", greens, forward_table, preferred_element_type=jnp.float32)
    site_space = jnp.stack(
        [
            (products[0, :momenta] - products[1, momenta:]) * norm_factor,
            (products[0, momenta:] + products[1, :momenta]) * norm_factor,
            (products[2, :momenta] - products[3, momenta:]) * norm_factor,
            (products[2, momenta:] + products[3, :momenta]) * norm_factor,
        ]
    ).astype(jnp.bfloat16)
    site_full = spread_times(
        regroup(pack_blocks(site_space, row_parts, col_parts)), tile_rows, tile_cols
    )
    site_block = lax.axis_index("trow") * col_parts + lax.axis_index("tcol")
    keep_pair = site_block * (local_count // 2) + jnp.arange(local_count // 2, dtype=jnp.int32) == 0
    mirror = mirrored(site_full, keep_pair).astype(jnp.float32)
    direct = site_full.astype(jnp.float32)
    time_steps = jnp.arange(window, dtype=jnp.int32)
    coupling_line = 1.0 + drive_depth * jnp.cos(
        ((time_offset[0] + time_steps) % PERIOD).astype(jnp.float32) * (2.0 * math.pi / PERIOD)
    )
    coupling = coupling_line[:, None] * coupling_line[None, :]
    self_lesser = second_born(direct[0], direct[1], mirror[2], mirror[3], coupling)
    self_greater = second_born(direct[2], direct[3], mirror[0], mirror[1], coupling)
    self_sites = jnp.stack(
        [self_lesser[0], self_lesser[1], self_greater[0], self_greater[1]]
    ).astype(jnp.bfloat16)
    self_tiles = regroup(gather_tiles(self_sites, row_parts, col_parts)).reshape(
        4, momenta, tile_cells
    )
    inverse_table = jnp.concatenate([cosines, sines], axis=0)
    spectral_terms = jnp.einsum(
        "cum,ju->cjm", self_tiles, inverse_table, preferred_element_type=jnp.float32
    )
    self_spectral = jnp.stack(
        [
            (spectral_terms[0, :momenta] + spectral_terms[1, momenta:]) * norm_factor,
            (spectral_terms[1, :momenta] - spectral_terms[0, momenta:]) * norm_factor,
            (spectral_terms[2, :momenta] + spectral_terms[3, momenta:]) * norm_factor,
            (spectral_terms[3, :momenta] - spectral_terms[2, momenta:]) * norm_factor,
        ]
    ).astype(jnp.bfloat16)
    self_moment = spread_times(
        regroup(pack_blocks(self_spectral, row_parts, col_parts)), tile_rows, tile_cols
    )
    lower_mask = time_steps[None, :] <= time_steps[:, None]
    upper_mask = time_steps[:, None] <= time_steps[None, :]
    retarded = jnp.where(
        lower_mask, self_moment[2:4].astype(jnp.float32) - self_moment[0:2].astype(jnp.float32), 0.0
    ).astype(jnp.bfloat16)
    advanced = jnp.where(
        upper_mask,
        green_moment[0:2].astype(jnp.float32) - green_moment[2:4].astype(jnp.float32),
        0.0,
    ).astype(jnp.bfloat16)
    lesser_out = collide(
        retarded[0],
        retarded[1],
        self_moment[0],
        self_moment[1],
        green_moment[0],
        green_moment[1],
        advanced[0],
        advanced[1],
    )
    greater_out = collide(
        retarded[0],
        retarded[1],
        self_moment[2],
        self_moment[3],
        green_moment[2],
        green_moment[3],
        advanced[0],
        advanced[1],
    )
    collisions = (
        jnp.stack([lesser_out[0], lesser_out[1], greater_out[0], greater_out[1]]) * step_size
    ).astype(jnp.bfloat16)
    out_tiles = regroup(gather_tiles(collisions, row_parts, col_parts)).reshape(
        4, momenta, tile_cells
    )
    out_tiles = out_tiles.transpose(0, 2, 1).reshape(4, tile_rows, tile_cols, momenta)
    return (out_tiles[0:2], out_tiles[2:4])


def vmem_params(mebibytes=48):
    return pltpu.CompilerParams(vmem_limit_bytes=mebibytes * 1024 * 1024)


def unread(arrays):
    return [pl.BlockSpec(memory_space=pl.ANY)] * len(arrays)


def whole(count):
    return [pl.BlockSpec(memory_space=pltpu.VMEM)] * count


def weight():
    return pl.CostEstimate(flops=10**11, bytes_accessed=2**20, transcendentals=0)


def scalars():
    return [pl.BlockSpec(memory_space=pltpu.SMEM)]


def spread_kernel(lesser, greater, out, lines):
    _, rows, _, count = lesser.shape
    for g, tile in enumerate((lesser, greater)):
        for t in range(rows):
            slab = jnp.concatenate([tile[0, t], tile[1, t]], axis=0)
            lines[pl.ds(g * rows + t, count, stride=2 * rows), :] = slab.astype(F32).T
    out[...] = lines[...].astype(BF16)


def spread(tiles, first, count):
    _, rows, cols, _ = tiles[0].shape
    height = 2 * rows * LANES
    tile_spec = pl.BlockSpec((2, rows, cols, LANES), lambda p: (0, 0, 0, first // LANES + p))
    return pl.pallas_call(
        spread_kernel,
        grid=(count // LANES,),
        out_shape=pltpu.HBM((count * 2 * rows, 2 * cols), BF16),
        in_specs=[tile_spec, tile_spec],
        out_specs=pl.BlockSpec((height, 2 * cols), lambda p: (p, 0)),
        scratch_shapes=[pltpu.VMEM((height, 2 * cols), F32)],
        compiler_params=vmem_params(58),
        name="spread",
    )(*tiles)


def collect_kernel(blocks_ref, lesser, greater, lines):
    _, rows, cols, count = lesser.shape
    blocks, height, _ = blocks_ref.shape
    for block in range(blocks):
        lines[block * height : (block + 1) * height] = blocks_ref[block].astype(F32)
    for k in range(2 * rows):
        slab = lines[pl.ds(k, count, stride=2 * rows), :].T.astype(BF16)
        out = lesser if k < rows else greater
        out[0, k % rows] = slab[:cols]
        out[1, k % rows] = slab[cols:]


def collect(blocks, tile_shape):
    shape = jax.ShapeDtypeStruct(tile_shape, BF16)
    sources, lines, lanes = blocks.shape
    height = lines // PARTS
    block_shape = tile_shape[:3] + (tile_shape[3] // PARTS,)
    tile_spec = pl.BlockSpec(block_shape, lambda p: (0, 0, 0, p))
    return pl.pallas_call(
        collect_kernel,
        grid=(PARTS,),
        out_shape=(shape, shape),
        in_specs=[pl.BlockSpec((sources, height, lanes), lambda p: (0, p, 0))],
        out_specs=(tile_spec, tile_spec),
        scratch_shapes=[pltpu.VMEM((sources * height, lanes), F32)],
        compiler_params=vmem_params(),
        name="collect",
    )(blocks)


def table_kernel(column_ref, table, inverse):
    momenta = column_ref.shape[0]
    positions = lax.broadcasted_iota(jnp.int32, (momenta, momenta), 1)
    phases = (column_ref[...] * positions % momenta).astype(F32) * (2.0 * math.pi / momenta)
    cosines = jnp.cos(phases).astype(BF16)
    sines = jnp.sin(phases).astype(BF16)
    inverse[:momenta, :momenta] = cosines
    inverse[:momenta, momenta:] = sines
    inverse[momenta:, :momenta] = -sines
    inverse[momenta:, momenta:] = cosines
    cosines = cosines.astype(F32).T.astype(BF16)
    sines = sines.astype(F32).T.astype(BF16)
    table[:momenta, :momenta] = cosines
    table[:momenta, momenta:] = -sines
    table[momenta:, :momenta] = sines
    table[momenta:, momenta:] = cosines


def make_tables(lattice_map):
    momenta = lattice_map.shape[0]
    shape = jax.ShapeDtypeStruct((2 * momenta, 2 * momenta), BF16)
    return pl.pallas_call(
        table_kernel,
        out_shape=(shape, shape),
        in_specs=whole(1),
        out_specs=tuple(whole(2)),
        compiler_params=vmem_params(),
        name="make_tables",
    )(lattice_map[:, None])


def site_kernel(norm_factor, lesser, greater, table, *rest):
    out = rest[-1]
    _, rows, cols, _ = lesser.shape
    wide = 4 * cols
    for pair in range(rows // 2):
        slabs = [
            jnp.concatenate([tile[0, t], tile[1, t]], axis=1)
            for t in (2 * pair, 2 * pair + 1)
            for tile in (lesser, greater)
        ]
        product = lax.dot_general(
            table[...],
            jnp.concatenate(slabs, axis=0),
            (((1,), (1,)), ((), ())),
            preferred_element_type=F32,
        )
        out[:, pair * wide : (pair + 1) * wide] = (product * norm_factor).astype(BF16)


def to_sites(tiles, table, norm_factor, after):
    _, rows, cols, momenta = tiles[0].shape
    return pl.pallas_call(
        functools.partial(site_kernel, norm_factor),
        out_shape=pltpu.HBM((2 * momenta, rows * 2 * cols), BF16),
        in_specs=whole(3) + unread(after),
        out_specs=whole(1)[0],
        compiler_params=vmem_params(24),
        name="to_sites",
    )(*tiles, table, *after)


def cross_kernel(rows, half_ref, own, far, *rest):
    out, mark = rest[-2:]
    mark[...] = jnp.zeros_like(mark)
    half = half_ref[0]
    blocks = far.shape[0]
    cols = blocks * rows
    for at in range(far.shape[1] // (2 * rows)):
        span = slice(at * 2 * rows, (at + 1) * 2 * rows)
        for source, offset, target in ((own, half * blocks, half), (far, 0, 1 - half)):
            loaded = [source[offset + block, span].astype(F32) for block in range(blocks)]
            stacked = jnp.concatenate(
                [lines[rows:] for lines in loaded] + [lines[:rows] for lines in loaded], axis=0
            )
            turned = stacked.T
            for block in range(blocks):
                out[target * blocks + block, span] = jnp.concatenate(
                    [
                        turned[block * rows : (block + 1) * rows],
                        turned[cols + block * rows : cols + (block + 1) * rows],
                    ],
                    axis=0,
                ).astype(BF16)


def to_crossed(half, own, far, rows, after, cost):
    sources, lines, lanes = own.shape
    blocks = far.shape[0]
    step = lines // STEPS
    spec = pl.BlockSpec((sources, step, lanes), lambda p: (0, p, 0))
    far_spec = pl.BlockSpec((blocks, step, lanes), lambda p: (0, p, 0))
    return pl.pallas_call(
        functools.partial(cross_kernel, rows),
        grid=(STEPS,),
        out_shape=(
            pltpu.HBM(own.shape, BF16),
            jax.ShapeDtypeStruct((8, LANES), F32),
        ),
        in_specs=scalars() + [spec, far_spec] + unread(after),
        out_specs=(spec, pl.BlockSpec((8, LANES), lambda p: (0, 0))),
        compiler_params=vmem_params(),
        cost_estimate=cost,
        name="to_crossed",
    )(half, own, far, *after)


def gate_kernel(*refs):
    del refs


def gate(array, after):
    return pl.pallas_call(
        gate_kernel,
        out_shape=jax.ShapeDtypeStruct(array.shape, array.dtype),
        in_specs=unread([array, *after]),
        out_specs=unread([array])[0],
        input_output_aliases={0: 0},
        name="gate",
    )(array, *after)


def mirrored_term(columns, read, first, count):
    wide = columns.shape[1] // 2
    rights = []
    for t in (first, first + 1):
        real = read[pl.ds(t, wide, stride=2 * count), :]
        imaginary = -read[pl.ds(count + t, wide, stride=2 * count), :]
        rights.append(jnp.concatenate([real, imaginary], axis=0).astype(BF16))
    return jnp.dot(columns, jnp.concatenate(rights, axis=1), preferred_element_type=F32)


def part_columns(table, part, parts):
    momenta = table.shape[1] // 2
    width = momenta // parts
    return jnp.concatenate(
        [
            table[:, part * width : (part + 1) * width],
            table[:, momenta + part * width : momenta + (part + 1) * width],
        ],
        axis=1,
    )


def mirror_kernel(part, parts, count, crossed, table, out, read):
    read[...] = crossed[...].astype(F32)
    wide = 2 * crossed.shape[1]
    columns = part_columns(table, part, parts)
    for pair in range(count // 2):
        out[:, pair * wide : (pair + 1) * wide] = mirrored_term(columns, read, 2 * pair, count)


def to_mirror(crossed, table, part, parts, count):
    lines, lanes = crossed.shape
    return pl.pallas_call(
        functools.partial(mirror_kernel, part, parts, count),
        out_shape=pltpu.HBM((table.shape[0], count * lanes), F32),
        in_specs=whole(2),
        out_specs=whole(1)[0],
        scratch_shapes=[pltpu.VMEM((lines, lanes), F32)],
        compiler_params=vmem_params(),
        name="to_mirror",
    )(crossed, table)


def sigma_kernel(
    norm_factor,
    coupling,
    mirror_from,
    crossed_from,
    sites_from,
    table_from,
    inverse_from,
    out,
    mirror,
    crossed,
    sites,
    columns,
    inverse,
    staged,
    read,
    written,
    sems,
):
    count = coupling.shape[0]
    momenta = inverse.shape[0] // 2
    width = columns.shape[1] // 2

    def column_load(at):
        return pltpu.make_async_copy(
            table_from.at[:, pl.ds((at * PARTS + PARTS - 1) * width, width)],
            columns.at[:, pl.ds(at * width, width)],
            sems.at[1 + at],
        )

    crossed_load = pltpu.make_async_copy(crossed_from, crossed, sems.at[0])
    column_loads = [column_load(0), column_load(1)]
    mirror_load = pltpu.make_async_copy(mirror_from, mirror, sems.at[3])
    sites_load = pltpu.make_async_copy(sites_from, sites, sems.at[4])
    inverse_load = pltpu.make_async_copy(inverse_from, inverse, sems.at[5])
    crossed_load.start()
    for load in column_loads:
        load.start()
    crossed_load.wait()
    mirror_load.start()
    sites_load.start()
    inverse_load.start()
    read[...] = crossed[...].astype(F32)
    for load in column_loads:
        load.wait()
    for first in range(0, count, 2):
        span = slice(first * LANES, (first + 2) * LANES)
        other = mirrored_term(columns[...], read, first, count)
        if first == 0:
            mirror_load.wait()
            sites_load.wait()
        other = other + mirror[:, span]
        other = (other * norm_factor).astype(BF16).astype(F32)
        self_real, self_imaginary = second_born(
            sites[:momenta, span].astype(F32),
            sites[momenta:, span].astype(F32),
            other[:momenta],
            -other[momenta:],
            jnp.concatenate([coupling[t : t + 1] for t in (first, first + 1)], axis=1),
        )
        if first == 0:
            inverse_load.wait()
        product = jnp.dot(
            inverse[...],
            jnp.concatenate([self_real, self_imaginary], axis=0).astype(BF16),
            preferred_element_type=F32,
        )
        product = product * norm_factor
        for at in range(2):
            for part in range(2):
                written[pl.ds(part * count + first + at, momenta, stride=2 * count), :] = product[
                    part * momenta : (part + 1) * momenta, at * LANES : (at + 1) * LANES
                ]
    blocks, height, _ = out.shape
    height = height // PARTS
    stores = []
    for part in range(PARTS):
        lines = pl.ds(part * height, height)
        for block in range(blocks):
            start = (part * blocks + block) * height
            staged[part, block] = written[start : start + height].astype(BF16)
        store = pltpu.make_async_copy(staged.at[part], out.at[:, lines], sems.at[6 + part])
        store.start()
        stores.append(store)
    for store in stores:
        store.wait()


def to_sigma(mirror, crossed, sites, table, inverse, coupling, norm_factor, blocks):
    lines, lanes = crossed.shape
    size = table.shape[0]
    far = pl.BlockSpec(memory_space=pltpu.HBM)
    return pl.pallas_call(
        functools.partial(sigma_kernel, norm_factor),
        out_shape=pltpu.HBM((blocks, PARTS * lines // blocks, lanes), BF16),
        in_specs=whole(1) + [far] * 5,
        out_specs=far,
        scratch_shapes=[
            pltpu.VMEM(mirror.shape, F32),
            pltpu.VMEM(crossed.shape, BF16),
            pltpu.VMEM(sites.shape, BF16),
            pltpu.VMEM((size, size // PARTS), BF16),
            pltpu.VMEM(inverse.shape, BF16),
            pltpu.VMEM((PARTS, blocks, lines // blocks, lanes), BF16),
            pltpu.VMEM((lines, lanes), F32),
            pltpu.VMEM((PARTS * lines, lanes), F32),
            pltpu.SemaphoreType.DMA((6 + PARTS,)),
        ],
        compiler_params=vmem_params(),
        name="to_sigma",
    )(coupling, mirror, crossed, sites, table, inverse)


def rights_kernel(rows, half_ref, own, near_ref, away_ref, *rest):
    out = rest[-1]
    half = half_ref[0]
    blocks = near_ref.shape[0]
    lanes = own.shape[2]
    cols = lanes // 2
    near = half * cols
    away = (1 - half) * cols
    row_at = lax.broadcasted_iota(jnp.int32, (lanes, 2 * lanes), 0)
    inner_times = jnp.where(row_at < cols, near + row_at, away + row_at - cols)
    lane_at = lax.broadcasted_iota(jnp.int32, (lanes, 2 * lanes), 1)
    last_times = jnp.where(lane_at < lanes, near, away) + lane_at % cols
    keep = inner_times <= last_times
    for at in range(out.shape[0]):
        span = slice(at * 2 * rows, (at + 1) * 2 * rows)

        def stacked(read):
            loaded = [read(block).astype(F32) for block in range(blocks)]
            return [
                jnp.concatenate([lines[g * rows : (g + 1) * rows] for lines in loaded], axis=0)
                for g in range(2)
            ]

        own_near = stacked(lambda block: own[half * blocks + block, span])
        own_away = stacked(lambda block: own[(1 - half) * blocks + block, span])
        far_near = stacked(lambda block: near_ref[block, span])
        far_away = stacked(lambda block: away_ref[0, block, span])
        greens = [
            jnp.concatenate(
                [
                    jnp.concatenate([own_near[g], own_away[g]], axis=1),
                    jnp.concatenate([far_near[g], far_away[g]], axis=1),
                ],
                axis=0,
            )
            for g in range(2)
        ]
        out[at, :lanes] = greens[0].astype(BF16)
        out[at, lanes : 2 * lanes] = greens[1].astype(BF16)
        out[at, 2 * lanes :] = jnp.where(keep, greens[0] - greens[1], 0.0).astype(BF16)


STEPS = 4
PARTS = 2


def make_rights(half, own, far_near, far_away, rows, part, before):
    sources, lines, lanes = own.shape
    blocks = far_near.shape[0]
    steps = STEPS // PARTS
    step = lines // steps
    momenta = step // (2 * rows)
    return pl.pallas_call(
        functools.partial(rights_kernel, rows),
        grid=(steps,),
        out_shape=jax.ShapeDtypeStruct((STEPS * momenta, 3 * lanes, 2 * lanes), BF16),
        in_specs=scalars()
        + [
            pl.BlockSpec((sources, step, lanes), lambda p: (0, p, 0)),
            pl.BlockSpec((blocks, step, lanes), lambda p: (0, p, 0)),
            pl.BlockSpec((1, blocks, step, lanes), lambda p: (part, 0, p, 0)),
        ]
        + unread(before),
        out_specs=pl.BlockSpec(
            (momenta, 3 * lanes, 2 * lanes), lambda p: (part * steps + p, 0, 0)
        ),
        input_output_aliases={4: 0} if part > 0 else {},
        compiler_params=vmem_params(),
        cost_estimate=weight(),
        name="make_rights",
    )(half, own, far_near, far_away, *before)


def volterra_kernel(rows, half_ref, sigma, rights, out):
    half = half_ref[0]
    blocks = sigma.shape[0] // 2
    lanes = sigma.shape[2]
    cols = lanes // 2
    near = half * cols
    away = (1 - half) * cols
    here = half * blocks
    there = (1 - half) * blocks
    first_times = near + lax.broadcasted_iota(jnp.int32, (cols, lanes), 0)
    left_lane = lax.broadcasted_iota(jnp.int32, (cols, lanes), 1)
    low_lanes = left_lane < cols
    left_times = jnp.where(low_lanes, near + left_lane, away + left_lane - cols)
    keep_left = left_times <= first_times
    for at in range(rights.shape[0]):
        span = slice(at * 2 * rows, (at + 1) * 2 * rows)

        def stacked(offset):
            loaded = [sigma[offset + block, span].astype(F32) for block in range(blocks)]
            return [
                jnp.concatenate([lines[part * rows : (part + 1) * rows] for lines in loaded], axis=0)
                for part in range(2)
            ]

        sigma_near = stacked(here)
        sigma_away = stacked(there)
        retarded = []
        lefts = [[], []]
        for part in range(2):
            lesser = jnp.where(
                low_lanes, sigma_near[part], pltpu.roll(sigma_away[part], cols, 1)
            )
            greater = jnp.where(
                low_lanes, pltpu.roll(sigma_near[part], cols, 1), sigma_away[part]
            )
            retarded.append(jnp.where(keep_left, greater - lesser, 0.0))
            lefts[0].append(lesser)
            lefts[1].append(greater)
        retarded = jnp.concatenate(retarded, axis=0).astype(BF16)
        results = []
        for g in range(2):
            left = jnp.concatenate(
                [retarded, jnp.concatenate(lefts[g], axis=0).astype(BF16)], axis=1
            )
            right = jnp.concatenate(
                [rights[at, g * lanes : (g + 1) * lanes], rights[at, 2 * lanes :]], axis=0
            )
            product = jnp.dot(left, right, preferred_element_type=F32)
            sides = []
            for side in range(2):
                straight = product[:cols, side * lanes : (side + 1) * lanes]
                turned = pltpu.roll(product[cols:, side * lanes : (side + 1) * lanes], cols, 1)
                sides.append((straight + jnp.where(low_lanes, -turned, turned)) * step_size)
            results.append(sides)
        for block in range(blocks):
            lines = slice(block * rows, (block + 1) * rows)
            for side, offset in enumerate((here, there)):
                out[offset + block, span] = jnp.concatenate(
                    [results[0][side][lines], results[1][side][lines]], axis=0
                ).astype(BF16)


def volterra(half, sigma, rights, rows):
    sources, lines, lanes = sigma.shape
    step = lines // STEPS
    momenta = step // (2 * rows)
    spec = pl.BlockSpec((sources, step, lanes), lambda p: (0, p, 0))
    return pl.pallas_call(
        functools.partial(volterra_kernel, rows),
        grid=(STEPS,),
        out_shape=jax.ShapeDtypeStruct(sigma.shape, BF16),
        in_specs=scalars()
        + [spec, pl.BlockSpec((momenta, 3 * lanes, 2 * lanes), lambda p: (p, 0, 0))],
        out_specs=spec,
        compiler_params=vmem_params(),
        name="volterra",
    )(half, sigma, rights)


def halved_body(green_lesser, green_greater, lattice_map, time_offset):
    _, rows, cols, momenta = green_lesser.shape
    half = lax.axis_index("half")
    line = lax.axis_index("line")
    side = lax.axis_index("tcol")
    lines = lax.axis_size("line")
    group = lines * lax.axis_size("tcol")
    window = rows * lines * lax.axis_size("half")
    norm_factor = 1.0 / math.sqrt(momenta)
    tiles = (green_lesser, green_greater)
    half_at = half[None]
    count = momenta // PARTS

    def exchange(blocks):
        return lax.all_to_all(blocks, ("tcol", "line"), 0, 0, tiled=True)

    def blocked(rows_array):
        return rows_array.reshape(group, rows_array.shape[0] // group, rows_array.shape[1])

    def swap(array):
        return lax.ppermute(array, "half", [(0, 1), (1, 0)])

    table, inverse = make_tables(lattice_map)
    time_steps = jnp.arange(window, dtype=jnp.int32)
    coupling_line = 1.0 + drive_depth * jnp.cos(
        ((time_offset[0] + time_steps) % PERIOD).astype(F32) * (2.0 * math.pi / PERIOD)
    )
    first = lax.dynamic_slice_in_dim(coupling_line, (half * lines + line) * rows, rows)
    second = lax.dynamic_slice_in_dim(coupling_line, side * cols, cols)
    coupling = first[:, None] * jnp.concatenate([second, second])[None, :]

    spread_parts = [spread(tiles, part * count, count) for part in range(PARTS)]
    own = [exchange(blocked(spread_parts[0]))]
    for rows_array in spread_parts[1:]:
        own.append(exchange(gate(blocked(rows_array), [table, coupling])))
    far_near = [swap(lax.dynamic_slice_in_dim(blocks, (1 - half) * lines, lines)) for blocks in own]

    kept = jnp.stack(
        [lax.dynamic_slice_in_dim(blocks, half * lines, lines) for blocks in own]
    )
    sent = []
    marks = []
    for part in range(PARTS):
        blocks, mark = to_crossed(
            half_at,
            own[part],
            far_near[part],
            rows,
            own[-1:] + marks[-1:] + ([kept] if part > 0 else []),
            None,
        )
        sent.append(blocks)
        marks.append(mark)
    crossed = [exchange(blocks) for blocks in sent]
    far_away = swap(gate(kept, marks[-1:] + crossed[:-1]))
    flat = [blocks.reshape(-1, 2 * cols) for blocks in crossed]
    sites = to_sites(tiles, table, norm_factor, marks[-1:])
    mirror = to_mirror(flat[0], table, 0, PARTS, rows)
    sigma_rows = to_sigma(mirror, flat[1], sites, table, inverse, coupling, norm_factor, group)
    sigma = exchange(sigma_rows)
    rights = []
    for part in range(PARTS):
        rights = [
            make_rights(
                half_at, own[part], far_near[part], far_away, rows, part, rights + [sigma_rows]
            )
        ]
    returned = exchange(volterra(half_at, sigma, rights[0], rows))
    return collect(returned, green_lesser.shape)


def solution(mesh):
    row_parts = mesh.shape["trow"]
    col_parts = mesh.shape["tcol"]

    def call(green_lesser, green_greater, lattice_map, time_offset):
        window, window_cols, momenta = green_lesser.shape[1:]
        rows = window // row_parts
        cols = window_cols // col_parts
        halved = (
            col_parts == 2
            and row_parts % 2 == 0
            and window == window_cols
            and 2 * cols == LANES
            and cols == rows * (row_parts // 2)
            and rows % 8 == 0
            and momenta % (2 * row_parts * STEPS) == 0
            and momenta % (PARTS * LANES) == 0
        )
        if halved:
            devices = mesh.devices.reshape(2, row_parts // 2, col_parts)
            used = Mesh(devices, ("half", "line", "tcol"))
            spec = P(None, ("half", "line"), "tcol", None)
            inner = halved_body
        else:
            used = mesh
            spec = P(None, "trow", "tcol", None)
            inner = general_body
        return jax.shard_map(
            inner, mesh=used, in_specs=(spec, spec, P(), P()), out_specs=(spec, spec), check_vma=False
        )(green_lesser, green_greater, lattice_map, time_offset)

    return call
```

```python
import functools
import math

import jax
import jax.numpy as jnp
from jax import lax
from jax.experimental import pallas as pl
from jax.experimental.pallas import tpu as pltpu
from jax.sharding import Mesh, PartitionSpec as P

F32 = jnp.float32
BF16 = jnp.bfloat16
LANES = 128

PERIOD = 64


step_size = 0.01
drive_depth = 0.5


def regroup(blocks):
    return lax.all_to_all(
        lax.all_to_all(blocks, "trow", split_axis=1, concat_axis=1, tiled=True),
        "tcol",
        split_axis=2,
        concat_axis=2,
        tiled=True,
    )


def pack_blocks(spectral, row_parts, col_parts):
    stacked, extent, tile_cells = spectral.shape
    return spectral.reshape(
        stacked, row_parts, col_parts, extent // (row_parts * col_parts), tile_cells
    )


def spread_times(blocks, tile_rows, tile_cols):
    stacked, row_parts, col_parts, local_count, tile_cells = blocks.shape
    shaped = blocks.reshape(stacked, row_parts, col_parts, local_count, tile_rows, tile_cols)
    return shaped.transpose(0, 3, 1, 4, 2, 5).reshape(
        stacked, local_count, row_parts * tile_rows, col_parts * tile_cols
    )


def gather_tiles(full, row_parts, col_parts):
    stacked, local_count, window, window_cols = full.shape
    tile_rows = window // row_parts
    tile_cols = window_cols // col_parts
    shaped = full.reshape(stacked, local_count, row_parts, tile_rows, col_parts, tile_cols)
    return shaped.transpose(0, 2, 4, 1, 3, 5).reshape(
        stacked, row_parts, col_parts, local_count, tile_rows * tile_cols
    )


def mirrored(full, keep_pair):
    stacked, local_count, window, window_cols = full.shape
    paired = full.reshape(stacked, local_count // 2, 2, window, window_cols)
    swapped = jnp.where(keep_pair[None, :, None, None, None], paired, paired[:, :, ::-1])
    return jnp.swapaxes(swapped.reshape(stacked, local_count, window, window_cols), 2, 3)


def second_born(first_real, first_imaginary, other_real, other_imaginary, coupling):
    square_real = first_real * first_real - first_imaginary * first_imaginary
    square_imaginary = 2.0 * first_real * first_imaginary
    out_real = coupling * (square_real * other_real - square_imaginary * other_imaginary)
    out_imaginary = coupling * (square_real * other_imaginary + square_imaginary * other_real)
    return (out_real, out_imaginary)


def collide(
    retarded_real,
    retarded_imaginary,
    self_real,
    self_imaginary,
    green_real,
    green_imaginary,
    advanced_real,
    advanced_imaginary,
):
    minus_left = jnp.concatenate(
        [retarded_real, -retarded_imaginary, self_real, -self_imaginary], axis=2
    )
    plus_left = jnp.concatenate(
        [retarded_real, retarded_imaginary, self_real, self_imaginary], axis=2
    )
    real_right = jnp.concatenate(
        [green_real, green_imaginary, advanced_real, advanced_imaginary], axis=1
    )
    imaginary_right = jnp.concatenate(
        [green_imaginary, green_real, advanced_imaginary, advanced_real], axis=1
    )
    out_real = jnp.einsum(
        "kts,ksu->ktu", minus_left, real_right, preferred_element_type=jnp.float32
    )
    out_imaginary = jnp.einsum(
        "kts,ksu->ktu", plus_left, imaginary_right, preferred_element_type=jnp.float32
    )
    return (out_real, out_imaginary)


def general_body(green_lesser, green_greater, lattice_map, time_offset):
    tile_rows = green_lesser.shape[1]
    tile_cols = green_lesser.shape[2]
    momenta = green_lesser.shape[3]
    row_parts = lax.axis_size("trow")
    col_parts = lax.axis_size("tcol")
    window = tile_rows * row_parts
    tile_cells = tile_rows * tile_cols
    local_count = momenta // (row_parts * col_parts)
    norm_factor = 1.0 / math.sqrt(momenta)
    greens = (
        jnp.concatenate([green_lesser, green_greater], axis=0)
        .reshape(4, tile_cells, momenta)
        .transpose(0, 2, 1)
    )
    positions = jnp.arange(momenta, dtype=jnp.int32)
    halves = positions // 2
    site_order = jnp.where(
        positions == 1, momenta // 2, jnp.where(positions % 2 == 0, halves, momenta - halves)
    )
    phases = (lattice_map[:, None] * site_order[None, :] % momenta).astype(jnp.float32) * (
        2.0 * math.pi / momenta
    )
    cosines = jnp.cos(phases).astype(jnp.bfloat16)
    sines = jnp.sin(phases).astype(jnp.bfloat16)
    ahead_blocks = lax.all_to_all(
        lax.all_to_all(
            pack_blocks(greens, row_parts, col_parts),
            "trow",
            split_axis=1,
            concat_axis=1,
            tiled=True,
        ),
        "tcol",
        split_axis=2,
        concat_axis=2,
        tiled=True,
    )
    green_moment = spread_times(ahead_blocks, tile_rows, tile_cols)
    forward_table = jnp.concatenate([cosines, sines], axis=1)
    products = jnp.einsum("cjm,jr->crm", greens, forward_table, preferred_element_type=jnp.float32)
    site_space = jnp.stack(
        [
            (products[0, :momenta] - products[1, momenta:]) * norm_factor,
            (products[0, momenta:] + products[1, :momenta]) * norm_factor,
            (products[2, :momenta] - products[3, momenta:]) * norm_factor,
            (products[2, momenta:] + products[3, :momenta]) * norm_factor,
        ]
    ).astype(jnp.bfloat16)
    site_full = spread_times(
        regroup(pack_blocks(site_space, row_parts, col_parts)), tile_rows, tile_cols
    )
    site_block = lax.axis_index("trow") * col_parts + lax.axis_index("tcol")
    keep_pair = site_block * (local_count // 2) + jnp.arange(local_count // 2, dtype=jnp.int32) == 0
    mirror = mirrored(site_full, keep_pair).astype(jnp.float32)
    direct = site_full.astype(jnp.float32)
    time_steps = jnp.arange(window, dtype=jnp.int32)
    coupling_line = 1.0 + drive_depth * jnp.cos(
        ((time_offset[0] + time_steps) % PERIOD).astype(jnp.float32) * (2.0 * math.pi / PERIOD)
    )
    coupling = coupling_line[:, None] * coupling_line[None, :]
    self_lesser = second_born(direct[0], direct[1], mirror[2], mirror[3], coupling)
    self_greater = second_born(direct[2], direct[3], mirror[0], mirror[1], coupling)
    self_sites = jnp.stack(
        [self_lesser[0], self_lesser[1], self_greater[0], self_greater[1]]
    ).astype(jnp.bfloat16)
    self_tiles = regroup(gather_tiles(self_sites, row_parts, col_parts)).reshape(
        4, momenta, tile_cells
    )
    inverse_table = jnp.concatenate([cosines, sines], axis=0)
    spectral_terms = jnp.einsum(
        "cum,ju->cjm", self_tiles, inverse_table, preferred_element_type=jnp.float32
    )
    self_spectral = jnp.stack(
        [
            (spectral_terms[0, :momenta] + spectral_terms[1, momenta:]) * norm_factor,
            (spectral_terms[1, :momenta] - spectral_terms[0, momenta:]) * norm_factor,
            (spectral_terms[2, :momenta] + spectral_terms[3, momenta:]) * norm_factor,
            (spectral_terms[3, :momenta] - spectral_terms[2, momenta:]) * norm_factor,
        ]
    ).astype(jnp.bfloat16)
    self_moment = spread_times(
        regroup(pack_blocks(self_spectral, row_parts, col_parts)), tile_rows, tile_cols
    )
    lower_mask = time_steps[None, :] <= time_steps[:, None]
    upper_mask = time_steps[:, None] <= time_steps[None, :]
    retarded = jnp.where(
        lower_mask, self_moment[2:4].astype(jnp.float32) - self_moment[0:2].astype(jnp.float32), 0.0
    ).astype(jnp.bfloat16)
    advanced = jnp.where(
        upper_mask,
        green_moment[0:2].astype(jnp.float32) - green_moment[2:4].astype(jnp.float32),
        0.0,
    ).astype(jnp.bfloat16)
    lesser_out = collide(
        retarded[0],
        retarded[1],
        self_moment[0],
        self_moment[1],
        green_moment[0],
        green_moment[1],
        advanced[0],
        advanced[1],
    )
    greater_out = collide(
        retarded[0],
        retarded[1],
        self_moment[2],
        self_moment[3],
        green_moment[2],
        green_moment[3],
        advanced[0],
        advanced[1],
    )
    collisions = (
        jnp.stack([lesser_out[0], lesser_out[1], greater_out[0], greater_out[1]]) * step_size
    ).astype(jnp.bfloat16)
    out_tiles = regroup(gather_tiles(collisions, row_parts, col_parts)).reshape(
        4, momenta, tile_cells
    )
    out_tiles = out_tiles.transpose(0, 2, 1).reshape(4, tile_rows, tile_cols, momenta)
    return (out_tiles[0:2], out_tiles[2:4])


def vmem_params(mebibytes=48):
    return pltpu.CompilerParams(vmem_limit_bytes=mebibytes * 1024 * 1024)


def unread(arrays):
    return [pl.BlockSpec(memory_space=pl.ANY)] * len(arrays)


def whole(count):
    return [pl.BlockSpec(memory_space=pltpu.VMEM)] * count


def weight():
    return pl.CostEstimate(flops=10**11, bytes_accessed=2**20, transcendentals=0)


def scalars():
    return [pl.BlockSpec(memory_space=pltpu.SMEM)]


def spread_kernel(lesser, greater, out, lines):
    _, rows, _, count = lesser.shape
    for g, tile in enumerate((lesser, greater)):
        for t in range(rows):
            slab = jnp.concatenate([tile[0, t], tile[1, t]], axis=0)
            lines[pl.ds(g * rows + t, count, stride=2 * rows), :] = slab.astype(F32).T
    out[...] = lines[...].astype(BF16)


def spread(tiles, first, count):
    _, rows, cols, _ = tiles[0].shape
    height = 2 * rows * LANES
    tile_spec = pl.BlockSpec((2, rows, cols, LANES), lambda p: (0, 0, 0, first // LANES + p))
    return pl.pallas_call(
        spread_kernel,
        grid=(count // LANES,),
        out_shape=pltpu.HBM((count * 2 * rows, 2 * cols), BF16),
        in_specs=[tile_spec, tile_spec],
        out_specs=pl.BlockSpec((height, 2 * cols), lambda p: (p, 0)),
        scratch_shapes=[pltpu.VMEM((height, 2 * cols), F32)],
        compiler_params=vmem_params(58),
        name="spread",
    )(*tiles)


def collect_kernel(blocks_ref, lesser, greater, lines):
    _, rows, cols, count = lesser.shape
    blocks, height, _ = blocks_ref.shape
    for block in range(blocks):
        lines[block * height : (block + 1) * height] = blocks_ref[block].astype(F32)
    for k in range(2 * rows):
        slab = lines[pl.ds(k, count, stride=2 * rows), :].T.astype(BF16)
        out = lesser if k < rows else greater
        out[0, k % rows] = slab[:cols]
        out[1, k % rows] = slab[cols:]


def collect(blocks, tile_shape):
    shape = jax.ShapeDtypeStruct(tile_shape, BF16)
    sources, lines, lanes = blocks.shape
    height = lines // PARTS
    block_shape = tile_shape[:3] + (tile_shape[3] // PARTS,)
    tile_spec = pl.BlockSpec(block_shape, lambda p: (0, 0, 0, p))
    return pl.pallas_call(
        collect_kernel,
        grid=(PARTS,),
        out_shape=(shape, shape),
        in_specs=[pl.BlockSpec((sources, height, lanes), lambda p: (0, p, 0))],
        out_specs=(tile_spec, tile_spec),
        scratch_shapes=[pltpu.VMEM((sources * height, lanes), F32)],
        compiler_params=vmem_params(),
        name="collect",
    )(blocks)


def table_kernel(column_ref, table, inverse):
    momenta = column_ref.shape[0]
    positions = lax.broadcasted_iota(jnp.int32, (momenta, momenta), 1)
    phases = (column_ref[...] * positions % momenta).astype(F32) * (2.0 * math.pi / momenta)
    cosines = jnp.cos(phases).astype(BF16)
    sines = jnp.sin(phases).astype(BF16)
    inverse[:momenta, :momenta] = cosines
    inverse[:momenta, momenta:] = sines
    inverse[momenta:, :momenta] = -sines
    inverse[momenta:, momenta:] = cosines
    cosines = cosines.astype(F32).T.astype(BF16)
    sines = sines.astype(F32).T.astype(BF16)
    table[:momenta, :momenta] = cosines
    table[:momenta, momenta:] = -sines
    table[momenta:, :momenta] = sines
    table[momenta:, momenta:] = cosines


def make_tables(lattice_map):
    momenta = lattice_map.shape[0]
    shape = pltpu.HBM((2 * momenta, 2 * momenta), BF16)
    return pl.pallas_call(
        table_kernel,
        out_shape=(shape, shape),
        in_specs=whole(1),
        out_specs=tuple(whole(2)),
        compiler_params=vmem_params(),
        name="make_tables",
    )(lattice_map[:, None])


def site_kernel(norm_factor, lesser, greater, table, *rest):
    out = rest[-1]
    _, rows, cols, _ = lesser.shape
    wide = 4 * cols
    for pair in range(rows // 2):
        slabs = [
            jnp.concatenate([tile[0, t], tile[1, t]], axis=1)
            for t in (2 * pair, 2 * pair + 1)
            for tile in (lesser, greater)
        ]
        product = lax.dot_general(
            table[...],
            jnp.concatenate(slabs, axis=0),
            (((1,), (1,)), ((), ())),
            preferred_element_type=F32,
        )
        out[:, pair * wide : (pair + 1) * wide] = (product * norm_factor).astype(BF16)


def to_sites(tiles, table, norm_factor, after):
    _, rows, cols, momenta = tiles[0].shape
    return pl.pallas_call(
        functools.partial(site_kernel, norm_factor),
        out_shape=pltpu.HBM((2 * momenta, rows * 2 * cols), BF16),
        in_specs=whole(3) + unread(after),
        out_specs=whole(1)[0],
        compiler_params=vmem_params(24),
        name="to_sites",
    )(*tiles, table, *after)


def cross_kernel(rows, half_ref, own, far, *rest):
    out, mark = rest[-2:]
    mark[...] = jnp.zeros_like(mark)
    half = half_ref[0]
    blocks = far.shape[0]
    cols = blocks * rows
    for at in range(far.shape[1] // (2 * rows)):
        span = slice(at * 2 * rows, (at + 1) * 2 * rows)
        for source, offset, target in ((own, half * blocks, half), (far, 0, 1 - half)):
            loaded = [source[offset + block, span].astype(F32) for block in range(blocks)]
            stacked = jnp.concatenate(
                [lines[rows:] for lines in loaded] + [lines[:rows] for lines in loaded], axis=0
            )
            turned = stacked.T
            for block in range(blocks):
                out[target * blocks + block, span] = jnp.concatenate(
                    [
                        turned[block * rows : (block + 1) * rows],
                        turned[cols + block * rows : cols + (block + 1) * rows],
                    ],
                    axis=0,
                ).astype(BF16)


def to_crossed(half, own, far, rows, after, cost):
    sources, lines, lanes = own.shape
    blocks = far.shape[0]
    step = lines // STEPS
    spec = pl.BlockSpec((sources, step, lanes), lambda p: (0, p, 0))
    far_spec = pl.BlockSpec((blocks, step, lanes), lambda p: (0, p, 0))
    return pl.pallas_call(
        functools.partial(cross_kernel, rows),
        grid=(STEPS,),
        out_shape=(
            pltpu.HBM(own.shape, BF16),
            jax.ShapeDtypeStruct((8, LANES), F32),
        ),
        in_specs=scalars() + [spec, far_spec] + unread(after),
        out_specs=(spec, pl.BlockSpec((8, LANES), lambda p: (0, 0))),
        compiler_params=vmem_params(),
        cost_estimate=cost,
        name="to_crossed",
    )(half, own, far, *after)


def gate_kernel(*refs):
    del refs


def gate(array, after):
    return pl.pallas_call(
        gate_kernel,
        out_shape=jax.ShapeDtypeStruct(array.shape, array.dtype),
        in_specs=unread([array, *after]),
        out_specs=unread([array])[0],
        input_output_aliases={0: 0},
        name="gate",
    )(array, *after)


def mirrored_term(columns, read, first, count):
    wide = columns.shape[1] // 2
    rights = []
    for t in (first, first + 1):
        real = read[pl.ds(t, wide, stride=2 * count), :]
        imaginary = -read[pl.ds(count + t, wide, stride=2 * count), :]
        rights.append(jnp.concatenate([real, imaginary], axis=0).astype(BF16))
    return jnp.dot(columns, jnp.concatenate(rights, axis=1), preferred_element_type=F32)


def part_columns(table, part, parts):
    momenta = table.shape[1] // 2
    width = momenta // parts
    return jnp.concatenate(
        [
            table[:, part * width : (part + 1) * width],
            table[:, momenta + part * width : momenta + (part + 1) * width],
        ],
        axis=1,
    )


def mirror_kernel(part, parts, count, crossed, table, out, read):
    read[...] = crossed[...].astype(F32)
    wide = 2 * crossed.shape[1]
    columns = part_columns(table, part, parts)
    for pair in range(count // 2):
        out[:, pair * wide : (pair + 1) * wide] = mirrored_term(columns, read, 2 * pair, count)


def to_mirror(crossed, table, part, parts, count):
    lines, lanes = crossed.shape
    return pl.pallas_call(
        functools.partial(mirror_kernel, part, parts, count),
        out_shape=pltpu.HBM((table.shape[0], count * lanes), F32),
        in_specs=whole(2),
        out_specs=whole(1)[0],
        scratch_shapes=[pltpu.VMEM((lines, lanes), F32)],
        compiler_params=vmem_params(),
        name="to_mirror",
    )(crossed, table)


def sigma_kernel(
    norm_factor,
    coupling,
    mirror_from,
    crossed_from,
    sites_from,
    table_from,
    inverse_from,
    out,
    mirror,
    crossed,
    sites,
    columns,
    inverse,
    staged,
    read,
    written,
    sems,
):
    count = coupling.shape[0]
    momenta = inverse.shape[0] // 2
    width = columns.shape[1] // 2

    def column_load(at):
        return pltpu.make_async_copy(
            table_from.at[:, pl.ds((at * PARTS + PARTS - 1) * width, width)],
            columns.at[:, pl.ds(at * width, width)],
            sems.at[1 + at],
        )

    crossed_load = pltpu.make_async_copy(crossed_from, crossed, sems.at[0])
    column_loads = [column_load(0), column_load(1)]
    mirror_load = pltpu.make_async_copy(mirror_from, mirror, sems.at[3])
    sites_load = pltpu.make_async_copy(sites_from, sites, sems.at[4])
    inverse_load = pltpu.make_async_copy(inverse_from, inverse, sems.at[5])
    crossed_load.start()
    for load in column_loads:
        load.start()
    crossed_load.wait()
    mirror_load.start()
    sites_load.start()
    inverse_load.start()
    read[...] = crossed[...].astype(F32)
    for load in column_loads:
        load.wait()
    for first in range(0, count, 2):
        span = slice(first * LANES, (first + 2) * LANES)
        other = mirrored_term(columns[...], read, first, count)
        if first == 0:
            mirror_load.wait()
            sites_load.wait()
        other = other + mirror[:, span]
        other = (other * norm_factor).astype(BF16).astype(F32)
        self_real, self_imaginary = second_born(
            sites[:momenta, span].astype(F32),
            sites[momenta:, span].astype(F32),
            other[:momenta],
            -other[momenta:],
            jnp.concatenate([coupling[t : t + 1] for t in (first, first + 1)], axis=1),
        )
        if first == 0:
            inverse_load.wait()
        product = jnp.dot(
            inverse[...],
            jnp.concatenate([self_real, self_imaginary], axis=0).astype(BF16),
            preferred_element_type=F32,
        )
        product = product * norm_factor
        for at in range(2):
            for part in range(2):
                written[pl.ds(part * count + first + at, momenta, stride=2 * count), :] = product[
                    part * momenta : (part + 1) * momenta, at * LANES : (at + 1) * LANES
                ]
    blocks, height, _ = out.shape
    height = height // PARTS
    stores = []
    for part in range(PARTS):
        lines = pl.ds(part * height, height)
        for block in range(blocks):
            start = (part * blocks + block) * height
            staged[part, block] = written[start : start + height].astype(BF16)
        store = pltpu.make_async_copy(staged.at[part], out.at[:, lines], sems.at[6 + part])
        store.start()
        stores.append(store)
    for store in stores:
        store.wait()


def to_sigma(mirror, crossed, sites, table, inverse, coupling, norm_factor, blocks):
    lines, lanes = crossed.shape
    size = table.shape[0]
    far = pl.BlockSpec(memory_space=pltpu.HBM)
    return pl.pallas_call(
        functools.partial(sigma_kernel, norm_factor),
        out_shape=pltpu.HBM((blocks, PARTS * lines // blocks, lanes), BF16),
        in_specs=whole(1) + [far] * 5,
        out_specs=far,
        scratch_shapes=[
            pltpu.VMEM(mirror.shape, F32),
            pltpu.VMEM(crossed.shape, BF16),
            pltpu.VMEM(sites.shape, BF16),
            pltpu.VMEM((size, size // PARTS), BF16),
            pltpu.VMEM(inverse.shape, BF16),
            pltpu.VMEM((PARTS, blocks, lines // blocks, lanes), BF16),
            pltpu.VMEM((lines, lanes), F32),
            pltpu.VMEM((PARTS * lines, lanes), F32),
            pltpu.SemaphoreType.DMA((6 + PARTS,)),
        ],
        compiler_params=vmem_params(),
        name="to_sigma",
    )(coupling, mirror, crossed, sites, table, inverse)


def rights_kernel(rows, half_ref, own, near_ref, away_ref, *rest):
    out = rest[-1]
    half = half_ref[0]
    blocks = near_ref.shape[0]
    lanes = own.shape[2]
    cols = lanes // 2
    near = half * cols
    away = (1 - half) * cols
    row_at = lax.broadcasted_iota(jnp.int32, (lanes, 2 * lanes), 0)
    inner_times = jnp.where(row_at < cols, near + row_at, away + row_at - cols)
    lane_at = lax.broadcasted_iota(jnp.int32, (lanes, 2 * lanes), 1)
    last_times = jnp.where(lane_at < lanes, near, away) + lane_at % cols
    keep = inner_times <= last_times
    for at in range(out.shape[0]):
        span = slice(at * 2 * rows, (at + 1) * 2 * rows)

        def stacked(read):
            loaded = [read(block).astype(F32) for block in range(blocks)]
            return [
                jnp.concatenate([lines[g * rows : (g + 1) * rows] for lines in loaded], axis=0)
                for g in range(2)
            ]

        own_near = stacked(lambda block: own[half * blocks + block, span])
        own_away = stacked(lambda block: own[(1 - half) * blocks + block, span])
        far_near = stacked(lambda block: near_ref[block, span])
        far_away = stacked(lambda block: away_ref[0, block, span])
        greens = [
            jnp.concatenate(
                [
                    jnp.concatenate([own_near[g], own_away[g]], axis=1),
                    jnp.concatenate([far_near[g], far_away[g]], axis=1),
                ],
                axis=0,
            )
            for g in range(2)
        ]
        out[at, :lanes] = greens[0].astype(BF16)
        out[at, lanes : 2 * lanes] = greens[1].astype(BF16)
        out[at, 2 * lanes :] = jnp.where(keep, greens[0] - greens[1], 0.0).astype(BF16)


STEPS = 4
PARTS = 2


def make_rights(half, own, far_near, far_away, rows, part, before):
    sources, lines, lanes = own.shape
    blocks = far_near.shape[0]
    steps = STEPS // PARTS
    step = lines // steps
    momenta = step // (2 * rows)
    return pl.pallas_call(
        functools.partial(rights_kernel, rows),
        grid=(steps,),
        out_shape=jax.ShapeDtypeStruct((STEPS * momenta, 3 * lanes, 2 * lanes), BF16),
        in_specs=scalars()
        + [
            pl.BlockSpec((sources, step, lanes), lambda p: (0, p, 0)),
            pl.BlockSpec((blocks, step, lanes), lambda p: (0, p, 0)),
            pl.BlockSpec((1, blocks, step, lanes), lambda p: (part, 0, p, 0)),
        ]
        + unread(before),
        out_specs=pl.BlockSpec(
            (momenta, 3 * lanes, 2 * lanes), lambda p: (part * steps + p, 0, 0)
        ),
        input_output_aliases={4: 0} if part > 0 else {},
        compiler_params=vmem_params(),
        cost_estimate=weight(),
        name="make_rights",
    )(half, own, far_near, far_away, *before)


def volterra_kernel(rows, half_ref, sigma, rights, out):
    half = half_ref[0]
    blocks = sigma.shape[0] // 2
    lanes = sigma.shape[2]
    cols = lanes // 2
    near = half * cols
    away = (1 - half) * cols
    here = half * blocks
    there = (1 - half) * blocks
    first_times = near + lax.broadcasted_iota(jnp.int32, (cols, lanes), 0)
    left_lane = lax.broadcasted_iota(jnp.int32, (cols, lanes), 1)
    low_lanes = left_lane < cols
    left_times = jnp.where(low_lanes, near + left_lane, away + left_lane - cols)
    keep_left = left_times <= first_times
    for at in range(rights.shape[0]):
        span = slice(at * 2 * rows, (at + 1) * 2 * rows)

        def stacked(offset):
            loaded = [sigma[offset + block, span].astype(F32) for block in range(blocks)]
            return [
                jnp.concatenate([lines[part * rows : (part + 1) * rows] for lines in loaded], axis=0)
                for part in range(2)
            ]

        sigma_near = stacked(here)
        sigma_away = stacked(there)
        retarded = []
        lefts = [[], []]
        for part in range(2):
            lesser = jnp.where(
                low_lanes, sigma_near[part], pltpu.roll(sigma_away[part], cols, 1)
            )
            greater = jnp.where(
                low_lanes, pltpu.roll(sigma_near[part], cols, 1), sigma_away[part]
            )
            retarded.append(jnp.where(keep_left, greater - lesser, 0.0))
            lefts[0].append(lesser)
            lefts[1].append(greater)
        retarded = jnp.concatenate(retarded, axis=0).astype(BF16)
        results = []
        for g in range(2):
            left = jnp.concatenate(
                [retarded, jnp.concatenate(lefts[g], axis=0).astype(BF16)], axis=1
            )
            right = jnp.concatenate(
                [rights[at, g * lanes : (g + 1) * lanes], rights[at, 2 * lanes :]], axis=0
            )
            product = jnp.dot(left, right, preferred_element_type=F32)
            sides = []
            for side in range(2):
                straight = product[:cols, side * lanes : (side + 1) * lanes]
                turned = pltpu.roll(product[cols:, side * lanes : (side + 1) * lanes], cols, 1)
                sides.append((straight + jnp.where(low_lanes, -turned, turned)) * step_size)
            results.append(sides)
        for block in range(blocks):
            lines = slice(block * rows, (block + 1) * rows)
            for side, offset in enumerate((here, there)):
                out[offset + block, span] = jnp.concatenate(
                    [results[0][side][lines], results[1][side][lines]], axis=0
                ).astype(BF16)


def volterra(half, sigma, rights, rows):
    sources, lines, lanes = sigma.shape
    step = lines // STEPS
    momenta = step // (2 * rows)
    spec = pl.BlockSpec((sources, step, lanes), lambda p: (0, p, 0))
    return pl.pallas_call(
        functools.partial(volterra_kernel, rows),
        grid=(STEPS,),
        out_shape=jax.ShapeDtypeStruct(sigma.shape, BF16),
        in_specs=scalars()
        + [spec, pl.BlockSpec((momenta, 3 * lanes, 2 * lanes), lambda p: (p, 0, 0))],
        out_specs=spec,
        compiler_params=vmem_params(),
        name="volterra",
    )(half, sigma, rights)


def halved_body(green_lesser, green_greater, lattice_map, time_offset):
    _, rows, cols, momenta = green_lesser.shape
    half = lax.axis_index("half")
    line = lax.axis_index("line")
    side = lax.axis_index("tcol")
    lines = lax.axis_size("line")
    group = lines * lax.axis_size("tcol")
    window = rows * lines * lax.axis_size("half")
    norm_factor = 1.0 / math.sqrt(momenta)
    tiles = (green_lesser, green_greater)
    half_at = half[None]
    count = momenta // PARTS

    def exchange(blocks):
        return lax.all_to_all(blocks, ("tcol", "line"), 0, 0, tiled=True)

    def blocked(rows_array):
        return rows_array.reshape(group, rows_array.shape[0] // group, rows_array.shape[1])

    def swap(array):
        return lax.ppermute(array, "half", [(0, 1), (1, 0)])

    table, inverse = make_tables(lattice_map)
    time_steps = jnp.arange(window, dtype=jnp.int32)
    coupling_line = 1.0 + drive_depth * jnp.cos(
        ((time_offset[0] + time_steps) % PERIOD).astype(F32) * (2.0 * math.pi / PERIOD)
    )
    first = lax.dynamic_slice_in_dim(coupling_line, (half * lines + line) * rows, rows)
    second = lax.dynamic_slice_in_dim(coupling_line, side * cols, cols)
    coupling = first[:, None] * jnp.concatenate([second, second])[None, :]

    spread_parts = [spread(tiles, part * count, count) for part in range(PARTS)]
    own = [exchange(blocked(spread_parts[0]))]
    for rows_array in spread_parts[1:]:
        own.append(exchange(gate(blocked(rows_array), [table, coupling])))
    far_near = [swap(lax.dynamic_slice_in_dim(blocks, (1 - half) * lines, lines)) for blocks in own]

    kept = jnp.stack(
        [lax.dynamic_slice_in_dim(blocks, half * lines, lines) for blocks in own]
    )
    sent = []
    marks = []
    for part in range(PARTS):
        blocks, mark = to_crossed(
            half_at,
            own[part],
            far_near[part],
            rows,
            own[-1:] + marks[-1:],
            None,
        )
        sent.append(blocks)
        marks.append(mark)
    crossed = [exchange(blocks) for blocks in sent]
    far_away = swap(gate(kept, marks[-1:] + crossed[:-1]))
    flat = [blocks.reshape(-1, 2 * cols) for blocks in crossed]
    sites = to_sites(tiles, table, norm_factor, marks[-1:])
    mirror = to_mirror(flat[0], table, 0, PARTS, rows)
    sigma_rows = to_sigma(mirror, flat[1], sites, table, inverse, coupling, norm_factor, group)
    sigma = exchange(sigma_rows)
    rights = []
    for part in range(PARTS):
        rights = [
            make_rights(
                half_at, own[part], far_near[part], far_away, rows, part, rights + [sigma_rows]
            )
        ]
    returned = exchange(volterra(half_at, sigma, rights[0], rows))
    return collect(returned, green_lesser.shape)


def solution(mesh):
    row_parts = mesh.shape["trow"]
    col_parts = mesh.shape["tcol"]

    def call(green_lesser, green_greater, lattice_map, time_offset):
        window, window_cols, momenta = green_lesser.shape[1:]
        rows = window // row_parts
        cols = window_cols // col_parts
        halved = (
            col_parts == 2
            and row_parts % 2 == 0
            and window == window_cols
            and 2 * cols == LANES
            and cols == rows * (row_parts // 2)
            and rows % 8 == 0
            and momenta % (2 * row_parts * STEPS) == 0
            and momenta % (PARTS * LANES) == 0
        )
        if halved:
            devices = mesh.devices.reshape(2, row_parts // 2, col_parts)
            used = Mesh(devices, ("half", "line", "tcol"))
            spec = P(None, ("half", "line"), "tcol", None)
            inner = halved_body
        else:
            used = mesh
            spec = P(None, "trow", "tcol", None)
            inner = general_body
        return jax.shard_map(
            inner, mesh=used, in_specs=(spec, spec, P(), P()), out_specs=(spec, spec), check_vma=False
        )(green_lesser, green_greater, lattice_map, time_offset)

    return call
```

```python
import functools
import math

import jax
import jax.numpy as jnp
from jax import lax
from jax.experimental import pallas as pl
from jax.experimental.pallas import tpu as pltpu
from jax.sharding import Mesh, PartitionSpec as P

F32 = jnp.float32
BF16 = jnp.bfloat16
LANES = 128

PERIOD = 64


step_size = 0.01
drive_depth = 0.5


def regroup(blocks):
    return lax.all_to_all(
        lax.all_to_all(blocks, "trow", split_axis=1, concat_axis=1, tiled=True),
        "tcol",
        split_axis=2,
        concat_axis=2,
        tiled=True,
    )


def pack_blocks(spectral, row_parts, col_parts):
    stacked, extent, tile_cells = spectral.shape
    return spectral.reshape(
        stacked, row_parts, col_parts, extent // (row_parts * col_parts), tile_cells
    )


def spread_times(blocks, tile_rows, tile_cols):
    stacked, row_parts, col_parts, local_count, tile_cells = blocks.shape
    shaped = blocks.reshape(stacked, row_parts, col_parts, local_count, tile_rows, tile_cols)
    return shaped.transpose(0, 3, 1, 4, 2, 5).reshape(
        stacked, local_count, row_parts * tile_rows, col_parts * tile_cols
    )


def gather_tiles(full, row_parts, col_parts):
    stacked, local_count, window, window_cols = full.shape
    tile_rows = window // row_parts
    tile_cols = window_cols // col_parts
    shaped = full.reshape(stacked, local_count, row_parts, tile_rows, col_parts, tile_cols)
    return shaped.transpose(0, 2, 4, 1, 3, 5).reshape(
        stacked, row_parts, col_parts, local_count, tile_rows * tile_cols
    )


def mirrored(full, keep_pair):
    stacked, local_count, window, window_cols = full.shape
    paired = full.reshape(stacked, local_count // 2, 2, window, window_cols)
    swapped = jnp.where(keep_pair[None, :, None, None, None], paired, paired[:, :, ::-1])
    return jnp.swapaxes(swapped.reshape(stacked, local_count, window, window_cols), 2, 3)


def second_born(first_real, first_imaginary, other_real, other_imaginary, coupling):
    square_real = first_real * first_real - first_imaginary * first_imaginary
    square_imaginary = 2.0 * first_real * first_imaginary
    out_real = coupling * (square_real * other_real - square_imaginary * other_imaginary)
    out_imaginary = coupling * (square_real * other_imaginary + square_imaginary * other_real)
    return (out_real, out_imaginary)


def collide(
    retarded_real,
    retarded_imaginary,
    self_real,
    self_imaginary,
    green_real,
    green_imaginary,
    advanced_real,
    advanced_imaginary,
):
    minus_left = jnp.concatenate(
        [retarded_real, -retarded_imaginary, self_real, -self_imaginary], axis=2
    )
    plus_left = jnp.concatenate(
        [retarded_real, retarded_imaginary, self_real, self_imaginary], axis=2
    )
    real_right = jnp.concatenate(
        [green_real, green_imaginary, advanced_real, advanced_imaginary], axis=1
    )
    imaginary_right = jnp.concatenate(
        [green_imaginary, green_real, advanced_imaginary, advanced_real], axis=1
    )
    out_real = jnp.einsum(
        "kts,ksu->ktu", minus_left, real_right, preferred_element_type=jnp.float32
    )
    out_imaginary = jnp.einsum(
        "kts,ksu->ktu", plus_left, imaginary_right, preferred_element_type=jnp.float32
    )
    return (out_real, out_imaginary)


def general_body(green_lesser, green_greater, lattice_map, time_offset):
    tile_rows = green_lesser.shape[1]
    tile_cols = green_lesser.shape[2]
    momenta = green_lesser.shape[3]
    row_parts = lax.axis_size("trow")
    col_parts = lax.axis_size("tcol")
    window = tile_rows * row_parts
    tile_cells = tile_rows * tile_cols
    local_count = momenta // (row_parts * col_parts)
    norm_factor = 1.0 / math.sqrt(momenta)
    greens = (
        jnp.concatenate([green_lesser, green_greater], axis=0)
        .reshape(4, tile_cells, momenta)
        .transpose(0, 2, 1)
    )
    positions = jnp.arange(momenta, dtype=jnp.int32)
    halves = positions // 2
    site_order = jnp.where(
        positions == 1, momenta // 2, jnp.where(positions % 2 == 0, halves, momenta - halves)
    )
    phases = (lattice_map[:, None] * site_order[None, :] % momenta).astype(jnp.float32) * (
        2.0 * math.pi / momenta
    )
    cosines = jnp.cos(phases).astype(jnp.bfloat16)
    sines = jnp.sin(phases).astype(jnp.bfloat16)
    ahead_blocks = lax.all_to_all(
        lax.all_to_all(
            pack_blocks(greens, row_parts, col_parts),
            "trow",
            split_axis=1,
            concat_axis=1,
            tiled=True,
        ),
        "tcol",
        split_axis=2,
        concat_axis=2,
        tiled=True,
    )
    green_moment = spread_times(ahead_blocks, tile_rows, tile_cols)
    forward_table = jnp.concatenate([cosines, sines], axis=1)
    products = jnp.einsum("cjm,jr->crm", greens, forward_table, preferred_element_type=jnp.float32)
    site_space = jnp.stack(
        [
            (products[0, :momenta] - products[1, momenta:]) * norm_factor,
            (products[0, momenta:] + products[1, :momenta]) * norm_factor,
            (products[2, :momenta] - products[3, momenta:]) * norm_factor,
            (products[2, momenta:] + products[3, :momenta]) * norm_factor,
        ]
    ).astype(jnp.bfloat16)
    site_full = spread_times(
        regroup(pack_blocks(site_space, row_parts, col_parts)), tile_rows, tile_cols
    )
    site_block = lax.axis_index("trow") * col_parts + lax.axis_index("tcol")
    keep_pair = site_block * (local_count // 2) + jnp.arange(local_count // 2, dtype=jnp.int32) == 0
    mirror = mirrored(site_full, keep_pair).astype(jnp.float32)
    direct = site_full.astype(jnp.float32)
    time_steps = jnp.arange(window, dtype=jnp.int32)
    coupling_line = 1.0 + drive_depth * jnp.cos(
        ((time_offset[0] + time_steps) % PERIOD).astype(jnp.float32) * (2.0 * math.pi / PERIOD)
    )
    coupling = coupling_line[:, None] * coupling_line[None, :]
    self_lesser = second_born(direct[0], direct[1], mirror[2], mirror[3], coupling)
    self_greater = second_born(direct[2], direct[3], mirror[0], mirror[1], coupling)
    self_sites = jnp.stack(
        [self_lesser[0], self_lesser[1], self_greater[0], self_greater[1]]
    ).astype(jnp.bfloat16)
    self_tiles = regroup(gather_tiles(self_sites, row_parts, col_parts)).reshape(
        4, momenta, tile_cells
    )
    inverse_table = jnp.concatenate([cosines, sines], axis=0)
    spectral_terms = jnp.einsum(
        "cum,ju->cjm", self_tiles, inverse_table, preferred_element_type=jnp.float32
    )
    self_spectral = jnp.stack(
        [
            (spectral_terms[0, :momenta] + spectral_terms[1, momenta:]) * norm_factor,
            (spectral_terms[1, :momenta] - spectral_terms[0, momenta:]) * norm_factor,
            (spectral_terms[2, :momenta] + spectral_terms[3, momenta:]) * norm_factor,
            (spectral_terms[3, :momenta] - spectral_terms[2, momenta:]) * norm_factor,
        ]
    ).astype(jnp.bfloat16)
    self_moment = spread_times(
        regroup(pack_blocks(self_spectral, row_parts, col_parts)), tile_rows, tile_cols
    )
    lower_mask = time_steps[None, :] <= time_steps[:, None]
    upper_mask = time_steps[:, None] <= time_steps[None, :]
    retarded = jnp.where(
        lower_mask, self_moment[2:4].astype(jnp.float32) - self_moment[0:2].astype(jnp.float32), 0.0
    ).astype(jnp.bfloat16)
    advanced = jnp.where(
        upper_mask,
        green_moment[0:2].astype(jnp.float32) - green_moment[2:4].astype(jnp.float32),
        0.0,
    ).astype(jnp.bfloat16)
    lesser_out = collide(
        retarded[0],
        retarded[1],
        self_moment[0],
        self_moment[1],
        green_moment[0],
        green_moment[1],
        advanced[0],
        advanced[1],
    )
    greater_out = collide(
        retarded[0],
        retarded[1],
        self_moment[2],
        self_moment[3],
        green_moment[2],
        green_moment[3],
        advanced[0],
        advanced[1],
    )
    collisions = (
        jnp.stack([lesser_out[0], lesser_out[1], greater_out[0], greater_out[1]]) * step_size
    ).astype(jnp.bfloat16)
    out_tiles = regroup(gather_tiles(collisions, row_parts, col_parts)).reshape(
        4, momenta, tile_cells
    )
    out_tiles = out_tiles.transpose(0, 2, 1).reshape(4, tile_rows, tile_cols, momenta)
    return (out_tiles[0:2], out_tiles[2:4])


def vmem_params(mebibytes=48):
    return pltpu.CompilerParams(vmem_limit_bytes=mebibytes * 1024 * 1024)


def unread(arrays):
    return [pl.BlockSpec(memory_space=pl.ANY)] * len(arrays)


def whole(count):
    return [pl.BlockSpec(memory_space=pltpu.VMEM)] * count


def weight():
    return pl.CostEstimate(flops=10**11, bytes_accessed=2**20, transcendentals=0)


def scalars():
    return [pl.BlockSpec(memory_space=pltpu.SMEM)]


def spread_kernel(lesser, greater, out, lines):
    _, rows, _, count = lesser.shape
    for g, tile in enumerate((lesser, greater)):
        for t in range(rows):
            slab = jnp.concatenate([tile[0, t], tile[1, t]], axis=0)
            lines[pl.ds(g * rows + t, count, stride=2 * rows), :] = slab.astype(F32).T
    out[...] = lines[...].astype(BF16)


def spread(tiles, first, count):
    _, rows, cols, _ = tiles[0].shape
    height = 2 * rows * LANES
    tile_spec = pl.BlockSpec((2, rows, cols, LANES), lambda p: (0, 0, 0, first // LANES + p))
    return pl.pallas_call(
        spread_kernel,
        grid=(count // LANES,),
        out_shape=pltpu.HBM((count * 2 * rows, 2 * cols), BF16),
        in_specs=[tile_spec, tile_spec],
        out_specs=pl.BlockSpec((height, 2 * cols), lambda p: (p, 0)),
        scratch_shapes=[pltpu.VMEM((height, 2 * cols), F32)],
        compiler_params=vmem_params(58),
        name="spread",
    )(*tiles)


def collect_kernel(blocks_ref, lesser, greater, lines):
    _, rows, cols, count = lesser.shape
    blocks, height, _ = blocks_ref.shape
    for block in range(blocks):
        lines[block * height : (block + 1) * height] = blocks_ref[block].astype(F32)
    for k in range(2 * rows):
        slab = lines[pl.ds(k, count, stride=2 * rows), :].T.astype(BF16)
        out = lesser if k < rows else greater
        out[0, k % rows] = slab[:cols]
        out[1, k % rows] = slab[cols:]


def collect(blocks, tile_shape):
    shape = jax.ShapeDtypeStruct(tile_shape, BF16)
    sources, lines, lanes = blocks.shape
    height = lines // PARTS
    block_shape = tile_shape[:3] + (tile_shape[3] // PARTS,)
    tile_spec = pl.BlockSpec(block_shape, lambda p: (0, 0, 0, p))
    return pl.pallas_call(
        collect_kernel,
        grid=(PARTS,),
        out_shape=(shape, shape),
        in_specs=[pl.BlockSpec((sources, height, lanes), lambda p: (0, p, 0))],
        out_specs=(tile_spec, tile_spec),
        scratch_shapes=[pltpu.VMEM((sources * height, lanes), F32)],
        compiler_params=vmem_params(),
        name="collect",
    )(blocks)


def table_kernel(column_ref, table, inverse):
    momenta = column_ref.shape[0]
    positions = lax.broadcasted_iota(jnp.int32, (momenta, momenta), 1)
    phases = (column_ref[...] * positions % momenta).astype(F32) * (2.0 * math.pi / momenta)
    cosines = jnp.cos(phases).astype(BF16)
    sines = jnp.sin(phases).astype(BF16)
    inverse[:momenta, :momenta] = cosines
    inverse[:momenta, momenta:] = sines
    inverse[momenta:, :momenta] = -sines
    inverse[momenta:, momenta:] = cosines
    cosines = cosines.astype(F32).T.astype(BF16)
    sines = sines.astype(F32).T.astype(BF16)
    table[:momenta, :momenta] = cosines
    table[:momenta, momenta:] = -sines
    table[momenta:, :momenta] = sines
    table[momenta:, momenta:] = cosines


def make_tables(lattice_map):
    momenta = lattice_map.shape[0]
    shape = jax.ShapeDtypeStruct((2 * momenta, 2 * momenta), BF16)
    return pl.pallas_call(
        table_kernel,
        out_shape=(shape, shape),
        in_specs=whole(1),
        out_specs=tuple(whole(2)),
        compiler_params=vmem_params(),
        name="make_tables",
    )(lattice_map[:, None])


def site_kernel(norm_factor, lesser, greater, table, *rest):
    out = rest[-1]
    _, rows, cols, _ = lesser.shape
    wide = 4 * cols
    for pair in range(rows // 2):
        slabs = [
            jnp.concatenate([tile[0, t], tile[1, t]], axis=1)
            for t in (2 * pair, 2 * pair + 1)
            for tile in (lesser, greater)
        ]
        product = lax.dot_general(
            table[...],
            jnp.concatenate(slabs, axis=0),
            (((1,), (1,)), ((), ())),
            preferred_element_type=F32,
        )
        out[:, pair * wide : (pair + 1) * wide] = (product * norm_factor).astype(BF16)


def to_sites(tiles, table, norm_factor, after):
    _, rows, cols, momenta = tiles[0].shape
    return pl.pallas_call(
        functools.partial(site_kernel, norm_factor),
        out_shape=jax.ShapeDtypeStruct((2 * momenta, rows * 2 * cols), BF16),
        in_specs=whole(3) + unread(after),
        out_specs=whole(1)[0],
        compiler_params=vmem_params(24),
        name="to_sites",
    )(*tiles, table, *after)


def cross_kernel(rows, half_ref, own, far, *rest):
    out, mark = rest[-2:]
    mark[...] = jnp.zeros_like(mark)
    half = half_ref[0]
    blocks = far.shape[0]
    cols = blocks * rows
    for at in range(far.shape[1] // (2 * rows)):
        span = slice(at * 2 * rows, (at + 1) * 2 * rows)
        for source, offset, target in ((own, half * blocks, half), (far, 0, 1 - half)):
            loaded = [source[offset + block, span].astype(F32) for block in range(blocks)]
            stacked = jnp.concatenate(
                [lines[rows:] for lines in loaded] + [lines[:rows] for lines in loaded], axis=0
            )
            turned = stacked.T
            for block in range(blocks):
                out[target * blocks + block, span] = jnp.concatenate(
                    [
                        turned[block * rows : (block + 1) * rows],
                        turned[cols + block * rows : cols + (block + 1) * rows],
                    ],
                    axis=0,
                ).astype(BF16)


def to_crossed(half, own, far, rows, after, cost):
    sources, lines, lanes = own.shape
    blocks = far.shape[0]
    step = lines // STEPS
    spec = pl.BlockSpec((sources, step, lanes), lambda p: (0, p, 0))
    far_spec = pl.BlockSpec((blocks, step, lanes), lambda p: (0, p, 0))
    return pl.pallas_call(
        functools.partial(cross_kernel, rows),
        grid=(STEPS,),
        out_shape=(
            pltpu.HBM(own.shape, BF16),
            jax.ShapeDtypeStruct((8, LANES), F32),
        ),
        in_specs=scalars() + [spec, far_spec] + unread(after),
        out_specs=(spec, pl.BlockSpec((8, LANES), lambda p: (0, 0))),
        compiler_params=vmem_params(),
        cost_estimate=cost,
        name="to_crossed",
    )(half, own, far, *after)


def gate_kernel(*refs):
    del refs


def gate(array, after):
    return pl.pallas_call(
        gate_kernel,
        out_shape=jax.ShapeDtypeStruct(array.shape, array.dtype),
        in_specs=unread([array, *after]),
        out_specs=unread([array])[0],
        input_output_aliases={0: 0},
        name="gate",
    )(array, *after)


def mirrored_term(columns, read, first, count):
    wide = columns.shape[1] // 2
    rights = []
    for t in (first, first + 1):
        real = read[pl.ds(t, wide, stride=2 * count), :]
        imaginary = -read[pl.ds(count + t, wide, stride=2 * count), :]
        rights.append(jnp.concatenate([real, imaginary], axis=0).astype(BF16))
    return jnp.dot(columns, jnp.concatenate(rights, axis=1), preferred_element_type=F32)


def part_columns(table, part, parts):
    momenta = table.shape[1] // 2
    width = momenta // parts
    return jnp.concatenate(
        [
            table[:, part * width : (part + 1) * width],
            table[:, momenta + part * width : momenta + (part + 1) * width],
        ],
        axis=1,
    )


def mirror_kernel(part, parts, count, crossed, table, inverse, out, columns, handed, read):
    read[...] = crossed[...].astype(F32)
    wide = 2 * crossed.shape[1]
    own = part_columns(table, part, parts)
    for pair in range(count // 2):
        out[:, pair * wide : (pair + 1) * wide] = mirrored_term(own, read, 2 * pair, count)
    columns[...] = part_columns(table, parts - 1, parts)
    handed[...] = inverse[...]


def to_mirror(crossed, table, inverse, part, parts, count):
    lines, lanes = crossed.shape
    size = table.shape[0]
    return pl.pallas_call(
        functools.partial(mirror_kernel, part, parts, count),
        out_shape=(
            jax.ShapeDtypeStruct((size, count * lanes), F32),
            jax.ShapeDtypeStruct((size, size // parts), BF16),
            jax.ShapeDtypeStruct((size, size), BF16),
        ),
        in_specs=whole(3),
        out_specs=tuple(whole(3)),
        scratch_shapes=[pltpu.VMEM((lines, lanes), F32)],
        compiler_params=vmem_params(24),
        name="to_mirror",
    )(crossed, table, inverse)


def sigma_kernel(
    norm_factor, mirror, crossed, sites, columns, inverse, coupling, out, read, written
):
    count = coupling.shape[0]
    momenta = inverse.shape[0] // 2
    read[...] = crossed[...].astype(F32)
    for first in range(0, count, 2):
        span = slice(first * LANES, (first + 2) * LANES)
        other = mirrored_term(columns[...], read, first, count) + mirror[:, span]
        other = (other * norm_factor).astype(BF16).astype(F32)
        self_real, self_imaginary = second_born(
            sites[:momenta, span].astype(F32),
            sites[momenta:, span].astype(F32),
            other[:momenta],
            -other[momenta:],
            jnp.concatenate([coupling[t : t + 1] for t in (first, first + 1)], axis=1),
        )
        product = jnp.dot(
            inverse[...],
            jnp.concatenate([self_real, self_imaginary], axis=0).astype(BF16),
            preferred_element_type=F32,
        )
        product = product * norm_factor
        for at in range(2):
            for part in range(2):
                written[pl.ds(part * count + first + at, momenta, stride=2 * count), :] = product[
                    part * momenta : (part + 1) * momenta, at * LANES : (at + 1) * LANES
                ]
    blocks, height, _ = out.shape
    height = height // PARTS
    for part in range(PARTS):
        for block in range(blocks):
            start = (part * blocks + block) * height
            out[block, part * height : (part + 1) * height] = written[
                start : start + height
            ].astype(BF16)


def to_sigma(mirror, crossed, sites, columns, inverse, coupling, norm_factor, blocks):
    lines, lanes = crossed.shape
    return pl.pallas_call(
        functools.partial(sigma_kernel, norm_factor),
        out_shape=pltpu.HBM((blocks, PARTS * lines // blocks, lanes), BF16),
        in_specs=whole(6),
        out_specs=whole(1)[0],
        scratch_shapes=[pltpu.VMEM((lines, lanes), F32), pltpu.VMEM((PARTS * lines, lanes), F32)],
        compiler_params=vmem_params(34),
        name="to_sigma",
    )(mirror, crossed, sites, columns, inverse, coupling)


def rights_kernel(rows, half_ref, own, near_ref, away_ref, *rest):
    out = rest[-1]
    half = half_ref[0]
    blocks = near_ref.shape[0]
    lanes = own.shape[2]
    cols = lanes // 2
    near = half * cols
    away = (1 - half) * cols
    row_at = lax.broadcasted_iota(jnp.int32, (lanes, 2 * lanes), 0)
    inner_times = jnp.where(row_at < cols, near + row_at, away + row_at - cols)
    lane_at = lax.broadcasted_iota(jnp.int32, (lanes, 2 * lanes), 1)
    last_times = jnp.where(lane_at < lanes, near, away) + lane_at % cols
    keep = inner_times <= last_times
    for at in range(out.shape[0]):
        span = slice(at * 2 * rows, (at + 1) * 2 * rows)

        def stacked(read):
            loaded = [read(block).astype(F32) for block in range(blocks)]
            return [
                jnp.concatenate([lines[g * rows : (g + 1) * rows] for lines in loaded], axis=0)
                for g in range(2)
            ]

        own_near = stacked(lambda block: own[half * blocks + block, span])
        own_away = stacked(lambda block: own[(1 - half) * blocks + block, span])
        far_near = stacked(lambda block: near_ref[block, span])
        far_away = stacked(lambda block: away_ref[0, block, span])
        greens = [
            jnp.concatenate(
                [
                    jnp.concatenate([own_near[g], own_away[g]], axis=1),
                    jnp.concatenate([far_near[g], far_away[g]], axis=1),
                ],
                axis=0,
            )
            for g in range(2)
        ]
        out[at, :lanes] = greens[0].astype(BF16)
        out[at, lanes : 2 * lanes] = greens[1].astype(BF16)
        out[at, 2 * lanes :] = jnp.where(keep, greens[0] - greens[1], 0.0).astype(BF16)


STEPS = 4
PARTS = 2


def make_rights(half, own, far_near, far_away, rows, part, before):
    sources, lines, lanes = own.shape
    blocks = far_near.shape[0]
    steps = STEPS // PARTS
    step = lines // steps
    momenta = step // (2 * rows)
    return pl.pallas_call(
        functools.partial(rights_kernel, rows),
        grid=(steps,),
        out_shape=jax.ShapeDtypeStruct((STEPS * momenta, 3 * lanes, 2 * lanes), BF16),
        in_specs=scalars()
        + [
            pl.BlockSpec((sources, step, lanes), lambda p: (0, p, 0)),
            pl.BlockSpec((blocks, step, lanes), lambda p: (0, p, 0)),
            pl.BlockSpec((1, blocks, step, lanes), lambda p: (part, 0, p, 0)),
        ]
        + unread(before),
        out_specs=pl.BlockSpec(
            (momenta, 3 * lanes, 2 * lanes), lambda p: (part * steps + p, 0, 0)
        ),
        input_output_aliases={4: 0} if part > 0 else {},
        compiler_params=vmem_params(),
        cost_estimate=weight(),
        name="make_rights",
    )(half, own, far_near, far_away, *before)


def volterra_kernel(rows, half_ref, sigma, rights, out):
    half = half_ref[0]
    blocks = sigma.shape[0] // 2
    lanes = sigma.shape[2]
    cols = lanes // 2
    near = half * cols
    away = (1 - half) * cols
    here = half * blocks
    there = (1 - half) * blocks
    first_times = near + lax.broadcasted_iota(jnp.int32, (cols, lanes), 0)
    left_lane = lax.broadcasted_iota(jnp.int32, (cols, lanes), 1)
    low_lanes = left_lane < cols
    left_times = jnp.where(low_lanes, near + left_lane, away + left_lane - cols)
    keep_left = left_times <= first_times
    for at in range(rights.shape[0]):
        span = slice(at * 2 * rows, (at + 1) * 2 * rows)

        def stacked(offset):
            loaded = [sigma[offset + block, span].astype(F32) for block in range(blocks)]
            return [
                jnp.concatenate([lines[part * rows : (part + 1) * rows] for lines in loaded], axis=0)
                for part in range(2)
            ]

        sigma_near = stacked(here)
        sigma_away = stacked(there)
        retarded = []
        lefts = [[], []]
        for part in range(2):
            lesser = jnp.where(
                low_lanes, sigma_near[part], pltpu.roll(sigma_away[part], cols, 1)
            )
            greater = jnp.where(
                low_lanes, pltpu.roll(sigma_near[part], cols, 1), sigma_away[part]
            )
            retarded.append(jnp.where(keep_left, greater - lesser, 0.0))
            lefts[0].append(lesser)
            lefts[1].append(greater)
        retarded = jnp.concatenate(retarded, axis=0).astype(BF16)
        results = []
        for g in range(2):
            left = jnp.concatenate(
                [retarded, jnp.concatenate(lefts[g], axis=0).astype(BF16)], axis=1
            )
            right = jnp.concatenate(
                [rights[at, g * lanes : (g + 1) * lanes], rights[at, 2 * lanes :]], axis=0
            )
            product = jnp.dot(left, right, preferred_element_type=F32)
            sides = []
            for side in range(2):
                straight = product[:cols, side * lanes : (side + 1) * lanes]
                turned = pltpu.roll(product[cols:, side * lanes : (side + 1) * lanes], cols, 1)
                sides.append((straight + jnp.where(low_lanes, -turned, turned)) * step_size)
            results.append(sides)
        for block in range(blocks):
            lines = slice(block * rows, (block + 1) * rows)
            for side, offset in enumerate((here, there)):
                out[offset + block, span] = jnp.concatenate(
                    [results[0][side][lines], results[1][side][lines]], axis=0
                ).astype(BF16)


def volterra(half, sigma, rights, rows):
    sources, lines, lanes = sigma.shape
    step = lines // STEPS
    momenta = step // (2 * rows)
    spec = pl.BlockSpec((sources, step, lanes), lambda p: (0, p, 0))
    return pl.pallas_call(
        functools.partial(volterra_kernel, rows),
        grid=(STEPS,),
        out_shape=jax.ShapeDtypeStruct(sigma.shape, BF16),
        in_specs=scalars()
        + [spec, pl.BlockSpec((momenta, 3 * lanes, 2 * lanes), lambda p: (p, 0, 0))],
        out_specs=spec,
        compiler_params=vmem_params(),
        name="volterra",
    )(half, sigma, rights)


def halved_body(green_lesser, green_greater, lattice_map, time_offset):
    _, rows, cols, momenta = green_lesser.shape
    half = lax.axis_index("half")
    line = lax.axis_index("line")
    side = lax.axis_index("tcol")
    lines = lax.axis_size("line")
    group = lines * lax.axis_size("tcol")
    window = rows * lines * lax.axis_size("half")
    norm_factor = 1.0 / math.sqrt(momenta)
    tiles = (green_lesser, green_greater)
    half_at = half[None]
    count = momenta // PARTS

    def exchange(blocks):
        return lax.all_to_all(blocks, ("tcol", "line"), 0, 0, tiled=True)

    def blocked(rows_array):
        return rows_array.reshape(group, rows_array.shape[0] // group, rows_array.shape[1])

    def swap(array):
        return lax.ppermute(array, "half", [(0, 1), (1, 0)])

    table, inverse = make_tables(lattice_map)
    time_steps = jnp.arange(window, dtype=jnp.int32)
    coupling_line = 1.0 + drive_depth * jnp.cos(
        ((time_offset[0] + time_steps) % PERIOD).astype(F32) * (2.0 * math.pi / PERIOD)
    )
    first = lax.dynamic_slice_in_dim(coupling_line, (half * lines + line) * rows, rows)
    second = lax.dynamic_slice_in_dim(coupling_line, side * cols, cols)
    coupling = first[:, None] * jnp.concatenate([second, second])[None, :]

    spread_parts = [spread(tiles, part * count, count) for part in range(PARTS)]
    own = [exchange(blocked(spread_parts[0]))]
    for rows_array in spread_parts[1:]:
        own.append(exchange(gate(blocked(rows_array), [table, coupling])))
    far_near = [swap(lax.dynamic_slice_in_dim(blocks, (1 - half) * lines, lines)) for blocks in own]

    sent = []
    marks = []
    for part in range(PARTS):
        blocks, mark = to_crossed(
            half_at,
            own[part],
            far_near[part],
            rows,
            own[-1:] + marks[-1:],
            None,
        )
        sent.append(blocks)
        marks.append(mark)
    crossed = [exchange(blocks) for blocks in sent]
    kept = jnp.stack(
        [lax.dynamic_slice_in_dim(blocks, half * lines, lines) for blocks in own]
    )
    far_away = swap(gate(kept, marks[-1:] + crossed[:-1]))
    flat = [blocks.reshape(-1, 2 * cols) for blocks in crossed]
    sites = to_sites(tiles, table, norm_factor, marks[-1:])
    mirror, columns, handed = to_mirror(flat[0], table, inverse, 0, PARTS, rows)
    sigma_rows = to_sigma(mirror, flat[1], sites, columns, handed, coupling, norm_factor, group)
    sigma = exchange(sigma_rows)
    rights = []
    for part in range(PARTS):
        rights = [
            make_rights(
                half_at, own[part], far_near[part], far_away, rows, part, rights + [sigma_rows]
            )
        ]
    returned = exchange(volterra(half_at, sigma, rights[0], rows))
    return collect(returned, green_lesser.shape)


def solution(mesh):
    row_parts = mesh.shape["trow"]
    col_parts = mesh.shape["tcol"]

    def call(green_lesser, green_greater, lattice_map, time_offset):
        window, window_cols, momenta = green_lesser.shape[1:]
        rows = window // row_parts
        cols = window_cols // col_parts
        halved = (
            col_parts == 2
            and row_parts % 2 == 0
            and window == window_cols
            and 2 * cols == LANES
            and cols == rows * (row_parts // 2)
            and rows % 8 == 0
            and momenta % (2 * row_parts * STEPS) == 0
            and momenta % (PARTS * LANES) == 0
        )
        if halved:
            devices = mesh.devices.reshape(2, row_parts // 2, col_parts)
            used = Mesh(devices, ("half", "line", "tcol"))
            spec = P(None, ("half", "line"), "tcol", None)
            inner = halved_body
        else:
            used = mesh
            spec = P(None, "trow", "tcol", None)
            inner = general_body
        return jax.shard_map(
            inner, mesh=used, in_specs=(spec, spec, P(), P()), out_specs=(spec, spec), check_vma=False
        )(green_lesser, green_greater, lattice_map, time_offset)

    return call
```

```python
import functools
import math

import jax
import jax.numpy as jnp
from jax import lax
from jax.experimental import pallas as pl
from jax.experimental.pallas import tpu as pltpu
from jax.sharding import Mesh, PartitionSpec as P

F32 = jnp.float32
BF16 = jnp.bfloat16
LANES = 128

PERIOD = 64


step_size = 0.01
drive_depth = 0.5


def regroup(blocks):
    return lax.all_to_all(
        lax.all_to_all(blocks, "trow", split_axis=1, concat_axis=1, tiled=True),
        "tcol",
        split_axis=2,
        concat_axis=2,
        tiled=True,
    )


def pack_blocks(spectral, row_parts, col_parts):
    stacked, extent, tile_cells = spectral.shape
    return spectral.reshape(
        stacked, row_parts, col_parts, extent // (row_parts * col_parts), tile_cells
    )


def spread_times(blocks, tile_rows, tile_cols):
    stacked, row_parts, col_parts, local_count, tile_cells = blocks.shape
    shaped = blocks.reshape(stacked, row_parts, col_parts, local_count, tile_rows, tile_cols)
    return shaped.transpose(0, 3, 1, 4, 2, 5).reshape(
        stacked, local_count, row_parts * tile_rows, col_parts * tile_cols
    )


def gather_tiles(full, row_parts, col_parts):
    stacked, local_count, window, window_cols = full.shape
    tile_rows = window // row_parts
    tile_cols = window_cols // col_parts
    shaped = full.reshape(stacked, local_count, row_parts, tile_rows, col_parts, tile_cols)
    return shaped.transpose(0, 2, 4, 1, 3, 5).reshape(
        stacked, row_parts, col_parts, local_count, tile_rows * tile_cols
    )


def mirrored(full, keep_pair):
    stacked, local_count, window, window_cols = full.shape
    paired = full.reshape(stacked, local_count // 2, 2, window, window_cols)
    swapped = jnp.where(keep_pair[None, :, None, None, None], paired, paired[:, :, ::-1])
    return jnp.swapaxes(swapped.reshape(stacked, local_count, window, window_cols), 2, 3)


def second_born(first_real, first_imaginary, other_real, other_imaginary, coupling):
    square_real = first_real * first_real - first_imaginary * first_imaginary
    square_imaginary = 2.0 * first_real * first_imaginary
    out_real = coupling * (square_real * other_real - square_imaginary * other_imaginary)
    out_imaginary = coupling * (square_real * other_imaginary + square_imaginary * other_real)
    return (out_real, out_imaginary)


def collide(
    retarded_real,
    retarded_imaginary,
    self_real,
    self_imaginary,
    green_real,
    green_imaginary,
    advanced_real,
    advanced_imaginary,
):
    minus_left = jnp.concatenate(
        [retarded_real, -retarded_imaginary, self_real, -self_imaginary], axis=2
    )
    plus_left = jnp.concatenate(
        [retarded_real, retarded_imaginary, self_real, self_imaginary], axis=2
    )
    real_right = jnp.concatenate(
        [green_real, green_imaginary, advanced_real, advanced_imaginary], axis=1
    )
    imaginary_right = jnp.concatenate(
        [green_imaginary, green_real, advanced_imaginary, advanced_real], axis=1
    )
    out_real = jnp.einsum(
        "kts,ksu->ktu", minus_left, real_right, preferred_element_type=jnp.float32
    )
    out_imaginary = jnp.einsum(
        "kts,ksu->ktu", plus_left, imaginary_right, preferred_element_type=jnp.float32
    )
    return (out_real, out_imaginary)


def general_body(green_lesser, green_greater, lattice_map, time_offset):
    tile_rows = green_lesser.shape[1]
    tile_cols = green_lesser.shape[2]
    momenta = green_lesser.shape[3]
    row_parts = lax.axis_size("trow")
    col_parts = lax.axis_size("tcol")
    window = tile_rows * row_parts
    tile_cells = tile_rows * tile_cols
    local_count = momenta // (row_parts * col_parts)
    norm_factor = 1.0 / math.sqrt(momenta)
    greens = (
        jnp.concatenate([green_lesser, green_greater], axis=0)
        .reshape(4, tile_cells, momenta)
        .transpose(0, 2, 1)
    )
    positions = jnp.arange(momenta, dtype=jnp.int32)
    halves = positions // 2
    site_order = jnp.where(
        positions == 1, momenta // 2, jnp.where(positions % 2 == 0, halves, momenta - halves)
    )
    phases = (lattice_map[:, None] * site_order[None, :] % momenta).astype(jnp.float32) * (
        2.0 * math.pi / momenta
    )
    cosines = jnp.cos(phases).astype(jnp.bfloat16)
    sines = jnp.sin(phases).astype(jnp.bfloat16)
    ahead_blocks = lax.all_to_all(
        lax.all_to_all(
            pack_blocks(greens, row_parts, col_parts),
            "trow",
            split_axis=1,
            concat_axis=1,
            tiled=True,
        ),
        "tcol",
        split_axis=2,
        concat_axis=2,
        tiled=True,
    )
    green_moment = spread_times(ahead_blocks, tile_rows, tile_cols)
    forward_table = jnp.concatenate([cosines, sines], axis=1)
    products = jnp.einsum("cjm,jr->crm", greens, forward_table, preferred_element_type=jnp.float32)
    site_space = jnp.stack(
        [
            (products[0, :momenta] - products[1, momenta:]) * norm_factor,
            (products[0, momenta:] + products[1, :momenta]) * norm_factor,
            (products[2, :momenta] - products[3, momenta:]) * norm_factor,
            (products[2, momenta:] + products[3, :momenta]) * norm_factor,
        ]
    ).astype(jnp.bfloat16)
    site_full = spread_times(
        regroup(pack_blocks(site_space, row_parts, col_parts)), tile_rows, tile_cols
    )
    site_block = lax.axis_index("trow") * col_parts + lax.axis_index("tcol")
    keep_pair = site_block * (local_count // 2) + jnp.arange(local_count // 2, dtype=jnp.int32) == 0
    mirror = mirrored(site_full, keep_pair).astype(jnp.float32)
    direct = site_full.astype(jnp.float32)
    time_steps = jnp.arange(window, dtype=jnp.int32)
    coupling_line = 1.0 + drive_depth * jnp.cos(
        ((time_offset[0] + time_steps) % PERIOD).astype(jnp.float32) * (2.0 * math.pi / PERIOD)
    )
    coupling = coupling_line[:, None] * coupling_line[None, :]
    self_lesser = second_born(direct[0], direct[1], mirror[2], mirror[3], coupling)
    self_greater = second_born(direct[2], direct[3], mirror[0], mirror[1], coupling)
    self_sites = jnp.stack(
        [self_lesser[0], self_lesser[1], self_greater[0], self_greater[1]]
    ).astype(jnp.bfloat16)
    self_tiles = regroup(gather_tiles(self_sites, row_parts, col_parts)).reshape(
        4, momenta, tile_cells
    )
    inverse_table = jnp.concatenate([cosines, sines], axis=0)
    spectral_terms = jnp.einsum(
        "cum,ju->cjm", self_tiles, inverse_table, preferred_element_type=jnp.float32
    )
    self_spectral = jnp.stack(
        [
            (spectral_terms[0, :momenta] + spectral_terms[1, momenta:]) * norm_factor,
            (spectral_terms[1, :momenta] - spectral_terms[0, momenta:]) * norm_factor,
            (spectral_terms[2, :momenta] + spectral_terms[3, momenta:]) * norm_factor,
            (spectral_terms[3, :momenta] - spectral_terms[2, momenta:]) * norm_factor,
        ]
    ).astype(jnp.bfloat16)
    self_moment = spread_times(
        regroup(pack_blocks(self_spectral, row_parts, col_parts)), tile_rows, tile_cols
    )
    lower_mask = time_steps[None, :] <= time_steps[:, None]
    upper_mask = time_steps[:, None] <= time_steps[None, :]
    retarded = jnp.where(
        lower_mask, self_moment[2:4].astype(jnp.float32) - self_moment[0:2].astype(jnp.float32), 0.0
    ).astype(jnp.bfloat16)
    advanced = jnp.where(
        upper_mask,
        green_moment[0:2].astype(jnp.float32) - green_moment[2:4].astype(jnp.float32),
        0.0,
    ).astype(jnp.bfloat16)
    lesser_out = collide(
        retarded[0],
        retarded[1],
        self_moment[0],
        self_moment[1],
        green_moment[0],
        green_moment[1],
        advanced[0],
        advanced[1],
    )
    greater_out = collide(
        retarded[0],
        retarded[1],
        self_moment[2],
        self_moment[3],
        green_moment[2],
        green_moment[3],
        advanced[0],
        advanced[1],
    )
    collisions = (
        jnp.stack([lesser_out[0], lesser_out[1], greater_out[0], greater_out[1]]) * step_size
    ).astype(jnp.bfloat16)
    out_tiles = regroup(gather_tiles(collisions, row_parts, col_parts)).reshape(
        4, momenta, tile_cells
    )
    out_tiles = out_tiles.transpose(0, 2, 1).reshape(4, tile_rows, tile_cols, momenta)
    return (out_tiles[0:2], out_tiles[2:4])


def vmem_params(mebibytes=48):
    return pltpu.CompilerParams(vmem_limit_bytes=mebibytes * 1024 * 1024)


def unread(arrays):
    return [pl.BlockSpec(memory_space=pl.ANY)] * len(arrays)


def whole(count):
    return [pl.BlockSpec(memory_space=pltpu.VMEM)] * count


def weight():
    return pl.CostEstimate(flops=10**11, bytes_accessed=2**20, transcendentals=0)


def scalars():
    return [pl.BlockSpec(memory_space=pltpu.SMEM)]


def spread_kernel(lesser, greater, out, lines):
    _, rows, _, count = lesser.shape
    for g, tile in enumerate((lesser, greater)):
        for t in range(rows):
            slab = jnp.concatenate([tile[0, t], tile[1, t]], axis=0)
            lines[pl.ds(g * rows + t, count, stride=2 * rows), :] = slab.astype(F32).T
    out[...] = lines[...].astype(BF16)


def spread(tiles, first, count):
    _, rows, cols, _ = tiles[0].shape
    height = 2 * rows * LANES
    tile_spec = pl.BlockSpec((2, rows, cols, LANES), lambda p: (0, 0, 0, first // LANES + p))
    return pl.pallas_call(
        spread_kernel,
        grid=(count // LANES,),
        out_shape=pltpu.HBM((count * 2 * rows, 2 * cols), BF16),
        in_specs=[tile_spec, tile_spec],
        out_specs=pl.BlockSpec((height, 2 * cols), lambda p: (p, 0)),
        scratch_shapes=[pltpu.VMEM((height, 2 * cols), F32)],
        compiler_params=vmem_params(58),
        name="spread",
    )(*tiles)


def collect_kernel(blocks_ref, lesser, greater, lines):
    _, rows, cols, count = lesser.shape
    blocks, height, _ = blocks_ref.shape
    for block in range(blocks):
        lines[block * height : (block + 1) * height] = blocks_ref[block].astype(F32)
    for k in range(2 * rows):
        slab = lines[pl.ds(k, count, stride=2 * rows), :].T.astype(BF16)
        out = lesser if k < rows else greater
        out[0, k % rows] = slab[:cols]
        out[1, k % rows] = slab[cols:]


def collect(blocks, tile_shape):
    shape = jax.ShapeDtypeStruct(tile_shape, BF16)
    sources, lines, lanes = blocks.shape
    height = lines // PARTS
    block_shape = tile_shape[:3] + (tile_shape[3] // PARTS,)
    tile_spec = pl.BlockSpec(block_shape, lambda p: (0, 0, 0, p))
    return pl.pallas_call(
        collect_kernel,
        grid=(PARTS,),
        out_shape=(shape, shape),
        in_specs=[pl.BlockSpec((sources, height, lanes), lambda p: (0, p, 0))],
        out_specs=(tile_spec, tile_spec),
        scratch_shapes=[pltpu.VMEM((sources * height, lanes), F32)],
        compiler_params=vmem_params(),
        name="collect",
    )(blocks)


def table_kernel(column_ref, table, inverse):
    momenta = column_ref.shape[0]
    positions = lax.broadcasted_iota(jnp.int32, (momenta, momenta), 1)
    phases = (column_ref[...] * positions % momenta).astype(F32) * (2.0 * math.pi / momenta)
    cosines = jnp.cos(phases).astype(BF16)
    sines = jnp.sin(phases).astype(BF16)
    inverse[:momenta, :momenta] = cosines
    inverse[:momenta, momenta:] = sines
    inverse[momenta:, :momenta] = -sines
    inverse[momenta:, momenta:] = cosines
    cosines = cosines.astype(F32).T.astype(BF16)
    sines = sines.astype(F32).T.astype(BF16)
    table[:momenta, :momenta] = cosines
    table[:momenta, momenta:] = -sines
    table[momenta:, :momenta] = sines
    table[momenta:, momenta:] = cosines


def make_tables(lattice_map):
    momenta = lattice_map.shape[0]
    shape = jax.ShapeDtypeStruct((2 * momenta, 2 * momenta), BF16)
    return pl.pallas_call(
        table_kernel,
        out_shape=(shape, shape),
        in_specs=whole(1),
        out_specs=tuple(whole(2)),
        compiler_params=vmem_params(),
        name="make_tables",
    )(lattice_map[:, None])


def site_kernel(norm_factor, lesser, greater, table, *rest):
    out = rest[-1]
    _, rows, cols, _ = lesser.shape
    wide = 4 * cols
    for pair in range(rows // 2):
        slabs = [
            jnp.concatenate([tile[0, t], tile[1, t]], axis=1)
            for t in (2 * pair, 2 * pair + 1)
            for tile in (lesser, greater)
        ]
        product = lax.dot_general(
            table[...],
            jnp.concatenate(slabs, axis=0),
            (((1,), (1,)), ((), ())),
            preferred_element_type=F32,
        )
        out[:, pair * wide : (pair + 1) * wide] = (product * norm_factor).astype(BF16)


def to_sites(tiles, table, norm_factor, after):
    _, rows, cols, momenta = tiles[0].shape
    return pl.pallas_call(
        functools.partial(site_kernel, norm_factor),
        out_shape=jax.ShapeDtypeStruct((2 * momenta, rows * 2 * cols), BF16),
        in_specs=whole(3) + unread(after),
        out_specs=whole(1)[0],
        compiler_params=vmem_params(24),
        name="to_sites",
    )(*tiles, table, *after)


def cross_kernel(rows, half_ref, own, far, *rest):
    out, mark = rest[-2:]
    mark[...] = jnp.zeros_like(mark)
    half = half_ref[0]
    blocks = far.shape[0]
    cols = blocks * rows
    for at in range(far.shape[1] // (2 * rows)):
        span = slice(at * 2 * rows, (at + 1) * 2 * rows)
        for source, offset, target in ((own, half * blocks, half), (far, 0, 1 - half)):
            loaded = [source[offset + block, span].astype(F32) for block in range(blocks)]
            stacked = jnp.concatenate(
                [lines[rows:] for lines in loaded] + [lines[:rows] for lines in loaded], axis=0
            )
            turned = stacked.T
            for block in range(blocks):
                out[target * blocks + block, span] = jnp.concatenate(
                    [
                        turned[block * rows : (block + 1) * rows],
                        turned[cols + block * rows : cols + (block + 1) * rows],
                    ],
                    axis=0,
                ).astype(BF16)


def to_crossed(half, own, far, rows, after, cost):
    sources, lines, lanes = own.shape
    blocks = far.shape[0]
    step = lines // STEPS
    spec = pl.BlockSpec((sources, step, lanes), lambda p: (0, p, 0))
    far_spec = pl.BlockSpec((blocks, step, lanes), lambda p: (0, p, 0))
    return pl.pallas_call(
        functools.partial(cross_kernel, rows),
        grid=(STEPS,),
        out_shape=(
            pltpu.HBM(own.shape, BF16),
            jax.ShapeDtypeStruct((8, LANES), F32),
        ),
        in_specs=scalars() + [spec, far_spec] + unread(after),
        out_specs=(spec, pl.BlockSpec((8, LANES), lambda p: (0, 0))),
        compiler_params=vmem_params(),
        cost_estimate=cost,
        name="to_crossed",
    )(half, own, far, *after)


def gate_kernel(*refs):
    del refs


def gate(array, after):
    return pl.pallas_call(
        gate_kernel,
        out_shape=jax.ShapeDtypeStruct(array.shape, array.dtype),
        in_specs=unread([array, *after]),
        out_specs=unread([array])[0],
        input_output_aliases={0: 0},
        name="gate",
    )(array, *after)


def mirrored_term(columns, read, first, count):
    wide = columns.shape[1] // 2
    rights = []
    for t in (first, first + 1):
        real = read[pl.ds(t, wide, stride=2 * count), :]
        imaginary = -read[pl.ds(count + t, wide, stride=2 * count), :]
        rights.append(jnp.concatenate([real, imaginary], axis=0).astype(BF16))
    return jnp.dot(columns, jnp.concatenate(rights, axis=1), preferred_element_type=F32)


def part_columns(table, part, parts):
    momenta = table.shape[1] // 2
    width = momenta // parts
    return jnp.concatenate(
        [
            table[:, part * width : (part + 1) * width],
            table[:, momenta + part * width : momenta + (part + 1) * width],
        ],
        axis=1,
    )


def mirror_kernel(part, parts, count, crossed, table, inverse, out, columns, handed, read):
    read[...] = crossed[...].astype(F32)
    wide = 2 * crossed.shape[1]
    own = part_columns(table, part, parts)
    for pair in range(count // 2):
        out[:, pair * wide : (pair + 1) * wide] = mirrored_term(own, read, 2 * pair, count)
    columns[...] = part_columns(table, parts - 1, parts)
    handed[...] = inverse[...]


def to_mirror(crossed, table, inverse, part, parts, count):
    lines, lanes = crossed.shape
    size = table.shape[0]
    return pl.pallas_call(
        functools.partial(mirror_kernel, part, parts, count),
        out_shape=(
            jax.ShapeDtypeStruct((size, count * lanes), F32),
            jax.ShapeDtypeStruct((size, size // parts), BF16),
            jax.ShapeDtypeStruct((size, size), BF16),
        ),
        in_specs=whole(3),
        out_specs=tuple(whole(3)),
        scratch_shapes=[pltpu.VMEM((lines, lanes), F32)],
        compiler_params=vmem_params(24),
        name="to_mirror",
    )(crossed, table, inverse)


def sigma_kernel(
    norm_factor, mirror, crossed, sites, columns, inverse, coupling, out, read, written
):
    count = coupling.shape[0]
    momenta = inverse.shape[0] // 2
    read[...] = crossed[...].astype(F32)
    for first in range(0, count, 2):
        span = slice(first * LANES, (first + 2) * LANES)
        other = mirrored_term(columns[...], read, first, count) + mirror[:, span]
        other = (other * norm_factor).astype(BF16).astype(F32)
        self_real, self_imaginary = second_born(
            sites[:momenta, span].astype(F32),
            sites[momenta:, span].astype(F32),
            other[:momenta],
            -other[momenta:],
            jnp.concatenate([coupling[t : t + 1] for t in (first, first + 1)], axis=1),
        )
        product = jnp.dot(
            inverse[...],
            jnp.concatenate([self_real, self_imaginary], axis=0).astype(BF16),
            preferred_element_type=F32,
        )
        product = product * norm_factor
        for at in range(2):
            for part in range(2):
                written[pl.ds(part * count + first + at, momenta, stride=2 * count), :] = product[
                    part * momenta : (part + 1) * momenta, at * LANES : (at + 1) * LANES
                ]
    blocks, height, _ = out.shape
    height = height // PARTS
    for part in range(PARTS):
        for block in range(blocks):
            start = (part * blocks + block) * height
            out[block, part * height : (part + 1) * height] = written[
                start : start + height
            ].astype(BF16)


def to_sigma(mirror, crossed, sites, columns, inverse, coupling, norm_factor, blocks):
    lines, lanes = crossed.shape
    return pl.pallas_call(
        functools.partial(sigma_kernel, norm_factor),
        out_shape=pltpu.HBM((blocks, PARTS * lines // blocks, lanes), BF16),
        in_specs=whole(6),
        out_specs=whole(1)[0],
        scratch_shapes=[pltpu.VMEM((lines, lanes), F32), pltpu.VMEM((PARTS * lines, lanes), F32)],
        compiler_params=vmem_params(34),
        name="to_sigma",
    )(mirror, crossed, sites, columns, inverse, coupling)


def rights_kernel(rows, half_ref, own, near_ref, away_ref, *rest):
    out = rest[-1]
    half = half_ref[0]
    blocks = near_ref.shape[0]
    lanes = own.shape[2]
    cols = lanes // 2
    near = half * cols
    away = (1 - half) * cols
    row_at = lax.broadcasted_iota(jnp.int32, (lanes, 2 * lanes), 0)
    inner_times = jnp.where(row_at < cols, near + row_at, away + row_at - cols)
    lane_at = lax.broadcasted_iota(jnp.int32, (lanes, 2 * lanes), 1)
    last_times = jnp.where(lane_at < lanes, near, away) + lane_at % cols
    keep = inner_times <= last_times
    for at in range(out.shape[0]):
        span = slice(at * 2 * rows, (at + 1) * 2 * rows)

        def stacked(read):
            loaded = [read(block).astype(F32) for block in range(blocks)]
            return [
                jnp.concatenate([lines[g * rows : (g + 1) * rows] for lines in loaded], axis=0)
                for g in range(2)
            ]

        own_near = stacked(lambda block: own[half * blocks + block, span])
        own_away = stacked(lambda block: own[(1 - half) * blocks + block, span])
        far_near = stacked(lambda block: near_ref[block, span])
        far_away = stacked(lambda block: away_ref[0, block, span])
        greens = [
            jnp.concatenate(
                [
                    jnp.concatenate([own_near[g], own_away[g]], axis=1),
                    jnp.concatenate([far_near[g], far_away[g]], axis=1),
                ],
                axis=0,
            )
            for g in range(2)
        ]
        out[at, :lanes] = greens[0].astype(BF16)
        out[at, lanes : 2 * lanes] = greens[1].astype(BF16)
        out[at, 2 * lanes :] = jnp.where(keep, greens[0] - greens[1], 0.0).astype(BF16)


STEPS = 8
PARTS = 2


def make_rights(half, own, far_near, far_away, rows, part, before):
    sources, lines, lanes = own.shape
    blocks = far_near.shape[0]
    steps = STEPS // PARTS
    step = lines // steps
    momenta = step // (2 * rows)
    return pl.pallas_call(
        functools.partial(rights_kernel, rows),
        grid=(steps,),
        out_shape=jax.ShapeDtypeStruct((STEPS * momenta, 3 * lanes, 2 * lanes), BF16),
        in_specs=scalars()
        + [
            pl.BlockSpec((sources, step, lanes), lambda p: (0, p, 0)),
            pl.BlockSpec((blocks, step, lanes), lambda p: (0, p, 0)),
            pl.BlockSpec((1, blocks, step, lanes), lambda p: (part, 0, p, 0)),
        ]
        + unread(before),
        out_specs=pl.BlockSpec(
            (momenta, 3 * lanes, 2 * lanes), lambda p: (part * steps + p, 0, 0)
        ),
        input_output_aliases={4: 0} if part > 0 else {},
        compiler_params=vmem_params(),
        cost_estimate=weight(),
        name="make_rights",
    )(half, own, far_near, far_away, *before)


def volterra_kernel(rows, half_ref, sigma, rights, out):
    half = half_ref[0]
    blocks = sigma.shape[0] // 2
    lanes = sigma.shape[2]
    cols = lanes // 2
    near = half * cols
    away = (1 - half) * cols
    here = half * blocks
    there = (1 - half) * blocks
    first_times = near + lax.broadcasted_iota(jnp.int32, (cols, lanes), 0)
    left_lane = lax.broadcasted_iota(jnp.int32, (cols, lanes), 1)
    low_lanes = left_lane < cols
    left_times = jnp.where(low_lanes, near + left_lane, away + left_lane - cols)
    keep_left = left_times <= first_times
    for at in range(rights.shape[0]):
        span = slice(at * 2 * rows, (at + 1) * 2 * rows)

        def stacked(offset):
            loaded = [sigma[offset + block, span].astype(F32) for block in range(blocks)]
            return [
                jnp.concatenate([lines[part * rows : (part + 1) * rows] for lines in loaded], axis=0)
                for part in range(2)
            ]

        sigma_near = stacked(here)
        sigma_away = stacked(there)
        retarded = []
        lefts = [[], []]
        for part in range(2):
            lesser = jnp.where(
                low_lanes, sigma_near[part], pltpu.roll(sigma_away[part], cols, 1)
            )
            greater = jnp.where(
                low_lanes, pltpu.roll(sigma_near[part], cols, 1), sigma_away[part]
            )
            retarded.append(jnp.where(keep_left, greater - lesser, 0.0))
            lefts[0].append(lesser)
            lefts[1].append(greater)
        retarded = jnp.concatenate(retarded, axis=0).astype(BF16)
        results = []
        for g in range(2):
            left = jnp.concatenate(
                [retarded, jnp.concatenate(lefts[g], axis=0).astype(BF16)], axis=1
            )
            right = jnp.concatenate(
                [rights[at, g * lanes : (g + 1) * lanes], rights[at, 2 * lanes :]], axis=0
            )
            product = jnp.dot(left, right, preferred_element_type=F32)
            sides = []
            for side in range(2):
                straight = product[:cols, side * lanes : (side + 1) * lanes]
                turned = pltpu.roll(product[cols:, side * lanes : (side + 1) * lanes], cols, 1)
                sides.append((straight + jnp.where(low_lanes, -turned, turned)) * step_size)
            results.append(sides)
        for block in range(blocks):
            lines = slice(block * rows, (block + 1) * rows)
            for side, offset in enumerate((here, there)):
                out[offset + block, span] = jnp.concatenate(
                    [results[0][side][lines], results[1][side][lines]], axis=0
                ).astype(BF16)


def volterra(half, sigma, rights, rows):
    sources, lines, lanes = sigma.shape
    step = lines // STEPS
    momenta = step // (2 * rows)
    spec = pl.BlockSpec((sources, step, lanes), lambda p: (0, p, 0))
    return pl.pallas_call(
        functools.partial(volterra_kernel, rows),
        grid=(STEPS,),
        out_shape=jax.ShapeDtypeStruct(sigma.shape, BF16),
        in_specs=scalars()
        + [spec, pl.BlockSpec((momenta, 3 * lanes, 2 * lanes), lambda p: (p, 0, 0))],
        out_specs=spec,
        compiler_params=vmem_params(),
        name="volterra",
    )(half, sigma, rights)


def halved_body(green_lesser, green_greater, lattice_map, time_offset):
    _, rows, cols, momenta = green_lesser.shape
    half = lax.axis_index("half")
    line = lax.axis_index("line")
    side = lax.axis_index("tcol")
    lines = lax.axis_size("line")
    group = lines * lax.axis_size("tcol")
    window = rows * lines * lax.axis_size("half")
    norm_factor = 1.0 / math.sqrt(momenta)
    tiles = (green_lesser, green_greater)
    half_at = half[None]
    count = momenta // PARTS

    def exchange(blocks):
        return lax.all_to_all(blocks, ("tcol", "line"), 0, 0, tiled=True)

    def blocked(rows_array):
        return rows_array.reshape(group, rows_array.shape[0] // group, rows_array.shape[1])

    def swap(array):
        return lax.ppermute(array, "half", [(0, 1), (1, 0)])

    table, inverse = make_tables(lattice_map)
    time_steps = jnp.arange(window, dtype=jnp.int32)
    coupling_line = 1.0 + drive_depth * jnp.cos(
        ((time_offset[0] + time_steps) % PERIOD).astype(F32) * (2.0 * math.pi / PERIOD)
    )
    first = lax.dynamic_slice_in_dim(coupling_line, (half * lines + line) * rows, rows)
    second = lax.dynamic_slice_in_dim(coupling_line, side * cols, cols)
    coupling = first[:, None] * jnp.concatenate([second, second])[None, :]

    spread_parts = [spread(tiles, part * count, count) for part in range(PARTS)]
    own = [exchange(blocked(spread_parts[0]))]
    for rows_array in spread_parts[1:]:
        own.append(exchange(gate(blocked(rows_array), [table, coupling])))
    far_near = [swap(lax.dynamic_slice_in_dim(blocks, (1 - half) * lines, lines)) for blocks in own]

    sent = []
    marks = []
    for part in range(PARTS):
        blocks, mark = to_crossed(
            half_at,
            own[part],
            far_near[part],
            rows,
            own[-1:] + marks[-1:],
            weight() if part > 0 else None,
        )
        sent.append(blocks)
        marks.append(mark)
    crossed = [exchange(blocks) for blocks in sent]
    kept = jnp.stack(
        [lax.dynamic_slice_in_dim(blocks, half * lines, lines) for blocks in own]
    )
    far_away = swap(gate(kept, marks[-1:] + crossed[:-1]))
    flat = [blocks.reshape(-1, 2 * cols) for blocks in crossed]
    sites = to_sites(tiles, table, norm_factor, marks[-1:])
    mirror, columns, handed = to_mirror(flat[0], table, inverse, 0, PARTS, rows)
    sigma_rows = to_sigma(mirror, flat[1], sites, columns, handed, coupling, norm_factor, group)
    sigma = exchange(sigma_rows)
    rights = []
    for part in range(PARTS):
        rights = [
            make_rights(
                half_at, own[part], far_near[part], far_away, rows, part, rights + [sigma_rows]
            )
        ]
    returned = exchange(volterra(half_at, sigma, rights[0], rows))
    return collect(returned, green_lesser.shape)


def solution(mesh):
    row_parts = mesh.shape["trow"]
    col_parts = mesh.shape["tcol"]

    def call(green_lesser, green_greater, lattice_map, time_offset):
        window, window_cols, momenta = green_lesser.shape[1:]
        rows = window // row_parts
        cols = window_cols // col_parts
        halved = (
            col_parts == 2
            and row_parts % 2 == 0
            and window == window_cols
            and 2 * cols == LANES
            and cols == rows * (row_parts // 2)
            and rows % 8 == 0
            and momenta % (2 * row_parts * STEPS) == 0
            and momenta % (PARTS * LANES) == 0
        )
        if halved:
            devices = mesh.devices.reshape(2, row_parts // 2, col_parts)
            used = Mesh(devices, ("half", "line", "tcol"))
            spec = P(None, ("half", "line"), "tcol", None)
            inner = halved_body
        else:
            used = mesh
            spec = P(None, "trow", "tcol", None)
            inner = general_body
        return jax.shard_map(
            inner, mesh=used, in_specs=(spec, spec, P(), P()), out_specs=(spec, spec), check_vma=False
        )(green_lesser, green_greater, lattice_map, time_offset)

    return call
```

```python
import functools
import math

import jax
import jax.numpy as jnp
from jax import lax
from jax.experimental import pallas as pl
from jax.experimental.pallas import tpu as pltpu
from jax.sharding import Mesh, PartitionSpec as P

F32 = jnp.float32
BF16 = jnp.bfloat16
LANES = 128

PERIOD = 64


step_size = 0.01
drive_depth = 0.5


def regroup(blocks):
    return lax.all_to_all(
        lax.all_to_all(blocks, "trow", split_axis=1, concat_axis=1, tiled=True),
        "tcol",
        split_axis=2,
        concat_axis=2,
        tiled=True,
    )


def pack_blocks(spectral, row_parts, col_parts):
    stacked, extent, tile_cells = spectral.shape
    return spectral.reshape(
        stacked, row_parts, col_parts, extent // (row_parts * col_parts), tile_cells
    )


def spread_times(blocks, tile_rows, tile_cols):
    stacked, row_parts, col_parts, local_count, tile_cells = blocks.shape
    shaped = blocks.reshape(stacked, row_parts, col_parts, local_count, tile_rows, tile_cols)
    return shaped.transpose(0, 3, 1, 4, 2, 5).reshape(
        stacked, local_count, row_parts * tile_rows, col_parts * tile_cols
    )


def gather_tiles(full, row_parts, col_parts):
    stacked, local_count, window, window_cols = full.shape
    tile_rows = window // row_parts
    tile_cols = window_cols // col_parts
    shaped = full.reshape(stacked, local_count, row_parts, tile_rows, col_parts, tile_cols)
    return shaped.transpose(0, 2, 4, 1, 3, 5).reshape(
        stacked, row_parts, col_parts, local_count, tile_rows * tile_cols
    )


def mirrored(full, keep_pair):
    stacked, local_count, window, window_cols = full.shape
    paired = full.reshape(stacked, local_count // 2, 2, window, window_cols)
    swapped = jnp.where(keep_pair[None, :, None, None, None], paired, paired[:, :, ::-1])
    return jnp.swapaxes(swapped.reshape(stacked, local_count, window, window_cols), 2, 3)


def second_born(first_real, first_imaginary, other_real, other_imaginary, coupling):
    square_real = first_real * first_real - first_imaginary * first_imaginary
    square_imaginary = 2.0 * first_real * first_imaginary
    out_real = coupling * (square_real * other_real - square_imaginary * other_imaginary)
    out_imaginary = coupling * (square_real * other_imaginary + square_imaginary * other_real)
    return (out_real, out_imaginary)


def collide(
    retarded_real,
    retarded_imaginary,
    self_real,
    self_imaginary,
    green_real,
    green_imaginary,
    advanced_real,
    advanced_imaginary,
):
    minus_left = jnp.concatenate(
        [retarded_real, -retarded_imaginary, self_real, -self_imaginary], axis=2
    )
    plus_left = jnp.concatenate(
        [retarded_real, retarded_imaginary, self_real, self_imaginary], axis=2
    )
    real_right = jnp.concatenate(
        [green_real, green_imaginary, advanced_real, advanced_imaginary], axis=1
    )
    imaginary_right = jnp.concatenate(
        [green_imaginary, green_real, advanced_imaginary, advanced_real], axis=1
    )
    out_real = jnp.einsum(
        "kts,ksu->ktu", minus_left, real_right, preferred_element_type=jnp.float32
    )
    out_imaginary = jnp.einsum(
        "kts,ksu->ktu", plus_left, imaginary_right, preferred_element_type=jnp.float32
    )
    return (out_real, out_imaginary)


def general_body(green_lesser, green_greater, lattice_map, time_offset):
    tile_rows = green_lesser.shape[1]
    tile_cols = green_lesser.shape[2]
    momenta = green_lesser.shape[3]
    row_parts = lax.axis_size("trow")
    col_parts = lax.axis_size("tcol")
    window = tile_rows * row_parts
    tile_cells = tile_rows * tile_cols
    local_count = momenta // (row_parts * col_parts)
    norm_factor = 1.0 / math.sqrt(momenta)
    greens = (
        jnp.concatenate([green_lesser, green_greater], axis=0)
        .reshape(4, tile_cells, momenta)
        .transpose(0, 2, 1)
    )
    positions = jnp.arange(momenta, dtype=jnp.int32)
    halves = positions // 2
    site_order = jnp.where(
        positions == 1, momenta // 2, jnp.where(positions % 2 == 0, halves, momenta - halves)
    )
    phases = (lattice_map[:, None] * site_order[None, :] % momenta).astype(jnp.float32) * (
        2.0 * math.pi / momenta
    )
    cosines = jnp.cos(phases).astype(jnp.bfloat16)
    sines = jnp.sin(phases).astype(jnp.bfloat16)
    ahead_blocks = lax.all_to_all(
        lax.all_to_all(
            pack_blocks(greens, row_parts, col_parts),
            "trow",
            split_axis=1,
            concat_axis=1,
            tiled=True,
        ),
        "tcol",
        split_axis=2,
        concat_axis=2,
        tiled=True,
    )
    green_moment = spread_times(ahead_blocks, tile_rows, tile_cols)
    forward_table = jnp.concatenate([cosines, sines], axis=1)
    products = jnp.einsum("cjm,jr->crm", greens, forward_table, preferred_element_type=jnp.float32)
    site_space = jnp.stack(
        [
            (products[0, :momenta] - products[1, momenta:]) * norm_factor,
            (products[0, momenta:] + products[1, :momenta]) * norm_factor,
            (products[2, :momenta] - products[3, momenta:]) * norm_factor,
            (products[2, momenta:] + products[3, :momenta]) * norm_factor,
        ]
    ).astype(jnp.bfloat16)
    site_full = spread_times(
        regroup(pack_blocks(site_space, row_parts, col_parts)), tile_rows, tile_cols
    )
    site_block = lax.axis_index("trow") * col_parts + lax.axis_index("tcol")
    keep_pair = site_block * (local_count // 2) + jnp.arange(local_count // 2, dtype=jnp.int32) == 0
    mirror = mirrored(site_full, keep_pair).astype(jnp.float32)
    direct = site_full.astype(jnp.float32)
    time_steps = jnp.arange(window, dtype=jnp.int32)
    coupling_line = 1.0 + drive_depth * jnp.cos(
        ((time_offset[0] + time_steps) % PERIOD).astype(jnp.float32) * (2.0 * math.pi / PERIOD)
    )
    coupling = coupling_line[:, None] * coupling_line[None, :]
    self_lesser = second_born(direct[0], direct[1], mirror[2], mirror[3], coupling)
    self_greater = second_born(direct[2], direct[3], mirror[0], mirror[1], coupling)
    self_sites = jnp.stack(
        [self_lesser[0], self_lesser[1], self_greater[0], self_greater[1]]
    ).astype(jnp.bfloat16)
    self_tiles = regroup(gather_tiles(self_sites, row_parts, col_parts)).reshape(
        4, momenta, tile_cells
    )
    inverse_table = jnp.concatenate([cosines, sines], axis=0)
    spectral_terms = jnp.einsum(
        "cum,ju->cjm", self_tiles, inverse_table, preferred_element_type=jnp.float32
    )
    self_spectral = jnp.stack(
        [
            (spectral_terms[0, :momenta] + spectral_terms[1, momenta:]) * norm_factor,
            (spectral_terms[1, :momenta] - spectral_terms[0, momenta:]) * norm_factor,
            (spectral_terms[2, :momenta] + spectral_terms[3, momenta:]) * norm_factor,
            (spectral_terms[3, :momenta] - spectral_terms[2, momenta:]) * norm_factor,
        ]
    ).astype(jnp.bfloat16)
    self_moment = spread_times(
        regroup(pack_blocks(self_spectral, row_parts, col_parts)), tile_rows, tile_cols
    )
    lower_mask = time_steps[None, :] <= time_steps[:, None]
    upper_mask = time_steps[:, None] <= time_steps[None, :]
    retarded = jnp.where(
        lower_mask, self_moment[2:4].astype(jnp.float32) - self_moment[0:2].astype(jnp.float32), 0.0
    ).astype(jnp.bfloat16)
    advanced = jnp.where(
        upper_mask,
        green_moment[0:2].astype(jnp.float32) - green_moment[2:4].astype(jnp.float32),
        0.0,
    ).astype(jnp.bfloat16)
    lesser_out = collide(
        retarded[0],
        retarded[1],
        self_moment[0],
        self_moment[1],
        green_moment[0],
        green_moment[1],
        advanced[0],
        advanced[1],
    )
    greater_out = collide(
        retarded[0],
        retarded[1],
        self_moment[2],
        self_moment[3],
        green_moment[2],
        green_moment[3],
        advanced[0],
        advanced[1],
    )
    collisions = (
        jnp.stack([lesser_out[0], lesser_out[1], greater_out[0], greater_out[1]]) * step_size
    ).astype(jnp.bfloat16)
    out_tiles = regroup(gather_tiles(collisions, row_parts, col_parts)).reshape(
        4, momenta, tile_cells
    )
    out_tiles = out_tiles.transpose(0, 2, 1).reshape(4, tile_rows, tile_cols, momenta)
    return (out_tiles[0:2], out_tiles[2:4])


def vmem_params(mebibytes=48):
    return pltpu.CompilerParams(vmem_limit_bytes=mebibytes * 1024 * 1024)


def unread(arrays):
    return [pl.BlockSpec(memory_space=pl.ANY)] * len(arrays)


def whole(count):
    return [pl.BlockSpec(memory_space=pltpu.VMEM)] * count


def weight():
    return pl.CostEstimate(flops=10**11, bytes_accessed=2**20, transcendentals=0)


def scalars():
    return [pl.BlockSpec(memory_space=pltpu.SMEM)]


def spread_kernel(lesser, greater, out, lines):
    _, rows, _, count = lesser.shape
    for g, tile in enumerate((lesser, greater)):
        for t in range(rows):
            slab = jnp.concatenate([tile[0, t], tile[1, t]], axis=0)
            lines[pl.ds(g * rows + t, count, stride=2 * rows), :] = slab.astype(F32).T
    out[...] = lines[...].astype(BF16)


def spread(tiles, first, count):
    _, rows, cols, _ = tiles[0].shape
    height = 2 * rows * LANES
    tile_spec = pl.BlockSpec((2, rows, cols, LANES), lambda p: (0, 0, 0, first // LANES + p))
    return pl.pallas_call(
        spread_kernel,
        grid=(count // LANES,),
        out_shape=pltpu.HBM((count * 2 * rows, 2 * cols), BF16),
        in_specs=[tile_spec, tile_spec],
        out_specs=pl.BlockSpec((height, 2 * cols), lambda p: (p, 0)),
        scratch_shapes=[pltpu.VMEM((height, 2 * cols), F32)],
        compiler_params=vmem_params(58),
        name="spread",
    )(*tiles)


def collect_kernel(blocks_ref, lesser, greater, lines):
    _, rows, cols, count = lesser.shape
    blocks, height, _ = blocks_ref.shape
    for block in range(blocks):
        lines[block * height : (block + 1) * height] = blocks_ref[block].astype(F32)
    for k in range(2 * rows):
        slab = lines[pl.ds(k, count, stride=2 * rows), :].T.astype(BF16)
        out = lesser if k < rows else greater
        out[0, k % rows] = slab[:cols]
        out[1, k % rows] = slab[cols:]


def collect(blocks, tile_shape):
    shape = jax.ShapeDtypeStruct(tile_shape, BF16)
    sources, lines, lanes = blocks.shape
    height = lines // PARTS
    block_shape = tile_shape[:3] + (tile_shape[3] // PARTS,)
    tile_spec = pl.BlockSpec(block_shape, lambda p: (0, 0, 0, p))
    return pl.pallas_call(
        collect_kernel,
        grid=(PARTS,),
        out_shape=(shape, shape),
        in_specs=[pl.BlockSpec((sources, height, lanes), lambda p: (0, p, 0))],
        out_specs=(tile_spec, tile_spec),
        scratch_shapes=[pltpu.VMEM((sources * height, lanes), F32)],
        compiler_params=vmem_params(),
        name="collect",
    )(blocks)


def table_kernel(column_ref, table, inverse):
    momenta = column_ref.shape[0]
    positions = lax.broadcasted_iota(jnp.int32, (momenta, momenta), 1)
    phases = (column_ref[...] * positions % momenta).astype(F32) * (2.0 * math.pi / momenta)
    cosines = jnp.cos(phases).astype(BF16)
    sines = jnp.sin(phases).astype(BF16)
    inverse[:momenta, :momenta] = cosines
    inverse[:momenta, momenta:] = sines
    inverse[momenta:, :momenta] = -sines
    inverse[momenta:, momenta:] = cosines
    cosines = cosines.astype(F32).T.astype(BF16)
    sines = sines.astype(F32).T.astype(BF16)
    table[:momenta, :momenta] = cosines
    table[:momenta, momenta:] = -sines
    table[momenta:, :momenta] = sines
    table[momenta:, momenta:] = cosines


def make_tables(lattice_map):
    momenta = lattice_map.shape[0]
    shape = jax.ShapeDtypeStruct((2 * momenta, 2 * momenta), BF16)
    return pl.pallas_call(
        table_kernel,
        out_shape=(shape, shape),
        in_specs=whole(1),
        out_specs=tuple(whole(2)),
        compiler_params=vmem_params(),
        name="make_tables",
    )(lattice_map[:, None])


def site_kernel(norm_factor, lesser, greater, table, *rest):
    out = rest[-1]
    _, rows, cols, _ = lesser.shape
    wide = 4 * cols
    for pair in range(rows // 2):
        slabs = [
            jnp.concatenate([tile[0, t], tile[1, t]], axis=1)
            for t in (2 * pair, 2 * pair + 1)
            for tile in (lesser, greater)
        ]
        product = lax.dot_general(
            table[...],
            jnp.concatenate(slabs, axis=0),
            (((1,), (1,)), ((), ())),
            preferred_element_type=F32,
        )
        out[:, pair * wide : (pair + 1) * wide] = (product * norm_factor).astype(BF16)


def to_sites(tiles, table, norm_factor, after):
    _, rows, cols, momenta = tiles[0].shape
    return pl.pallas_call(
        functools.partial(site_kernel, norm_factor),
        out_shape=jax.ShapeDtypeStruct((2 * momenta, rows * 2 * cols), BF16),
        in_specs=whole(3) + unread(after),
        out_specs=whole(1)[0],
        compiler_params=vmem_params(24),
        name="to_sites",
    )(*tiles, table, *after)


def cross_kernel(rows, half_ref, own, far, *rest):
    out, mark = rest[-2:]
    mark[...] = jnp.zeros_like(mark)
    half = half_ref[0]
    blocks = far.shape[0]
    cols = blocks * rows
    for at in range(far.shape[1] // (2 * rows)):
        span = slice(at * 2 * rows, (at + 1) * 2 * rows)
        for source, offset, target in ((own, half * blocks, half), (far, 0, 1 - half)):
            loaded = [source[offset + block, span].astype(F32) for block in range(blocks)]
            stacked = jnp.concatenate(
                [lines[rows:] for lines in loaded] + [lines[:rows] for lines in loaded], axis=0
            )
            turned = stacked.T
            for block in range(blocks):
                out[target * blocks + block, span] = jnp.concatenate(
                    [
                        turned[block * rows : (block + 1) * rows],
                        turned[cols + block * rows : cols + (block + 1) * rows],
                    ],
                    axis=0,
                ).astype(BF16)


def to_crossed(half, own, far, rows, after, cost):
    sources, lines, lanes = own.shape
    blocks = far.shape[0]
    step = lines // STEPS
    spec = pl.BlockSpec((sources, step, lanes), lambda p: (0, p, 0))
    far_spec = pl.BlockSpec((blocks, step, lanes), lambda p: (0, p, 0))
    return pl.pallas_call(
        functools.partial(cross_kernel, rows),
        grid=(STEPS,),
        out_shape=(
            pltpu.HBM(own.shape, BF16),
            jax.ShapeDtypeStruct((8, LANES), F32),
        ),
        in_specs=scalars() + [spec, far_spec] + unread(after),
        out_specs=(spec, pl.BlockSpec((8, LANES), lambda p: (0, 0))),
        compiler_params=vmem_params(),
        cost_estimate=cost,
        name="to_crossed",
    )(half, own, far, *after)


def gate_kernel(*refs):
    del refs


def gate(array, after):
    return pl.pallas_call(
        gate_kernel,
        out_shape=jax.ShapeDtypeStruct(array.shape, array.dtype),
        in_specs=unread([array, *after]),
        out_specs=unread([array])[0],
        input_output_aliases={0: 0},
        name="gate",
    )(array, *after)


def mirrored_term(columns, read, first, count):
    wide = columns.shape[1] // 2
    rights = []
    for t in (first, first + 1):
        real = read[pl.ds(t, wide, stride=2 * count), :]
        imaginary = -read[pl.ds(count + t, wide, stride=2 * count), :]
        rights.append(jnp.concatenate([real, imaginary], axis=0).astype(BF16))
    return jnp.dot(columns, jnp.concatenate(rights, axis=1), preferred_element_type=F32)


def part_columns(table, part, parts):
    momenta = table.shape[1] // 2
    width = momenta // parts
    return jnp.concatenate(
        [
            table[:, part * width : (part + 1) * width],
            table[:, momenta + part * width : momenta + (part + 1) * width],
        ],
        axis=1,
    )


def mirror_kernel(part, parts, count, crossed, table, inverse, out, columns, handed, read):
    read[...] = crossed[...].astype(F32)
    wide = 2 * crossed.shape[1]
    own = part_columns(table, part, parts)
    for pair in range(count // 2):
        out[:, pair * wide : (pair + 1) * wide] = mirrored_term(own, read, 2 * pair, count)
    columns[...] = part_columns(table, parts - 1, parts)
    handed[...] = inverse[...]


def to_mirror(crossed, table, inverse, part, parts, count):
    lines, lanes = crossed.shape
    size = table.shape[0]
    return pl.pallas_call(
        functools.partial(mirror_kernel, part, parts, count),
        out_shape=(
            jax.ShapeDtypeStruct((size, count * lanes), F32),
            jax.ShapeDtypeStruct((size, size // parts), BF16),
            jax.ShapeDtypeStruct((size, size), BF16),
        ),
        in_specs=whole(3),
        out_specs=tuple(whole(3)),
        scratch_shapes=[pltpu.VMEM((lines, lanes), F32)],
        compiler_params=vmem_params(24),
        name="to_mirror",
    )(crossed, table, inverse)


def sigma_kernel(
    norm_factor, mirror, crossed, sites, columns, inverse, coupling, out, read, written
):
    count = coupling.shape[0]
    momenta = inverse.shape[0] // 2
    read[...] = crossed[...].astype(F32)
    for first in range(0, count, 2):
        span = slice(first * LANES, (first + 2) * LANES)
        other = mirrored_term(columns[...], read, first, count) + mirror[:, span]
        other = (other * norm_factor).astype(BF16).astype(F32)
        self_real, self_imaginary = second_born(
            sites[:momenta, span].astype(F32),
            sites[momenta:, span].astype(F32),
            other[:momenta],
            -other[momenta:],
            jnp.concatenate([coupling[t : t + 1] for t in (first, first + 1)], axis=1),
        )
        product = jnp.dot(
            inverse[...],
            jnp.concatenate([self_real, self_imaginary], axis=0).astype(BF16),
            preferred_element_type=F32,
        )
        product = product * norm_factor
        for at in range(2):
            for part in range(2):
                written[pl.ds(part * count + first + at, momenta, stride=2 * count), :] = product[
                    part * momenta : (part + 1) * momenta, at * LANES : (at + 1) * LANES
                ]
    blocks, height, _ = out.shape
    height = height // PARTS
    for part in range(PARTS):
        for block in range(blocks):
            start = (part * blocks + block) * height
            out[block, part * height : (part + 1) * height] = written[
                start : start + height
            ].astype(BF16)


def to_sigma(mirror, crossed, sites, columns, inverse, coupling, norm_factor, blocks):
    lines, lanes = crossed.shape
    return pl.pallas_call(
        functools.partial(sigma_kernel, norm_factor),
        out_shape=pltpu.HBM((blocks, PARTS * lines // blocks, lanes), BF16),
        in_specs=whole(6),
        out_specs=whole(1)[0],
        scratch_shapes=[pltpu.VMEM((lines, lanes), F32), pltpu.VMEM((PARTS * lines, lanes), F32)],
        compiler_params=vmem_params(34),
        name="to_sigma",
    )(mirror, crossed, sites, columns, inverse, coupling)


def rights_kernel(rows, half_ref, own, near_ref, away_ref, *rest):
    out = rest[-1]
    half = half_ref[0]
    blocks = near_ref.shape[0]
    lanes = own.shape[2]
    cols = lanes // 2
    near = half * cols
    away = (1 - half) * cols
    row_at = lax.broadcasted_iota(jnp.int32, (lanes, 2 * lanes), 0)
    inner_times = jnp.where(row_at < cols, near + row_at, away + row_at - cols)
    lane_at = lax.broadcasted_iota(jnp.int32, (lanes, 2 * lanes), 1)
    last_times = jnp.where(lane_at < lanes, near, away) + lane_at % cols
    keep = inner_times <= last_times
    for at in range(out.shape[0]):
        span = slice(at * 2 * rows, (at + 1) * 2 * rows)

        def stacked(read):
            loaded = [read(block).astype(F32) for block in range(blocks)]
            return [
                jnp.concatenate([lines[g * rows : (g + 1) * rows] for lines in loaded], axis=0)
                for g in range(2)
            ]

        own_near = stacked(lambda block: own[half * blocks + block, span])
        own_away = stacked(lambda block: own[(1 - half) * blocks + block, span])
        far_near = stacked(lambda block: near_ref[block, span])
        far_away = stacked(lambda block: away_ref[0, block, span])
        greens = [
            jnp.concatenate(
                [
                    jnp.concatenate([own_near[g], own_away[g]], axis=1),
                    jnp.concatenate([far_near[g], far_away[g]], axis=1),
                ],
                axis=0,
            )
            for g in range(2)
        ]
        out[at, :lanes] = greens[0].astype(BF16)
        out[at, lanes : 2 * lanes] = greens[1].astype(BF16)
        out[at, 2 * lanes :] = jnp.where(keep, greens[0] - greens[1], 0.0).astype(BF16)


STEPS = 2
PARTS = 2


def make_rights(half, own, far_near, far_away, rows, part, before):
    sources, lines, lanes = own.shape
    blocks = far_near.shape[0]
    steps = STEPS // PARTS
    step = lines // steps
    momenta = step // (2 * rows)
    return pl.pallas_call(
        functools.partial(rights_kernel, rows),
        grid=(steps,),
        out_shape=jax.ShapeDtypeStruct((STEPS * momenta, 3 * lanes, 2 * lanes), BF16),
        in_specs=scalars()
        + [
            pl.BlockSpec((sources, step, lanes), lambda p: (0, p, 0)),
            pl.BlockSpec((blocks, step, lanes), lambda p: (0, p, 0)),
            pl.BlockSpec((1, blocks, step, lanes), lambda p: (part, 0, p, 0)),
        ]
        + unread(before),
        out_specs=pl.BlockSpec(
            (momenta, 3 * lanes, 2 * lanes), lambda p: (part * steps + p, 0, 0)
        ),
        input_output_aliases={4: 0} if part > 0 else {},
        compiler_params=vmem_params(),
        cost_estimate=weight(),
        name="make_rights",
    )(half, own, far_near, far_away, *before)


def volterra_kernel(rows, half_ref, sigma, rights, out):
    half = half_ref[0]
    blocks = sigma.shape[0] // 2
    lanes = sigma.shape[2]
    cols = lanes // 2
    near = half * cols
    away = (1 - half) * cols
    here = half * blocks
    there = (1 - half) * blocks
    first_times = near + lax.broadcasted_iota(jnp.int32, (cols, lanes), 0)
    left_lane = lax.broadcasted_iota(jnp.int32, (cols, lanes), 1)
    low_lanes = left_lane < cols
    left_times = jnp.where(low_lanes, near + left_lane, away + left_lane - cols)
    keep_left = left_times <= first_times
    for at in range(rights.shape[0]):
        span = slice(at * 2 * rows, (at + 1) * 2 * rows)

        def stacked(offset):
            loaded = [sigma[offset + block, span].astype(F32) for block in range(blocks)]
            return [
                jnp.concatenate([lines[part * rows : (part + 1) * rows] for lines in loaded], axis=0)
                for part in range(2)
            ]

        sigma_near = stacked(here)
        sigma_away = stacked(there)
        retarded = []
        lefts = [[], []]
        for part in range(2):
            lesser = jnp.where(
                low_lanes, sigma_near[part], pltpu.roll(sigma_away[part], cols, 1)
            )
            greater = jnp.where(
                low_lanes, pltpu.roll(sigma_near[part], cols, 1), sigma_away[part]
            )
            retarded.append(jnp.where(keep_left, greater - lesser, 0.0))
            lefts[0].append(lesser)
            lefts[1].append(greater)
        retarded = jnp.concatenate(retarded, axis=0).astype(BF16)
        results = []
        for g in range(2):
            left = jnp.concatenate(
                [retarded, jnp.concatenate(lefts[g], axis=0).astype(BF16)], axis=1
            )
            right = jnp.concatenate(
                [rights[at, g * lanes : (g + 1) * lanes], rights[at, 2 * lanes :]], axis=0
            )
            product = jnp.dot(left, right, preferred_element_type=F32)
            sides = []
            for side in range(2):
                straight = product[:cols, side * lanes : (side + 1) * lanes]
                turned = pltpu.roll(product[cols:, side * lanes : (side + 1) * lanes], cols, 1)
                sides.append((straight + jnp.where(low_lanes, -turned, turned)) * step_size)
            results.append(sides)
        for block in range(blocks):
            lines = slice(block * rows, (block + 1) * rows)
            for side, offset in enumerate((here, there)):
                out[offset + block, span] = jnp.concatenate(
                    [results[0][side][lines], results[1][side][lines]], axis=0
                ).astype(BF16)


def volterra(half, sigma, rights, rows):
    sources, lines, lanes = sigma.shape
    step = lines // STEPS
    momenta = step // (2 * rows)
    spec = pl.BlockSpec((sources, step, lanes), lambda p: (0, p, 0))
    return pl.pallas_call(
        functools.partial(volterra_kernel, rows),
        grid=(STEPS,),
        out_shape=jax.ShapeDtypeStruct(sigma.shape, BF16),
        in_specs=scalars()
        + [spec, pl.BlockSpec((momenta, 3 * lanes, 2 * lanes), lambda p: (p, 0, 0))],
        out_specs=spec,
        compiler_params=vmem_params(),
        name="volterra",
    )(half, sigma, rights)


def halved_body(green_lesser, green_greater, lattice_map, time_offset):
    _, rows, cols, momenta = green_lesser.shape
    half = lax.axis_index("half")
    line = lax.axis_index("line")
    side = lax.axis_index("tcol")
    lines = lax.axis_size("line")
    group = lines * lax.axis_size("tcol")
    window = rows * lines * lax.axis_size("half")
    norm_factor = 1.0 / math.sqrt(momenta)
    tiles = (green_lesser, green_greater)
    half_at = half[None]
    count = momenta // PARTS

    def exchange(blocks):
        return lax.all_to_all(blocks, ("tcol", "line"), 0, 0, tiled=True)

    def blocked(rows_array):
        return rows_array.reshape(group, rows_array.shape[0] // group, rows_array.shape[1])

    def swap(array):
        return lax.ppermute(array, "half", [(0, 1), (1, 0)])

    table, inverse = make_tables(lattice_map)
    time_steps = jnp.arange(window, dtype=jnp.int32)
    coupling_line = 1.0 + drive_depth * jnp.cos(
        ((time_offset[0] + time_steps) % PERIOD).astype(F32) * (2.0 * math.pi / PERIOD)
    )
    first = lax.dynamic_slice_in_dim(coupling_line, (half * lines + line) * rows, rows)
    second = lax.dynamic_slice_in_dim(coupling_line, side * cols, cols)
    coupling = first[:, None] * jnp.concatenate([second, second])[None, :]

    spread_parts = [spread(tiles, part * count, count) for part in range(PARTS)]
    own = [exchange(blocked(spread_parts[0]))]
    for rows_array in spread_parts[1:]:
        own.append(exchange(gate(blocked(rows_array), [table, coupling])))
    far_near = [swap(lax.dynamic_slice_in_dim(blocks, (1 - half) * lines, lines)) for blocks in own]

    sent = []
    marks = []
    for part in range(PARTS):
        blocks, mark = to_crossed(
            half_at,
            own[part],
            far_near[part],
            rows,
            own[-1:] + marks[-1:],
            weight() if part > 0 else None,
        )
        sent.append(blocks)
        marks.append(mark)
    crossed = [exchange(blocks) for blocks in sent]
    kept = jnp.stack(
        [lax.dynamic_slice_in_dim(blocks, half * lines, lines) for blocks in own]
    )
    far_away = swap(gate(kept, marks[-1:] + crossed[:-1]))
    flat = [blocks.reshape(-1, 2 * cols) for blocks in crossed]
    sites = to_sites(tiles, table, norm_factor, marks[-1:])
    mirror, columns, handed = to_mirror(flat[0], table, inverse, 0, PARTS, rows)
    sigma_rows = to_sigma(mirror, flat[1], sites, columns, handed, coupling, norm_factor, group)
    sigma = exchange(sigma_rows)
    rights = []
    for part in range(PARTS):
        rights = [
            make_rights(
                half_at, own[part], far_near[part], far_away, rows, part, rights + [sigma_rows]
            )
        ]
    returned = exchange(volterra(half_at, sigma, rights[0], rows))
    return collect(returned, green_lesser.shape)


def solution(mesh):
    row_parts = mesh.shape["trow"]
    col_parts = mesh.shape["tcol"]

    def call(green_lesser, green_greater, lattice_map, time_offset):
        window, window_cols, momenta = green_lesser.shape[1:]
        rows = window // row_parts
        cols = window_cols // col_parts
        halved = (
            col_parts == 2
            and row_parts % 2 == 0
            and window == window_cols
            and 2 * cols == LANES
            and cols == rows * (row_parts // 2)
            and rows % 8 == 0
            and momenta % (2 * row_parts * STEPS) == 0
            and momenta % (PARTS * LANES) == 0
        )
        if halved:
            devices = mesh.devices.reshape(2, row_parts // 2, col_parts)
            used = Mesh(devices, ("half", "line", "tcol"))
            spec = P(None, ("half", "line"), "tcol", None)
            inner = halved_body
        else:
            used = mesh
            spec = P(None, "trow", "tcol", None)
            inner = general_body
        return jax.shard_map(
            inner, mesh=used, in_specs=(spec, spec, P(), P()), out_specs=(spec, spec), check_vma=False
        )(green_lesser, green_greater, lattice_map, time_offset)

    return call
```
